128 devices in a mesh: rep: 8 (over x_hi, y), shard: 16 (over z, x_lo, core).
Axes of the slice: x: 4 (x_hi: 2, x_lo: 2; x = x_hi * 2 + x_lo), y: 4, z: 4, core: 2. Of those that a mesh axis runs over, the one named last changes fastest.
Arguments:
- tokens: bfloat16 [16384, 2048], P(('rep', 'shard')), may hold values from -6 to 6
- ln_gain: bfloat16 [2048], P('shard'), may hold values from 0.5 to 1.5
- ln_shift: bfloat16 [2048], P('shard'), may hold values from -1.75 to 1.75
- qkv_weight: bfloat16 [2048, 6144], P('shard'), may hold values from -0.125 to 0.125
- qkv_bias: bfloat16 [6144], P('shard'), may hold values from -1.75 to 1.75
- dense_weight: bfloat16 [2048, 2048], P('shard'), may hold values from -1 to 1
- dense_bias: bfloat16 [2048], P('shard'), may hold values from -1.75 to 1.75
- fc1_weight: bfloat16 [2048, 8192], P('shard'), may hold values from -0.125 to 0.125
- fc1_bias: bfloat16 [8192], P('shard'), may hold values from -1.75 to 1.75
- fc2_weight: bfloat16 [8192, 2048], P('shard'), may hold values from -0.0625 to 0.0625
- fc2_bias: bfloat16 [2048], P('shard'), may hold values from -1.75 to 1.75
- cotangent: bfloat16 [16384, 2048], P(('rep', 'shard')), may hold values from -6 to 6
Outputs:
- layer_out: bfloat16 [16384, 2048], P(('rep', 'shard'))
- input_grad: float32 [16384, 2048], P(('rep', 'shard'))
- ln_gain_grad: float32 [2048], P('shard')
- ln_shift_grad: float32 [2048], P('shard')
- qkv_weight_grad: float32 [2048, 6144], P('shard')
- qkv_bias_grad: float32 [6144], P('shard')
- dense_weight_grad: float32 [2048, 2048], P('shard')
- dense_bias_grad: float32 [2048], P('shard')
- fc1_weight_grad: float32 [2048, 8192], P('shard')
- fc1_bias_grad: float32 [8192], P('shard')
- fc2_weight_grad: float32 [8192, 2048], P('shard')
- fc2_bias_grad: float32 [2048], P('shard')
The draws below stay inside these ranges and needn't reach their ends.
All inputs are finite; a program needn't handle non-finite values.
Results may differ from the reference program's by a relative error of at most 0.02.
Values may be sent and summed in bfloat16 or wider, within the bound.
No kernel may reach another device: no remote copies, remote signals or barrier semaphores. Data moves between devices by JAX's collectives and lax.ppermute only.
A program may use at most 448 MiB of HBM per device.

```python
import math
import jax
import jax.numpy as jnp
from jax import lax

D = 2048
HEADS = 32
HEAD_DIM = 64
ROTARY = 32
FF = 8192
SEQ = 2048
TOKENS = 16384


def levels(key, extent, cuts, low, high):
    loudness, own = 1.0, jax.random.fold_in(key, 6)
    for axis_at, blocks in cuts:
        draws = jnp.exp(jax.random.uniform(jax.random.fold_in(own, axis_at), (blocks,), jnp.float32, low / len(cuts), high / len(cuts)))
        loudness = loudness * jnp.repeat(draws, extent[axis_at] // blocks).reshape([-1 if axis == axis_at else 1 for axis in range(len(extent))])
    return loudness


def centred(stream_key, extent, width, limit, pieces=(), held_as=jnp.bfloat16):
    drawn = jax.random.normal(stream_key, extent, jnp.float32) * width
    if len(pieces) > 0:
        drawn = levels(stream_key, extent, pieces, -0.22, 0.18) * drawn
    return jnp.clip(drawn, min=-limit, max=limit).astype(held_as)


def setup_inputs(seed: int = 0) -> dict:
    arg_keys = jax.random.split(jax.random.key(seed), 13)
    return {
        "tokens": centred(arg_keys[0], (TOKENS, D), 1.0, 6.0, ((0, 128),)),
        "ln_gain": jnp.clip(1.0 + 0.1 * jax.random.normal(arg_keys[1], (D,), jnp.float32), 0.5, 1.5).astype(jnp.bfloat16),
        "ln_shift": centred(arg_keys[2], (D,), 0.3, 1.75, ((0, 16),)),
        "qkv_weight": centred(arg_keys[3], (D, 3 * D), D ** -0.5, 0.125, ((0, 16),)),
        "qkv_bias": centred(arg_keys[4], (3 * D,), 0.3, 1.75, ((0, 16),)),
        "dense_weight": centred(arg_keys[5], (D, D), (max(D // 64, 1)) ** -0.5, 1.0, ((0, 16),)),
        "dense_bias": centred(arg_keys[6], (D,), 0.3, 1.75, ((0, 16),)),
        "fc1_weight": centred(arg_keys[7], (D, FF), D ** -0.5, 0.125, ((0, 16),)),
        "fc1_bias": centred(arg_keys[8], (FF,), 0.3, 1.75, ((0, 16),)),
        "fc2_weight": centred(arg_keys[9], (FF, D), FF ** -0.5, 0.0625, ((0, 16),)),
        "fc2_bias": centred(arg_keys[10], (D,), 0.3, 1.75, ((0, 16),)),
        "cotangent": centred(arg_keys[11], (TOKENS, D), 1.0, 6.0, ((0, 128),)),
    }


@jax.custom_vjp
def low(v):
    return lax.optimization_barrier(v.astype(jnp.bfloat16)).astype(jnp.float32)

@jax.custom_vjp
def low_back(v):
    return v

def low_keep(v):
    return (low(v), None)

def low_pass(kept, grad):
    return (grad,)

def back_keep(v):
    return (v, None)

def back_low(kept, grad):
    return (low(grad),)
low.defvjp(low_keep, low_pass)
low_back.defvjp(back_keep, back_low)
HIGHEST = lax.Precision.HIGHEST

def matmul(left, right):
    return jnp.dot(left, right, precision=HIGHEST, preferred_element_type=jnp.float32)

def rotary_angles(length):
    freq_index = jnp.arange(ROTARY // 2, dtype=jnp.float32)
    inverse_freq = jnp.exp(freq_index * (-2.0 * math.log(10000.0) / ROTARY))
    position = jnp.arange(length, dtype=jnp.float32)
    angles = position[:, None] * inverse_freq[None, :]
    return (jnp.cos(angles), jnp.sin(angles))

def rotate(values, cosine, sine):
    first = values[..., :ROTARY // 2]
    second = values[..., ROTARY // 2:ROTARY]
    remainder = values[..., ROTARY:]
    cosine = cosine[:, None, :]
    sine = sine[:, None, :]
    return jnp.concatenate([first * cosine - second * sine, second * cosine + first * sine, remainder], axis=-1)

def attend_block(query_block, start, keys, values):
    rows = query_block.shape[0]
    length = keys.shape[0]
    score_scale = HEAD_DIM ** (-0.5)
    scores = jnp.einsum('qhd,khd->hqk', query_block, keys, precision=HIGHEST) * score_scale
    scores = low_back(scores)
    query_place = start + lax.broadcasted_iota(jnp.int32, (rows, length), 0)
    key_place = lax.broadcasted_iota(jnp.int32, (rows, length), 1)
    causal = query_place >= key_place
    scores = jnp.where(causal[None], scores, -1e+30)
    top_score = lax.optimization_barrier(jnp.max(scores, axis=-1, keepdims=True))
    weights = jnp.exp(scores - top_score)
    probs = low(weights / lax.optimization_barrier(jnp.sum(weights, axis=-1, keepdims=True)))
    return jnp.einsum('hqk,khd->qhd', probs, values, precision=HIGHEST)

def attend(triple):
    queries, keys, values = triple
    length = queries.shape[0]
    rows = min(512, length)
    blocks = queries.reshape(length // rows, rows, HEADS, HEAD_DIM)
    starts = (jnp.arange(length // rows, dtype=jnp.int32) * rows).astype(jnp.int32)
    checked = jax.checkpoint(attend_block)
    result = lax.map(lambda item: checked(item[0], item[1], keys, values), (blocks, starts))
    return result.reshape(length, HEADS, HEAD_DIM)

def forward(inputs, ln_gain, ln_shift, qkv_weight, qkv_bias, dense_weight, dense_bias, fc1_weight, fc1_bias, fc2_weight, fc2_bias):
    centered = inputs - lax.optimization_barrier(jnp.mean(inputs, axis=-1, keepdims=True))
    inv_std = lax.rsqrt(lax.optimization_barrier(jnp.mean(centered * centered, axis=-1, keepdims=True)) + 1e-05)
    normed = low(centered * inv_std * ln_gain + ln_shift)
    mixed = low_back(matmul(normed, qkv_weight) + qkv_bias)
    count = inputs.shape[0] // SEQ
    shaped = mixed.reshape(count, SEQ, 3, HEADS, HEAD_DIM)
    cosine, sine = rotary_angles(SEQ)
    queries = low(rotate(shaped[:, :, 0], cosine, sine))
    keys = low(rotate(shaped[:, :, 1], cosine, sine))
    values = low(shaped[:, :, 2])
    attended = lax.map(attend, (queries, keys, values))
    attended = low(low_back(attended.reshape(inputs.shape[0], D)))
    activated = low(jax.nn.gelu(low_back(matmul(normed, fc1_weight) + fc1_bias), approximate=True))
    attn_out = matmul(attended, dense_weight) + dense_bias
    mlp_out = matmul(activated, fc2_weight) + fc2_bias
    return inputs + attn_out + mlp_out

def reference(tokens, ln_gain, ln_shift, qkv_weight, qkv_bias, dense_weight, dense_bias, fc1_weight, fc1_bias, fc2_weight, fc2_bias, cotangent):
    floats = tuple((item.astype(jnp.float32) for item in (tokens, ln_gain, ln_shift, qkv_weight, qkv_bias, dense_weight, dense_bias, fc1_weight, fc1_bias, fc2_weight, fc2_bias)))
    output, pullback = jax.vjp(forward, *floats)
    grads = pullback(cotangent.astype(jnp.float32))
    return (output.astype(jnp.bfloat16), grads[0], grads[1], grads[2], grads[3], grads[4], grads[5], grads[6], grads[7], grads[8], grads[9], grads[10])
```

```python
import math

import jax
import jax.numpy as jnp
import numpy as np
from jax import lax
from jax.experimental import pallas as pl
from jax.experimental.pallas import tpu as pltpu
from jax.sharding import PartitionSpec as P

D = 2048
HEADS = 32
HEAD_DIM = 64
ROTARY = 32
FF = 8192
SEQ = 2048
T = 128
QKV = 384
FFL = 512
COLS = QKV + FFL
BF = jnp.bfloat16
F32 = jnp.float32
AXES = ("rep", "shard")
MIB = 1 << 20
LOG2E = math.log2(math.e)

PLACES = [
    (xh, y, z, xl, c)
    for xh in range(2)
    for y in range(4)
    for z in range(4)
    for xl in range(2)
    for c in range(2)
]


def flat(xh, y, z, xl, c):
    return (xh * 4 + y % 4) * 16 + (z % 4) * 4 + xl * 2 + c


def fetch_from(x, source):
    return lax.ppermute(x, AXES, [(flat(*source(*p)), flat(*p)) for p in PLACES])


def fetch(x, dz=0, dx=0, dc=0, dy=0, dh=0):
    return fetch_from(
        x, lambda xh, y, z, xl, c: (xh ^ dh, y + dy, z + dz, xl ^ dx, c ^ dc)
    )


def dot(a, b, ca=1, cb=0):
    return lax.dot_general(a, b, (((ca,), (cb,)), ((), ())), preferred_element_type=F32)


def add(*terms):
    total = terms[0].astype(F32)
    for term in terms[1:]:
        total = total + term.astype(F32)
    return total


def gather_group(own):
    half = own.shape[0] // 2
    a = {(0, 0): own}
    a[0, 1] = fetch(own, dx=1)
    a[1, 0] = fetch(own, dz=1)
    a[3, 0] = fetch(own, dz=-1)
    a[1, 1] = fetch(a[1, 0], dx=1)
    a[3, 1] = fetch(a[0, 1], dz=-1)
    a[2, 0] = fetch(a[1, 0], dz=1)
    first = fetch(a[1, 1][:half], dz=1)
    second = fetch(a[3, 1][half:], dz=-1)
    a[2, 1] = jnp.concatenate([first, second])
    return {k: (v, fetch(v, dc=1)) for k, v in a.items()}


CHIPS = [(dz, dx) for dz in range(4) for dx in range(2)]
WAVES = [[(2, 1)], [(1, 1), (3, 1), (2, 0)], [(1, 0), (3, 0), (0, 1)], [(0, 0)]]


def scatter_group(waves):
    q = {}
    for chips, (mine, other) in zip(WAVES, waves, strict=True):
        both = add(mine, fetch(other, dc=1)).astype(BF)
        for n, chip in enumerate(chips):
            q[chip] = both[n * T : (n + 1) * T]
    half = T // 2
    far = q[2, 1]
    a = fetch(far[:half], dz=-1)
    b = fetch(far[half:], dz=1)
    q11 = jnp.concatenate([add(q[1, 1][:half], a).astype(BF), q[1, 1][half:]])
    q31 = jnp.concatenate([q[3, 1][:half], add(q[3, 1][half:], b).astype(BF)])
    q10 = add(q[1, 0], fetch(q11, dx=1), fetch(q[2, 0], dz=-1)).astype(BF)
    q01 = add(q[0, 1], fetch(q31, dz=1)).astype(BF)
    return q[0, 0], fetch(q10, dz=-1), fetch(q[3, 0], dz=1), fetch(q01, dx=1)


def reduce_y(g):
    half = g[0].shape[0] // 2
    a = fetch(g[2][:half], dy=-1)
    b = fetch(g[2][half:], dy=1)
    g1 = jnp.concatenate([add(g[1][:half], a).astype(BF), g[1][half:]])
    g3 = jnp.concatenate([g[3][:half], add(g[3][half:], b).astype(BF)])
    return add(g[0], fetch(g1, dy=-1), fetch(g3, dy=1))


def gather_y(own):
    half = own.shape[0] // 2
    one, three = fetch(own, dy=1), fetch(own, dy=-1)
    two = jnp.concatenate([fetch(one[:half], dy=1), fetch(three[half:], dy=-1)])
    return [own, one, two, three]


def gather_rep(own):
    pair = jnp.concatenate([own, fetch(own, dh=1)])
    return jnp.concatenate(gather_y(pair))


def move_blocks(x, index, out_shape, out_block, out_map, in_block, in_map, grid, body=None):
    def kernel(index_ref, x_ref, o_ref):
        if body is None:
            o_ref[...] = x_ref[...].astype(o_ref.dtype)
        else:
            body(x_ref, o_ref)

    return pl.pallas_call(
        kernel,
        grid_spec=pltpu.PrefetchScalarGridSpec(
            num_scalar_prefetch=1,
            grid=grid,
            in_specs=[pl.BlockSpec(in_block, in_map)],
            out_specs=pl.BlockSpec(out_block, out_map),
        ),
        out_shape=out_shape,
        cost_estimate=pl.CostEstimate(
            flops=0,
            transcendentals=0,
            bytes_accessed=x.size * x.dtype.itemsize
            + math.prod(out_shape.shape) * out_shape.dtype.itemsize,
        ),
    )(index, x)


TQ = 512
TK = 512


def attention_kernel(
    place,
    mixed_ref,
    grad_ref,
    cos_ref,
    sin_ref,
    att_ref,
    out_ref,
    q_ref,
    k_ref,
    v_ref,
    do_ref,
    dq_ref,
    dk_ref,
    dv_ref,
    o_ref,
    s_ref,
    e_ref,
):
    lane = lax.broadcasted_iota(jnp.int32, (T, 128), 1)
    low_head = lane < HEAD_DIM
    first = (lane % HEAD_DIM) < ROTARY // 2

    def turned(x):
        return jnp.where(
            first, pltpu.roll(x, 128 - ROTARY // 2, 1), pltpu.roll(x, ROTARY // 2, 1)
        )

    def load(slot, _):
        rows = pl.ds(pl.multiple_of(slot * T, T), T)
        at = pl.ds(pl.multiple_of(place[slot] * T, T), T)
        c, s = cos_ref[at, :], sin_ref[at, :]
        query = mixed_ref[rows, 0:128]
        key = mixed_ref[rows, 128:256]
        query = (query * c + turned(query) * s).astype(BF).astype(F32) * (HEAD_DIM**-0.5)
        q_ref[0, at, :] = jnp.where(low_head, query, 0.0).astype(BF)
        q_ref[1, at, :] = jnp.where(low_head, 0.0, query).astype(BF)
        k_ref[at, :] = (key * c + turned(key) * s).astype(BF)
        v_ref[at, 0:128] = mixed_ref[rows, 256:384].astype(BF)
        v_ref[at, 128:256] = jnp.ones((T, 128), BF)
        grad = grad_ref[rows, :].astype(F32)
        do_ref[0, at, :] = jnp.where(low_head, grad, 0.0)
        do_ref[1, at, :] = jnp.where(low_head, 0.0, grad)
        dk_ref[at, :] = jnp.zeros((T, 128), F32)
        dv_ref[at, :] = jnp.zeros((T, 128), F32)
        return 0

    lax.fori_loop(0, 16, load, 0)

    lane_q = lax.broadcasted_iota(jnp.int32, (TQ, 128), 1)
    low_q = lane_q < HEAD_DIM

    def block(i, _):
        rows = pl.ds(pl.multiple_of(i * TQ, TQ), TQ)
        qs = [q_ref[h, rows, :] for h in range(2)]

        def scores(j, tops, masked):
            at = pl.ds(pl.multiple_of(j * TK, TK), TK)
            keys = k_ref[at, :]
            new = []
            for h in range(2):
                s = dot(qs[h], keys, 1, 1)
                if masked:
                    row = lax.broadcasted_iota(jnp.int32, (TQ, TK), 0)
                    col = lax.broadcasted_iota(jnp.int32, (TQ, TK), 1)
                    s = jnp.where(row >= col, s, -1e30)
                s_ref[h, :, at] = s
                top = tops[h]
                for n in range(TK // 128):
                    top = jnp.maximum(top, s[:, n * 128 : (n + 1) * 128])
                new.append(top)
            return tuple(new)

        low = jnp.full((TQ, 128), -1e30, F32)
        tops = lax.fori_loop(0, i, lambda j, t: scores(j, t, False), (low, low))
        tops = scores(i, tops, True)
        tops = [jnp.max(t, axis=1, keepdims=True) for t in tops]

        def weigh(j, sums):
            at = pl.ds(pl.multiple_of(j * TK, TK), TK)
            values = v_ref[at, :]
            new = []
            for h in range(2):
                e = jnp.exp2((s_ref[h, :, at] - tops[h]) * LOG2E).astype(BF)
                e_ref[h, :, at] = e
                new.append(sums[h] + dot(e, values))
            return tuple(new)

        zero = jnp.zeros((TQ, 256), F32)
        sums = lax.fori_loop(0, i + 1, weigh, (zero, zero))
        att, low_grads, deltas = [], [], []
        for h in range(2):
            inverse = 1.0 / sums[h][:, 128:]
            o = sums[h][:, :128] * inverse
            grad = do_ref[h, rows, :] * inverse
            att.append(o)
            deltas.append(jnp.sum(grad * o, axis=1, keepdims=True))
            low_grads.append(grad.astype(BF))
        o_ref[rows, :] = jnp.where(low_q, att[0], att[1]).astype(BF)

        def back(j, sums):
            at = pl.ds(pl.multiple_of(j * TK, TK), TK)
            keys = k_ref[at, :]
            values = v_ref[at, 0:128]
            new = []
            dk = dk_ref[at, :]
            dv = dv_ref[at, :]
            for h in range(2):
                e = e_ref[h, :, at]
                dp = dot(low_grads[h], values, 1, 1)
                ds = (e.astype(F32) * (dp - deltas[h])).astype(BF)
                new.append(sums[h] + dot(ds, keys))
                dk = dk + dot(ds, qs[h], 0, 0)
                dv = dv + dot(e, low_grads[h], 0, 0)
            dk_ref[at, :] = dk
            dv_ref[at, :] = dv
            return tuple(new)

        zero = jnp.zeros((TQ, 128), F32)
        dqs = lax.fori_loop(0, i + 1, back, (zero, zero))
        dq_ref[rows, :] = jnp.where(low_q, dqs[0], dqs[1]) * (HEAD_DIM**-0.5)
        return 0

    lax.fori_loop(0, SEQ // TQ, block, 0)

    def store(slot, _):
        rows = pl.ds(pl.multiple_of(slot * T, T), T)
        at = pl.ds(pl.multiple_of(place[slot] * T, T), T)
        c, s = cos_ref[at, :], sin_ref[at, :]
        att_ref[rows, :] = o_ref[at, :]
        dq, dk = dq_ref[at, :], dk_ref[at, :]
        out_ref[rows, 0:128] = (dq * c - turned(dq) * s).astype(BF)
        out_ref[rows, 128:256] = (dk * c - turned(dk) * s).astype(BF)
        out_ref[rows, 256:384] = dv_ref[at, :].astype(BF)
        return 0

    lax.fori_loop(0, 16, store, 0)


def attention(place, mixed, attended_grad, cosine, sine):
    vmem = pl.BlockSpec(memory_space=pltpu.VMEM)
    return pl.pallas_call(
        attention_kernel,
        in_specs=[pl.BlockSpec(memory_space=pltpu.SMEM)] + [vmem] * 4,
        out_specs=[vmem, vmem],
        out_shape=[
            jax.ShapeDtypeStruct((SEQ, 128), BF),
            jax.ShapeDtypeStruct((SEQ, QKV), BF),
        ],
        scratch_shapes=[
            pltpu.VMEM((2, SEQ, 128), BF),
            pltpu.VMEM((SEQ, 128), BF),
            pltpu.VMEM((SEQ, 256), BF),
            pltpu.VMEM((2, SEQ, 128), F32),
            pltpu.VMEM((SEQ, 128), F32),
            pltpu.VMEM((SEQ, 128), F32),
            pltpu.VMEM((SEQ, 128), F32),
            pltpu.VMEM((SEQ, 128), BF),
            pltpu.VMEM((2, TQ, SEQ), F32),
            pltpu.VMEM((2, TQ, SEQ), BF),
        ],
        compiler_params=pltpu.CompilerParams(vmem_limit_bytes=48 * MIB),
        cost_estimate=pl.CostEstimate(
            flops=14 * SEQ * SEQ * 64 * 2, transcendentals=SEQ * SEQ, bytes_accessed=8 * MIB
        ),
    )(place, mixed, attended_grad, cosine, sine)


def out_terms(chips, attended, activated, dense, fc2):
    order = jnp.array([dz * 2 + dx for dz, dx in chips], jnp.int32)
    n = len(chips)

    def kernel(order_ref, a_ref, f_ref, d_ref, w_ref, mine_ref, other_ref):
        total = dot(a_ref[...], d_ref[...]) + dot(f_ref[...], w_ref[...])
        mine_ref[...] = total[:T].astype(BF)
        other_ref[...] = total[T:].astype(BF)

    row = lambda i, order_ref: (order_ref[i], 0)
    whole = lambda i, order_ref: (0, 0)
    here = lambda i, order_ref: (i, 0)
    return pl.pallas_call(
        kernel,
        grid_spec=pltpu.PrefetchScalarGridSpec(
            num_scalar_prefetch=1,
            grid=(n,),
            in_specs=[
                pl.BlockSpec((2 * T, T), row),
                pl.BlockSpec((2 * T, FFL), row),
                pl.BlockSpec((T, D), whole),
                pl.BlockSpec((FFL, D), whole),
            ],
            out_specs=[pl.BlockSpec((T, D), here)] * 2,
        ),
        out_shape=[jax.ShapeDtypeStruct((n * T, D), BF)] * 2,
        compiler_params=pltpu.CompilerParams(vmem_limit_bytes=32 * MIB),
        cost_estimate=pl.CostEstimate(
            flops=2 * n * 2 * T * (T + FFL) * D,
            transcendentals=0,
            bytes_accessed=2 * (n * 2 * T * (T + FFL) + (T + FFL) * D + n * 2 * T * D),
        ),
    )(order, attended, activated, dense, fc2)


def normed_terms(chips, mixed_grad, pre_grad, weight, normed, shift):
    order = jnp.array([dz * 2 + dx for dz, dx in chips], jnp.int32)
    n = len(chips)

    def kernel(
        order_ref, m_ref, p_ref, w_ref, n_ref, s_ref, mine_ref, other_ref, gain_ref, total_ref
    ):
        total = dot(m_ref[...], w_ref[:, :QKV], 1, 1) + dot(p_ref[...], w_ref[:, QKV:], 1, 1)
        mine_ref[...] = total[:T].astype(BF)
        other_ref[...] = total[T:].astype(BF)
        unit = n_ref[...].astype(F32) - s_ref[...]
        gain = jnp.sum((total * unit).reshape(2 * T // 8, 8, D), axis=0)
        shifts = jnp.sum(total.reshape(2 * T // 8, 8, D), axis=0)

        @pl.when(pl.program_id(0) == 0)
        def _():
            gain_ref[...] = jnp.zeros_like(gain_ref)
            total_ref[...] = jnp.zeros_like(total_ref)

        gain_ref[...] += gain
        total_ref[...] += shifts

    row = lambda i, order_ref: (order_ref[i], 0)
    whole = lambda i, order_ref: (0, 0)
    here = lambda i, order_ref: (i, 0)
    return pl.pallas_call(
        kernel,
        grid_spec=pltpu.PrefetchScalarGridSpec(
            num_scalar_prefetch=1,
            grid=(n,),
            in_specs=[
                pl.BlockSpec((2 * T, QKV), row),
                pl.BlockSpec((2 * T, FFL), row),
                pl.BlockSpec((D, COLS), whole),
                pl.BlockSpec((2 * T, D), row),
                pl.BlockSpec((1, D), whole),
            ],
            out_specs=[pl.BlockSpec((T, D), here)] * 2 + [pl.BlockSpec((8, D), whole)] * 2,
        ),
        out_shape=[jax.ShapeDtypeStruct((n * T, D), BF)] * 2
        + [jax.ShapeDtypeStruct((8, D), F32)] * 2,
        compiler_params=pltpu.CompilerParams(vmem_limit_bytes=40 * MIB),
        cost_estimate=pl.CostEstimate(
            flops=2 * n * 2 * T * COLS * D,
            transcendentals=0,
            bytes_accessed=2 * (n * 2 * T * COLS + COLS * D + n * 4 * T * D),
        ),
    )(order, mixed_grad, pre_grad, weight, normed, shift)


def rotary_tables():
    lane = lax.broadcasted_iota(jnp.int32, (SEQ, 128), 1) % HEAD_DIM
    place = lax.broadcasted_iota(jnp.int32, (SEQ, 128), 0).astype(F32)
    freq = (lane % (ROTARY // 2)).astype(F32)
    angle = place * jnp.exp(freq * (-2.0 * math.log(10000.0) / ROTARY))
    turns = lane < ROTARY
    cosine = jnp.where(turns, jnp.cos(angle), 1.0)
    sine = jnp.where(turns, jnp.sin(angle), 0.0)
    return cosine, jnp.where(lane < ROTARY // 2, -sine, sine)


def body(
    tokens,
    ln_gain,
    ln_shift,
    qkv_weight,
    qkv_bias,
    dense_weight,
    dense_bias,
    fc1_weight,
    fc1_bias,
    fc2_weight,
    fc2_bias,
    cotangent,
):
    rep, shard = lax.axis_index("rep"), lax.axis_index("shard")
    xh, y = rep // 4, rep % 4
    z, xl, c = shard // 4, (shard // 2) % 2, shard % 2
    slots = [(dz, dx, dc) for dz in range(4) for dx in range(2) for dc in range(2)]
    token_place = jnp.stack(
        [((z + dz) % 4) * 4 + (xl ^ dx) * 2 + (c ^ dc) for dz, dx, dc in slots]
    ).astype(jnp.int32)
    row_place = jnp.stack(
        [((z + y + dy) % 4) * 4 + (xl ^ xh ^ dh) * 2 + (c ^ dc) for dy, dh, dc in slots]
    ).astype(jnp.int32)
    col_place = jnp.stack(
        [((z - y - dy) % 4) * 4 + (xl ^ xh ^ dh) * 2 + (c ^ dc) for dy, dh, dc in slots]
    ).astype(jnp.int32)
    part_place = jnp.stack(
        [((y + dy) % 4) * 2 + (xh ^ dh) for dy in range(4) for dh in range(2)]
    ).astype(jnp.int32)

    vectors = jnp.concatenate([qkv_bias, ln_gain, ln_shift, dense_bias, fc2_bias])
    vectors = jnp.pad(vectors[None, :], ((0, 7), (0, D - vectors.shape[0])))
    blocks = gather_group(jnp.concatenate([tokens, cotangent, vectors]))
    ordered = [blocks[dz, dx][dc] for dz, dx, dc in slots]
    all_tokens = jnp.concatenate([b[:T] for b in ordered])
    all_cot = jnp.concatenate([b[T : 2 * T] for b in ordered])
    vecs = jnp.concatenate([b[2 * T : 2 * T + 1, :COLS] for b in ordered])
    order = (token_place[None, :] == jnp.arange(16)[:, None]).astype(BF)
    vecs = dot(order, vecs)
    gain = vecs[:, 384:512].reshape(1, D)
    shift = vecs[:, 512:640].reshape(1, D)
    out_bias = (vecs[:, 640:768] + vecs[:, 768:896]).reshape(1, D)
    all_qkv_bias = vecs[:, :384].reshape(3 * D)
    own_qkv_bias = jnp.concatenate(
        [lax.dynamic_slice(all_qkv_bias, (part * D + shard * T,), (T,)) for part in range(3)]
    )

    to_chip = ((z - y) % 4) * 2 + (xl ^ xh)
    pieces = [
        lax.dynamic_slice(qkv_weight, (0, part * D + to_chip * 2 * T), (T, 2 * T))
        for part in range(3)
    ]
    pieces_fc1 = lax.dynamic_slice(fc1_weight, (0, to_chip * 2 * FFL), (T, 2 * FFL))
    for_cores = jnp.concatenate(
        [
            jnp.concatenate(
                [p[:, core * T : (core + 1) * T] for p in pieces]
                + [pieces_fc1[:, core * FFL : (core + 1) * FFL]],
                axis=1,
            )
            for core in range(2)
        ]
    )
    both = fetch_from(for_cores, lambda xh, y, z, xl, c: (xh, y, z + y, xl ^ xh, c))
    mine = lax.dynamic_slice(both, (c * T, 0), (T, COLS))
    other = lax.dynamic_slice(both, ((1 - c) * T, 0), (T, COLS))
    rows = gather_rep(jnp.concatenate([mine, fetch(other, dc=1)]))
    weight = move_blocks(
        rows,
        row_place,
        jax.ShapeDtypeStruct((D, COLS), BF),
        (T, COLS),
        lambda i, at: (at[i], 0),
        (T, COLS),
        lambda i, at: (i, 0),
        (16,),
    )
    cosine, sine = rotary_tables()

    inputs = all_tokens.astype(F32)
    centered = inputs - jnp.mean(inputs, axis=-1, keepdims=True)
    spread = lax.rsqrt(jnp.mean(centered * centered, axis=-1, keepdims=True) + 1e-05)
    normed = (centered * spread * gain + shift).astype(BF)

    pre = dot(normed, weight[:, QKV:]) + fc1_bias.astype(F32)[None, :]
    root = math.sqrt(2.0 / math.pi)
    squared = pre * pre
    tanh = jnp.tanh(root * pre * (1.0 + 0.044715 * squared))
    activated = (0.5 * pre * (1.0 + tanh)).astype(BF)
    slope = 0.5 * (1.0 + tanh) + 0.5 * pre * (1.0 - tanh * tanh) * root * (
        1.0 + 3 * 0.044715 * squared
    )
    pre_grad = (dot(all_cot, fc2_weight, 1, 1) * slope).astype(BF)
    fc1_bias_part = jnp.sum(pre_grad.astype(F32), axis=0)
    fc1_grad = dot(normed, pre_grad, 0, 0).astype(BF)
    fc2_grad = dot(activated, all_cot, 0, 0).astype(BF)

    mixed = dot(normed, weight[:, :QKV]) + own_qkv_bias[None, :]
    attended_grad = dot(all_cot, dense_weight, 1, 1).astype(BF)
    attended, mixed_grad = attention(token_place, mixed, attended_grad, cosine, sine)
    qkv_bias_part = jnp.sum(mixed_grad.astype(F32), axis=0)
    qkv_grad = dot(normed, mixed_grad, 0, 0).astype(BF)
    dense_grad = dot(attended, all_cot, 0, 0).astype(BF)

    terms = scatter_group(
        [out_terms(w, attended, activated, dense_weight, fc2_weight) for w in WAVES]
    )
    own = tokens.astype(F32)
    layer_out = (own + out_bias + add(*terms)).astype(BF)

    pieces = [normed_terms(w, mixed_grad, pre_grad, weight, normed, shift) for w in WAVES]
    normed_grad = add(*scatter_group([(p[0], p[1]) for p in pieces]))
    gain_part = jnp.sum(sum(p[2] for p in pieces), axis=0) / gain[0]
    shift_part = jnp.sum(sum(p[3] for p in pieces), axis=0)
    center = own - jnp.mean(own, axis=-1, keepdims=True)
    inv_std = lax.rsqrt(jnp.mean(center * center, axis=-1, keepdims=True) + 1e-05)
    unit = center * inv_std
    scaled = normed_grad * gain
    input_grad = cotangent.astype(F32) + inv_std * (
        scaled
        - jnp.mean(scaled, axis=-1, keepdims=True)
        - unit * jnp.mean(scaled * unit, axis=-1, keepdims=True)
    )

    def rows_for(grad):
        return move_blocks(
            grad,
            row_place,
            jax.ShapeDtypeStruct(grad.shape, BF),
            (T, grad.shape[1]),
            lambda i, at: (i, 0),
            (T, grad.shape[1]),
            lambda i, at: (at[i], 0),
            (16,),
        )

    def eighth(grad, dy, dh):
        at = ((y + dy) % 4) * 2 + (xh ^ dh)
        return lax.dynamic_slice(grad, (0, at * 256), (grad.shape[0], 256))

    def reduced(parts):
        total = reduce_y([jnp.concatenate(p) for p in parts])
        half = total.shape[0] // 2
        return add(total[:half], fetch(total[half:].astype(BF), dh=1)).astype(BF)

    def to_owner(part):
        stacked = jnp.concatenate([part[:T], fetch(part[T:], dc=1)])
        return fetch_from(stacked, lambda xh, y, z, xl, c: (xh, y, z - y, xl ^ xh, c))

    fc1_rows = rows_for(fc1_grad)
    early = []
    for dy in range(4):
        halves = []
        for dh in range(2):
            at = (dy * 2 + dh) * 2 * T
            part = eighth(fc2_grad, dy, dh)
            part = jnp.concatenate([part[:256], part[256:]], axis=1)
            halves.append(jnp.concatenate([fc1_rows[at : at + 2 * T], part]))
        early.append(halves)
    summed = reduced(early)
    early = gather_rep(jnp.concatenate([to_owner(summed[:256]), summed[256:]]))

    qkv_rows = rows_for(qkv_grad)
    late = []
    for dy in range(4):
        halves = []
        for dh in range(2):
            at = (dy * 2 + dh) * 2 * T
            part = eighth(dense_grad, dy, dh)
            part = jnp.concatenate([part[:, :128], part[:, 128:]])
            halves.append(jnp.concatenate([qkv_rows[at : at + 2 * T], part], axis=1))
        late.append(halves)
    summed = reduced(late)
    late = gather_rep(jnp.concatenate([to_owner(summed[:, :QKV]), summed[:, QKV:]], axis=1))

    fc1_total = move_blocks(
        early,
        col_place,
        jax.ShapeDtypeStruct((T, FF), F32),
        (T, FFL),
        lambda i, at: (0, at[i]),
        (T, FFL),
        lambda i, at: ((i // 2) * 4 + i % 2, 0),
        (16,),
    )

    def unfold_rows(x_ref, o_ref):
        o_ref[:256, :] = x_ref[:, :256].astype(F32)
        o_ref[256:, :] = x_ref[:, 256:].astype(F32)

    fc2_total = move_blocks(
        early,
        part_place,
        jax.ShapeDtypeStruct((FFL, D), F32),
        (FFL, 256),
        lambda i, at: (0, at[i]),
        (256, FFL),
        lambda i, at: (i * 2 + 1, 0),
        (8,),
        unfold_rows,
    )
    qkv_total = move_blocks(
        late,
        col_place,
        jax.ShapeDtypeStruct((T, 3 * D), F32),
        (T, 128),
        lambda i, j, at: (0, j * 16 + at[i]),
        (T, 128),
        lambda i, j, at: (i, j),
        (16, 3),
    )
    dense_total = move_blocks(
        late,
        part_place,
        jax.ShapeDtypeStruct((T, D), F32),
        (T, 128),
        lambda i, j, at: (0, at[i] * 2 + j),
        (T, 128),
        lambda i, j, at: (i * 2 + j, 3),
        (8, 2),
    )

    own_cot = lax.dynamic_slice(all_cot, (0, shard * T), (SEQ, T))
    out_bias_part = jnp.sum(own_cot.astype(F32), axis=0)
    biases = jnp.zeros((3 * D,), F32)
    for part in range(3):
        biases = lax.dynamic_update_slice(
            biases, qkv_bias_part[part * T : (part + 1) * T], (part * D + shard * T,)
        )
    vec = jnp.concatenate([gain_part, shift_part, biases]).reshape(80, 128)
    vec = vec + fetch(vec, dc=1)
    vec = vec + fetch(vec, dx=1)
    vec = (vec + fetch(vec, dz=2)) + (fetch(vec, dz=1) + fetch(vec, dz=-1))
    own_vec = jnp.concatenate(
        [
            lax.dynamic_slice(vec, (shard, 0), (1, 128)),
            lax.dynamic_slice(vec, (16 + shard, 0), (1, 128)),
            lax.dynamic_slice(vec, (32 + 3 * shard, 0), (3, 128)),
            fc1_bias_part.reshape(4, 128),
            out_bias_part.reshape(1, 128),
            jnp.zeros((6, 128), F32),
        ]
    )
    own_vec = own_vec + fetch(own_vec, dh=1)
    own_vec = (own_vec + fetch(own_vec, dy=2)) + (fetch(own_vec, dy=1) + fetch(own_vec, dy=-1))
    out_bias_total = own_vec[9]

    return (
        layer_out,
        input_grad,
        own_vec[0],
        own_vec[1],
        qkv_total,
        own_vec[2:5].reshape(QKV),
        dense_total,
        out_bias_total,
        fc1_total,
        own_vec[5:9].reshape(FFL),
        fc2_total,
        out_bias_total,
    )


def solution(mesh):
    return jax.shard_map(
        body,
        mesh=mesh,
        in_specs=(
            P(AXES, None),
            P("shard"),
            P("shard"),
            P("shard", None),
            P("shard"),
            P("shard", None),
            P("shard"),
            P("shard", None),
            P("shard"),
            P("shard", None),
            P("shard"),
            P(AXES, None),
        ),
        out_specs=(
            P(AXES, None),
            P(AXES, None),
            P("shard"),
            P("shard"),
            P("shard", None),
            P("shard"),
            P("shard", None),
            P("shard"),
            P("shard", None),
            P("shard"),
            P("shard", None),
            P("shard"),
        ),
        check_vma=False,
    )
```

```python
import math

import jax
import jax.numpy as jnp
import numpy as np
from jax import lax
from jax.experimental import pallas as pl
from jax.experimental.pallas import tpu as pltpu
from jax.sharding import PartitionSpec as P

D = 2048
HEADS = 32
HEAD_DIM = 64
ROTARY = 32
FF = 8192
SEQ = 2048
T = 128
QKV = 384
FFL = 512
COLS = QKV + FFL
BF = jnp.bfloat16
F32 = jnp.float32
AXES = ("rep", "shard")
MIB = 1 << 20
LOG2E = math.log2(math.e)

PLACES = [
    (xh, y, z, xl, c)
    for xh in range(2)
    for y in range(4)
    for z in range(4)
    for xl in range(2)
    for c in range(2)
]


def flat(xh, y, z, xl, c):
    return (xh * 4 + y % 4) * 16 + (z % 4) * 4 + xl * 2 + c


def fetch_from(x, source):
    return lax.ppermute(x, AXES, [(flat(*source(*p)), flat(*p)) for p in PLACES])


def fetch(x, dz=0, dx=0, dc=0, dy=0, dh=0):
    return fetch_from(
        x, lambda xh, y, z, xl, c: (xh ^ dh, y + dy, z + dz, xl ^ dx, c ^ dc)
    )


def dot(a, b, ca=1, cb=0):
    return lax.dot_general(a, b, (((ca,), (cb,)), ((), ())), preferred_element_type=F32)


def add(*terms):
    total = terms[0].astype(F32)
    for term in terms[1:]:
        total = total + term.astype(F32)
    return total


def gather_group(own):
    half = own.shape[0] // 2
    a = {(0, 0): own}
    a[0, 1] = fetch(own, dx=1)
    a[1, 0] = fetch(own, dz=1)
    a[3, 0] = fetch(own, dz=-1)
    a[1, 1] = fetch(a[1, 0], dx=1)
    a[3, 1] = fetch(a[0, 1], dz=-1)
    a[2, 0] = fetch(a[1, 0], dz=1)
    first = fetch(a[1, 1][:half], dz=1)
    second = fetch(a[3, 1][half:], dz=-1)
    pairs = {k: (v, fetch(v, dc=1)) for k, v in a.items()}
    pairs[2, 1] = ((first, second), (fetch(first, dc=1), fetch(second, dc=1)))
    return pairs


def group_pieces(pairs):
    arrays, rows = [], []
    for n, (dz, dx, dc) in enumerate(SLOTS):
        block = pairs[dz, dx][dc]
        parts = block if isinstance(block, tuple) else (block,)
        at = n * T
        for part in parts:
            arrays.append(part)
            rows.append((at, part.shape[0]))
            at += part.shape[0]
    return arrays, rows


SLOTS = [(dz, dx, dc) for dz in range(4) for dx in range(2) for dc in range(2)]
CHIPS = [(dz, dx) for dz in range(4) for dx in range(2)]
WAVES = [[(2, 1)], [(1, 1), (3, 1), (2, 0)], [(1, 0), (3, 0), (0, 1)], [(0, 0)]]


def scatter_group(waves):
    q = {}
    for chips, (mine, other) in zip(WAVES, waves, strict=True):
        both = add(mine, fetch(other, dc=1)).astype(BF)
        for n, chip in enumerate(chips):
            q[chip] = both[n * T : (n + 1) * T]
    half = T // 2
    far = q[2, 1]
    a = fetch(far[:half], dz=-1)
    b = fetch(far[half:], dz=1)
    q11 = jnp.concatenate([add(q[1, 1][:half], a).astype(BF), q[1, 1][half:]])
    q31 = jnp.concatenate([q[3, 1][:half], add(q[3, 1][half:], b).astype(BF)])
    q10 = add(q[1, 0], fetch(q11, dx=1), fetch(q[2, 0], dz=-1)).astype(BF)
    q01 = add(q[0, 1], fetch(q31, dz=1)).astype(BF)
    return q[0, 0], fetch(q10, dz=-1), fetch(q[3, 0], dz=1), fetch(q01, dx=1)


def reduce_y(g):
    half = g[0].shape[0] // 2
    a = fetch(g[2][:half], dy=-1)
    b = fetch(g[2][half:], dy=1)
    g1 = jnp.concatenate([add(g[1][:half], a).astype(BF), g[1][half:]])
    g3 = jnp.concatenate([g[3][:half], add(g[3][half:], b).astype(BF)])
    return add(g[0], fetch(g1, dy=-1), fetch(g3, dy=1))


def gather_rep(own):
    pair = jnp.concatenate([own, fetch(own, dh=1)])
    half = own.shape[0]
    one, three = fetch(pair, dy=1), fetch(pair, dy=-1)
    return pair, one, three, fetch(one[:half], dy=1), fetch(three[half:], dy=-1)


def of_rep(refs, dy, dh, n):
    own, one, three, first, second = refs
    if dy == 2:
        return (second if dh else first), 0
    return (own, one, None, three)[dy], dh * n


VMEM = pl.BlockSpec(memory_space=pltpu.VMEM)
SMEM = pl.BlockSpec(memory_space=pltpu.SMEM)
ANY = pl.BlockSpec(memory_space=pl.ANY)


def lanes(at, n):
    return pl.ds(pl.multiple_of(at * n, n), n)


def call(kernel, ins, outs, args, scratch=(), vmem=56, flops=0, nbytes=0, exps=0):
    return pl.pallas_call(
        kernel,
        in_specs=ins,
        out_specs=[VMEM] * len(outs),
        out_shape=[jax.ShapeDtypeStruct(*o) for o in outs],
        scratch_shapes=list(scratch),
        compiler_params=pltpu.CompilerParams(vmem_limit_bytes=vmem * MIB),
        cost_estimate=pl.CostEstimate(flops=flops, transcendentals=exps, bytes_accessed=nbytes),
    )(*args)


def backward_inputs(pieces, rows, fc2, dense, me):
    n = len(pieces)

    def kernel(me_ref, *refs):
        cot = refs[:n]
        fc2_ref, dense_ref, cot_ref, act_ref, att_ref, sum_ref, sems = refs[n:]
        copies = [
            pltpu.make_async_copy(
                cot[i], cot_ref.at[pl.ds(rows[i][0], rows[i][1])], sems.at[i]
            )
            for i in range(n)
        ]
        for copy in copies:
            copy.start()
        for copy in copies:
            copy.wait()

        def tile(i, total):
            at = lanes(i, 256)
            x = cot_ref[at, :]
            act_ref[at, :] = dot(x, fc2_ref[...], 1, 1)
            att_ref[at, :] = dot(x, dense_ref[...], 1, 1).astype(BF)
            own = cot_ref[at, lanes(me_ref[0], T)].astype(F32)
            return total + jnp.sum(own.reshape(32, 8, T), axis=0)

        sum_ref[...] = lax.fori_loop(0, 8, tile, jnp.zeros((8, T), F32))

    return call(
        kernel,
        [SMEM] + [ANY] * n + [VMEM] * 2,
        [((SEQ, D), BF), ((SEQ, FFL), F32), ((SEQ, T), BF), ((8, T), F32)],
        [me] + pieces + [fc2, dense],
        [pltpu.SemaphoreType.DMA((n,))],
        flops=2 * SEQ * D * (FFL + T),
        nbytes=20 * MIB,
    )


ROOT = math.sqrt(2.0 / math.pi)


def forward_inputs(pieces, rows, weights, bias, act_grad, token_place, row_place, me):
    n = len(pieces)

    def kernel(t_ref, r_ref, me_ref, *refs):
        tok = refs[:n]
        w_refs = refs[n : n + 5]
        (
            bias_ref,
            grad_ref,
            normed_ref,
            w_ref,
            act_ref,
            pre_ref,
            mixed_ref,
            vec_ref,
            own_ref,
            fc1b_ref,
            small_ref,
            flat_ref,
            sems,
        ) = refs[n + 5 :]
        copies = []
        for i in range(n):
            at, size = rows[i]
            copies.append(
                pltpu.make_async_copy(
                    tok[i].at[:, pl.ds(0, D)], normed_ref.at[pl.ds(at, size)], sems.at[len(copies)]
                )
            )
            if at % T == 0:
                copies.append(
                    pltpu.make_async_copy(
                        tok[i].at[pl.ds(0, 16), pl.ds(D, T)],
                        small_ref.at[pl.ds(at // T * 16, 16)],
                        sems.at[len(copies)],
                    )
                )
        for i, (dy, dh, dc) in enumerate(SLOTS):
            ref, at = of_rep(w_refs, dy, dh, 2 * T)
            copies.append(
                pltpu.make_async_copy(
                    ref.at[pl.ds(at + dc * T, T)],
                    w_ref.at[lanes(r_ref[i], T)],
                    sems.at[len(copies)],
                )
            )
        for copy in copies:
            copy.start()
        for copy in copies:
            copy.wait()

        for i in range(16):
            at = t_ref[i]
            small = small_ref[i * 16 : (i + 1) * 16, :].astype(F32)
            for part in range(3):
                flat_ref[0:1, lanes(at * 3 + part, T)] = small[part : part + 1]
            vec_ref[0:1, lanes(at, T)] = small[3:4]
            vec_ref[1:2, lanes(at, T)] = small[4:5]
            vec_ref[2:3, lanes(at, T)] = small[5:6] + small[6:7]
        for part in range(3):
            own_ref[0:1, part * T : (part + 1) * T] = flat_ref[
                0:1, lanes(part * 16 + me_ref[0], T)
            ]
        gain, shift = vec_ref[0:1, :], vec_ref[1:2, :]

        def norm(i, _):
            at = lanes(i, 16)
            x = normed_ref[at, :].astype(F32)
            x = x - jnp.sum(x, axis=1, keepdims=True) * (1.0 / D)
            scale = lax.rsqrt(jnp.sum(x * x, axis=1, keepdims=True) * (1.0 / D) + 1e-05)
            normed_ref[at, :] = (x * scale * gain + shift).astype(BF)
            return 0

        def tile(i, total):
            lax.fori_loop(i * 16, (i + 1) * 16, norm, 0)
            at = lanes(i, 256)
            x = normed_ref[at, :]
            mixed_ref[at, :] = dot(x, w_ref[:, :QKV]) + own_ref[...]
            pre = dot(x, w_ref[:, QKV:]) + bias_ref[...]
            squared = pre * pre
            tanh = jnp.tanh(ROOT * pre * (1.0 + 0.044715 * squared))
            act_ref[at, :] = (0.5 * pre * (1.0 + tanh)).astype(BF)
            slope = 0.5 * (1.0 + tanh) + 0.5 * pre * (1.0 - tanh * tanh) * ROOT * (
                1.0 + 3 * 0.044715 * squared
            )
            back = (grad_ref[at, :] * slope).astype(BF)
            pre_ref[at, :] = back
            return total + jnp.sum(back.astype(F32).reshape(32, 8, FFL), axis=0)

        fc1b_ref[...] = lax.fori_loop(0, 8, tile, jnp.zeros((8, FFL), F32))

    return call(
        kernel,
        [SMEM] * 3 + [ANY] * (n + 5) + [VMEM] * 2,
        [
            ((SEQ, D), BF),
            ((D, COLS), BF),
            ((SEQ, FFL), BF),
            ((SEQ, FFL), BF),
            ((SEQ, QKV), F32),
            ((8, D), F32),
            ((1, QKV), F32),
            ((8, FFL), F32),
        ],
        [token_place, row_place, me] + pieces + list(weights) + [bias, act_grad],
        [
            pltpu.VMEM((256, T), BF),
            pltpu.VMEM((1, 3 * D), F32),
            pltpu.SemaphoreType.DMA((n + 32,)),
        ],
        flops=2 * SEQ * D * COLS,
        nbytes=30 * MIB,
        exps=SEQ * FFL,
    )


def column_grads(normed, pre_grad, activated, cot, row_place, part_place, core):
    def kernel(r_ref, p_ref, core_ref, n_ref, g_ref, a_ref, c_ref, *outs):
        for dy in (2, 1, 3, 0):
            out = outs[dy]
            for dh in range(2):
                base = dh * 512
                chip = r_ref[(dy * 2 + dh) * 2] // 2
                rows = dot(n_ref[:, lanes(chip, 256)], g_ref[...], 0, 0).astype(BF)
                out[lanes(dh * 4 + core_ref[0], T), :] = rows[:T]
                out[lanes(dh * 4 + 1 - core_ref[0], T), :] = rows[T:]
                part = dot(a_ref[...], c_ref[:, lanes(p_ref[dy * 2 + dh], 256)], 0, 0).astype(BF)
                out[base + 256 : base + 512, 0:256] = part[:256]
                out[base + 256 : base + 512, 256:512] = part[256:]

    return call(
        kernel,
        [SMEM] * 3 + [VMEM] * 4,
        [((1024, 512), BF)] * 4,
        [row_place, part_place, core, normed, pre_grad, activated, cot],
        flops=4 * SEQ * D * FFL,
        nbytes=24 * MIB,
    )


def head_grads(normed, mixed_grad, attended, cot, row_place, part_place, core):
    def kernel(r_ref, p_ref, core_ref, n_ref, m_ref, a_ref, c_ref, *outs):
        for dy in (2, 1, 3, 0):
            out = outs[dy]
            for dh in range(2):
                base = dh * 256
                chip = r_ref[(dy * 2 + dh) * 2] // 2
                rows = dot(n_ref[:, lanes(chip, 256)], m_ref[...], 0, 0).astype(BF)
                out[lanes(dh * 2 + core_ref[0], T), 0:QKV] = rows[:T]
                out[lanes(dh * 2 + 1 - core_ref[0], T), 0:QKV] = rows[T:]
                part = dot(a_ref[...], c_ref[:, lanes(p_ref[dy * 2 + dh], 256)], 0, 0).astype(BF)
                out[base : base + T, QKV:] = part[:, :T]
                out[base + T : base + 2 * T, QKV:] = part[:, T:]

        def tile(i, total):
            rows = m_ref[lanes(i, 256), :].astype(F32)
            return total + jnp.sum(rows.reshape(32, 8, QKV), axis=0)

        outs[4][...] = lax.fori_loop(0, 8, tile, jnp.zeros((8, QKV), F32))

    return call(
        kernel,
        [SMEM] * 3 + [VMEM] * 4,
        [((512, 512), BF)] * 4 + [((8, QKV), F32)],
        [row_place, part_place, core, normed, mixed_grad, attended, cot],
        flops=2 * SEQ * D * (QKV + T),
        nbytes=20 * MIB,
    )


def place_columns(pieces, col_place, part_place):
    def kernel(c_ref, p_ref, *refs):
        fc1_ref, fc2_ref = refs[5:]
        for i, (dy, dh, dc) in enumerate(SLOTS):
            ref, at = of_rep(refs[:5], dy, dh, 512)
            fc1_ref[:, lanes(c_ref[i], FFL)] = ref[at + dc * T : at + (dc + 1) * T, :].astype(F32)
            if dc == 0:
                part = p_ref[dy * 2 + dh]
                fc2_ref[0:256, lanes(part, 256)] = ref[at + 256 : at + 512, 0:256].astype(F32)
                fc2_ref[256:512, lanes(part, 256)] = ref[at + 256 : at + 512, 256:512].astype(F32)

    return call(
        kernel,
        [SMEM] * 2 + [VMEM] * 5,
        [((T, FF), F32), ((FFL, D), F32)],
        [col_place, part_place] + list(pieces),
        nbytes=12 * MIB,
    )


def place_heads(pieces, col_place, part_place):
    def kernel(c_ref, p_ref, *refs):
        qkv_ref, dense_ref = refs[5:]
        for i, (dy, dh, dc) in enumerate(SLOTS):
            ref, at = of_rep(refs[:5], dy, dh, 256)
            rows = slice(at + dc * T, at + (dc + 1) * T)
            for part in range(3):
                qkv_ref[:, lanes(c_ref[i] + part * 16, T)] = ref[
                    rows, part * T : (part + 1) * T
                ].astype(F32)
            dense_ref[:, lanes(p_ref[dy * 2 + dh] * 2 + dc, T)] = ref[rows, QKV:].astype(F32)

    return call(
        kernel,
        [SMEM] * 2 + [VMEM] * 5,
        [((T, 3 * D), F32), ((T, D), F32)],
        [col_place, part_place] + list(pieces),
        nbytes=6 * MIB,
    )


TQ = 512
TK = 512


def attention_kernel(
    place,
    mixed_ref,
    grad_ref,
    cos_ref,
    sin_ref,
    att_ref,
    out_ref,
    q_ref,
    k_ref,
    v_ref,
    do_ref,
    dq_ref,
    dk_ref,
    dv_ref,
    o_ref,
    s_ref,
    e_ref,
):
    lane = lax.broadcasted_iota(jnp.int32, (T, 128), 1)
    low_head = lane < HEAD_DIM
    first = (lane % HEAD_DIM) < ROTARY // 2

    def turned(x):
        return jnp.where(
            first, pltpu.roll(x, 128 - ROTARY // 2, 1), pltpu.roll(x, ROTARY // 2, 1)
        )

    def load(slot, _):
        rows = pl.ds(pl.multiple_of(slot * T, T), T)
        at = pl.ds(pl.multiple_of(place[slot] * T, T), T)
        c, s = cos_ref[at, :], sin_ref[at, :]
        query = mixed_ref[rows, 0:128]
        key = mixed_ref[rows, 128:256]
        query = (query * c + turned(query) * s).astype(BF).astype(F32) * (HEAD_DIM**-0.5)
        q_ref[0, at, :] = jnp.where(low_head, query, 0.0).astype(BF)
        q_ref[1, at, :] = jnp.where(low_head, 0.0, query).astype(BF)
        k_ref[at, :] = (key * c + turned(key) * s).astype(BF)
        v_ref[at, 0:128] = mixed_ref[rows, 256:384].astype(BF)
        v_ref[at, 128:256] = jnp.ones((T, 128), BF)
        grad = grad_ref[rows, :].astype(F32)
        do_ref[0, at, :] = jnp.where(low_head, grad, 0.0)
        do_ref[1, at, :] = jnp.where(low_head, 0.0, grad)
        dk_ref[at, :] = jnp.zeros((T, 128), F32)
        dv_ref[at, :] = jnp.zeros((T, 128), F32)
        return 0

    lax.fori_loop(0, 16, load, 0)

    lane_q = lax.broadcasted_iota(jnp.int32, (TQ, 128), 1)
    low_q = lane_q < HEAD_DIM

    def block(i, _):
        rows = pl.ds(pl.multiple_of(i * TQ, TQ), TQ)
        qs = [q_ref[h, rows, :] for h in range(2)]

        def scores(j, tops, masked):
            at = pl.ds(pl.multiple_of(j * TK, TK), TK)
            keys = k_ref[at, :]
            new = []
            for h in range(2):
                s = dot(qs[h], keys, 1, 1)
                if masked:
                    row = lax.broadcasted_iota(jnp.int32, (TQ, TK), 0)
                    col = lax.broadcasted_iota(jnp.int32, (TQ, TK), 1)
                    s = jnp.where(row >= col, s, -1e30)
                s_ref[h, :, at] = s
                top = tops[h]
                for n in range(TK // 128):
                    top = jnp.maximum(top, s[:, n * 128 : (n + 1) * 128])
                new.append(top)
            return tuple(new)

        low = jnp.full((TQ, 128), -1e30, F32)
        tops = lax.fori_loop(0, i, lambda j, t: scores(j, t, False), (low, low))
        tops = scores(i, tops, True)
        tops = [jnp.max(t, axis=1, keepdims=True) for t in tops]

        def weigh(j, sums):
            at = pl.ds(pl.multiple_of(j * TK, TK), TK)
            values = v_ref[at, :]
            new = []
            for h in range(2):
                e = jnp.exp2((s_ref[h, :, at] - tops[h]) * LOG2E).astype(BF)
                e_ref[h, :, at] = e
                new.append(sums[h] + dot(e, values))
            return tuple(new)

        zero = jnp.zeros((TQ, 256), F32)
        sums = lax.fori_loop(0, i + 1, weigh, (zero, zero))
        att, low_grads, deltas = [], [], []
        for h in range(2):
            inverse = 1.0 / sums[h][:, 128:]
            o = sums[h][:, :128] * inverse
            grad = do_ref[h, rows, :] * inverse
            att.append(o)
            deltas.append(jnp.sum(grad * o, axis=1, keepdims=True))
            low_grads.append(grad.astype(BF))
        o_ref[rows, :] = jnp.where(low_q, att[0], att[1]).astype(BF)

        def back(j, sums):
            at = pl.ds(pl.multiple_of(j * TK, TK), TK)
            keys = k_ref[at, :]
            values = v_ref[at, 0:128]
            new = []
            dk = dk_ref[at, :]
            dv = dv_ref[at, :]
            for h in range(2):
                e = e_ref[h, :, at]
                dp = dot(low_grads[h], values, 1, 1)
                ds = (e.astype(F32) * (dp - deltas[h])).astype(BF)
                new.append(sums[h] + dot(ds, keys))
                dk = dk + dot(ds, qs[h], 0, 0)
                dv = dv + dot(e, low_grads[h], 0, 0)
            dk_ref[at, :] = dk
            dv_ref[at, :] = dv
            return tuple(new)

        zero = jnp.zeros((TQ, 128), F32)
        dqs = lax.fori_loop(0, i + 1, back, (zero, zero))
        dq_ref[rows, :] = jnp.where(low_q, dqs[0], dqs[1]) * (HEAD_DIM**-0.5)
        return 0

    lax.fori_loop(0, SEQ // TQ, block, 0)

    def store(slot, _):
        rows = pl.ds(pl.multiple_of(slot * T, T), T)
        at = pl.ds(pl.multiple_of(place[slot] * T, T), T)
        c, s = cos_ref[at, :], sin_ref[at, :]
        att_ref[rows, :] = o_ref[at, :]
        dq, dk = dq_ref[at, :], dk_ref[at, :]
        out_ref[rows, 0:128] = (dq * c - turned(dq) * s).astype(BF)
        out_ref[rows, 128:256] = (dk * c - turned(dk) * s).astype(BF)
        out_ref[rows, 256:384] = dv_ref[at, :].astype(BF)
        return 0

    lax.fori_loop(0, 16, store, 0)


def attention(place, mixed, attended_grad, cosine, sine):
    vmem = pl.BlockSpec(memory_space=pltpu.VMEM)
    return pl.pallas_call(
        attention_kernel,
        in_specs=[pl.BlockSpec(memory_space=pltpu.SMEM)] + [vmem] * 4,
        out_specs=[vmem, vmem],
        out_shape=[
            jax.ShapeDtypeStruct((SEQ, 128), BF),
            jax.ShapeDtypeStruct((SEQ, QKV), BF),
        ],
        scratch_shapes=[
            pltpu.VMEM((2, SEQ, 128), BF),
            pltpu.VMEM((SEQ, 128), BF),
            pltpu.VMEM((SEQ, 256), BF),
            pltpu.VMEM((2, SEQ, 128), F32),
            pltpu.VMEM((SEQ, 128), F32),
            pltpu.VMEM((SEQ, 128), F32),
            pltpu.VMEM((SEQ, 128), F32),
            pltpu.VMEM((SEQ, 128), BF),
            pltpu.VMEM((2, TQ, SEQ), F32),
            pltpu.VMEM((2, TQ, SEQ), BF),
        ],
        compiler_params=pltpu.CompilerParams(vmem_limit_bytes=48 * MIB),
        cost_estimate=pl.CostEstimate(
            flops=14 * SEQ * SEQ * 64 * 2, transcendentals=SEQ * SEQ, bytes_accessed=8 * MIB
        ),
    )(place, mixed, attended_grad, cosine, sine)


def out_terms(chips, attended, activated, dense, fc2):
    order = jnp.array([dz * 2 + dx for dz, dx in chips], jnp.int32)
    n = len(chips)

    def kernel(order_ref, a_ref, f_ref, d_ref, w_ref, mine_ref, other_ref):
        total = dot(a_ref[...], d_ref[...]) + dot(f_ref[...], w_ref[...])
        mine_ref[...] = total[:T].astype(BF)
        other_ref[...] = total[T:].astype(BF)

    row = lambda i, order_ref: (order_ref[i], 0)
    whole = lambda i, order_ref: (0, 0)
    here = lambda i, order_ref: (i, 0)
    return pl.pallas_call(
        kernel,
        grid_spec=pltpu.PrefetchScalarGridSpec(
            num_scalar_prefetch=1,
            grid=(n,),
            in_specs=[
                pl.BlockSpec((2 * T, T), row),
                pl.BlockSpec((2 * T, FFL), row),
                pl.BlockSpec((T, D), whole),
                pl.BlockSpec((FFL, D), whole),
            ],
            out_specs=[pl.BlockSpec((T, D), here)] * 2,
        ),
        out_shape=[jax.ShapeDtypeStruct((n * T, D), BF)] * 2,
        compiler_params=pltpu.CompilerParams(vmem_limit_bytes=32 * MIB),
        cost_estimate=pl.CostEstimate(
            flops=2 * n * 2 * T * (T + FFL) * D,
            transcendentals=0,
            bytes_accessed=2 * (n * 2 * T * (T + FFL) + (T + FFL) * D + n * 2 * T * D),
        ),
    )(order, attended, activated, dense, fc2)


def normed_terms(chips, mixed_grad, pre_grad, weight, normed, shift):
    order = jnp.array([dz * 2 + dx for dz, dx in chips], jnp.int32)
    n = len(chips)

    def kernel(
        order_ref, m_ref, p_ref, w_ref, n_ref, s_ref, mine_ref, other_ref, gain_ref, total_ref
    ):
        total = dot(m_ref[...], w_ref[:, :QKV], 1, 1) + dot(p_ref[...], w_ref[:, QKV:], 1, 1)
        mine_ref[...] = total[:T].astype(BF)
        other_ref[...] = total[T:].astype(BF)
        unit = n_ref[...].astype(F32) - s_ref[...]
        gain = jnp.sum((total * unit).reshape(2 * T // 8, 8, D), axis=0)
        shifts = jnp.sum(total.reshape(2 * T // 8, 8, D), axis=0)

        @pl.when(pl.program_id(0) == 0)
        def _():
            gain_ref[...] = jnp.zeros_like(gain_ref)
            total_ref[...] = jnp.zeros_like(total_ref)

        gain_ref[...] += gain
        total_ref[...] += shifts

    row = lambda i, order_ref: (order_ref[i], 0)
    whole = lambda i, order_ref: (0, 0)
    here = lambda i, order_ref: (i, 0)
    return pl.pallas_call(
        kernel,
        grid_spec=pltpu.PrefetchScalarGridSpec(
            num_scalar_prefetch=1,
            grid=(n,),
            in_specs=[
                pl.BlockSpec((2 * T, QKV), row),
                pl.BlockSpec((2 * T, FFL), row),
                pl.BlockSpec((D, COLS), whole),
                pl.BlockSpec((2 * T, D), row),
                pl.BlockSpec((1, D), whole),
            ],
            out_specs=[pl.BlockSpec((T, D), here)] * 2 + [pl.BlockSpec((8, D), whole)] * 2,
        ),
        out_shape=[jax.ShapeDtypeStruct((n * T, D), BF)] * 2
        + [jax.ShapeDtypeStruct((8, D), F32)] * 2,
        compiler_params=pltpu.CompilerParams(vmem_limit_bytes=40 * MIB),
        cost_estimate=pl.CostEstimate(
            flops=2 * n * 2 * T * COLS * D,
            transcendentals=0,
            bytes_accessed=2 * (n * 2 * T * COLS + COLS * D + n * 4 * T * D),
        ),
    )(order, mixed_grad, pre_grad, weight, normed, shift)


def rotary_tables():
    lane = lax.broadcasted_iota(jnp.int32, (SEQ, 128), 1) % HEAD_DIM
    place = lax.broadcasted_iota(jnp.int32, (SEQ, 128), 0).astype(F32)
    freq = (lane % (ROTARY // 2)).astype(F32)
    angle = place * jnp.exp(freq * (-2.0 * math.log(10000.0) / ROTARY))
    turns = lane < ROTARY
    cosine = jnp.where(turns, jnp.cos(angle), 1.0)
    sine = jnp.where(turns, jnp.sin(angle), 0.0)
    return cosine, jnp.where(lane < ROTARY // 2, -sine, sine)


def body(
    tokens,
    ln_gain,
    ln_shift,
    qkv_weight,
    qkv_bias,
    dense_weight,
    dense_bias,
    fc1_weight,
    fc1_bias,
    fc2_weight,
    fc2_bias,
    cotangent,
):
    rep, shard = lax.axis_index("rep"), lax.axis_index("shard")
    xh, y = rep // 4, rep % 4
    z, xl, c = shard // 4, (shard // 2) % 2, shard % 2
    token_place = jnp.stack(
        [((z + dz) % 4) * 4 + (xl ^ dx) * 2 + (c ^ dc) for dz, dx, dc in SLOTS]
    ).astype(jnp.int32)
    row_place = jnp.stack(
        [((z + y + dy) % 4) * 4 + (xl ^ xh ^ dh) * 2 + (c ^ dc) for dy, dh, dc in SLOTS]
    ).astype(jnp.int32)
    col_place = jnp.stack(
        [((z - y - dy) % 4) * 4 + (xl ^ xh ^ dh) * 2 + (c ^ dc) for dy, dh, dc in SLOTS]
    ).astype(jnp.int32)
    part_place = jnp.stack(
        [((y + dy) % 4) * 2 + (xh ^ dh) for dy in range(4) for dh in range(2)]
    ).astype(jnp.int32)
    me, core = shard.reshape(1).astype(jnp.int32), c.reshape(1).astype(jnp.int32)

    cot_pieces, cot_rows = group_pieces(gather_group(cotangent))

    to_chip = ((z - y) % 4) * 2 + (xl ^ xh)
    pieces = [
        lax.dynamic_slice(qkv_weight, (0, part * D + to_chip * 2 * T), (T, 2 * T))
        for part in range(3)
    ]
    pieces_fc1 = lax.dynamic_slice(fc1_weight, (0, to_chip * 2 * FFL), (T, 2 * FFL))
    for_cores = jnp.concatenate(
        [
            jnp.concatenate(
                [p[:, at * T : (at + 1) * T] for p in pieces]
                + [pieces_fc1[:, at * FFL : (at + 1) * FFL]],
                axis=1,
            )
            for at in range(2)
        ]
    )
    both = fetch_from(for_cores, lambda xh, y, z, xl, c: (xh, y, z + y, xl ^ xh, c))
    mine = lax.dynamic_slice(both, (c * T, 0), (T, COLS))
    other = lax.dynamic_slice(both, ((1 - c) * T, 0), (T, COLS))
    weights = gather_rep(jnp.concatenate([mine, fetch(other, dc=1)]))

    vectors = [
        v.reshape(-1, T) for v in (qkv_bias, ln_gain, ln_shift, dense_bias, fc2_bias)
    ]
    vectors = jnp.concatenate(vectors + [jnp.zeros((T - 7, T), BF)])
    tok_pieces, tok_rows = group_pieces(
        gather_group(jnp.concatenate([tokens, vectors], axis=1))
    )
    cosine, sine = rotary_tables()

    all_cot, act_grad, attended_grad, out_bias_part = backward_inputs(
        cot_pieces, cot_rows, fc2_weight, dense_weight, me
    )
    normed, weight, activated, pre_grad, mixed, vecs, _, fc1_bias_part = forward_inputs(
        tok_pieces,
        tok_rows,
        weights,
        fc1_bias.astype(F32).reshape(1, FFL),
        act_grad,
        token_place,
        row_place,
        me,
    )
    gain, shift, out_bias = vecs[0:1], vecs[1:2], vecs[2:3]

    def reduced(g):
        total = reduce_y(g)
        half = total.shape[0] // 2
        return add(total[:half], fetch(total[half:].astype(BF), dh=1)).astype(BF)

    def to_owner(part):
        stacked = jnp.concatenate([part[:T], fetch(part[T:], dc=1)])
        return fetch_from(stacked, lambda xh, y, z, xl, c: (xh, y, z - y, xl ^ xh, c))

    early = column_grads(normed, pre_grad, activated, all_cot, row_place, part_place, core)
    mixed, *early = lax.optimization_barrier((mixed, *early))
    summed = reduced(early)
    early = gather_rep(jnp.concatenate([to_owner(summed[:256]), summed[256:]]))
    fc1_total, fc2_total = place_columns(early, col_place, part_place)

    attended, mixed_grad = attention(token_place, mixed, attended_grad, cosine, sine)
    *late, qkv_bias_part = head_grads(
        normed, mixed_grad, attended, all_cot, row_place, part_place, core
    )
    mixed_grad, attended, *late = lax.optimization_barrier((mixed_grad, attended, *late))
    summed = reduced(late)
    late = gather_rep(jnp.concatenate([to_owner(summed[:, :QKV]), summed[:, QKV:]], axis=1))
    qkv_total, dense_total = place_heads(late, col_place, part_place)

    own = tokens.astype(F32)
    pieces = [normed_terms(w, mixed_grad, pre_grad, weight, normed, shift) for w in WAVES]
    normed_grad = add(*scatter_group([(p[0], p[1]) for p in pieces]))
    gain_part = jnp.sum(sum(p[2] for p in pieces), axis=0) / gain[0]
    shift_part = jnp.sum(sum(p[3] for p in pieces), axis=0)
    center = own - jnp.mean(own, axis=-1, keepdims=True)
    inv_std = lax.rsqrt(jnp.mean(center * center, axis=-1, keepdims=True) + 1e-05)
    unit = center * inv_std
    scaled = normed_grad * gain
    input_grad = cotangent.astype(F32) + inv_std * (
        scaled
        - jnp.mean(scaled, axis=-1, keepdims=True)
        - unit * jnp.mean(scaled * unit, axis=-1, keepdims=True)
    )

    terms = scatter_group(
        [out_terms(w, attended, activated, dense_weight, fc2_weight) for w in WAVES]
    )
    layer_out = (own + out_bias + add(*terms)).astype(BF)

    qkv_bias_part = jnp.sum(qkv_bias_part, axis=0)
    biases = jnp.zeros((3 * D,), F32)
    for part in range(3):
        biases = lax.dynamic_update_slice(
            biases, qkv_bias_part[part * T : (part + 1) * T], (part * D + shard * T,)
        )
    vec = jnp.concatenate([gain_part, shift_part, biases]).reshape(80, 128)
    vec = vec + fetch(vec, dc=1)
    vec = vec + fetch(vec, dx=1)
    vec = (vec + fetch(vec, dz=2)) + (fetch(vec, dz=1) + fetch(vec, dz=-1))
    own_vec = jnp.concatenate(
        [
            lax.dynamic_slice(vec, (shard, 0), (1, 128)),
            lax.dynamic_slice(vec, (16 + shard, 0), (1, 128)),
            lax.dynamic_slice(vec, (32 + 3 * shard, 0), (3, 128)),
            jnp.sum(fc1_bias_part, axis=0).reshape(4, 128),
            jnp.sum(out_bias_part, axis=0).reshape(1, 128),
            jnp.zeros((6, 128), F32),
        ]
    )
    own_vec = own_vec + fetch(own_vec, dh=1)
    own_vec = (own_vec + fetch(own_vec, dy=2)) + (fetch(own_vec, dy=1) + fetch(own_vec, dy=-1))
    out_bias_total = own_vec[9]

    return (
        layer_out,
        input_grad,
        own_vec[0],
        own_vec[1],
        qkv_total,
        own_vec[2:5].reshape(QKV),
        dense_total,
        out_bias_total,
        fc1_total,
        own_vec[5:9].reshape(FFL),
        fc2_total,
        out_bias_total,
    )


def solution(mesh):
    return jax.shard_map(
        body,
        mesh=mesh,
        in_specs=(
            P(AXES, None),
            P("shard"),
            P("shard"),
            P("shard", None),
            P("shard"),
            P("shard", None),
            P("shard"),
            P("shard", None),
            P("shard"),
            P("shard", None),
            P("shard"),
            P(AXES, None),
        ),
        out_specs=(
            P(AXES, None),
            P(AXES, None),
            P("shard"),
            P("shard"),
            P("shard", None),
            P("shard"),
            P("shard", None),
            P("shard"),
            P("shard", None),
            P("shard"),
            P("shard", None),
            P("shard"),
        ),
        check_vma=False,
    )
```

```python
import functools
import math

import jax
import jax.numpy as jnp
from jax import lax
from jax.experimental import pallas as pl
from jax.experimental.pallas import tpu as pltpu
from jax.sharding import PartitionSpec as P

D = 2048
HEADS = 32
HEAD_DIM = 64
ROTARY = 32
FF = 8192
SEQ = 2048
T = 128
QKV = 384
FFL = 512
COLS = QKV + FFL
BF = jnp.bfloat16
F32 = jnp.float32
AXES = ("rep", "shard")
MIB = 1 << 20
LOG2E = math.log2(math.e)

PLACES = [
    (xh, y, z, xl, c)
    for xh in range(2)
    for y in range(4)
    for z in range(4)
    for xl in range(2)
    for c in range(2)
]


def flat(xh, y, z, xl, c):
    return (xh * 4 + y % 4) * 16 + (z % 4) * 4 + xl * 2 + c


def fetch_from(x, source):
    return lax.ppermute(x, AXES, [(flat(*source(*p)), flat(*p)) for p in PLACES])


def fetch(x, dz=0, dx=0, dc=0, dy=0, dh=0):
    return fetch_from(
        x, lambda xh, y, z, xl, c: (xh ^ dh, y + dy, z + dz, xl ^ dx, c ^ dc)
    )


def dot(a, b, ca=1, cb=0):
    return lax.dot_general(a, b, (((ca,), (cb,)), ((), ())), preferred_element_type=F32)


def add(*terms):
    total = terms[0].astype(F32)
    for term in terms[1:]:
        total = total + term.astype(F32)
    return total


def after(x, *others):
    return lax.optimization_barrier((x, *others))[0]


def gather_near(own):
    return {
        (0, 0): own,
        (1, 0): fetch(own, dz=1),
        (3, 0): fetch(own, dz=-1),
        (0, 1): fetch(own, dx=1),
    }


def gather_next(a):
    return {
        (1, 1): fetch(a[1, 0], dx=1),
        (3, 1): fetch(a[0, 1], dz=-1),
        (2, 0): fetch(a[1, 0], dz=1),
    }


def gather_far(a):
    half = a[1, 1].shape[0] // 2
    return fetch(a[1, 1][:half], dz=1), fetch(a[3, 1][half:], dz=-1)


def both_cores(a):
    pieces = []
    for (dz, dx), own in a.items():
        for dc in range(2):
            at = ((dz * 2 + dx) * 2 + dc) * T
            for part in own if isinstance(own, tuple) else (own,):
                pieces.append((fetch(part, dc=1) if dc else part, at))
                at += part.shape[0]
    return pieces


SLOTS = [(dz, dx, dc) for dz in range(4) for dx in range(2) for dc in range(2)]
WAVES = [[(2, 1), (1, 1), (3, 1), (2, 0)], [(1, 0), (3, 0), (0, 1), (0, 0)]]


def scatter_group(waves):
    q = {}
    for chips, (mine, other) in zip(WAVES, waves, strict=True):
        other = fetch(other, dc=1)
        for n, chip in enumerate(chips):
            at = slice(n * T, (n + 1) * T)
            q[chip] = add(mine[at], other[at]).astype(BF)
    half = T // 2
    far = q[2, 1]
    a = fetch(far[:half], dz=-1)
    b = fetch(far[half:], dz=1)
    q11 = jnp.concatenate([add(q[1, 1][:half], a).astype(BF), q[1, 1][half:]])
    q31 = jnp.concatenate([q[3, 1][:half], add(q[3, 1][half:], b).astype(BF)])
    q10 = add(q[1, 0], fetch(q11, dx=1), fetch(q[2, 0], dz=-1)).astype(BF)
    q01 = add(q[0, 1], fetch(q31, dz=1)).astype(BF)
    return q[0, 0], fetch(q10, dz=-1), fetch(q[3, 0], dz=1), fetch(q01, dx=1)


def reduce_y_first(g):
    half = g[0].shape[0] // 2
    a = fetch(g[2][:half], dy=-1)
    b = fetch(g[2][half:], dy=1)
    g1 = jnp.concatenate([add(g[1][:half], a).astype(BF), g[1][half:]])
    g3 = jnp.concatenate([g[3][:half], add(g[3][half:], b).astype(BF)])
    return g[0], g1, g3


def reduce_y_last(g):
    return add(g[0], fetch(g[1], dy=-1), fetch(g[2], dy=1))


def gather_rep(own):
    pair = jnp.concatenate([own, fetch(own, dh=1)])
    half = own.shape[0]
    one, three = fetch(pair, dy=1), fetch(pair, dy=-1)
    return pair, one, three, fetch(one[:half], dy=1), fetch(three[half:], dy=-1)


def of_rep(refs, dy, dh, n):
    own, one, three, first, second = refs
    if dy == 2:
        return (second if dh else first), 0
    return (own, one, None, three)[dy], dh * n


VMEM = pl.BlockSpec(memory_space=pltpu.VMEM)
SMEM = pl.BlockSpec(memory_space=pltpu.SMEM)
ANY = pl.BlockSpec(memory_space=pl.ANY)


def lanes(at, n):
    return pl.ds(pl.multiple_of(at * n, n), n)


def call(kernel, ins, outs, args, scratch=(), vmem=16, flops=0, nbytes=0, exps=0, aliases={}):
    return pl.pallas_call(
        kernel,
        in_specs=ins,
        out_specs=[VMEM] * len(outs),
        out_shape=[
            pltpu.VMEM(o[0], o[1]) if len(o) > 2 else jax.ShapeDtypeStruct(*o) for o in outs
        ],
        scratch_shapes=list(scratch),
        input_output_aliases=aliases,
        compiler_params=pltpu.CompilerParams(vmem_limit_bytes=vmem * MIB),
        cost_estimate=pl.CostEstimate(flops=flops, transcendentals=exps, bytes_accessed=nbytes),
    )(*args)


ROOT = math.sqrt(2.0 / math.pi)


def start_copies(pieces, place, sems):
    copies = [
        pltpu.make_async_copy(src, dst, sems.at[place + i]) for i, (src, dst) in enumerate(pieces)
    ]
    for copy in copies:
        copy.start()
    return copies


def backward_inputs(pieces, fc2, dense, token_place, me):
    n = len(pieces)

    def kernel(t_ref, me_ref, *refs):
        cot = refs[:n]
        (
            fc2_ref,
            dense_ref,
            cot_ref,
            act_ref,
            att_ref,
            sum_ref,
            vec_ref,
            own_ref,
            small_ref,
            flat_ref,
            sems,
        ) = refs[n:]
        moves = []
        for (array, at), ref in zip(pieces, cot, strict=True):
            size = array.shape[0]
            moves.append((ref.at[:, pl.ds(0, D)], cot_ref.at[pl.ds(at, size)]))
            if at % T == 0:
                small = small_ref.at[pl.ds(at // T * 16, 16)]
                moves.append((ref.at[pl.ds(0, 16), pl.ds(D, T)], small))
        for copy in start_copies(moves, 0, sems):
            copy.wait()

        def tile(i, total):
            at = lanes(i, 256)
            x = cot_ref[at, :]
            act_ref[at, :] = dot(x, fc2_ref[...], 1, 1)
            att_ref[at, :] = dot(x, dense_ref[...], 1, 1).astype(BF)
            own = cot_ref[at, lanes(me_ref[0], T)].astype(F32)
            return total + jnp.sum(own.reshape(32, 8, T), axis=0)

        sum_ref[...] = lax.fori_loop(0, 8, tile, jnp.zeros((8, T), F32))
        for i in range(16):
            at = t_ref[i]
            small = small_ref[i * 16 : (i + 1) * 16, :].astype(F32)
            for part in range(3):
                flat_ref[0:1, lanes(at * 3 + part, T)] = small[part : part + 1]
            vec_ref[0:1, lanes(at, T)] = small[3:4]
            vec_ref[1:2, lanes(at, T)] = small[4:5]
            vec_ref[2:3, lanes(at, T)] = small[5:6] + small[6:7]
        for part in range(3):
            own_ref[0:1, part * T : (part + 1) * T] = flat_ref[
                0:1, lanes(part * 16 + me_ref[0], T)
            ]

    return call(
        kernel,
        [SMEM] * 2 + [ANY] * n + [VMEM] * 2,
        [
            ((SEQ, D), BF, 1),
            ((SEQ, FFL), F32, 1),
            ((SEQ, T), BF),
            ((8, T), F32),
            ((8, D), F32),
            ((1, QKV), F32),
        ],
        [token_place, me] + [p for p, _ in pieces] + [fc2, dense],
        [
            pltpu.VMEM((256, T), BF),
            pltpu.VMEM((1, 3 * D), F32),
            pltpu.SemaphoreType.DMA((n + 16,)),
        ],
        flops=2 * SEQ * D * (FFL + T),
        nbytes=20 * MIB,
    )


def norm_rows(normed_ref, gain, shift, first, count):
    def strip(i, _):
        at = lanes(i, 64)
        x = normed_ref[at, :].astype(F32)
        x = x - jnp.sum(x, axis=1, keepdims=True) * (1.0 / D)
        scale = lax.rsqrt(jnp.sum(x * x, axis=1, keepdims=True) * (1.0 / D) + 1e-05)
        normed_ref[at, :] = (x * scale * gain + shift).astype(BF)
        return 0

    lax.fori_loop(first // 64, (first + count) // 64, strip, 0)


def norm_inputs(pieces, vecs):
    n = len(pieces)

    def kernel(*refs):
        vec_ref, normed_ref, sems = refs[n:]
        moves = [
            (ref, normed_ref.at[pl.ds(at, array.shape[0])])
            for (array, at), ref in zip(pieces, refs[:n], strict=True)
        ]
        copies = start_copies(moves, 0, sems)
        gain, shift = vec_ref[0:1, :], vec_ref[1:2, :]
        for copy, (array, at) in zip(copies, pieces, strict=True):
            copy.wait()
            norm_rows(normed_ref, gain, shift, at, array.shape[0])

    return call(
        kernel,
        [ANY] * n + [VMEM],
        [((SEQ, D), BF, 1)],
        [p for p, _ in pieces] + [vecs],
        [pltpu.SemaphoreType.DMA((n,))],
        flops=10 * SEQ * D,
        nbytes=12 * MIB,
    )[0]


def forward_inputs(normed, pieces, weights, vecs, bias, own_bias, act_grad, row_place):
    n = len(pieces)

    def kernel(r_ref, in_ref, *refs):
        tok = refs[:n]
        w_refs = refs[n : n + 5]
        (
            vec_ref,
            bias_ref,
            own_ref,
            grad_ref,
            normed_ref,
            w_ref,
            act_ref,
            pre_ref,
            act_t_ref,
            pre_t_ref,
            mixed_ref,
            fc1b_ref,
            sems,
        ) = refs[n + 5 :]
        moves = [
            (ref, normed_ref.at[pl.ds(at, array.shape[0])])
            for (array, at), ref in zip(pieces, tok, strict=True)
        ]
        for i, (dy, dh, dc) in enumerate(SLOTS):
            ref, at = of_rep(w_refs, dy, dh, 2 * T)
            moves.append((ref.at[pl.ds(at + dc * T, T)], w_ref.at[lanes(r_ref[i], T)]))
        for copy in start_copies(moves, 0, sems):
            copy.wait()
        gain, shift = vec_ref[0:1, :], vec_ref[1:2, :]
        for array, at in pieces:
            norm_rows(normed_ref, gain, shift, at, array.shape[0])

        def tile(i, total):
            at = lanes(i, 256)
            x = normed_ref[at, :]
            mixed_ref[at, :] = dot(x, w_ref[:, :QKV]) + own_ref[...]
            pre = dot(x, w_ref[:, QKV:]) + bias_ref[...]
            squared = pre * pre
            tanh = jnp.tanh(ROOT * pre * (1.0 + 0.044715 * squared))
            act = (0.5 * pre * (1.0 + tanh)).astype(BF)
            act_ref[at, :] = act
            act_t_ref[:, at] = act.T
            slope = 0.5 * (1.0 + tanh) + 0.5 * pre * (1.0 - tanh * tanh) * ROOT * (
                1.0 + 3 * 0.044715 * squared
            )
            back = (grad_ref[at, :] * slope).astype(BF)
            pre_ref[at, :] = back
            pre_t_ref[:, at] = back.T
            return total + jnp.sum(back.astype(F32).reshape(32, 8, FFL), axis=0)

        fc1b_ref[...] = lax.fori_loop(0, 8, tile, jnp.zeros((8, FFL), F32))

    return call(
        kernel,
        [SMEM, VMEM] + [ANY] * (n + 5) + [VMEM] * 4,
        [
            ((SEQ, D), BF, 1),
            ((D, COLS), BF, 1),
            ((SEQ, FFL), BF, 1),
            ((SEQ, FFL), BF, 1),
            ((FFL, SEQ), BF, 1),
            ((FFL, SEQ), BF, 1),
            ((SEQ, QKV), F32, 1),
            ((8, FFL), F32),
        ],
        [row_place, normed] + [p for p, _ in pieces] + list(weights) + [vecs, bias, own_bias, act_grad],
        [pltpu.SemaphoreType.DMA((n + 16,))],
        aliases={1: 0},
        flops=2 * SEQ * D * COLS,
        nbytes=8 * MIB,
        exps=SEQ * FFL,
    )


def column_grads(normed, pre_t, act_t, cot, row_place, part_place, core):
    def kernel(r_ref, p_ref, core_ref, n_ref, g_ref, a_ref, c_ref, *outs):
        for dy in (2, 1, 3, 0):
            out = outs[dy]
            for dh in range(2):
                at = slice(dh * FFL, (dh + 1) * FFL)
                chip = r_ref[(dy * 2 + dh) * 2] // 2
                cols = dot(g_ref[...], n_ref[:, lanes(chip, 256)]).astype(BF)
                out[at, lanes(core_ref[0], T)] = cols[:, :T]
                out[at, lanes(1 - core_ref[0], T)] = cols[:, T:]
                part = c_ref[:, lanes(p_ref[dy * 2 + dh], 256)]
                out[at, 256:512] = dot(a_ref[...], part).astype(BF)

    return call(
        kernel,
        [SMEM] * 3 + [VMEM] * 4,
        [((1024, 512), BF)] * 4,
        [row_place, part_place, core, normed, pre_t, act_t, cot],
        flops=4 * SEQ * D * FFL,
        nbytes=4 * MIB,
    )


def head_grads(normed, mixed_t, attended_t, cot, row_place, part_place, core):
    def kernel(r_ref, p_ref, core_ref, n_ref, m_ref, a_ref, c_ref, *outs):
        for dy in (2, 1, 3, 0):
            out = outs[dy]
            for dh in range(2):
                base = dh * FFL
                chip = r_ref[(dy * 2 + dh) * 2] // 2
                cols = dot(m_ref[...], n_ref[:, lanes(chip, 256)]).astype(BF)
                out[base : base + QKV, lanes(core_ref[0], T)] = cols[:, :T]
                out[base : base + QKV, lanes(1 - core_ref[0], T)] = cols[:, T:]
                part = c_ref[:, lanes(p_ref[dy * 2 + dh], 256)]
                out[base + QKV : base + FFL, :] = dot(a_ref[...], part).astype(BF)

    return call(
        kernel,
        [SMEM] * 3 + [VMEM] * 4,
        [((1024, 256), BF)] * 4,
        [row_place, part_place, core, normed, mixed_t, attended_t, cot],
        flops=2 * SEQ * D * (QKV + T),
        nbytes=2 * MIB,
    )


def place_columns(pieces, col_place, part_place):
    def kernel(c_ref, p_ref, *refs):
        fc1_ref, fc2_ref = refs[5:]
        for i, (dy, dh, dc) in enumerate(SLOTS):
            ref, at = of_rep(refs[:5], dy, dh, FFL)
            part = ref[at : at + FFL, dc * T : (dc + 1) * T]
            fc1_ref[:, lanes(c_ref[i], FFL)] = part.astype(F32).T
            if dc == 0:
                to = lanes(p_ref[dy * 2 + dh], 256)
                fc2_ref[:, to] = ref[at : at + FFL, 256:512].astype(F32)

    return call(
        kernel,
        [SMEM] * 2 + [VMEM] * 5,
        [((T, FF), F32), ((FFL, D), F32)],
        [col_place, part_place] + list(pieces),
        vmem=20,
        nbytes=12 * MIB,
    )


def place_heads(pieces, col_place, part_place):
    def kernel(c_ref, p_ref, *refs):
        qkv_ref, dense_ref = refs[5:]
        for i, (dy, dh, dc) in enumerate(SLOTS):
            ref, at = of_rep(refs[:5], dy, dh, FFL)
            for part in range(3):
                rows = slice(at + part * T, at + (part + 1) * T)
                block = ref[rows, dc * T : (dc + 1) * T].astype(F32)
                qkv_ref[:, lanes(c_ref[i] + part * 16, T)] = block.T
            if dc == 0:
                to = lanes(p_ref[dy * 2 + dh], 256)
                dense_ref[:, to] = ref[at + QKV : at + FFL, :].astype(F32)

    return call(
        kernel,
        [SMEM] * 2 + [VMEM] * 5,
        [((T, 3 * D), F32), ((T, D), F32)],
        [col_place, part_place] + list(pieces),
        nbytes=6 * MIB,
    )


def out_terms(chips, attended, activated, dense, fc2):
    n = len(chips)

    def kernel(a_ref, f_ref, d_ref, w_ref, mine_ref, other_ref):
        for i, (dz, dx) in enumerate(chips):
            at = slice((dz * 2 + dx) * 256, (dz * 2 + dx + 1) * 256)
            total = dot(a_ref[at, :], d_ref[...]) + dot(f_ref[at, :], w_ref[...])
            mine_ref[i * T : (i + 1) * T, :] = total[:T].astype(BF)
            other_ref[i * T : (i + 1) * T, :] = total[T:].astype(BF)

    return call(
        kernel,
        [VMEM] * 4,
        [((n * T, D), BF)] * 2,
        [attended, activated, dense, fc2],
        flops=2 * n * 2 * T * (T + FFL) * D,
        nbytes=8 * MIB,
    )


def normed_terms(chips, mixed_grad, pre_grad, weight, normed, vecs, when):
    n = len(chips)

    def kernel(when_ref, m_ref, p_ref, w_ref, n_ref, vec_ref, mine_ref, other_ref, gain_ref, total_ref):
        shift = vec_ref[1:2, :]
        gain_ref[...] = jnp.zeros_like(gain_ref)
        total_ref[...] = jnp.zeros_like(total_ref)
        for i, (dz, dx) in enumerate(chips):
            at = slice((dz * 2 + dx) * 256, (dz * 2 + dx + 1) * 256)
            for col in range(4):
                to = slice(col * 512, (col + 1) * 512)
                total = dot(m_ref[at, :], w_ref[to, :QKV], 1, 1) + dot(
                    p_ref[at, :], w_ref[to, QKV:], 1, 1
                )
                mine_ref[i * T : (i + 1) * T, to] = total[:T].astype(BF)
                other_ref[i * T : (i + 1) * T, to] = total[T:].astype(BF)
                unit = n_ref[at, to].astype(F32) - shift[:, to]
                gain_ref[:, to] += jnp.sum((total * unit).reshape(32, 8, 512), axis=0)
                total_ref[:, to] += jnp.sum(total.reshape(32, 8, 512), axis=0)

    return call(
        kernel,
        [SMEM] + [VMEM] * 5,
        [((n * T, D), BF)] * 2 + [((8, D), F32)] * 2,
        [when, mixed_grad, pre_grad, weight, normed, vecs],
        flops=2 * n * 2 * T * COLS * D,
        nbytes=4 * MIB,
    )


TQ = 512
TK = 512


def attention_kernel(
    blocks, last, place, mixed_ref, grad_ref, cos_ref, sin_ref, *refs
):
    if last:
        first_refs, refs = refs[:8], refs[8:]
        att_ref, out_ref, att_t_ref, out_t_ref, bias_ref = refs[:5]
        q_ref, k_ref, v_ref, do_ref = first_refs[:4]
        dq_ref, dk_ref, dv_ref, o_ref, s_ref, e_ref = refs[5:]
    else:
        q_ref, k_ref, v_ref, do_ref, dq_ref, dk_ref, dv_ref, o_ref, s_ref, e_ref = refs
    lane = lax.broadcasted_iota(jnp.int32, (T, 128), 1)
    low_head = lane < HEAD_DIM
    first = (lane % HEAD_DIM) < ROTARY // 2

    def turned(x):
        return jnp.where(
            first, pltpu.roll(x, 128 - ROTARY // 2, 1), pltpu.roll(x, ROTARY // 2, 1)
        )

    def load(slot, _):
        rows = pl.ds(pl.multiple_of(slot * T, T), T)
        at = pl.ds(pl.multiple_of(place[slot] * T, T), T)
        c, s = cos_ref[at, :], sin_ref[at, :]
        query = mixed_ref[rows, 0:128]
        key = mixed_ref[rows, 128:256]
        query = (query * c + turned(query) * s).astype(BF).astype(F32) * (HEAD_DIM**-0.5)
        q_ref[0, at, :] = jnp.where(low_head, query, 0.0).astype(BF)
        q_ref[1, at, :] = jnp.where(low_head, 0.0, query).astype(BF)
        k_ref[at, :] = (key * c + turned(key) * s).astype(BF)
        v_ref[at, 0:128] = mixed_ref[rows, 256:384].astype(BF)
        v_ref[at, 128:256] = jnp.ones((T, 128), BF)
        grad = grad_ref[rows, :].astype(F32)
        do_ref[0, at, :] = jnp.where(low_head, grad, 0.0).astype(BF)
        do_ref[1, at, :] = jnp.where(low_head, 0.0, grad).astype(BF)
        dk_ref[at, :] = jnp.zeros((T, 128), F32)
        dv_ref[at, :] = jnp.zeros((T, 128), F32)
        return 0

    if last:
        for to, at in ((dq_ref, 4), (dk_ref, 5), (dv_ref, 6), (o_ref, 7)):
            to[...] = first_refs[at][...]
    else:
        lax.fori_loop(0, 16, load, 0)

    lane_q = lax.broadcasted_iota(jnp.int32, (TQ, 128), 1)
    low_q = lane_q < HEAD_DIM

    def block(i, _):
        rows = pl.ds(pl.multiple_of(i * TQ, TQ), TQ)
        qs = [q_ref[h, rows, :] for h in range(2)]

        def scores(j, tops, masked):
            at = pl.ds(pl.multiple_of(j * TK, TK), TK)
            keys = k_ref[at, :]
            new = []
            for h in range(2):
                s = dot(qs[h], keys, 1, 1)
                if masked:
                    row = lax.broadcasted_iota(jnp.int32, (TQ, TK), 0)
                    col = lax.broadcasted_iota(jnp.int32, (TQ, TK), 1)
                    s = jnp.where(row >= col, s, -1e30)
                s_ref[h, :, at] = s
                top = tops[h]
                for n in range(TK // 128):
                    top = jnp.maximum(top, s[:, n * 128 : (n + 1) * 128])
                new.append(top)
            return tuple(new)

        low = jnp.full((TQ, 128), -1e30, F32)
        tops = lax.fori_loop(0, i, lambda j, t: scores(j, t, False), (low, low))
        tops = scores(i, tops, True)
        tops = [jnp.max(t, axis=1, keepdims=True) for t in tops]

        def weigh(j, sums):
            at = pl.ds(pl.multiple_of(j * TK, TK), TK)
            values = v_ref[at, :]
            new = []
            for h in range(2):
                e = jnp.exp2((s_ref[h, :, at] - tops[h]) * LOG2E).astype(BF)
                e_ref[h, :, at] = e
                new.append(sums[h] + dot(e, values))
            return tuple(new)

        zero = jnp.zeros((TQ, 256), F32)
        sums = lax.fori_loop(0, i + 1, weigh, (zero, zero))
        att, low_grads, deltas = [], [], []
        for h in range(2):
            inverse = 1.0 / sums[h][:, 128:]
            o = sums[h][:, :128] * inverse
            grad = do_ref[h, rows, :].astype(F32) * inverse
            att.append(o)
            deltas.append(jnp.sum(grad * o, axis=1, keepdims=True))
            low_grads.append(grad.astype(BF))
        o_ref[rows, :] = jnp.where(low_q, att[0], att[1]).astype(BF)

        def back(j, sums):
            at = pl.ds(pl.multiple_of(j * TK, TK), TK)
            keys = k_ref[at, :]
            values = v_ref[at, 0:128]
            new = []
            dk = dk_ref[at, :]
            dv = dv_ref[at, :]
            for h in range(2):
                e = e_ref[h, :, at]
                dp = dot(low_grads[h], values, 1, 1)
                ds = (e.astype(F32) * (dp - deltas[h])).astype(BF)
                new.append(sums[h] + dot(ds, keys))
                dk = dk + dot(ds, qs[h], 0, 0)
                dv = dv + dot(e, low_grads[h], 0, 0)
            dk_ref[at, :] = dk
            dv_ref[at, :] = dv
            return tuple(new)

        zero = jnp.zeros((TQ, 128), F32)
        dqs = lax.fori_loop(0, i + 1, back, (zero, zero))
        dq_ref[rows, :] = jnp.where(low_q, dqs[0], dqs[1]) * (HEAD_DIM**-0.5)
        return 0

    lax.fori_loop(blocks[0], blocks[1], block, 0)
    if not last:
        return

    def store(slot, total):
        rows = pl.ds(pl.multiple_of(slot * T, T), T)
        at = pl.ds(pl.multiple_of(place[slot] * T, T), T)
        c, s = cos_ref[at, :], sin_ref[at, :]
        att = o_ref[at, :]
        att_ref[rows, :] = att
        att_t_ref[:, rows] = att.T
        dq, dk = dq_ref[at, :], dk_ref[at, :]
        new = []
        for part, grad in enumerate(
            (dq * c - turned(dq) * s, dk * c - turned(dk) * s, dv_ref[at, :])
        ):
            low = grad.astype(BF)
            cols = slice(part * T, (part + 1) * T)
            out_ref[rows, cols] = low
            out_t_ref[cols, rows] = low.T
            new.append(total[part] + jnp.sum(low.astype(F32).reshape(16, 8, T), axis=0))
        return tuple(new)

    zero = jnp.zeros((8, T), F32)
    sums = lax.fori_loop(0, 16, store, (zero, zero, zero))
    for part in range(3):
        bias_ref[:, part * T : (part + 1) * T] = sums[part]


def attention_first(place, mixed, attended_grad, cosine, sine):
    return call(
        functools.partial(attention_kernel, (0, 3), False),
        [SMEM] + [VMEM] * 4,
        [
            ((2, SEQ, 128), BF, 1),
            ((SEQ, 128), BF, 1),
            ((SEQ, 256), BF, 1),
            ((2, SEQ, 128), BF, 1),
            ((SEQ, 128), F32, 1),
            ((SEQ, 128), F32, 1),
            ((SEQ, 128), F32, 1),
            ((SEQ, 128), BF, 1),
        ],
        [place, mixed, attended_grad, cosine, sine],
        [pltpu.VMEM((2, TQ, SEQ), F32), pltpu.VMEM((2, TQ, SEQ), BF)],
        vmem=20,
        flops=8 * SEQ * SEQ * 64 * 2,
        exps=SEQ * SEQ // 2,
        nbytes=3 * MIB,
    )


def attention_last(place, mixed, attended_grad, cosine, sine, state):
    return call(
        functools.partial(attention_kernel, (3, 4), True),
        [SMEM] + [VMEM] * 12,
        [
            ((SEQ, T), BF, 1),
            ((SEQ, QKV), BF, 1),
            ((T, SEQ), BF, 1),
            ((QKV, SEQ), BF, 1),
            ((8, QKV), F32),
        ],
        [place, mixed, attended_grad, cosine, sine] + list(state),
        [
            pltpu.VMEM((SEQ, 128), F32),
            pltpu.VMEM((SEQ, 128), F32),
            pltpu.VMEM((SEQ, 128), F32),
            pltpu.VMEM((SEQ, 128), BF),
            pltpu.VMEM((2, TQ, SEQ), F32),
            pltpu.VMEM((2, TQ, SEQ), BF),
        ],
        vmem=20,
        flops=6 * SEQ * SEQ * 64 * 2,
        exps=SEQ * SEQ // 2,
        nbytes=3 * MIB,
    )


def rotary_tables():
    lane = lax.broadcasted_iota(jnp.int32, (SEQ, 128), 1) % HEAD_DIM
    place = lax.broadcasted_iota(jnp.int32, (SEQ, 128), 0).astype(F32)
    freq = (lane % (ROTARY // 2)).astype(F32)
    angle = place * jnp.exp(freq * (-2.0 * math.log(10000.0) / ROTARY))
    turns = lane < ROTARY
    cosine = jnp.where(turns, jnp.cos(angle), 1.0)
    sine = jnp.where(turns, jnp.sin(angle), 0.0)
    return cosine, jnp.where(lane < ROTARY // 2, -sine, sine)


def body(
    tokens,
    ln_gain,
    ln_shift,
    qkv_weight,
    qkv_bias,
    dense_weight,
    dense_bias,
    fc1_weight,
    fc1_bias,
    fc2_weight,
    fc2_bias,
    cotangent,
):
    rep, shard = lax.axis_index("rep"), lax.axis_index("shard")
    xh, y = rep // 4, rep % 4
    z, xl, c = shard // 4, (shard // 2) % 2, shard % 2
    token_place = jnp.stack(
        [((z + dz) % 4) * 4 + (xl ^ dx) * 2 + (c ^ dc) for dz, dx, dc in SLOTS]
    ).astype(jnp.int32)
    row_place = jnp.stack(
        [((z + y + dy) % 4) * 4 + (xl ^ xh ^ dh) * 2 + (c ^ dc) for dy, dh, dc in SLOTS]
    ).astype(jnp.int32)
    col_place = jnp.stack(
        [((z - y - dy) % 4) * 4 + (xl ^ xh ^ dh) * 2 + (c ^ dc) for dy, dh, dc in SLOTS]
    ).astype(jnp.int32)
    part_place = jnp.stack(
        [((y + dy) % 4) * 2 + (xh ^ dh) for dy in range(4) for dh in range(2)]
    ).astype(jnp.int32)
    me, core = shard.reshape(1).astype(jnp.int32), c.reshape(1).astype(jnp.int32)

    to_chip = ((z - y) % 4) * 2 + (xl ^ xh)
    pieces = [
        lax.dynamic_slice(qkv_weight, (0, part * D + to_chip * 2 * T), (T, 2 * T))
        for part in range(3)
    ]
    pieces_fc1 = lax.dynamic_slice(fc1_weight, (0, to_chip * 2 * FFL), (T, 2 * FFL))
    for_cores = jnp.concatenate(
        [
            jnp.concatenate(
                [p[:, at * T : (at + 1) * T] for p in pieces]
                + [pieces_fc1[:, at * FFL : (at + 1) * FFL]],
                axis=1,
            )
            for at in range(2)
        ]
    )
    weights = fetch_from(for_cores, lambda xh, y, z, xl, c: (xh, y, z + y, xl ^ xh, c))

    vectors = [v.reshape(-1, T) for v in (qkv_bias, ln_gain, ln_shift, dense_bias, fc2_bias)]
    vectors = jnp.concatenate(vectors + [jnp.zeros((T - 7, T), BF)])
    cots = gather_near(jnp.concatenate([cotangent, vectors], axis=1))
    mine = lax.dynamic_slice(weights, (c * T, 0), (T, COLS))
    other = lax.dynamic_slice(weights, ((1 - c) * T, 0), (T, COLS))
    weights = jnp.concatenate([mine, fetch(other, dc=1)])
    weights, c00, c10, c30, c01, first_tokens = lax.optimization_barrier(
        (weights, cots[0, 0], cots[1, 0], cots[3, 0], cots[0, 1], tokens)
    )
    weights_far = fetch(weights, dh=1)
    cots = {(0, 0): c00, (1, 0): c10, (3, 0): c30, (0, 1): c01}
    cots |= gather_next(cots)
    toks = gather_near(first_tokens)
    weights = jnp.concatenate([weights, weights_far])
    weights, c11, c31, t10, t01 = lax.optimization_barrier(
        (weights, cots[1, 1], cots[3, 1], toks[1, 0], toks[0, 1])
    )
    half = 2 * T
    weights_one, weights_three = fetch(weights, dy=1), fetch(weights, dy=-1)
    cots[2, 1] = gather_far({(1, 1): c11, (3, 1): c31})
    toks |= {(1, 0): t10, (0, 1): t01}
    toks |= gather_next(toks)
    weights_one, weights_three, t11, t31 = lax.optimization_barrier(
        (weights_one, weights_three, toks[1, 1], toks[3, 1])
    )
    weights = (
        weights,
        weights_one,
        weights_three,
        fetch(weights_one[:half], dy=1),
        fetch(weights_three[half:], dy=-1),
    )
    toks |= {(1, 1): t11, (3, 1): t31}
    cosine, sine = rotary_tables()
    all_cot, act_grad, attended_grad, out_bias_part, vecs, own_qkv_bias = backward_inputs(
        both_cores(cots), fc2_weight, dense_weight, token_place, me
    )
    gain, shift, out_bias = vecs[0:1], vecs[1:2], vecs[2:3]
    normed = norm_inputs(both_cores(toks), vecs)
    last_tokens = both_cores({(2, 1): gather_far(toks)})
    (normed, weight, activated, pre_grad, act_t, pre_t, mixed, fc1_bias_part) = forward_inputs(
        normed,
        last_tokens,
        weights,
        vecs,
        fc1_bias.astype(F32).reshape(1, FFL),
        own_qkv_bias,
        act_grad,
        row_place,
    )

    def reduced(g):
        half = g.shape[0] // 2
        return g[half:].astype(BF), g[:half]

    def to_owner(part):
        stacked = jnp.concatenate([part[:, :T], fetch(part[:, T:], dc=1)], axis=1)
        return fetch_from(stacked, lambda xh, y, z, xl, c: (xh, y, z - y, xl ^ xh, c))

    early = column_grads(normed, pre_t, act_t, all_cot, row_place, part_place, core)
    attention_place = after(token_place, *early)
    state = attention_first(attention_place, mixed, attended_grad, cosine, sine)
    early = reduce_y_first(early)
    *early, attention_place = lax.optimization_barrier((*early, attention_place))
    attended, mixed_grad, attended_t, mixed_t, qkv_bias_part = attention_last(
        attention_place, mixed, attended_grad, cosine, sine, state
    )
    late = head_grads(normed, mixed_t, attended_t, all_cot, row_place, part_place, core)
    early_far, early = reduced(reduce_y_last(early))
    *late, early_far, when = lax.optimization_barrier((*late, early_far, core))
    early = add(early, fetch(early_far, dh=1)).astype(BF)
    late = reduce_y_last(reduce_y_first(late))
    early = jnp.concatenate([to_owner(early[:, :256]), early[:, 256:]], axis=1)
    early = gather_rep(early)
    fc1_total, fc2_total = place_columns(early, col_place, part_place)
    late_far, late = reduced(late)
    late = add(late, fetch(late_far, dh=1)).astype(BF)
    late = jnp.concatenate([to_owner(late[:QKV]), late[QKV:]])
    late = gather_rep(late)
    qkv_total, dense_total = place_heads(late, col_place, part_place)

    own = tokens.astype(F32)
    pieces = [
        normed_terms(w, mixed_grad, pre_grad, weight, normed, vecs, when) for w in WAVES
    ]
    normed_grad = add(*scatter_group([(p[0], p[1]) for p in pieces]))
    gain_part = jnp.sum(sum(p[2] for p in pieces), axis=0) / gain[0]
    shift_part = jnp.sum(sum(p[3] for p in pieces), axis=0)
    center = own - jnp.mean(own, axis=-1, keepdims=True)
    inv_std = lax.rsqrt(jnp.mean(center * center, axis=-1, keepdims=True) + 1e-05)
    unit = center * inv_std
    scaled = normed_grad * gain
    input_grad = cotangent.astype(F32) + inv_std * (
        scaled
        - jnp.mean(scaled, axis=-1, keepdims=True)
        - unit * jnp.mean(scaled * unit, axis=-1, keepdims=True)
    )

    terms = scatter_group(
        [out_terms(w, attended, activated, dense_weight, fc2_weight) for w in WAVES]
    )
    layer_out = (own + out_bias + add(*terms)).astype(BF)

    qkv_bias_part = jnp.sum(qkv_bias_part, axis=0)
    biases = jnp.zeros((3 * D,), F32)
    for part in range(3):
        biases = lax.dynamic_update_slice(
            biases, qkv_bias_part[part * T : (part + 1) * T], (part * D + shard * T,)
        )
    vec = jnp.concatenate([gain_part, shift_part, biases]).reshape(80, 128)
    vec = vec + fetch(vec, dc=1)
    vec = vec + fetch(vec, dx=1)
    vec = (vec + fetch(vec, dz=2)) + (fetch(vec, dz=1) + fetch(vec, dz=-1))
    own_vec = jnp.concatenate(
        [
            lax.dynamic_slice(vec, (shard, 0), (1, 128)),
            lax.dynamic_slice(vec, (16 + shard, 0), (1, 128)),
            lax.dynamic_slice(vec, (32 + 3 * shard, 0), (3, 128)),
            jnp.sum(fc1_bias_part, axis=0).reshape(4, 128),
            jnp.sum(out_bias_part, axis=0).reshape(1, 128),
            jnp.zeros((6, 128), F32),
        ]
    )
    own_vec = own_vec + fetch(own_vec, dh=1)
    own_vec = (own_vec + fetch(own_vec, dy=2)) + (fetch(own_vec, dy=1) + fetch(own_vec, dy=-1))
    out_bias_total = own_vec[9]

    return (
        layer_out,
        input_grad,
        own_vec[0],
        own_vec[1],
        qkv_total,
        own_vec[2:5].reshape(QKV),
        dense_total,
        out_bias_total,
        fc1_total,
        own_vec[5:9].reshape(FFL),
        fc2_total,
        out_bias_total,
    )


def solution(mesh):
    return jax.shard_map(
        body,
        mesh=mesh,
        in_specs=(
            P(AXES, None),
            P("shard"),
            P("shard"),
            P("shard", None),
            P("shard"),
            P("shard", None),
            P("shard"),
            P("shard", None),
            P("shard"),
            P("shard", None),
            P("shard"),
            P(AXES, None),
        ),
        out_specs=(
            P(AXES, None),
            P(AXES, None),
            P("shard"),
            P("shard"),
            P("shard", None),
            P("shard"),
            P("shard", None),
            P("shard"),
            P("shard", None),
            P("shard"),
            P("shard", None),
            P("shard"),
        ),
        check_vma=False,
    )
```

```python
import functools
import math

import jax
import jax.numpy as jnp
from jax import lax
from jax.experimental import pallas as pl
from jax.experimental.pallas import tpu as pltpu
from jax.sharding import PartitionSpec as P

D = 2048
HEADS = 32
HEAD_DIM = 64
ROTARY = 32
FF = 8192
SEQ = 2048
T = 128
QKV = 384
FFL = 512
COLS = QKV + FFL
BF = jnp.bfloat16
F32 = jnp.float32
AXES = ("rep", "shard")
MIB = 1 << 20
LOG2E = math.log2(math.e)

PLACES = [
    (xh, y, z, xl, c)
    for xh in range(2)
    for y in range(4)
    for z in range(4)
    for xl in range(2)
    for c in range(2)
]


def flat(xh, y, z, xl, c):
    return (xh * 4 + y % 4) * 16 + (z % 4) * 4 + xl * 2 + c


def fetch_from(x, source):
    return lax.ppermute(x, AXES, [(flat(*source(*p)), flat(*p)) for p in PLACES])


def fetch(x, dz=0, dx=0, dc=0, dy=0, dh=0):
    return fetch_from(
        x, lambda xh, y, z, xl, c: (xh ^ dh, y + dy, z + dz, xl ^ dx, c ^ dc)
    )


def dot(a, b, ca=1, cb=0):
    return lax.dot_general(a, b, (((ca,), (cb,)), ((), ())), preferred_element_type=F32)


def add(*terms):
    total = terms[0].astype(F32)
    for term in terms[1:]:
        total = total + term.astype(F32)
    return total


def zero_of(x):
    return x[0, 0].astype(F32) * 0.0


def gather_near(own):
    return {
        (0, 0): own,
        (1, 0): fetch(own, dz=1),
        (3, 0): fetch(own, dz=-1),
        (0, 1): fetch(own, dx=1),
    }


def gather_next(a):
    return {
        (1, 1): fetch(a[1, 0], dx=1),
        (3, 1): fetch(a[0, 1], dz=-1),
        (2, 0): fetch(a[1, 0], dz=1),
    }


def gather_far(a):
    half = a[1, 1].shape[0] // 2
    return fetch(a[1, 1][:half], dz=1), fetch(a[3, 1][half:], dz=-1)


def both_cores(a):
    pieces = []
    for (dz, dx), own in a.items():
        for dc in range(2):
            at = ((dz * 2 + dx) * 2 + dc) * T
            for part in own if isinstance(own, tuple) else (own,):
                pieces.append((fetch(part, dc=1) if dc else part, at))
                at += part.shape[0]
    return pieces


SLOTS = [(dz, dx, dc) for dz in range(4) for dx in range(2) for dc in range(2)]
WAVES = [[(2, 1), (1, 1), (3, 1), (2, 0)], [(1, 0), (3, 0), (0, 1), (0, 0)]]


def scatter_far(q):
    half = T // 2
    return fetch(q[2, 1][:half], dz=-1), fetch(q[2, 1][half:], dz=1)


def scatter_next(q, far):
    half = T // 2
    q11 = jnp.concatenate([add(q[1, 1][:half], far[0]).astype(BF), q[1, 1][half:]])
    q31 = jnp.concatenate([q[3, 1][:half], add(q[3, 1][half:], far[1]).astype(BF)])
    return fetch(q11, dx=1), fetch(q[2, 0], dz=-1), fetch(q31, dz=1)


def scatter_near(q, further):
    q10 = add(q[1, 0], further[0], further[1]).astype(BF)
    q01 = add(q[0, 1], further[2]).astype(BF)
    return fetch(q10, dz=-1), fetch(q[3, 0], dz=1), fetch(q01, dx=1)


def reduce_far(g):
    half = g[0].shape[0] // 2
    return fetch(g[2][:half], dy=-1), fetch(g[2][half:], dy=1)


def reduce_near(g, far, zero):
    half = g[0].shape[0] // 2
    g1 = jnp.concatenate([add(g[1][:half], far[0], zero).astype(BF), g[1][half:]])
    g3 = jnp.concatenate([g[3][:half], add(g[3][half:], far[1], zero).astype(BF)])
    return g1, g3


def of_rep(refs, dy, dh, n):
    own, one, three, first, second = refs
    if dy == 2:
        return (second if dh else first), 0
    return (own, one, None, three)[dy], dh * n


VMEM = pl.BlockSpec(memory_space=pltpu.VMEM)
SMEM = pl.BlockSpec(memory_space=pltpu.SMEM)
HBM = pl.BlockSpec(memory_space=pltpu.HBM)
ANY = pl.BlockSpec(memory_space=pl.ANY)


def lanes(at, n):
    return pl.ds(pl.multiple_of(at * n, n), n)


def call(kernel, ins, outs, args, scratch=(), vmem=6, flops=0, nbytes=0, exps=0, aliases={}):
    return pl.pallas_call(
        kernel,
        in_specs=ins,
        out_specs=[VMEM] * len(outs),
        out_shape=[
            pltpu.VMEM(o[0], o[1]) if len(o) > 2 else jax.ShapeDtypeStruct(*o) for o in outs
        ],
        scratch_shapes=list(scratch),
        input_output_aliases=aliases,
        compiler_params=pltpu.CompilerParams(vmem_limit_bytes=vmem * MIB),
        cost_estimate=pl.CostEstimate(flops=flops, transcendentals=exps, bytes_accessed=nbytes),
    )(*args)


ROOT = math.sqrt(2.0 / math.pi)


def start_copies(pieces, place, sems):
    copies = [
        pltpu.make_async_copy(src, dst, sems.at[place + i]) for i, (src, dst) in enumerate(pieces)
    ]
    for copy in copies:
        copy.start()
    return copies


def norm_rows(normed_ref, gain, shift, first, count):
    def strip(i, _):
        at = lanes(i, 64)
        x = normed_ref[at, :].astype(F32)
        x = x - jnp.sum(x, axis=1, keepdims=True) * (1.0 / D)
        scale = lax.rsqrt(jnp.sum(x * x, axis=1, keepdims=True) * (1.0 / D) + 1e-05)
        normed_ref[at, :] = (x * scale * gain + shift).astype(BF)
        return 0

    lax.fori_loop(first // 64, (first + count) // 64, strip, 0)


def message_moves(refs, pieces, normed_ref, cot_ref):
    moves = []
    for (array, at), ref in zip(pieces, refs, strict=True):
        to = pl.ds(at, array.shape[0])
        moves.append((ref.at[:, pl.ds(0, D)], normed_ref.at[to]))
        moves.append((ref.at[:, pl.ds(D, D)], cot_ref.at[to]))
    return moves


def near_inputs(pieces, far_vectors, fc2, dense, token_place, me):
    n = len(pieces)
    chips = sorted({at // 256 for _, at in pieces})

    def kernel(t_ref, me_ref, *refs):
        (
            far_ref,
            fc2_ref,
            dense_ref,
            normed_ref,
            cot_ref,
            grad_ref,
            att_ref,
            vec_ref,
            own_ref,
            small_ref,
            flat_ref,
            sems,
        ) = refs[n:]
        moves = [
            (ref.at[pl.ds(0, 16), pl.ds(2 * D, T)], small_ref.at[pl.ds(at // T * 16, 16)])
            for (_, at), ref in zip(pieces, refs[:n], strict=True)
        ]
        for dc in range(2):
            to = small_ref.at[pl.ds((5 * 2 + dc) * 16, 16)]
            moves.append((far_ref.at[pl.ds(dc * 16, 16)], to))
        small_copies = start_copies(moves, 0, sems)
        copies = start_copies(
            message_moves(refs[:n], pieces, normed_ref, cot_ref), n + 2, sems
        )
        for copy in small_copies:
            copy.wait()
        for i in range(16):
            at = t_ref[i]
            small = small_ref[i * 16 : (i + 1) * 16, :].astype(F32)
            for part in range(3):
                flat_ref[0:1, lanes(at * 3 + part, T)] = small[part : part + 1]
            vec_ref[0:1, lanes(at, T)] = small[3:4]
            vec_ref[1:2, lanes(at, T)] = small[4:5]
            vec_ref[2:3, lanes(at, T)] = small[5:6] + small[6:7]
        for part in range(3):
            own_ref[0:1, part * T : (part + 1) * T] = flat_ref[
                0:1, lanes(part * 16 + me_ref[0], T)
            ]
        gain, shift = vec_ref[0:1, :], vec_ref[1:2, :]
        for chip in chips:
            for (_, at), token_copy, cot_copy in zip(pieces, copies[0::2], copies[1::2]):
                if at // 256 == chip:
                    token_copy.wait()
                    cot_copy.wait()
            at = slice(chip * 256, (chip + 1) * 256)
            norm_rows(normed_ref, gain, shift, chip * 256, 256)
            x = cot_ref[at, :]
            grad_ref[at, :] = dot(x, fc2_ref[...], 1, 1).astype(BF)
            att_ref[at, :] = dot(x, dense_ref[...], 1, 1).astype(BF)

    return call(
        kernel,
        [SMEM] * 2 + [HBM] * (n + 1) + [VMEM] * 2,
        [
            ((SEQ, D), BF, 1),
            ((SEQ, D), BF, 1),
            ((SEQ, FFL), BF, 1),
            ((SEQ, T), BF, 1),
            ((8, D), F32, 1),
            ((1, QKV), F32, 1),
        ],
        [token_place, me] + [p for p, _ in pieces] + [far_vectors, fc2, dense],
        [
            pltpu.VMEM((256, T), BF),
            pltpu.VMEM((1, 3 * D), F32),
            pltpu.SemaphoreType.DMA((3 * n + 2,)),
        ],
        flops=2 * SEQ * D * (FFL + T),
        nbytes=20 * MIB,
    )


def forward_inputs(arrays, pieces, weights, vecs, bias, own_bias, fc2, dense, row_place, me):
    n = len(pieces)
    chip = pieces[0][1] // 256

    def kernel(r_ref, me_ref, *refs):
        tok = refs[4 : 4 + n]
        w_refs = refs[4 + n : 9 + n]
        (
            vec_ref,
            bias_ref,
            own_ref,
            fc2_ref,
            dense_ref,
            normed_ref,
            cot_ref,
            grad_ref,
            att_ref,
            w_ref,
            act_ref,
            pre_ref,
            act_t_ref,
            pre_t_ref,
            mixed_ref,
            fc1b_ref,
            outb_ref,
            sems,
        ) = refs[9 + n :]
        copies = start_copies(message_moves(tok, pieces, normed_ref, cot_ref), 0, sems)
        moves = []
        for i, (dy, dx, dc) in enumerate(SLOTS):
            ref, at = of_rep(w_refs, dy, dx, 2 * T)
            moves.append((ref.at[pl.ds(at + dc * T, T)], w_ref.at[lanes(r_ref[i], T)]))
        w_copies = start_copies(moves, 2 * n, sems)
        for copy in copies:
            copy.wait()
        norm_rows(normed_ref, vec_ref[0:1, :], vec_ref[1:2, :], chip * 256, 256)
        rows = slice(chip * 256, (chip + 1) * 256)
        x = cot_ref[rows, :]
        grad_ref[rows, :] = dot(x, fc2_ref[...], 1, 1).astype(BF)
        att_ref[rows, :] = dot(x, dense_ref[...], 1, 1).astype(BF)
        for copy in w_copies:
            copy.wait()

        def product(i):
            at = lanes(i, 256)
            x = normed_ref[at, :]
            mixed_ref[at, :] = dot(x, w_ref[:, :QKV]) + own_ref[...]
            return dot(x, w_ref[:, QKV:]) + bias_ref[...]

        def gelu(i, pre, total):
            at = lanes(i, 256)
            squared = pre * pre
            tanh = jnp.tanh(ROOT * pre * (1.0 + 0.044715 * squared))
            act = (0.5 * pre * (1.0 + tanh)).astype(BF)
            act_ref[at, :] = act
            act_t_ref[:, at] = act.T
            slope = 0.5 * (1.0 + tanh) + 0.5 * pre * (1.0 - tanh * tanh) * ROOT * (
                1.0 + 3 * 0.044715 * squared
            )
            back = (grad_ref[at, :].astype(F32) * slope).astype(BF)
            pre_ref[at, :] = back
            pre_t_ref[:, at] = back.T
            return total + jnp.sum(back.astype(F32).reshape(32, 8, FFL), axis=0)

        def tile(i, carry):
            pre, total = carry
            return product(i), gelu(i - 1, pre, total)

        pre, total = lax.fori_loop(1, 8, tile, (product(0), jnp.zeros((8, FFL), F32)))
        fc1b_ref[...] = gelu(7, pre, total)

        def sums(i, total):
            own = cot_ref[lanes(i, 256), lanes(me_ref[0], T)].astype(F32)
            return total + jnp.sum(own.reshape(32, 8, T), axis=0)

        outb_ref[...] = lax.fori_loop(0, 8, sums, jnp.zeros((8, T), F32))

    return call(
        kernel,
        [SMEM] * 2 + [VMEM] * 4 + [HBM] * (n + 5) + [VMEM] * 5,
        [
            ((SEQ, D), BF, 1),
            ((SEQ, D), BF, 1),
            ((SEQ, FFL), BF, 1),
            ((SEQ, T), BF, 1),
            ((D, COLS), BF, 1),
            ((SEQ, FFL), BF, 1),
            ((SEQ, FFL), BF, 1),
            ((FFL, SEQ), BF, 1),
            ((FFL, SEQ), BF, 1),
            ((SEQ, QKV), F32, 1),
            ((8, FFL), F32),
            ((8, T), F32),
        ],
        [row_place, me]
        + list(arrays)
        + [p for p, _ in pieces]
        + list(weights)
        + [vecs, bias, own_bias, fc2, dense],
        [pltpu.SemaphoreType.DMA((2 * n + 16,))],
        aliases={2: 0, 3: 1, 4: 2, 5: 3},
        flops=2 * SEQ * D * COLS,
        nbytes=8 * MIB,
        exps=SEQ * FFL,
    )


def column_grads(normed, pre_t, act_t, cot, row_place, part_place, core):
    def kernel(r_ref, p_ref, core_ref, n_ref, g_ref, a_ref, c_ref, *outs):
        for dy in (2, 1, 3, 0):
            out = outs[dy]
            for dh in range(2):
                at = slice(dh * FFL, (dh + 1) * FFL)
                chip = r_ref[(dy * 2 + dh) * 2] // 2
                cols = dot(g_ref[...], n_ref[:, lanes(chip, 256)]).astype(BF)
                out[at, lanes(core_ref[0], T)] = cols[:, :T]
                out[at, lanes(1 - core_ref[0], T)] = cols[:, T:]
                part = c_ref[:, lanes(p_ref[dy * 2 + dh], 256)]
                out[at, 256:512] = dot(a_ref[...], part).astype(BF)

    return call(
        kernel,
        [SMEM] * 3 + [VMEM] * 4,
        [((1024, 512), BF)] * 4,
        [row_place, part_place, core, normed, pre_t, act_t, cot],
        flops=4 * SEQ * D * FFL,
        nbytes=4 * MIB,
    )


def head_grads(normed, mixed_t, attended_t, cot, row_place, part_place, core):
    def kernel(r_ref, p_ref, core_ref, n_ref, m_ref, a_ref, c_ref, *outs):
        for dy in (2, 1, 3, 0):
            out = outs[dy]
            for dh in range(2):
                base = dh * FFL
                chip = r_ref[(dy * 2 + dh) * 2] // 2
                cols = dot(m_ref[...], n_ref[:, lanes(chip, 256)]).astype(BF)
                out[base : base + QKV, lanes(core_ref[0], T)] = cols[:, :T]
                out[base : base + QKV, lanes(1 - core_ref[0], T)] = cols[:, T:]
                part = c_ref[:, lanes(p_ref[dy * 2 + dh], 256)]
                out[base + QKV : base + FFL, :] = dot(a_ref[...], part).astype(BF)

    return call(
        kernel,
        [SMEM] * 3 + [VMEM] * 4,
        [((1024, 256), BF)] * 4,
        [row_place, part_place, core, normed, mixed_t, attended_t, cot],
        flops=2 * SEQ * D * (QKV + T),
        nbytes=2 * MIB,
    )


def place_columns(pieces, col_place, part_place):
    def kernel(c_ref, p_ref, *refs):
        fc1_ref, fc2_ref = refs[5:]
        for i, (dy, dh, dc) in enumerate(SLOTS):
            ref, at = of_rep(refs[:5], dy, dh, FFL)
            part = ref[at : at + FFL, dc * T : (dc + 1) * T]
            fc1_ref[:, lanes(c_ref[i], FFL)] = part.astype(F32).T
            if dc == 0:
                to = lanes(p_ref[dy * 2 + dh], 256)
                fc2_ref[:, to] = ref[at : at + FFL, 256:512].astype(F32)

    return call(
        kernel,
        [SMEM] * 2 + [VMEM] * 5,
        [((T, FF), F32), ((FFL, D), F32)],
        [col_place, part_place] + list(pieces),
        vmem=20,
        nbytes=12 * MIB,
    )


def place_heads(pieces, col_place, part_place):
    def kernel(c_ref, p_ref, *refs):
        qkv_ref, dense_ref = refs[5:]
        for i, (dy, dh, dc) in enumerate(SLOTS):
            ref, at = of_rep(refs[:5], dy, dh, FFL)
            for part in range(3):
                rows = slice(at + part * T, at + (part + 1) * T)
                block = ref[rows, dc * T : (dc + 1) * T].astype(F32)
                qkv_ref[:, lanes(c_ref[i] + part * 16, T)] = block.T
            if dc == 0:
                to = lanes(p_ref[dy * 2 + dh], 256)
                dense_ref[:, to] = ref[at + QKV : at + FFL, :].astype(F32)

    return call(
        kernel,
        [SMEM] * 2 + [VMEM] * 5,
        [((T, 3 * D), F32), ((T, D), F32)],
        [col_place, part_place] + list(pieces),
        nbytes=6 * MIB,
    )


def terms(
    chips, attended, activated, dense, fc2, mixed_grad, pre_grad, weight, normed, vecs, before
):
    n = len(chips)

    def kernel(
        before_ref, a_ref, f_ref, d_ref, v_ref, m_ref, p_ref, w_ref, n_ref, vec_ref, *outs
    ):
        mine_ref, other_ref, gain_ref, total_ref = outs
        shift = vec_ref[1:2, :]
        gain_ref[...] = jnp.zeros_like(gain_ref)
        total_ref[...] = jnp.zeros_like(total_ref)
        for i, (dz, dx) in enumerate(chips):
            at = slice((dz * 2 + dx) * 256, (dz * 2 + dx + 1) * 256)
            mine, other = slice(i * T, (i + 1) * T), slice(i * T, (i + 1) * T)
            for col in range(4):
                to = slice(col * 512, (col + 1) * 512)
                total = dot(m_ref[at, :], w_ref[to, :QKV], 1, 1) + dot(
                    p_ref[at, :], w_ref[to, QKV:], 1, 1
                )
                mine_ref[mine, to] = total[:T].astype(BF)
                other_ref[other, to] = total[T:].astype(BF)
                unit = n_ref[at, to].astype(F32) - shift[:, to]
                gain_ref[:, to] += jnp.sum((total * unit).reshape(32, 8, 512), axis=0)
                total_ref[:, to] += jnp.sum(total.reshape(32, 8, 512), axis=0)
                total = dot(a_ref[at, :], d_ref[:, to]) + dot(f_ref[at, :], v_ref[:, to])
                to = slice(D + col * 512, D + (col + 1) * 512)
                mine_ref[mine, to] = total[:T].astype(BF)
                other_ref[other, to] = total[T:].astype(BF)

    return call(
        kernel,
        [ANY] + [VMEM] * 9,
        [((n * T, 2 * D), BF)] * 2 + [((8, D), F32)] * 2,
        [before, attended, activated, dense, fc2, mixed_grad, pre_grad, weight, normed, vecs],
        flops=2 * n * 2 * T * (COLS + T + FFL) * D,
        nbytes=8 * MIB,
    )


TQ = 512
TK = 512


def attention_kernel(blocks, last, n_before, place, cos_ref, sin_ref, *refs):
    refs = refs[n_before:]
    if last:
        first_refs, refs = refs[:8], refs[8:]
        att_ref, out_ref, att_t_ref, out_t_ref, bias_ref = refs[:5]
        q_ref, k_ref, v_ref, do_ref = first_refs[:4]
        dq_ref, dk_ref, dv_ref, o_ref, s_ref, e_ref = refs[5:]
    else:
        mixed_ref, grad_ref, *refs = refs
        refs, done_ref = refs[:8] + refs[9:], refs[8]
        done_ref[...] = jnp.zeros_like(done_ref)
        q_ref, k_ref, v_ref, do_ref, dq_ref, dk_ref, dv_ref, o_ref, s_ref, e_ref = refs
    lane = lax.broadcasted_iota(jnp.int32, (T, 128), 1)
    low_head = lane < HEAD_DIM
    first = (lane % HEAD_DIM) < ROTARY // 2

    def turned(x):
        return jnp.where(
            first, pltpu.roll(x, 128 - ROTARY // 2, 1), pltpu.roll(x, ROTARY // 2, 1)
        )

    def load(slot, _):
        rows = pl.ds(pl.multiple_of(slot * T, T), T)
        at = pl.ds(pl.multiple_of(place[slot] * T, T), T)
        c, s = cos_ref[at, :], sin_ref[at, :]
        query = mixed_ref[rows, 0:128]
        key = mixed_ref[rows, 128:256]
        query = (query * c + turned(query) * s).astype(BF).astype(F32) * (HEAD_DIM**-0.5)
        q_ref[0, at, :] = jnp.where(low_head, query, 0.0).astype(BF)
        q_ref[1, at, :] = jnp.where(low_head, 0.0, query).astype(BF)
        k_ref[at, :] = (key * c + turned(key) * s).astype(BF)
        v_ref[at, 0:128] = mixed_ref[rows, 256:384].astype(BF)
        v_ref[at, 128:256] = jnp.ones((T, 128), BF)
        grad = grad_ref[rows, :].astype(F32)
        do_ref[0, at, :] = jnp.where(low_head, grad, 0.0).astype(BF)
        do_ref[1, at, :] = jnp.where(low_head, 0.0, grad).astype(BF)
        dk_ref[at, :] = jnp.zeros((T, 128), F32)
        dv_ref[at, :] = jnp.zeros((T, 128), F32)
        return 0

    if last:
        for to, at in ((dq_ref, 4), (dk_ref, 5), (dv_ref, 6), (o_ref, 7)):
            to[...] = first_refs[at][...]
    else:
        lax.fori_loop(0, 16, load, 0)

    lane_q = lax.broadcasted_iota(jnp.int32, (TQ, 128), 1)
    low_q = lane_q < HEAD_DIM

    def head(h, i, rows):
        query = q_ref[h, rows, :]

        def scores(j, top, masked):
            at = lanes(j, TK)
            s = dot(query, k_ref[at, :], 1, 1)
            if masked:
                row = lax.broadcasted_iota(jnp.int32, (TQ, TK), 0)
                col = lax.broadcasted_iota(jnp.int32, (TQ, TK), 1)
                s = jnp.where(row >= col, s, -1e30)
            s_ref[:, at] = s
            for n in range(TK // 128):
                top = jnp.maximum(top, s[:, n * 128 : (n + 1) * 128])
            return top

        top = jnp.full((TQ, 128), -1e30, F32)
        top = lax.fori_loop(0, i, lambda j, t: scores(j, t, False), top)
        top = jnp.max(scores(i, top, True), axis=1, keepdims=True)

        def weigh(j, total):
            at = lanes(j, TK)
            e = jnp.exp2((s_ref[:, at] - top) * LOG2E).astype(BF)
            e_ref[:, at] = e
            return total + dot(e, v_ref[at, :])

        total = lax.fori_loop(0, i + 1, weigh, jnp.zeros((TQ, 256), F32))
        inverse = 1.0 / total[:, 128:]
        o = total[:, :128] * inverse
        grad = do_ref[h, rows, :].astype(F32) * inverse
        delta = jnp.sum(grad * o, axis=1, keepdims=True)
        grad = grad.astype(BF)

        def back(j, total):
            at = lanes(j, TK)
            e = e_ref[:, at]
            dp = dot(grad, v_ref[at, 0:128], 1, 1)
            ds = (e.astype(F32) * (dp - delta)).astype(BF)
            dk_ref[at, :] += dot(ds, query, 0, 0)
            dv_ref[at, :] += dot(e, grad, 0, 0)
            return total + dot(ds, k_ref[at, :])

        return o, lax.fori_loop(0, i + 1, back, jnp.zeros((TQ, 128), F32))

    def block(i, _):
        rows = lanes(i, TQ)
        o_low, dq_low = head(0, i, rows)
        o_high, dq_high = head(1, i, rows)
        o_ref[rows, :] = jnp.where(low_q, o_low, o_high).astype(BF)
        dq_ref[rows, :] = jnp.where(low_q, dq_low, dq_high) * (HEAD_DIM**-0.5)
        return 0

    lax.fori_loop(blocks[0], blocks[1], block, 0)
    if not last:
        return

    def store(slot, total):
        rows = pl.ds(pl.multiple_of(slot * T, T), T)
        at = pl.ds(pl.multiple_of(place[slot] * T, T), T)
        c, s = cos_ref[at, :], sin_ref[at, :]
        att = o_ref[at, :]
        att_ref[rows, :] = att
        att_t_ref[:, rows] = att.T
        dq, dk = dq_ref[at, :], dk_ref[at, :]
        new = []
        for part, grad in enumerate(
            (dq * c - turned(dq) * s, dk * c - turned(dk) * s, dv_ref[at, :])
        ):
            low = grad.astype(BF)
            cols = slice(part * T, (part + 1) * T)
            out_ref[rows, cols] = low
            out_t_ref[cols, rows] = low.T
            new.append(total[part] + jnp.sum(low.astype(F32).reshape(16, 8, T), axis=0))
        return tuple(new)

    zero = jnp.zeros((8, T), F32)
    sums = lax.fori_loop(0, 16, store, (zero, zero, zero))
    for part in range(3):
        bias_ref[:, part * T : (part + 1) * T] = sums[part]


def attention_first(place, cosine, sine, mixed, attended_grad, before):
    return call(
        functools.partial(attention_kernel, (0, 3), False, len(before)),
        [SMEM] + [VMEM] * 2 + [ANY] * len(before) + [VMEM] * 2,
        [
            ((2, SEQ, 128), BF, 1),
            ((SEQ, 128), BF, 1),
            ((SEQ, 256), BF, 1),
            ((2, SEQ, 128), BF, 1),
            ((SEQ, 128), F32, 1),
            ((SEQ, 128), F32, 1),
            ((SEQ, 128), F32, 1),
            ((SEQ, 128), BF, 1),
            ((8, 128), jnp.int32),
        ],
        [place, cosine, sine, *before, mixed, attended_grad],
        [pltpu.VMEM((TQ, SEQ), F32), pltpu.VMEM((TQ, SEQ), BF)],
        vmem=12,
        flops=8 * SEQ * SEQ * 64 * 2,
        exps=SEQ * SEQ // 2,
        nbytes=3 * MIB,
    )


def attention_last(place, cosine, sine, state, before):
    return call(
        functools.partial(attention_kernel, (3, 4), True, len(before)),
        [SMEM] + [VMEM] * 2 + [ANY] * len(before) + [VMEM] * 8,
        [
            ((SEQ, T), BF, 1),
            ((SEQ, QKV), BF, 1),
            ((T, SEQ), BF, 1),
            ((QKV, SEQ), BF, 1),
            ((8, QKV), F32),
        ],
        [place, cosine, sine, *before] + list(state),
        [
            pltpu.VMEM((SEQ, 128), F32),
            pltpu.VMEM((SEQ, 128), F32),
            pltpu.VMEM((SEQ, 128), F32),
            pltpu.VMEM((SEQ, 128), BF),
            pltpu.VMEM((TQ, SEQ), F32),
            pltpu.VMEM((TQ, SEQ), BF),
        ],
        vmem=16,
        flops=6 * SEQ * SEQ * 64 * 2,
        exps=SEQ * SEQ // 2,
        nbytes=3 * MIB,
    )


def rotary_tables():
    lane = lax.broadcasted_iota(jnp.int32, (SEQ, 128), 1) % HEAD_DIM
    place = lax.broadcasted_iota(jnp.int32, (SEQ, 128), 0).astype(F32)
    freq = (lane % (ROTARY // 2)).astype(F32)
    angle = place * jnp.exp(freq * (-2.0 * math.log(10000.0) / ROTARY))
    turns = lane < ROTARY
    cosine = jnp.where(turns, jnp.cos(angle), 1.0)
    sine = jnp.where(turns, jnp.sin(angle), 0.0)
    return cosine, jnp.where(lane < ROTARY // 2, -sine, sine)


def body(
    tokens,
    ln_gain,
    ln_shift,
    qkv_weight,
    qkv_bias,
    dense_weight,
    dense_bias,
    fc1_weight,
    fc1_bias,
    fc2_weight,
    fc2_bias,
    cotangent,
):
    rep, shard = lax.axis_index("rep"), lax.axis_index("shard")
    xh, y = rep // 4, rep % 4
    z, xl, c = shard // 4, (shard // 2) % 2, shard % 2
    token_place = jnp.stack(
        [((z + dz) % 4) * 4 + (xl ^ dx) * 2 + (c ^ dc) for dz, dx, dc in SLOTS]
    ).astype(jnp.int32)
    weight_place = jnp.stack(
        [((z + y + dy) % 4) * 4 + (xl ^ dx) * 2 + (c ^ dc) for dy, dx, dc in SLOTS]
    ).astype(jnp.int32)
    row_place = jnp.stack(
        [((z + y + dy) % 4) * 4 + (xl ^ xh ^ dh) * 2 + (c ^ dc) for dy, dh, dc in SLOTS]
    ).astype(jnp.int32)
    col_place = jnp.stack(
        [((z - y - dy) % 4) * 4 + (xl ^ xh ^ dh) * 2 + (c ^ dc) for dy, dh, dc in SLOTS]
    ).astype(jnp.int32)
    part_place = jnp.stack(
        [((y + dy) % 4) * 2 + (xh ^ dh) for dy in range(4) for dh in range(2)]
    ).astype(jnp.int32)
    me, core = shard.reshape(1).astype(jnp.int32), c.reshape(1).astype(jnp.int32)

    def columns_of(dx):
        chip = ((z - y) % 4) * 2 + (xl ^ dx)
        qkv = [
            lax.dynamic_slice(qkv_weight, (0, part * D + chip * 2 * T), (T, 2 * T))
            for part in range(3)
        ]
        fc1 = lax.dynamic_slice(fc1_weight, (0, chip * 2 * FFL), (T, 2 * FFL))
        return jnp.concatenate(
            [
                jnp.concatenate(
                    [p[:, at * T : (at + 1) * T] for p in qkv]
                    + [fc1[:, at * FFL : (at + 1) * FFL]],
                    axis=1,
                )
                for at in range(2)
            ]
        )

    columns = [columns_of(dx) for dx in range(2)]
    both = [
        fetch_from(columns[dx], lambda xh, y, z, xl, c: (xh, y, z + y, xl ^ dx, c))
        for dx in range(2)
    ]

    vectors = [v.reshape(-1, T) for v in (qkv_bias, ln_gain, ln_shift, dense_bias, fc2_bias)]
    vectors = jnp.concatenate(vectors + [jnp.zeros((T - 7, T), BF)])
    wait = (zero_of(columns[0]) + zero_of(columns[1])).astype(BF)
    message = jnp.concatenate([tokens + wait, cotangent, vectors], axis=1)
    near = gather_near(message)
    far_vectors = fetch(vectors[:16], dz=2, dx=1)
    far_vectors = jnp.concatenate([far_vectors, fetch(far_vectors, dc=1)])
    mine = [lax.dynamic_slice(b, (c * T, 0), (T, COLS)) for b in both]
    other = [lax.dynamic_slice(b, ((1 - c) * T, 0), (T, COLS)) for b in both]
    other = fetch(jnp.concatenate(other), dc=1)
    own_rows = jnp.concatenate([mine[0], other[:T], mine[1], other[T:]])
    cosine, sine = rotary_tables()
    one, three = fetch(own_rows, dy=1), fetch(own_rows, dy=-1)
    further = gather_next(near)
    weights = (own_rows, one, three, fetch(one[: 2 * T], dy=1), fetch(three[2 * T :], dy=-1))
    far = {(2, 1): gather_far(further)}
    *arrays, vecs, own_qkv_bias = near_inputs(
        both_cores(near | further), far_vectors, fc2_weight, dense_weight, token_place, me
    )
    gain, out_bias = vecs[0:1], vecs[2:3]
    (
        normed,
        all_cot,
        _,
        attended_grad,
        weight,
        activated,
        pre_grad,
        act_t,
        pre_t,
        mixed,
        fc1_bias_part,
        out_bias_part,
    ) = forward_inputs(
        arrays,
        both_cores(far),
        weights,
        vecs,
        fc1_bias.astype(F32).reshape(1, FFL),
        own_qkv_bias,
        fc2_weight,
        dense_weight,
        weight_place,
        me,
    )

    early = column_grads(normed, pre_t, act_t, all_cot, row_place, part_place, core)
    *state, done = attention_first(token_place, cosine, sine, mixed, attended_grad, early)
    early_near = reduce_near(early, reduce_far(early), done[0, 0].astype(F32))
    attended, mixed_grad, attended_t, mixed_t, qkv_bias_part = attention_last(
        token_place, cosine, sine, state, early_near
    )
    late = head_grads(normed, mixed_t, attended_t, all_cot, row_place, part_place, core)
    early = add(early[0], fetch(early_near[0], dy=-1), fetch(early_near[1], dy=1))
    early_far_own = early[FFL:].astype(BF)

    def the_terms(chips, before):
        return terms(
            chips,
            attended,
            activated,
            dense_weight,
            fc2_weight,
            mixed_grad,
            pre_grad,
            weight,
            normed,
            vecs,
            before,
        )

    early_far = fetch(early_far_own, dh=1)
    late_far = reduce_far(late)
    mine0, other0, gain0, shift0 = the_terms(WAVES[0], early_far_own)
    other0 = fetch(other0, dc=1)
    mine1, other1, gain1, shift1 = the_terms(WAVES[1], gain0)
    zero = zero_of(gain1)

    early = add(early[:FFL], early_far, zero).astype(BF)
    late_near = reduce_near(late, late_far, zero)
    late_near = fetch(late_near[0], dy=-1), fetch(late_near[1], dy=1)
    other1 = fetch(other1, dc=1)
    early_owner = jnp.concatenate([early[:, :T], fetch(early[:, T : 2 * T], dc=1)], axis=1)
    to_owner = lambda xh, y, z, xl, c: (xh, y, z - y, xl ^ xh, c)
    early_owner = fetch_from(early_owner, to_owner)
    qkv_bias_part = jnp.sum(qkv_bias_part, axis=0)
    biases = jnp.zeros((3 * D,), F32)
    for part in range(3):
        biases = lax.dynamic_update_slice(
            biases, qkv_bias_part[part * T : (part + 1) * T], (part * D + shard * T,)
        )
    gain_part = jnp.sum(gain0 + gain1, axis=0) / gain[0]
    shift_part = jnp.sum(shift0 + shift1, axis=0)
    vec = jnp.concatenate([gain_part, shift_part, biases]).reshape(80, 128)
    vec = vec + fetch(vec, dc=1)

    late = add(late[0], *late_near)
    late_far = fetch(late[FFL:].astype(BF), dh=1)
    early = jnp.concatenate([early_owner, early[:, 2 * T :]], axis=1)
    early_far = fetch(early, dh=1)
    q = {}
    for chips, mine, other in zip(WAVES, (mine0, mine1), (other0, other1)):
        for n, chip in enumerate(chips):
            at = slice(n * T, (n + 1) * T)
            q[chip] = add(mine[at], other[at]).astype(BF)
    far = scatter_far(q)
    vec = vec + fetch(vec, dx=1)

    early = jnp.concatenate([early, early_far])
    early_one, early_three = fetch(early, dy=1), fetch(early, dy=-1)
    late = add(late[:FFL], late_far).astype(BF)
    late_owner = jnp.concatenate([late[:QKV, :T], fetch(late[:QKV, T:], dc=1)], axis=1)
    late_owner = fetch_from(late_owner, to_owner)
    further = scatter_next(q, far)
    vec = (vec + fetch(vec, dz=2)) + (fetch(vec, dz=1) + fetch(vec, dz=-1))

    late = jnp.concatenate([late_owner, late[QKV:]])
    late_far = fetch(late, dh=1)
    nearest = scatter_near(q, further)
    own_vec = jnp.concatenate(
        [
            lax.dynamic_slice(vec, (shard, 0), (1, 128)),
            lax.dynamic_slice(vec, (16 + shard, 0), (1, 128)),
            lax.dynamic_slice(vec, (32 + 3 * shard, 0), (3, 128)),
            jnp.sum(fc1_bias_part, axis=0).reshape(4, 128),
            jnp.sum(out_bias_part, axis=0).reshape(1, 128),
            jnp.zeros((6, 128), F32),
        ]
    )
    own_vec = own_vec + fetch(own_vec, dh=1)

    late = jnp.concatenate([late, late_far])
    late_one, late_three = fetch(late, dy=1), fetch(late, dy=-1)
    early = (
        early,
        early_one,
        early_three,
        fetch(early_one[:FFL], dy=1),
        fetch(early_three[FFL:], dy=-1),
    )
    own_vec = (own_vec + fetch(own_vec, dy=2)) + (fetch(own_vec, dy=1) + fetch(own_vec, dy=-1))
    total = add(q[0, 0], *nearest)
    own = tokens.astype(F32)
    layer_out = (own + out_bias + total[:, D:]).astype(BF)
    center = own - jnp.mean(own, axis=-1, keepdims=True)
    inv_std = lax.rsqrt(jnp.mean(center * center, axis=-1, keepdims=True) + 1e-05)
    unit = center * inv_std
    scaled = total[:, :D] * gain
    input_grad = cotangent.astype(F32) + inv_std * (
        scaled
        - jnp.mean(scaled, axis=-1, keepdims=True)
        - unit * jnp.mean(scaled * unit, axis=-1, keepdims=True)
    )

    late = (
        late,
        late_one,
        late_three,
        fetch(late_one[:FFL], dy=1),
        fetch(late_three[FFL:], dy=-1),
    )
    fc1_total, fc2_total = place_columns(early, col_place, part_place)
    qkv_total, dense_total = place_heads(late, col_place, part_place)
    out_bias_total = own_vec[9]

    return (
        layer_out,
        input_grad,
        own_vec[0],
        own_vec[1],
        qkv_total,
        own_vec[2:5].reshape(QKV),
        dense_total,
        out_bias_total,
        fc1_total,
        own_vec[5:9].reshape(FFL),
        fc2_total,
        out_bias_total,
    )


def solution(mesh):
    return jax.shard_map(
        body,
        mesh=mesh,
        in_specs=(
            P(AXES, None),
            P("shard"),
            P("shard"),
            P("shard", None),
            P("shard"),
            P("shard", None),
            P("shard"),
            P("shard", None),
            P("shard"),
            P("shard", None),
            P("shard"),
            P(AXES, None),
        ),
        out_specs=(
            P(AXES, None),
            P(AXES, None),
            P("shard"),
            P("shard"),
            P("shard", None),
            P("shard"),
            P("shard", None),
            P("shard"),
            P("shard", None),
            P("shard"),
            P("shard", None),
            P("shard"),
        ),
        check_vma=False,
    )
```

```python
import functools
import math

import jax
import jax.numpy as jnp
from jax import lax
from jax.experimental import pallas as pl
from jax.experimental.pallas import tpu as pltpu
from jax.sharding import PartitionSpec as P

D = 2048
HEADS = 32
HEAD_DIM = 64
ROTARY = 32
FF = 8192
SEQ = 2048
T = 128
QKV = 384
FFL = 512
COLS = QKV + FFL
BF = jnp.bfloat16
F32 = jnp.float32
AXES = ("rep", "shard")
MIB = 1 << 20
LOG2E = math.log2(math.e)

PLACES = [
    (xh, y, z, xl, c)
    for xh in range(2)
    for y in range(4)
    for z in range(4)
    for xl in range(2)
    for c in range(2)
]


def flat(xh, y, z, xl, c):
    return (xh * 4 + y % 4) * 16 + (z % 4) * 4 + xl * 2 + c


def fetch_from(x, source):
    return lax.ppermute(x, AXES, [(flat(*source(*p)), flat(*p)) for p in PLACES])


def fetch(x, dz=0, dx=0, dc=0, dy=0, dh=0):
    return fetch_from(
        x, lambda xh, y, z, xl, c: (xh ^ dh, y + dy, z + dz, xl ^ dx, c ^ dc)
    )


def dot(a, b, ca=1, cb=0):
    return lax.dot_general(a, b, (((ca,), (cb,)), ((), ())), preferred_element_type=F32)


def add(*terms):
    total = terms[0].astype(F32)
    for term in terms[1:]:
        total = total + term.astype(F32)
    return total


def zero_of(x):
    return x[0, 0].astype(F32) * 0.0


def gather_near(own):
    return {
        (0, 0): own,
        (1, 0): fetch(own, dz=1),
        (3, 0): fetch(own, dz=-1),
        (0, 1): fetch(own, dx=1),
    }


def gather_next(a):
    return {
        (1, 1): fetch(a[1, 0], dx=1),
        (3, 1): fetch(a[0, 1], dz=-1),
        (2, 0): fetch(a[1, 0], dz=1),
    }


def gather_far(a):
    half = a[1, 1].shape[0] // 2
    return fetch(a[1, 1][:half], dz=1), fetch(a[3, 1][half:], dz=-1)


def both_cores(a):
    pieces = []
    for (dz, dx), own in a.items():
        for dc in range(2):
            at = ((dz * 2 + dx) * 2 + dc) * T
            for part in own if isinstance(own, tuple) else (own,):
                pieces.append((fetch(part, dc=1) if dc else part, at))
                at += part.shape[0]
    return pieces


SLOTS = [(dz, dx, dc) for dz in range(4) for dx in range(2) for dc in range(2)]
WAVES = [[(2, 1)], [(1, 1), (3, 1), (2, 0)], [(1, 0), (3, 0)], [(0, 1), (0, 0)]]


def scatter_far(q):
    half = T // 2
    return fetch(q[2, 1][:half], dz=-1), fetch(q[2, 1][half:], dz=1)


def scatter_next(q, far, zero):
    half = T // 2
    q11 = jnp.concatenate([add(q[1, 1][:half], far[0], zero).astype(BF), q[1, 1][half:]])
    q31 = jnp.concatenate([q[3, 1][:half], add(q[3, 1][half:], far[1], zero).astype(BF)])
    return fetch(q[2, 0], dz=-1), fetch(q31, dz=1), fetch(q11, dx=1)


def scatter_near(q, further, zero):
    q10 = add(q[1, 0], further[0], further[2], zero).astype(BF)
    q01 = add(q[0, 1], further[1], zero).astype(BF)
    return fetch(q10, dz=-1), fetch(q[3, 0], dz=1), fetch(q01, dx=1)


def reduce_far(g):
    half = g[0].shape[0] // 2
    return fetch(g[2][:half], dy=-1), fetch(g[2][half:], dy=1)


def reduce_near(g, far, zero):
    half = g[0].shape[0] // 2
    g1 = jnp.concatenate([add(g[1][:half], far[0], zero).astype(BF), g[1][half:]])
    g3 = jnp.concatenate([g[3][:half], add(g[3][half:], far[1], zero).astype(BF)])
    return g1, g3


def of_rep(refs, dy, dx, n):
    own, one, three, first, second = refs
    if dy == 2:
        return (second if dx else first), 0
    return (own, one, None, three)[dy], dx * n


VMEM = pl.BlockSpec(memory_space=pltpu.VMEM)
SMEM = pl.BlockSpec(memory_space=pltpu.SMEM)
HBM = pl.BlockSpec(memory_space=pltpu.HBM)
ANY = pl.BlockSpec(memory_space=pl.ANY)


def lanes(at, n):
    return pl.ds(pl.multiple_of(at * n, n), n)


def call(kernel, ins, outs, args, scratch=(), vmem=10, flops=0, nbytes=0, exps=0, aliases={}):
    return pl.pallas_call(
        kernel,
        in_specs=ins,
        out_specs=[VMEM] * len(outs),
        out_shape=[
            pltpu.VMEM(o[0], o[1]) if len(o) > 2 else jax.ShapeDtypeStruct(*o) for o in outs
        ],
        scratch_shapes=list(scratch),
        input_output_aliases=aliases,
        compiler_params=pltpu.CompilerParams(vmem_limit_bytes=vmem * MIB),
        cost_estimate=pl.CostEstimate(flops=flops, transcendentals=exps, bytes_accessed=nbytes),
    )(*args)


ROOT = math.sqrt(2.0 / math.pi)


def start_copies(pieces, place, sems):
    copies = [
        pltpu.make_async_copy(src, dst, sems.at[place + i]) for i, (src, dst) in enumerate(pieces)
    ]
    for copy in copies:
        copy.start()
    return copies


def norm_rows(normed_ref, gain, shift, first, count):
    def strip(i, _):
        at = lanes(i, 64)
        x = normed_ref[at, :].astype(F32)
        x = x - jnp.sum(x, axis=1, keepdims=True) * (1.0 / D)
        scale = lax.rsqrt(jnp.sum(x * x, axis=1, keepdims=True) * (1.0 / D) + 1e-05)
        normed_ref[at, :] = (x * scale * gain + shift).astype(BF)
        return 0

    lax.fori_loop(first // 64, (first + count) // 64, strip, 0)


def message_moves(refs, pieces, normed_ref, cot_ref):
    moves = []
    for (array, at), ref in zip(pieces, refs, strict=True):
        to = pl.ds(at, array.shape[0])
        moves.append((ref.at[:, pl.ds(0, D)], normed_ref.at[to]))
        moves.append((ref.at[:, pl.ds(D, D)], cot_ref.at[to]))
    return moves


def near_inputs(pieces, far_vectors, fc2, dense, token_place, me):
    n = len(pieces)
    chips = sorted({at // 256 for _, at in pieces})

    def kernel(t_ref, me_ref, *refs):
        (
            far_ref,
            fc2_ref,
            dense_ref,
            normed_ref,
            cot_ref,
            grad_ref,
            att_ref,
            vec_ref,
            own_ref,
            small_ref,
            flat_ref,
            sems,
        ) = refs[n:]
        moves = [
            (ref.at[pl.ds(0, 16), pl.ds(2 * D, T)], small_ref.at[pl.ds(at // T * 16, 16)])
            for (_, at), ref in zip(pieces, refs[:n], strict=True)
        ]
        for dc in range(2):
            to = small_ref.at[pl.ds((5 * 2 + dc) * 16, 16)]
            moves.append((far_ref.at[pl.ds(dc * 16, 16)], to))
        small_copies = start_copies(moves, 0, sems)
        copies = start_copies(
            message_moves(refs[:n], pieces, normed_ref, cot_ref), n + 2, sems
        )
        for copy in small_copies:
            copy.wait()
        for i in range(16):
            at = t_ref[i]
            small = small_ref[i * 16 : (i + 1) * 16, :].astype(F32)
            for part in range(3):
                flat_ref[0:1, lanes(at * 3 + part, T)] = small[part : part + 1]
            vec_ref[0:1, lanes(at, T)] = small[3:4]
            vec_ref[1:2, lanes(at, T)] = small[4:5]
            vec_ref[2:3, lanes(at, T)] = small[5:6] + small[6:7]
        for part in range(3):
            own_ref[0:1, part * T : (part + 1) * T] = flat_ref[
                0:1, lanes(part * 16 + me_ref[0], T)
            ]
        gain, shift = vec_ref[0:1, :], vec_ref[1:2, :]
        for chip in chips:
            for (_, at), token_copy, cot_copy in zip(pieces, copies[0::2], copies[1::2]):
                if at // 256 == chip:
                    token_copy.wait()
                    cot_copy.wait()
            norm_rows(normed_ref, gain, shift, chip * 256, 256)

        def tile(i, _):
            at = lanes(i, TM)
            x = cot_ref[at, :]
            grad_ref[at, :] = dot(x, fc2_ref[...], 1, 1).astype(BF)
            att_ref[at, :] = dot(x, dense_ref[...], 1, 1).astype(BF)
            return 0

        lax.fori_loop(0, SEQ // TM, tile, 0)

    return call(
        kernel,
        [SMEM] * 2 + [HBM] * (n + 1) + [VMEM] * 2,
        [
            ((SEQ, D), BF, 1),
            ((SEQ, D), BF, 1),
            ((SEQ, FFL), BF, 1),
            ((SEQ, T), BF, 1),
            ((8, D), F32, 1),
            ((1, QKV), F32, 1),
        ],
        [token_place, me] + [p for p, _ in pieces] + [far_vectors, fc2, dense],
        [
            pltpu.VMEM((256, T), BF),
            pltpu.VMEM((1, 3 * D), F32),
            pltpu.SemaphoreType.DMA((3 * n + 2,)),
        ],
        flops=2 * SEQ * D * (FFL + T),
        nbytes=20 * MIB,
    )


def forward_inputs(arrays, pieces, weights, vecs, bias, own_bias, fc2, dense, row_place, me):
    n = len(pieces)
    chip = pieces[0][1] // 256

    def kernel(r_ref, me_ref, *refs):
        tok = refs[4 : 4 + n]
        w_refs = refs[4 + n : 9 + n]
        (
            vec_ref,
            bias_ref,
            own_ref,
            fc2_ref,
            dense_ref,
            normed_ref,
            cot_ref,
            grad_ref,
            att_ref,
            w_ref,
            act_ref,
            pre_ref,
            act_t_ref,
            pre_t_ref,
            mixed_ref,
            fc1b_ref,
            outb_ref,
            sems,
        ) = refs[9 + n :]
        copies = start_copies(message_moves(tok, pieces, normed_ref, cot_ref), 0, sems)
        moves = []
        for i, (dy, dx, dc) in enumerate(SLOTS):
            ref, at = of_rep(w_refs, dy, dx, 2 * T)
            moves.append((ref.at[pl.ds(at + dc * T, T)], w_ref.at[lanes(r_ref[i], T)]))
        w_copies = start_copies(moves, 2 * n, sems)
        for copy in copies:
            copy.wait()
        norm_rows(normed_ref, vec_ref[0:1, :], vec_ref[1:2, :], chip * 256, 256)
        rows = slice(chip * 256, (chip + 1) * 256)
        x = cot_ref[rows, :]
        grad_ref[rows, :] = dot(x, fc2_ref[...], 1, 1).astype(BF)
        att_ref[rows, :] = dot(x, dense_ref[...], 1, 1).astype(BF)
        for copy in w_copies:
            copy.wait()

        def product(i):
            at = lanes(i, TM)
            x = normed_ref[at, :]
            mixed_ref[at, :] = dot(x, w_ref[:, :QKV]) + own_ref[...]
            return dot(x, w_ref[:, QKV:]) + bias_ref[...]

        def gelu(i, pre, total):
            at = lanes(i, TM)
            squared = pre * pre
            tanh = jnp.tanh(ROOT * pre * (1.0 + 0.044715 * squared))
            act = (0.5 * pre * (1.0 + tanh)).astype(BF)
            act_ref[at, :] = act
            act_t_ref[:, at] = act.T
            slope = 0.5 * (1.0 + tanh) + 0.5 * pre * (1.0 - tanh * tanh) * ROOT * (
                1.0 + 3 * 0.044715 * squared
            )
            back = (grad_ref[at, :].astype(F32) * slope).astype(BF)
            pre_ref[at, :] = back
            pre_t_ref[:, at] = back.T
            return total + jnp.sum(back.astype(F32).reshape(TM // 8, 8, FFL), axis=0)

        def tile(i, carry):
            pre, total = carry
            return product(i), gelu(i - 1, pre, total)

        pre, total = lax.fori_loop(1, SEQ // TM, tile, (product(0), jnp.zeros((8, FFL), F32)))
        fc1b_ref[...] = gelu(SEQ // TM - 1, pre, total)

        def sums(i, total):
            own = cot_ref[lanes(i, 256), lanes(me_ref[0], T)].astype(F32)
            return total + jnp.sum(own.reshape(32, 8, T), axis=0)

        outb_ref[...] = lax.fori_loop(0, 8, sums, jnp.zeros((8, T), F32))

    return call(
        kernel,
        [SMEM] * 2 + [VMEM] * 4 + [HBM] * (n + 5) + [VMEM] * 5,
        [
            ((SEQ, D), BF, 1),
            ((SEQ, D), BF, 1),
            ((SEQ, FFL), BF, 1),
            ((SEQ, T), BF, 1),
            ((D, COLS), BF, 1),
            ((SEQ, FFL), BF, 1),
            ((SEQ, FFL), BF, 1),
            ((FFL, SEQ), BF, 1),
            ((FFL, SEQ), BF, 1),
            ((SEQ, QKV), F32, 1),
            ((8, FFL), F32),
            ((8, T), F32),
        ],
        [row_place, me]
        + list(arrays)
        + [p for p, _ in pieces]
        + list(weights)
        + [vecs, bias, own_bias, fc2, dense],
        [pltpu.SemaphoreType.DMA((2 * n + 16,))],
        aliases={2: 0, 3: 1, 4: 2, 5: 3},
        flops=2 * SEQ * D * COLS,
        nbytes=8 * MIB,
        exps=SEQ * FFL,
    )


def column_grads(normed, pre_t, act_t, cot, row_place, part_place, core):
    def kernel(r_ref, p_ref, core_ref, n_ref, g_ref, a_ref, c_ref, *outs):
        for dy in (2, 1, 3, 0):
            out = outs[dy]
            for dh in range(2):
                at = slice(dh * FFL, (dh + 1) * FFL)
                chip = r_ref[(dy * 2 + dh) * 2] // 2
                cols = dot(g_ref[...], n_ref[:, lanes(chip, 256)]).astype(BF)
                out[at, lanes(core_ref[0], T)] = cols[:, :T]
                out[at, lanes(1 - core_ref[0], T)] = cols[:, T:]
                part = c_ref[:, lanes(p_ref[dy * 2 + dh], 256)]
                out[at, 256:512] = dot(a_ref[...], part).astype(BF)

    return call(
        kernel,
        [SMEM] * 3 + [VMEM] * 4,
        [((1024, 512), BF)] * 4,
        [row_place, part_place, core, normed, pre_t, act_t, cot],
        flops=4 * SEQ * D * FFL,
        nbytes=4 * MIB,
    )


def head_grads(normed, mixed_t, attended_t, cot, row_place, part_place, core, me, bias_parts):
    def kernel(
        r_ref, p_ref, core_ref, me_ref, n_ref, m_ref, a_ref, c_ref, qkv_ref, fc1_ref, out_ref, *outs
    ):
        vec_ref = outs[4]
        vec_ref[...] = jnp.zeros_like(vec_ref)
        at = me_ref[0]
        sums = jnp.sum(qkv_ref[...], axis=0, keepdims=True)
        for part in range(3):
            vec_ref[pl.ds(32 + part * 16 + at, 1), :] = sums[:, part * T : (part + 1) * T]
        sums = jnp.sum(fc1_ref[...], axis=0, keepdims=True)
        for part in range(4):
            vec_ref[pl.ds(80 + at * 4 + part, 1), :] = sums[:, part * T : (part + 1) * T]
        vec_ref[pl.ds(144 + at, 1), :] = jnp.sum(out_ref[...], axis=0, keepdims=True)
        for dy in (2, 1, 3, 0):
            out = outs[dy]
            for dh in range(2):
                base = dh * FFL
                chip = r_ref[(dy * 2 + dh) * 2] // 2
                cols = dot(m_ref[...], n_ref[:, lanes(chip, 256)]).astype(BF)
                out[base : base + QKV, lanes(core_ref[0], T)] = cols[:, :T]
                out[base : base + QKV, lanes(1 - core_ref[0], T)] = cols[:, T:]
                part = c_ref[:, lanes(p_ref[dy * 2 + dh], 256)]
                out[base + QKV : base + FFL, :] = dot(a_ref[...], part).astype(BF)

    return call(
        kernel,
        [SMEM] * 4 + [VMEM] * 7,
        [((1024, 256), BF)] * 4 + [((160, T), F32)],
        [row_place, part_place, core, me, normed, mixed_t, attended_t, cot, *bias_parts],
        flops=2 * SEQ * D * (QKV + T),
        nbytes=2 * MIB,
    )


def place_columns(pieces, col_place, part_place):
    def kernel(c_ref, p_ref, *refs):
        fc1_ref, fc2_ref = refs[5:]
        for i, (dy, dh, dc) in enumerate(SLOTS):
            ref, at = of_rep(refs[:5], dy, dh, FFL)
            part = ref[at : at + FFL, dc * T : (dc + 1) * T]
            fc1_ref[:, lanes(c_ref[i], FFL)] = part.astype(F32).T
            if dc == 0:
                to = lanes(p_ref[dy * 2 + dh], 256)
                fc2_ref[:, to] = ref[at : at + FFL, 256:512].astype(F32)

    return call(
        kernel,
        [SMEM] * 2 + [VMEM] * 5,
        [((T, FF), F32), ((FFL, D), F32)],
        [col_place, part_place] + list(pieces),
        vmem=20,
        nbytes=12 * MIB,
    )


def place_heads(pieces, col_place, part_place):
    def kernel(c_ref, p_ref, *refs):
        qkv_ref, dense_ref = refs[5:]
        for i, (dy, dh, dc) in enumerate(SLOTS):
            ref, at = of_rep(refs[:5], dy, dh, FFL)
            for part in range(3):
                rows = slice(at + part * T, at + (part + 1) * T)
                block = ref[rows, dc * T : (dc + 1) * T].astype(F32)
                qkv_ref[:, lanes(c_ref[i] + part * 16, T)] = block.T
            if dc == 0:
                to = lanes(p_ref[dy * 2 + dh], 256)
                dense_ref[:, to] = ref[at + QKV : at + FFL, :].astype(F32)

    return call(
        kernel,
        [SMEM] * 2 + [VMEM] * 5,
        [((T, 3 * D), F32), ((T, D), F32)],
        [col_place, part_place] + list(pieces),
        nbytes=6 * MIB,
    )


def terms(
    chips, attended, activated, dense, fc2, mixed_grad, pre_grad, weight, normed, vecs, sums, before
):
    n = len(chips)

    def kernel(
        *refs
    ):
        refs = refs[len(before) :]
        a_ref, f_ref, d_ref, v_ref, m_ref, p_ref, w_ref, n_ref, vec_ref = refs[:9]
        mine_ref, other_ref, gain_ref, total_ref = refs[-4:]
        shift = vec_ref[1:2, :]
        if sums:
            gain_ref[...] = refs[9][...]
            total_ref[...] = refs[10][...]
        else:
            gain_ref[...] = jnp.zeros_like(gain_ref)
            total_ref[...] = jnp.zeros_like(total_ref)

        def rows(ref, cols=slice(None)):
            return jnp.concatenate(
                [ref[(dz * 2 + dx) * 256 : (dz * 2 + dx + 1) * 256, cols] for dz, dx in chips]
            )

        left, right = jnp.concatenate([rows(m_ref), rows(p_ref)], axis=1), jnp.concatenate(
            [rows(f_ref), rows(a_ref)], axis=1
        )

        def store(total, to):
            for i in range(n):
                at = slice(i * T, (i + 1) * T)
                mine_ref[at, to] = total[i * 256 : i * 256 + T].astype(BF)
                other_ref[at, to] = total[i * 256 + T : (i + 1) * 256].astype(BF)

        for col in range(4):
            to = slice(col * 512, (col + 1) * 512)
            total = dot(left, w_ref[to, :], 1, 1)
            store(total, to)
            unit = rows(n_ref, to).astype(F32) - shift[:, to]
            gain_ref[:, to] += jnp.sum((total * unit).reshape(n * 32, 8, 512), axis=0)
            total_ref[:, to] += jnp.sum(total.reshape(n * 32, 8, 512), axis=0)
            weights = jnp.concatenate([v_ref[:, to], d_ref[:, to]])
            store(dot(right, weights), slice(D + col * 512, D + (col + 1) * 512))

    return call(
        kernel,
        [ANY] * len(before) + [VMEM] * (9 + len(sums)),
        [((n * T, 2 * D), BF)] * 2 + [((8, D), F32)] * 2,
        [*before, attended, activated, dense, fc2, mixed_grad, pre_grad, weight, normed, vecs, *sums],
        flops=2 * n * 2 * T * (COLS + T + FFL) * D,
        nbytes=8 * MIB,
    )


TM = 512
TQ = 512
TK = 512


def attention_kernel(blocks, last, n_before, place, cos_ref, sin_ref, *refs):
    refs = refs[n_before:]
    if last:
        first_refs, refs = refs[:8], refs[8:]
        att_ref, out_ref, att_t_ref, out_t_ref, bias_ref = refs[:5]
        q_ref, k_ref, v_ref, do_ref = first_refs[:4]
        dq_ref, dk_ref, dv_ref, o_ref, s_ref, e_ref = refs[5:]
    else:
        mixed_ref, grad_ref, *refs = refs
        refs, done_ref = refs[:8] + refs[9:], refs[8]
        done_ref[...] = jnp.zeros_like(done_ref)
        q_ref, k_ref, v_ref, do_ref, dq_ref, dk_ref, dv_ref, o_ref, s_ref, e_ref = refs
    lane = lax.broadcasted_iota(jnp.int32, (T, 128), 1)
    low_head = lane < HEAD_DIM
    first = (lane % HEAD_DIM) < ROTARY // 2

    def turned(x):
        return jnp.where(
            first, pltpu.roll(x, 128 - ROTARY // 2, 1), pltpu.roll(x, ROTARY // 2, 1)
        )

    def load(slot, _):
        rows = pl.ds(pl.multiple_of(slot * T, T), T)
        at = pl.ds(pl.multiple_of(place[slot] * T, T), T)
        c, s = cos_ref[at, :], sin_ref[at, :]
        query = mixed_ref[rows, 0:128]
        key = mixed_ref[rows, 128:256]
        query = (query * c + turned(query) * s).astype(BF).astype(F32) * (HEAD_DIM**-0.5)
        q_ref[0, at, :] = jnp.where(low_head, query, 0.0).astype(BF)
        q_ref[1, at, :] = jnp.where(low_head, 0.0, query).astype(BF)
        k_ref[at, :] = (key * c + turned(key) * s).astype(BF)
        v_ref[at, 0:128] = mixed_ref[rows, 256:384].astype(BF)
        v_ref[at, 128:256] = jnp.ones((T, 128), BF)
        grad = grad_ref[rows, :].astype(F32)
        do_ref[0, at, :] = jnp.where(low_head, grad, 0.0).astype(BF)
        do_ref[1, at, :] = jnp.where(low_head, 0.0, grad).astype(BF)
        dk_ref[:, at] = jnp.zeros((128, T), F32)
        dv_ref[:, at] = jnp.zeros((128, T), F32)
        return 0

    if last:
        for to, at in ((dq_ref, 4), (dk_ref, 5), (dv_ref, 6), (o_ref, 7)):
            to[...] = first_refs[at][...]
    else:
        lax.fori_loop(0, 16, load, 0)

    lane_q = lax.broadcasted_iota(jnp.int32, (TQ, 128), 1)
    low_q = lane_q < HEAD_DIM

    def block(i, _):
        rows = lanes(i, TQ)
        queries = [q_ref[h, rows, :] for h in range(2)]

        def scores(j, tops, masked):
            at = lanes(j, TK)
            keys = k_ref[at, :]
            new = []
            for h in range(2):
                s = dot(queries[h], keys, 1, 1)
                if masked:
                    row = lax.broadcasted_iota(jnp.int32, (TQ, TK), 0)
                    col = lax.broadcasted_iota(jnp.int32, (TQ, TK), 1)
                    s = jnp.where(row >= col, s, -1e30)
                s_ref[h, :, at] = s
                top = tops[h]
                for n in range(TK // 128):
                    top = jnp.maximum(top, s[:, n * 128 : (n + 1) * 128])
                new.append(top)
            return tuple(new)

        low = jnp.full((TQ, 128), -1e30, F32)
        tops = lax.fori_loop(0, i, lambda j, t: scores(j, t, False), (low, low))
        tops = [jnp.max(t, axis=1, keepdims=True) for t in scores(i, tops, True)]

        def weigh(j, totals):
            at = lanes(j, TK)
            values = v_ref[at, :]
            new = []
            for h in range(2):
                e = jnp.exp2((s_ref[h, :, at] - tops[h]) * LOG2E).astype(BF)
                e_ref[h, :, at] = e
                new.append(totals[h] + dot(e, values))
            return tuple(new)

        zero = jnp.zeros((TQ, 256), F32)
        totals = lax.fori_loop(0, i + 1, weigh, (zero, zero))
        outs, grads, deltas = [], [], []
        for h in range(2):
            inverse = 1.0 / totals[h][:, 128:]
            o = totals[h][:, :128] * inverse
            grad = do_ref[h, rows, :].astype(F32) * inverse
            outs.append(o)
            deltas.append(jnp.sum(grad * o, axis=1, keepdims=True))
            grads.append(grad.astype(BF))
        o_ref[rows, :] = jnp.where(low_q, outs[0], outs[1]).astype(BF)
        queries_t = [q.T for q in queries]
        grads_t = [g.T for g in grads]

        def back(j, totals):
            at = lanes(j, TK)
            keys = k_ref[at, :]
            values = v_ref[at, 0:128]
            new, dk, dv = [], None, None
            for h in range(2):
                e = e_ref[h, :, at]
                dp = dot(grads[h], values, 1, 1)
                ds = (e.astype(F32) * (dp - deltas[h])).astype(BF)
                new.append(totals[h] + dot(ds, keys))
                k_part = dot(queries_t[h], ds)
                v_part = dot(grads_t[h], e)
                dk = k_part if dk is None else dk + k_part
                dv = v_part if dv is None else dv + v_part
            dk_ref[:, at] += dk
            dv_ref[:, at] += dv
            return tuple(new)

        zero = jnp.zeros((TQ, 128), F32)
        dqs = lax.fori_loop(0, i + 1, back, (zero, zero))
        dq_ref[rows, :] = jnp.where(low_q, dqs[0], dqs[1]) * (HEAD_DIM**-0.5)
        return 0

    lax.fori_loop(blocks[0], blocks[1], block, 0)
    if not last:
        return

    def store(slot, total):
        rows = pl.ds(pl.multiple_of(slot * T, T), T)
        at = pl.ds(pl.multiple_of(place[slot] * T, T), T)
        c, s = cos_ref[at, :], sin_ref[at, :]
        att = o_ref[at, :]
        att_ref[rows, :] = att
        att_t_ref[:, rows] = att.T
        dq, dk = dq_ref[at, :], dk_ref[:, at].T
        new = []
        for part, grad in enumerate(
            (dq * c - turned(dq) * s, dk * c - turned(dk) * s, dv_ref[:, at].T)
        ):
            low = grad.astype(BF)
            cols = slice(part * T, (part + 1) * T)
            out_ref[rows, cols] = low
            out_t_ref[cols, rows] = low.T
            new.append(total[part] + jnp.sum(low.astype(F32).reshape(16, 8, T), axis=0))
        return tuple(new)

    zero = jnp.zeros((8, T), F32)
    sums = lax.fori_loop(0, 16, store, (zero, zero, zero))
    for part in range(3):
        bias_ref[:, part * T : (part + 1) * T] = sums[part]


def attention_first(place, cosine, sine, mixed, attended_grad, before):
    return call(
        functools.partial(attention_kernel, (0, 3), False, len(before)),
        [SMEM] + [VMEM] * 2 + [ANY] * len(before) + [VMEM] * 2,
        [
            ((2, SEQ, 128), BF, 1),
            ((SEQ, 128), BF, 1),
            ((SEQ, 256), BF, 1),
            ((2, SEQ, 128), BF, 1),
            ((SEQ, 128), F32, 1),
            ((128, SEQ), F32, 1),
            ((128, SEQ), F32, 1),
            ((SEQ, 128), BF, 1),
            ((8, 128), jnp.int32),
        ],
        [place, cosine, sine, *before, mixed, attended_grad],
        [pltpu.VMEM((2, TQ, SEQ), F32), pltpu.VMEM((2, TQ, SEQ), BF)],
        vmem=20,
        flops=8 * SEQ * SEQ * 64 * 2,
        exps=SEQ * SEQ // 2,
        nbytes=3 * MIB,
    )


def attention_last(place, cosine, sine, state, before):
    return call(
        functools.partial(attention_kernel, (3, 4), True, len(before)),
        [SMEM] + [VMEM] * 2 + [ANY] * len(before) + [VMEM] * 8,
        [
            ((SEQ, T), BF, 1),
            ((SEQ, QKV), BF, 1),
            ((T, SEQ), BF, 1),
            ((QKV, SEQ), BF, 1),
            ((8, QKV), F32),
        ],
        [place, cosine, sine, *before] + list(state),
        [
            pltpu.VMEM((SEQ, 128), F32),
            pltpu.VMEM((128, SEQ), F32),
            pltpu.VMEM((128, SEQ), F32),
            pltpu.VMEM((SEQ, 128), BF),
            pltpu.VMEM((2, TQ, SEQ), F32),
            pltpu.VMEM((2, TQ, SEQ), BF),
        ],
        vmem=24,
        flops=6 * SEQ * SEQ * 64 * 2,
        exps=SEQ * SEQ // 2,
        nbytes=3 * MIB,
    )


def rotary_tables():
    lane = lax.broadcasted_iota(jnp.int32, (SEQ, 128), 1) % HEAD_DIM
    place = lax.broadcasted_iota(jnp.int32, (SEQ, 128), 0).astype(F32)
    freq = (lane % (ROTARY // 2)).astype(F32)
    angle = place * jnp.exp(freq * (-2.0 * math.log(10000.0) / ROTARY))
    turns = lane < ROTARY
    cosine = jnp.where(turns, jnp.cos(angle), 1.0)
    sine = jnp.where(turns, jnp.sin(angle), 0.0)
    return cosine, jnp.where(lane < ROTARY // 2, -sine, sine)


def body(
    tokens,
    ln_gain,
    ln_shift,
    qkv_weight,
    qkv_bias,
    dense_weight,
    dense_bias,
    fc1_weight,
    fc1_bias,
    fc2_weight,
    fc2_bias,
    cotangent,
):
    rep, shard = lax.axis_index("rep"), lax.axis_index("shard")
    xh, y = rep // 4, rep % 4
    z, xl, c = shard // 4, (shard // 2) % 2, shard % 2
    token_place = jnp.stack(
        [((z + dz) % 4) * 4 + (xl ^ dx) * 2 + (c ^ dc) for dz, dx, dc in SLOTS]
    ).astype(jnp.int32)
    row_place = jnp.stack(
        [((z + y + dy) % 4) * 4 + (xl ^ dx) * 2 + (c ^ dc) for dy, dx, dc in SLOTS]
    ).astype(jnp.int32)
    col_place = jnp.stack(
        [((z - y - dy) % 4) * 4 + (xl ^ dx) * 2 + (c ^ dc) for dy, dx, dc in SLOTS]
    ).astype(jnp.int32)
    part_place = jnp.stack(
        [((y + dy) % 4) * 2 + dx for dy in range(4) for dx in range(2)]
    ).astype(jnp.int32)
    me, core = shard.reshape(1).astype(jnp.int32), c.reshape(1).astype(jnp.int32)

    vectors = [v.reshape(-1, T) for v in (qkv_bias, ln_gain, ln_shift, dense_bias, fc2_bias)]
    vectors = jnp.concatenate(vectors + [jnp.zeros((T - 7, T), BF)])
    message = jnp.concatenate([tokens, cotangent, vectors], axis=1)
    near = gather_near(message)

    wait = zero_of(message).astype(BF)

    def columns_of(dx):
        chip = ((z - y) % 4) * 2 + (xl ^ dx)
        qkv = [
            lax.dynamic_slice(qkv_weight, (0, part * D + chip * 2 * T), (T, 2 * T))
            for part in range(3)
        ]
        fc1 = lax.dynamic_slice(fc1_weight, (0, chip * 2 * FFL), (T, 2 * FFL))
        return jnp.concatenate(
            [
                jnp.concatenate(
                    [p[:, at * T : (at + 1) * T] + wait for p in qkv]
                    + [fc1[:, at * FFL : (at + 1) * FFL] + wait],
                    axis=1,
                )
                for at in range(2)
            ]
        )

    columns = [columns_of(dx) for dx in range(2)]
    both = [
        fetch_from(columns[dx], lambda xh, y, z, xl, c: (xh, y, z + y, xl ^ dx, c))
        for dx in range(2)
    ]

    far_vectors = fetch(vectors[:16], dz=2, dx=1)
    far_vectors = jnp.concatenate([far_vectors, fetch(far_vectors, dc=1)])
    mine = [lax.dynamic_slice(b, (c * T, 0), (T, COLS)) for b in both]
    other = [lax.dynamic_slice(b, ((1 - c) * T, 0), (T, COLS)) for b in both]
    other = fetch(jnp.concatenate(other), dc=1)
    own_rows = jnp.concatenate([mine[0], other[:T], mine[1], other[T:]])
    cosine, sine = rotary_tables()
    one, three = fetch(own_rows, dy=1), fetch(own_rows, dy=-1)
    further = gather_next(near)
    weights = (own_rows, one, three, fetch(one[: 2 * T], dy=1), fetch(three[2 * T :], dy=-1))
    far = gather_far(further)
    *arrays, vecs, own_qkv_bias = near_inputs(
        both_cores(near | further), far_vectors, fc2_weight, dense_weight, token_place, me
    )
    far_other = fetch(jnp.concatenate(far) + zero_of(vecs).astype(BF), dc=1)
    far = [(far[0], 10 * T), (far[1], 10 * T + T // 2), (far_other, 11 * T)]
    gain, out_bias = vecs[0:1], vecs[2:3]
    (
        normed,
        all_cot,
        _,
        attended_grad,
        weight,
        activated,
        pre_grad,
        act_t,
        pre_t,
        mixed,
        fc1_bias_part,
        out_bias_part,
    ) = forward_inputs(
        arrays,
        far,
        weights,
        vecs,
        fc1_bias.astype(F32).reshape(1, FFL),
        own_qkv_bias,
        fc2_weight,
        dense_weight,
        row_place,
        me,
    )

    early = column_grads(normed, pre_t, act_t, all_cot, row_place, part_place, core)
    *state, done = attention_first(token_place, cosine, sine, mixed, attended_grad, early)
    early_near = reduce_near(early, reduce_far(early), done[0, 0].astype(F32))
    attended, mixed_grad, attended_t, mixed_t, qkv_bias_part = attention_last(
        token_place, cosine, sine, state, early_near
    )
    *late, biases = head_grads(
        normed,
        mixed_t,
        attended_t,
        all_cot,
        row_place,
        part_place,
        core,
        me,
        (qkv_bias_part, fc1_bias_part, out_bias_part),
    )
    early = add(early[0], fetch(early_near[0], dy=-1), fetch(early_near[1], dy=1))
    early = early.astype(BF)

    early_other = fetch(early, dh=1)
    late_far = reduce_far(late)

    def the_terms(chips, sums, before):
        mine, other, *sums = terms(
            chips,
            attended,
            activated,
            dense_weight,
            fc2_weight,
            mixed_grad,
            pre_grad,
            weight,
            normed,
            vecs,
            sums,
            before,
        )
        return mine, fetch(other, dc=1), sums

    def own_terms(chips, mine, other, zero):
        return {
            chip: add(mine[n * T : (n + 1) * T], other[n * T : (n + 1) * T], zero).astype(BF)
            for n, chip in enumerate(chips)
        }

    mine0, other0, sums = the_terms(WAVES[0], [], [early, *late])
    mine1, other1, sums = the_terms(WAVES[1], sums, [])
    zero = zero_of(sums[0])
    q = own_terms(WAVES[0], mine0, other0, zero)
    far = scatter_far(q)
    late_near = reduce_near(late, late_far, zero)
    mine2, other2, sums = the_terms(WAVES[2], sums, [q[2, 1], *late_near])
    zero = zero_of(sums[0])
    late = late[0], fetch(late_near[0], dy=-1), fetch(late_near[1], dy=1)
    early = add(early, early_other, zero).astype(BF)
    early_swap = fetch(early[:, T : 2 * T], dc=1)
    mine3, other3, sums = the_terms(WAVES[3], sums, [early])
    zero = zero_of(sums[0])

    def from_owners(rows):
        return [
            fetch_from(rows[dx], lambda xh, y, z, xl, c: (xh, y, z - y, xl ^ dx, c))
            for dx in range(2)
        ]

    early_own = jnp.concatenate([early[:, :T], early_swap], axis=1)
    early_own = from_owners([early_own[:FFL], early_own[FFL:]])
    q |= own_terms(WAVES[1], mine1, other1, zero)
    further = scatter_next(q, far, zero)
    gain_part = jnp.sum(sums[0], axis=0, keepdims=True) / gain
    shift_part = jnp.sum(sums[1], axis=0, keepdims=True)
    vec = jnp.concatenate(
        [gain_part.reshape(16, T), shift_part.reshape(16, T), biases[32:]]
    )
    vec = vec + fetch(vec, dc=1)
    vec = (vec + fetch(vec, dy=2)) + (fetch(vec, dy=1) + fetch(vec, dy=-1))
    late = add(*late, zero).astype(BF)
    late_other = fetch(late, dh=1)

    early = jnp.concatenate(
        [
            jnp.concatenate([early_own[dx], early[dx * FFL : (dx + 1) * FFL, 2 * T :]], axis=1)
            for dx in range(2)
        ]
    )
    early_one, early_three = fetch(early, dy=1), fetch(early, dy=-1)
    late = add(late, late_other).astype(BF)
    late_qkv = jnp.concatenate([late[:QKV], late[FFL : FFL + QKV]])
    late_own = jnp.concatenate([late_qkv[:, :T], fetch(late_qkv[:, T:], dc=1)], axis=1)
    late_own = from_owners([late_own[:QKV], late_own[QKV:]])
    late = jnp.concatenate([late_own[0], late[QKV:FFL], late_own[1], late[FFL + QKV :]])
    zero = zero_of(vec) + zero_of(late)
    q |= own_terms(WAVES[2], mine2, other2, zero) | own_terms(WAVES[3], mine3, other3, zero)
    nearest = scatter_near(q, further, zero)
    vec = (vec + fetch(vec, dz=2)) + (fetch(vec, dz=1) + fetch(vec, dz=-1))

    late_one, late_three = fetch(late, dy=1), fetch(late, dy=-1)
    early = (
        early,
        early_one,
        early_three,
        fetch(early_one[:FFL], dy=1),
        fetch(early_three[FFL:], dy=-1),
    )
    total = add(q[0, 0], *nearest, zero_of(early_one) + zero_of(early_three) + zero_of(vec))
    vec = (vec + fetch(vec, dx=1)) + (fetch(vec, dh=1) + fetch(vec, dx=1, dh=1))
    own = tokens.astype(F32)
    layer_out = (own + out_bias + total[:, D:]).astype(BF)
    center = own - jnp.mean(own, axis=-1, keepdims=True)
    inv_std = lax.rsqrt(jnp.mean(center * center, axis=-1, keepdims=True) + 1e-05)
    unit = center * inv_std
    scaled = total[:, :D] * gain
    input_grad = cotangent.astype(F32) + inv_std * (
        scaled
        - jnp.mean(scaled, axis=-1, keepdims=True)
        - unit * jnp.mean(scaled * unit, axis=-1, keepdims=True)
    )
    late = (
        late,
        late_one,
        late_three,
        fetch(late_one[:FFL], dy=1),
        fetch(late_three[FFL:], dy=-1),
    )
    fc1_total, fc2_total = place_columns(early, col_place, part_place)
    qkv_total, dense_total = place_heads(late, col_place, part_place)
    out_bias_total = lax.dynamic_slice(vec, (144 + shard, 0), (1, T)).reshape(T)

    return (
        layer_out,
        input_grad,
        lax.dynamic_slice(vec, (shard, 0), (1, T)).reshape(T),
        lax.dynamic_slice(vec, (16 + shard, 0), (1, T)).reshape(T),
        qkv_total,
        lax.dynamic_slice(vec, (32 + 3 * shard, 0), (3, T)).reshape(QKV),
        dense_total,
        out_bias_total,
        fc1_total,
        lax.dynamic_slice(vec, (80 + 4 * shard, 0), (4, T)).reshape(FFL),
        fc2_total,
        out_bias_total,
    )


def solution(mesh):
    return jax.shard_map(
        body,
        mesh=mesh,
        in_specs=(
            P(AXES, None),
            P("shard"),
            P("shard"),
            P("shard", None),
            P("shard"),
            P("shard", None),
            P("shard"),
            P("shard", None),
            P("shard"),
            P("shard", None),
            P("shard"),
            P(AXES, None),
        ),
        out_specs=(
            P(AXES, None),
            P(AXES, None),
            P("shard"),
            P("shard"),
            P("shard", None),
            P("shard"),
            P("shard", None),
            P("shard"),
            P("shard", None),
            P("shard"),
            P("shard", None),
            P("shard"),
        ),
        check_vma=False,
    )
```

```python
import functools
import math

import jax
import jax.numpy as jnp
from jax import lax
from jax.experimental import pallas as pl
from jax.experimental.pallas import tpu as pltpu
from jax.sharding import PartitionSpec as P

D = 2048
HEADS = 32
HEAD_DIM = 64
ROTARY = 32
FF = 8192
SEQ = 2048
T = 128
QKV = 384
FFL = 512
COLS = QKV + FFL
BF = jnp.bfloat16
F32 = jnp.float32
AXES = ("rep", "shard")
MIB = 1 << 20
LOG2E = math.log2(math.e)

PLACES = [
    (xh, y, z, xl, c)
    for xh in range(2)
    for y in range(4)
    for z in range(4)
    for xl in range(2)
    for c in range(2)
]


def flat(xh, y, z, xl, c):
    return (xh * 4 + y % 4) * 16 + (z % 4) * 4 + xl * 2 + c


def fetch_from(x, source):
    return lax.ppermute(x, AXES, [(flat(*source(*p)), flat(*p)) for p in PLACES])


def fetch(x, dz=0, dx=0, dc=0, dy=0, dh=0):
    return fetch_from(
        x, lambda xh, y, z, xl, c: (xh ^ dh, y + dy, z + dz, xl ^ dx, c ^ dc)
    )


def dot(a, b, ca=1, cb=0):
    return lax.dot_general(a, b, (((ca,), (cb,)), ((), ())), preferred_element_type=F32)


def add(*terms):
    total = terms[0].astype(F32)
    for term in terms[1:]:
        total = total + (term if isinstance(term, float) else term.astype(F32))
    return total


def zero_of(x):
    return x[0, 0].astype(F32) * 0.0


def together(*groups):
    leaves, tree = jax.tree.flatten(groups)
    n = len(leaves)
    leaves = pl.pallas_call(
        lambda *refs: None,
        in_specs=[pl.BlockSpec(memory_space=pl.ANY)] * n,
        out_specs=[pl.BlockSpec(memory_space=pl.ANY)] * n,
        out_shape=[jax.ShapeDtypeStruct(x.shape, x.dtype) for x in leaves],
        input_output_aliases={i: i for i in range(n)},
    )(*leaves)
    return jax.tree.unflatten(tree, leaves)


def gather_near(own):
    return {
        (0, 0): own,
        (1, 0): fetch(own, dz=1),
        (3, 0): fetch(own, dz=-1),
        (0, 1): fetch(own, dx=1),
    }


def gather_next(a):
    return {
        (1, 1): fetch(a[1, 0], dx=1),
        (3, 1): fetch(a[0, 1], dz=-1),
        (2, 0): fetch(a[1, 0], dz=1),
    }


def gather_far(a):
    half = a[1, 1].shape[0] // 2
    return fetch(a[1, 1][:half], dz=1), fetch(a[3, 1][half:], dz=-1)


def gather_swap(own):
    return fetch(own, dc=1)


def both_cores(a):
    pieces = []
    for (dz, dx), own in a.items():
        pair = own if isinstance(own, tuple) else (own, gather_swap(own))
        pieces += [(pair[dc], ((dz * 2 + dx) * 2 + dc) * T) for dc in range(2)]
    return pieces


SLOTS = [(dz, dx, dc) for dz in range(4) for dx in range(2) for dc in range(2)]
WAVES = [[(2, 1)], [(1, 1), (3, 1), (2, 0)], [(1, 0), (3, 0), (0, 1), (0, 0)]]


def scatter_far(q):
    half = T // 2
    return fetch(q[2, 1][:half], dz=-1), fetch(q[2, 1][half:], dz=1)


def scatter_next(q, far, zero):
    half = T // 2
    q11 = jnp.concatenate([add(q[1, 1][:half], far[0], zero).astype(BF), q[1, 1][half:]])
    q31 = jnp.concatenate([q[3, 1][:half], add(q[3, 1][half:], far[1], zero).astype(BF)])
    return fetch(q[2, 0], dz=-1), fetch(q31, dz=1), fetch(q11, dx=1)


def scatter_near(q, further, zero):
    q10 = add(q[1, 0], further[0], further[2], zero).astype(BF)
    q01 = add(q[0, 1], further[1], zero).astype(BF)
    return fetch(q10, dz=-1), fetch(q[3, 0], dz=1), fetch(q01, dx=1)


def reduce_far(g):
    half = g[0].shape[0] // 2
    return fetch(g[2][:half], dy=-1), fetch(g[2][half:], dy=1)


def reduce_near(g, far, zero):
    half = g[0].shape[0] // 2
    g1 = jnp.concatenate([add(g[1][:half], far[0], zero).astype(BF), g[1][half:]])
    g3 = jnp.concatenate([g[3][:half], add(g[3][half:], far[1], zero).astype(BF)])
    return g1, g3


def of_rep(refs, dy, dx, n):
    own, one, three, first, second = refs
    if dy == 2:
        return (second if dx else first), 0
    return (own, one, None, three)[dy], dx * n


VMEM = pl.BlockSpec(memory_space=pltpu.VMEM)
SMEM = pl.BlockSpec(memory_space=pltpu.SMEM)
HBM = pl.BlockSpec(memory_space=pltpu.HBM)
ANY = pl.BlockSpec(memory_space=pl.ANY)


def lanes(at, n):
    return pl.ds(pl.multiple_of(at * n, n), n)


def call(kernel, ins, outs, args, scratch=(), vmem=8, flops=0, nbytes=0, exps=0, aliases={}):
    return pl.pallas_call(
        kernel,
        in_specs=ins,
        out_specs=[VMEM] * len(outs),
        out_shape=[
            pltpu.VMEM(o[0], o[1]) if len(o) > 2 else jax.ShapeDtypeStruct(*o) for o in outs
        ],
        scratch_shapes=list(scratch),
        input_output_aliases=aliases,
        compiler_params=pltpu.CompilerParams(vmem_limit_bytes=vmem * MIB),
        cost_estimate=pl.CostEstimate(flops=flops, transcendentals=exps, bytes_accessed=nbytes),
    )(*args)


ROOT = math.sqrt(2.0 / math.pi)


def start_copies(pieces, place, sems):
    copies = [
        pltpu.make_async_copy(src, dst, sems.at[place + i]) for i, (src, dst) in enumerate(pieces)
    ]
    for copy in copies:
        copy.start()
    return copies


def norm_rows(normed_ref, gain, shift, first, count):
    def strip(i, _):
        at = lanes(i, 64)
        x = normed_ref[at, :].astype(F32)
        x = x - jnp.sum(x, axis=1, keepdims=True) * (1.0 / D)
        scale = lax.rsqrt(jnp.sum(x * x, axis=1, keepdims=True) * (1.0 / D) + 1e-05)
        normed_ref[at, :] = (x * scale * gain + shift).astype(BF)
        return 0

    lax.fori_loop(first // 64, (first + count) // 64, strip, 0)


def message_moves(refs, pieces, normed_ref, cot_ref):
    moves = []
    for (array, at), ref in zip(pieces, refs, strict=True):
        to = pl.ds(at, array.shape[0])
        moves.append((ref.at[:, pl.ds(0, D)], normed_ref.at[to]))
        moves.append((ref.at[:, pl.ds(D, D)], cot_ref.at[to]))
    return moves


def near_inputs(pieces, far_vectors, fc2, dense, token_place, me, before):
    n = len(pieces)
    chips = sorted({at // 256 for _, at in pieces})

    def kernel(t_ref, me_ref, *refs):
        refs = refs[len(before) :]
        (
            far_ref,
            fc2_ref,
            dense_ref,
            normed_ref,
            cot_ref,
            grad_ref,
            att_ref,
            vec_ref,
            own_ref,
            small_ref,
            flat_ref,
            sems,
        ) = refs[n:]
        moves = [
            (ref.at[pl.ds(0, 16), pl.ds(2 * D, T)], small_ref.at[pl.ds(at // T * 16, 16)])
            for (_, at), ref in zip(pieces, refs[:n], strict=True)
        ]
        for dc in range(2):
            to = small_ref.at[pl.ds((5 * 2 + dc) * 16, 16)]
            moves.append((far_ref.at[pl.ds(dc * 16, 16)], to))
        small_copies = start_copies(moves, 0, sems)
        copies = start_copies(
            message_moves(refs[:n], pieces, normed_ref, cot_ref), n + 2, sems
        )
        for copy in small_copies:
            copy.wait()
        for i in range(16):
            at = t_ref[i]
            small = small_ref[i * 16 : (i + 1) * 16, :].astype(F32)
            for part in range(3):
                flat_ref[0:1, lanes(at * 3 + part, T)] = small[part : part + 1]
            vec_ref[0:1, lanes(at, T)] = small[3:4]
            vec_ref[1:2, lanes(at, T)] = small[4:5]
            vec_ref[2:3, lanes(at, T)] = small[5:6] + small[6:7]
        for part in range(3):
            own_ref[0:1, part * T : (part + 1) * T] = flat_ref[
                0:1, lanes(part * 16 + me_ref[0], T)
            ]
        gain, shift = vec_ref[0:1, :], vec_ref[1:2, :]
        for chip in chips:
            for (_, at), token_copy, cot_copy in zip(pieces, copies[0::2], copies[1::2]):
                if at // 256 == chip:
                    token_copy.wait()
                    cot_copy.wait()
            norm_rows(normed_ref, gain, shift, chip * 256, 256)

        def tile(i, _):
            at = lanes(i, TM)
            x = cot_ref[at, :]
            grad_ref[at, :] = dot(x, fc2_ref[...], 1, 1).astype(BF)
            att_ref[at, :] = dot(x, dense_ref[...], 1, 1).astype(BF)
            return 0

        lax.fori_loop(0, SEQ // TM, tile, 0)

    return call(
        kernel,
        [SMEM] * 2 + [ANY] * len(before) + [HBM] * (n + 1) + [VMEM] * 2,
        [
            ((SEQ, D), BF, 1),
            ((SEQ, D), BF, 1),
            ((SEQ, FFL), BF, 1),
            ((SEQ, T), BF, 1),
            ((8, D), F32, 1),
            ((1, QKV), F32, 1),
        ],
        [token_place, me, *before] + [p for p, _ in pieces] + [far_vectors, fc2, dense],
        [
            pltpu.VMEM((256, T), BF),
            pltpu.VMEM((1, 3 * D), F32),
            pltpu.SemaphoreType.DMA((3 * n + 2,)),
        ],
        flops=2 * SEQ * D * (FFL + T),
        nbytes=20 * MIB,
    )


def forward_inputs(arrays, pieces, weights, vecs, bias, own_bias, fc2, dense, row_place, me):
    n = len(pieces)
    chip = pieces[0][1] // 256

    def kernel(r_ref, me_ref, *refs):
        tok = refs[4 : 4 + n]
        w_refs = refs[4 + n : 9 + n]
        (
            vec_ref,
            bias_ref,
            own_ref,
            fc2_ref,
            dense_ref,
            normed_ref,
            cot_ref,
            grad_ref,
            att_ref,
            w_ref,
            act_ref,
            pre_ref,
            act_t_ref,
            pre_t_ref,
            mixed_ref,
            fc1b_ref,
            outb_ref,
            sems,
        ) = refs[9 + n :]
        copies = start_copies(message_moves(tok, pieces, normed_ref, cot_ref), 0, sems)
        moves = []
        for i, (dy, dx, dc) in enumerate(SLOTS):
            ref, at = of_rep(w_refs, dy, dx, 2 * T)
            moves.append((ref.at[pl.ds(at + dc * T, T)], w_ref.at[lanes(r_ref[i], T)]))
        w_copies = start_copies(moves, 2 * n, sems)
        for copy in copies:
            copy.wait()
        norm_rows(normed_ref, vec_ref[0:1, :], vec_ref[1:2, :], chip * 256, 256)
        rows = slice(chip * 256, (chip + 1) * 256)
        x = cot_ref[rows, :]
        grad_ref[rows, :] = dot(x, fc2_ref[...], 1, 1).astype(BF)
        att_ref[rows, :] = dot(x, dense_ref[...], 1, 1).astype(BF)
        for copy in w_copies:
            copy.wait()

        def product(i):
            at = lanes(i, TM)
            x = normed_ref[at, :]
            mixed_ref[at, :] = dot(x, w_ref[:, :QKV]) + own_ref[...]
            return dot(x, w_ref[:, QKV:]) + bias_ref[...]

        def gelu(i, pre, total):
            at = lanes(i, TM)
            squared = pre * pre
            tanh = jnp.tanh(ROOT * pre * (1.0 + 0.044715 * squared))
            act = (0.5 * pre * (1.0 + tanh)).astype(BF)
            act_ref[at, :] = act
            act_t_ref[:, at] = act.T
            slope = 0.5 * (1.0 + tanh) + 0.5 * pre * (1.0 - tanh * tanh) * ROOT * (
                1.0 + 3 * 0.044715 * squared
            )
            back = (grad_ref[at, :].astype(F32) * slope).astype(BF)
            pre_ref[at, :] = back
            pre_t_ref[:, at] = back.T
            return total + jnp.sum(back.astype(F32).reshape(TM // 8, 8, FFL), axis=0)

        def tile(i, carry):
            pre, total = carry
            return product(i), gelu(i - 1, pre, total)

        pre, total = lax.fori_loop(1, SEQ // TM, tile, (product(0), jnp.zeros((8, FFL), F32)))
        fc1b_ref[...] = gelu(SEQ // TM - 1, pre, total)

        def sums(i, total):
            own = cot_ref[lanes(i, 256), lanes(me_ref[0], T)].astype(F32)
            return total + jnp.sum(own.reshape(32, 8, T), axis=0)

        outb_ref[...] = lax.fori_loop(0, 8, sums, jnp.zeros((8, T), F32))

    return call(
        kernel,
        [SMEM] * 2 + [VMEM] * 4 + [HBM] * (n + 5) + [VMEM] * 5,
        [
            ((SEQ, D), BF, 1),
            ((SEQ, D), BF, 1),
            ((SEQ, FFL), BF, 1),
            ((SEQ, T), BF, 1),
            ((D, COLS), BF, 1),
            ((SEQ, FFL), BF, 1),
            ((SEQ, FFL), BF, 1),
            ((FFL, SEQ), BF, 1),
            ((FFL, SEQ), BF, 1),
            ((SEQ, QKV), F32, 1),
            ((8, FFL), F32),
            ((8, T), F32),
        ],
        [row_place, me]
        + list(arrays)
        + [p for p, _ in pieces]
        + list(weights)
        + [vecs, bias, own_bias, fc2, dense],
        [pltpu.SemaphoreType.DMA((2 * n + 16,))],
        aliases={2: 0, 3: 1, 4: 2, 5: 3},
        flops=2 * SEQ * D * COLS,
        nbytes=8 * MIB,
        exps=SEQ * FFL,
    )


def column_grads(normed, pre_t, act_t, cot, row_place, part_place, core):
    def kernel(r_ref, p_ref, core_ref, n_ref, g_ref, a_ref, c_ref, *outs):
        for dy in (2, 1, 3, 0):
            out = outs[dy]
            for dh in range(2):
                at = slice(dh * FFL, (dh + 1) * FFL)
                chip = r_ref[(dy * 2 + dh) * 2] // 2
                cols = dot(g_ref[...], n_ref[:, lanes(chip, 256)]).astype(BF)
                out[at, lanes(core_ref[0], T)] = cols[:, :T]
                out[at, lanes(1 - core_ref[0], T)] = cols[:, T:]
                part = c_ref[:, lanes(p_ref[dy * 2 + dh], 256)]
                out[at, 256:512] = dot(a_ref[...], part).astype(BF)

    return call(
        kernel,
        [SMEM] * 3 + [VMEM] * 4,
        [((1024, 512), BF)] * 4,
        [row_place, part_place, core, normed, pre_t, act_t, cot],
        flops=4 * SEQ * D * FFL,
        nbytes=4 * MIB,
    )


FOR_OWNER = QKV + 16
LATE = FOR_OWNER + T + 16


def head_grads(
    normed,
    mixed_t,
    attended_t,
    cot,
    places,
    part_place,
    core,
    me,
    gain,
    sums,
    bias_parts,
    before,
):
    def kernel(r_ref, p_ref, core_ref, me_ref, n_ref, m_ref, a_ref, c_ref, *refs):
        refs = refs[len(before) :]
        gain_ref, gains_ref, shifts_ref, qkvb_ref, fc1b_ref, outb_ref = refs[:6]
        outs, owners_ref, own_ref = refs[6:10], refs[10], refs[11]
        owners_ref[...] = jnp.zeros_like(owners_ref)
        owners_ref[0:1, :] = jnp.sum(gains_ref[...], axis=0, keepdims=True) / gain_ref[...]
        owners_ref[1:2, :] = jnp.sum(shifts_ref[...], axis=0, keepdims=True)
        qkvb = jnp.sum(qkvb_ref[...], axis=0, keepdims=True)
        for part in range(3):
            at = part * 16 + me_ref[0]
            third = at % 3
            row = lax.broadcasted_iota(jnp.int32, (8, T), 0)
            value = jnp.where(row == 2 + third, qkvb[:, part * T : (part + 1) * T], 0.0)
            owners_ref[0:8, lanes(at // 3, T)] += value
        own_ref[...] = jnp.zeros_like(own_ref)
        own_ref[0:1, :FFL] = jnp.sum(fc1b_ref[...], axis=0, keepdims=True)
        own_ref[0:1, FFL : FFL + T] = jnp.sum(outb_ref[...], axis=0, keepdims=True)
        for dy in (2, 1, 3, 0):
            out = outs[dy]
            for dx in range(2):
                base = dx * LATE
                chip = r_ref[(dy * 2 + dx) * 2] // 2
                cols = dot(m_ref[...], n_ref[:, lanes(chip, 256)]).astype(BF)
                extra = owners_ref[:, lanes(chip, 256)].astype(BF)
                mine, other = lanes(core_ref[0], T), lanes(1 - core_ref[0], T)
                out[base : base + QKV, mine] = cols[:, :T]
                out[base : base + QKV, other] = cols[:, T:]
                out[base + QKV : base + FOR_OWNER, mine] = extra[:, :T]
                out[base + QKV : base + FOR_OWNER, other] = extra[:, T:]
                base += FOR_OWNER
                part = p_ref[dy * 2 + dx]
                out[base : base + T, :] = dot(a_ref[...], c_ref[:, lanes(part, 256)]).astype(BF)
                out[base + T : base + T + 16, 0:T] = own_ref[:, lanes(part, T)].astype(BF)
                out[base + T : base + T + 16, T:] = jnp.zeros((16, T), BF)

    return call(
        kernel,
        [SMEM] * 4 + [VMEM] * 4 + [ANY] * len(before) + [VMEM] * 6,
        [((2 * LATE, 256), BF)] * 4,
        [
            places,
            part_place,
            core,
            me,
            normed,
            mixed_t,
            attended_t,
            cot,
            *before,
            gain,
            *sums,
            *bias_parts,
        ],
        [pltpu.VMEM((16, D), F32), pltpu.VMEM((16, 1024), F32)],
        flops=2 * SEQ * D * (QKV + T),
        nbytes=2 * MIB,
    )


def place_columns(pieces, col_place, part_place):
    def kernel(c_ref, p_ref, *refs):
        fc1_ref, fc2_ref = refs[5:]
        for i, (dy, dh, dc) in enumerate(SLOTS):
            ref, at = of_rep(refs[:5], dy, dh, FFL)
            part = ref[at : at + FFL, dc * T : (dc + 1) * T]
            fc1_ref[:, lanes(c_ref[i], FFL)] = part.astype(F32).T
            if dc == 0:
                to = lanes(p_ref[dy * 2 + dh], 256)
                fc2_ref[:, to] = ref[at : at + FFL, 256:512].astype(F32)

    return call(
        kernel,
        [SMEM] * 2 + [VMEM] * 5,
        [((T, FF), F32), ((FFL, D), F32)],
        [col_place, part_place] + list(pieces),
        vmem=20,
        nbytes=12 * MIB,
    )


def place_heads(pieces, col_place, part_place):
    def kernel(c_ref, p_ref, *refs):
        qkv_ref, dense_ref, owner_ref, own_ref = refs[5:]
        total = jnp.zeros((16, T), F32)
        for i, (dy, dx, dc) in enumerate(SLOTS):
            ref, at = of_rep(refs[:5], dy, dx, LATE)
            cols = slice(dc * T, (dc + 1) * T)
            for part in range(3):
                block = ref[at + part * T : at + (part + 1) * T, cols].astype(F32)
                qkv_ref[:, lanes(c_ref[i] + part * 16, T)] = block.T
            total += ref[at + QKV : at + FOR_OWNER, cols].astype(F32)
            if dc == 0:
                part = p_ref[dy * 2 + dx]
                rows = slice(at + FOR_OWNER, at + FOR_OWNER + T)
                dense_ref[:, lanes(part, 256)] = ref[rows, :].astype(F32)
                rows = slice(at + FOR_OWNER + T, at + LATE)
                own_ref[:, lanes(part, T)] = ref[rows, 0:T].astype(F32)
        owner_ref[...] = total

    return call(
        kernel,
        [SMEM] * 2 + [VMEM] * 5,
        [((T, 3 * D), F32), ((T, D), F32), ((16, T), F32), ((16, 1024), F32)],
        [col_place, part_place] + list(pieces),
        vmem=14,
        nbytes=6 * MIB,
    )


def terms(
    chips, attended, activated, dense, fc2, mixed_grad, pre_grad, weight, normed, vecs, sums, before
):
    n = len(chips)

    def kernel(
        *refs
    ):
        refs = refs[len(before) :]
        a_ref, f_ref, d_ref, v_ref, m_ref, p_ref, w_ref, n_ref, vec_ref = refs[:9]
        mine_ref, other_ref, gain_ref, total_ref = refs[-4:]
        shift = vec_ref[1:2, :]
        if sums:
            gain_ref[...] = refs[9][...]
            total_ref[...] = refs[10][...]
        else:
            gain_ref[...] = jnp.zeros_like(gain_ref)
            total_ref[...] = jnp.zeros_like(total_ref)

        def rows(ref, cols=slice(None)):
            return jnp.concatenate(
                [ref[(dz * 2 + dx) * 256 : (dz * 2 + dx + 1) * 256, cols] for dz, dx in chips]
            )

        left, right = jnp.concatenate([rows(m_ref), rows(p_ref)], axis=1), jnp.concatenate(
            [rows(f_ref), rows(a_ref)], axis=1
        )

        def store(total, to):
            for i in range(n):
                at = slice(i * T, (i + 1) * T)
                mine_ref[at, to] = total[i * 256 : i * 256 + T].astype(BF)
                other_ref[at, to] = total[i * 256 + T : (i + 1) * 256].astype(BF)

        for col in range(4):
            to = slice(col * 512, (col + 1) * 512)
            total = dot(left, w_ref[to, :], 1, 1)
            store(total, to)
            unit = rows(n_ref, to).astype(F32) - shift[:, to]
            gain_ref[:, to] += jnp.sum((total * unit).reshape(n * 32, 8, 512), axis=0)
            total_ref[:, to] += jnp.sum(total.reshape(n * 32, 8, 512), axis=0)
            weights = jnp.concatenate([v_ref[:, to], d_ref[:, to]])
            store(dot(right, weights), slice(D + col * 512, D + (col + 1) * 512))

    return call(
        kernel,
        [ANY] * len(before) + [VMEM] * (9 + len(sums)),
        [((n * T, 2 * D), BF)] * 2 + [((8, D), F32)] * 2,
        [*before, attended, activated, dense, fc2, mixed_grad, pre_grad, weight, normed, vecs, *sums],
        flops=2 * n * 2 * T * (COLS + T + FFL) * D,
        nbytes=8 * MIB,
    )


TM = 512
TQ = 512
TK = 512


def attention_kernel(blocks, last, n_before, place, cos_ref, sin_ref, *refs):
    refs = refs[n_before:]
    if last:
        first_refs, refs = refs[:8], refs[8:]
        att_ref, out_ref, att_t_ref, out_t_ref, bias_ref = refs[:5]
        q_ref, k_ref, v_ref, do_ref = first_refs[:4]
        dq_ref, dk_ref, dv_ref, o_ref, s_ref, e_ref = refs[5:]
    else:
        mixed_ref, grad_ref, *refs = refs
        refs, done_ref = refs[:8] + refs[9:], refs[8]
        done_ref[...] = jnp.zeros_like(done_ref)
        q_ref, k_ref, v_ref, do_ref, dq_ref, dk_ref, dv_ref, o_ref, s_ref, e_ref = refs
    lane = lax.broadcasted_iota(jnp.int32, (T, 128), 1)
    low_head = lane < HEAD_DIM
    first = (lane % HEAD_DIM) < ROTARY // 2

    def turned(x):
        return jnp.where(
            first, pltpu.roll(x, 128 - ROTARY // 2, 1), pltpu.roll(x, ROTARY // 2, 1)
        )

    def load(slot, _):
        rows = pl.ds(pl.multiple_of(slot * T, T), T)
        at = pl.ds(pl.multiple_of(place[slot] * T, T), T)
        c, s = cos_ref[at, :], sin_ref[at, :]
        query = mixed_ref[rows, 0:128]
        key = mixed_ref[rows, 128:256]
        query = (query * c + turned(query) * s).astype(BF).astype(F32) * (HEAD_DIM**-0.5)
        q_ref[0, at, :] = jnp.where(low_head, query, 0.0).astype(BF)
        q_ref[1, at, :] = jnp.where(low_head, 0.0, query).astype(BF)
        k_ref[at, :] = (key * c + turned(key) * s).astype(BF)
        v_ref[at, 0:128] = mixed_ref[rows, 256:384].astype(BF)
        v_ref[at, 128:256] = jnp.ones((T, 128), BF)
        grad = grad_ref[rows, :].astype(F32)
        do_ref[0, at, :] = jnp.where(low_head, grad, 0.0).astype(BF)
        do_ref[1, at, :] = jnp.where(low_head, 0.0, grad).astype(BF)
        dk_ref[:, at] = jnp.zeros((128, T), F32)
        dv_ref[:, at] = jnp.zeros((128, T), F32)
        return 0

    if last:
        for to, at in ((dq_ref, 4), (dk_ref, 5), (dv_ref, 6), (o_ref, 7)):
            to[...] = first_refs[at][...]
    else:
        lax.fori_loop(0, 16, load, 0)

    lane_q = lax.broadcasted_iota(jnp.int32, (TQ, 128), 1)
    low_q = lane_q < HEAD_DIM

    def block(i, _):
        rows = lanes(i, TQ)
        queries = [q_ref[h, rows, :] for h in range(2)]

        def scores(j, tops, masked):
            at = lanes(j, TK)
            keys = k_ref[at, :]
            new = []
            for h in range(2):
                s = dot(queries[h], keys, 1, 1)
                if masked:
                    row = lax.broadcasted_iota(jnp.int32, (TQ, TK), 0)
                    col = lax.broadcasted_iota(jnp.int32, (TQ, TK), 1)
                    s = jnp.where(row >= col, s, -1e30)
                s_ref[h, :, at] = s
                top = tops[h]
                for n in range(TK // 128):
                    top = jnp.maximum(top, s[:, n * 128 : (n + 1) * 128])
                new.append(top)
            return tuple(new)

        low = jnp.full((TQ, 128), -1e30, F32)
        tops = lax.fori_loop(0, i, lambda j, t: scores(j, t, False), (low, low))
        tops = [jnp.max(t, axis=1, keepdims=True) for t in scores(i, tops, True)]

        def weigh(j, totals):
            at = lanes(j, TK)
            values = v_ref[at, :]
            new = []
            for h in range(2):
                e = jnp.exp2((s_ref[h, :, at] - tops[h]) * LOG2E).astype(BF)
                e_ref[h, :, at] = e
                new.append(totals[h] + dot(e, values))
            return tuple(new)

        zero = jnp.zeros((TQ, 256), F32)
        totals = lax.fori_loop(0, i + 1, weigh, (zero, zero))
        outs, grads, deltas = [], [], []
        for h in range(2):
            inverse = 1.0 / totals[h][:, 128:]
            o = totals[h][:, :128] * inverse
            grad = do_ref[h, rows, :].astype(F32) * inverse
            outs.append(o)
            deltas.append(jnp.sum(grad * o, axis=1, keepdims=True))
            grads.append(grad.astype(BF))
        o_ref[rows, :] = jnp.where(low_q, outs[0], outs[1]).astype(BF)
        queries_t = [q.T for q in queries]
        grads_t = [g.T for g in grads]

        def back(j, totals):
            at = lanes(j, TK)
            keys = k_ref[at, :]
            values = v_ref[at, 0:128]
            new, dk, dv = [], None, None
            for h in range(2):
                e = e_ref[h, :, at]
                dp = dot(grads[h], values, 1, 1)
                ds = (e.astype(F32) * (dp - deltas[h])).astype(BF)
                new.append(totals[h] + dot(ds, keys))
                k_part = dot(queries_t[h], ds)
                v_part = dot(grads_t[h], e)
                dk = k_part if dk is None else dk + k_part
                dv = v_part if dv is None else dv + v_part
            dk_ref[:, at] += dk
            dv_ref[:, at] += dv
            return tuple(new)

        zero = jnp.zeros((TQ, 128), F32)
        dqs = lax.fori_loop(0, i + 1, back, (zero, zero))
        dq_ref[rows, :] = jnp.where(low_q, dqs[0], dqs[1]) * (HEAD_DIM**-0.5)
        return 0

    lax.fori_loop(blocks[0], blocks[1], block, 0)
    if not last:
        return

    def store(slot, total):
        rows = pl.ds(pl.multiple_of(slot * T, T), T)
        at = pl.ds(pl.multiple_of(place[slot] * T, T), T)
        c, s = cos_ref[at, :], sin_ref[at, :]
        att = o_ref[at, :]
        att_ref[rows, :] = att
        att_t_ref[:, rows] = att.T
        dq, dk = dq_ref[at, :], dk_ref[:, at].T
        new = []
        for part, grad in enumerate(
            (dq * c - turned(dq) * s, dk * c - turned(dk) * s, dv_ref[:, at].T)
        ):
            low = grad.astype(BF)
            cols = slice(part * T, (part + 1) * T)
            out_ref[rows, cols] = low
            out_t_ref[cols, rows] = low.T
            new.append(total[part] + jnp.sum(low.astype(F32).reshape(16, 8, T), axis=0))
        return tuple(new)

    zero = jnp.zeros((8, T), F32)
    sums = lax.fori_loop(0, 16, store, (zero, zero, zero))
    for part in range(3):
        bias_ref[:, part * T : (part + 1) * T] = sums[part]


def attention_first(place, cosine, sine, mixed, attended_grad, before):
    return call(
        functools.partial(attention_kernel, (0, 3), False, len(before)),
        [SMEM] + [VMEM] * 2 + [ANY] * len(before) + [VMEM] * 2,
        [
            ((2, SEQ, 128), BF, 1),
            ((SEQ, 128), BF, 1),
            ((SEQ, 256), BF, 1),
            ((2, SEQ, 128), BF, 1),
            ((SEQ, 128), F32, 1),
            ((128, SEQ), F32, 1),
            ((128, SEQ), F32, 1),
            ((SEQ, 128), BF, 1),
            ((8, 128), jnp.int32),
        ],
        [place, cosine, sine, *before, mixed, attended_grad],
        [pltpu.VMEM((2, TQ, SEQ), F32), pltpu.VMEM((2, TQ, SEQ), BF)],
        vmem=20,
        flops=8 * SEQ * SEQ * 64 * 2,
        exps=SEQ * SEQ // 2,
        nbytes=3 * MIB,
    )


def attention_last(place, cosine, sine, state, before):
    return call(
        functools.partial(attention_kernel, (3, 4), True, len(before)),
        [SMEM] + [VMEM] * 2 + [ANY] * len(before) + [VMEM] * 8,
        [
            ((SEQ, T), BF, 1),
            ((SEQ, QKV), BF, 1),
            ((T, SEQ), BF, 1),
            ((QKV, SEQ), BF, 1),
            ((8, QKV), F32),
        ],
        [place, cosine, sine, *before] + list(state),
        [
            pltpu.VMEM((SEQ, 128), F32),
            pltpu.VMEM((128, SEQ), F32),
            pltpu.VMEM((128, SEQ), F32),
            pltpu.VMEM((SEQ, 128), BF),
            pltpu.VMEM((2, TQ, SEQ), F32),
            pltpu.VMEM((2, TQ, SEQ), BF),
        ],
        vmem=22,
        flops=6 * SEQ * SEQ * 64 * 2,
        exps=SEQ * SEQ // 2,
        nbytes=3 * MIB,
    )


def rotary_tables():
    lane = lax.broadcasted_iota(jnp.int32, (SEQ, 128), 1) % HEAD_DIM
    place = lax.broadcasted_iota(jnp.int32, (SEQ, 128), 0).astype(F32)
    freq = (lane % (ROTARY // 2)).astype(F32)
    angle = place * jnp.exp(freq * (-2.0 * math.log(10000.0) / ROTARY))
    turns = lane < ROTARY
    cosine = jnp.where(turns, jnp.cos(angle), 1.0)
    sine = jnp.where(turns, jnp.sin(angle), 0.0)
    return cosine, jnp.where(lane < ROTARY // 2, -sine, sine)


def body(
    tokens,
    ln_gain,
    ln_shift,
    qkv_weight,
    qkv_bias,
    dense_weight,
    dense_bias,
    fc1_weight,
    fc1_bias,
    fc2_weight,
    fc2_bias,
    cotangent,
):
    rep, shard = lax.axis_index("rep"), lax.axis_index("shard")
    xh, y = rep // 4, rep % 4
    z, xl, c = shard // 4, (shard // 2) % 2, shard % 2
    token_place = jnp.stack(
        [((z + dz) % 4) * 4 + (xl ^ dx) * 2 + (c ^ dc) for dz, dx, dc in SLOTS]
    ).astype(jnp.int32)
    row_place = jnp.stack(
        [((z + y + dy) % 4) * 4 + (xl ^ dx) * 2 + (c ^ dc) for dy, dx, dc in SLOTS]
    ).astype(jnp.int32)
    col_place = jnp.stack(
        [((z - y - dy) % 4) * 4 + (xl ^ dx) * 2 + (c ^ dc) for dy, dx, dc in SLOTS]
    ).astype(jnp.int32)
    part_place = jnp.stack(
        [((y + dy) % 4) * 2 + dx for dy in range(4) for dx in range(2)]
    ).astype(jnp.int32)
    me, core = shard.reshape(1).astype(jnp.int32), c.reshape(1).astype(jnp.int32)

    vectors = [v.reshape(-1, T) for v in (qkv_bias, ln_gain, ln_shift, dense_bias, fc2_bias)]
    vectors = jnp.concatenate(vectors + [jnp.zeros((T - 7, T), BF)])
    message = jnp.concatenate([tokens, cotangent, vectors], axis=1)
    near = gather_near(message)

    def columns_for(chip):
        qkv = [
            lax.dynamic_slice(qkv_weight, (0, part * D + chip * 2 * T), (T, 2 * T))
            for part in range(3)
        ]
        fc1 = lax.dynamic_slice(fc1_weight, (0, chip * 2 * FFL), (T, 2 * FFL))
        return jnp.concatenate(
            [
                jnp.concatenate(
                    [p[:, at * T : (at + 1) * T] for p in qkv]
                    + [fc1[:, at * FFL : (at + 1) * FFL]],
                    axis=1,
                )
                for at in range(2)
            ]
        )

    to_chip = ((z - y) % 4) * 2 + xl
    mine, other = columns_for(to_chip ^ c), columns_for(to_chip ^ c ^ 1)
    other = fetch(other, dc=1)
    rows = fetch_from(
        jnp.concatenate([mine, other]), lambda xh, y, z, xl, c: (xh, y, z + y, xl ^ c, c)
    )
    own_pair = message, gather_swap(message)
    far_vectors = fetch(vectors[:16], dz=2, dx=1)
    cosine, sine = rotary_tables()
    rows, near, own_pair, cosine, sine = together(rows, near, own_pair, cosine, sine)

    def columns_of(rows, core):
        return jnp.concatenate(
            [
                lax.dynamic_slice(rows, (n * 2 * T + core * T, 0), (T, COLS))
                for n in range(2)
            ]
        )

    mine = columns_of(rows, c)
    other = fetch(columns_of(rows, 1 - c), dc=1)
    here = jnp.where(c == 0, mine, jnp.concatenate([other[T:], other[:T]]))
    there = jnp.where(c == 0, jnp.concatenate([other[T:], other[:T]]), mine)
    own_rows = jnp.concatenate([here, there])
    near_pairs = {k: own_pair if k == (0, 0) else (v, gather_swap(v)) for k, v in near.items()}
    further = gather_next(near)
    far_vectors = jnp.concatenate([far_vectors, fetch(far_vectors, dc=1)])
    one, three = fetch(own_rows, dy=1), fetch(own_rows, dy=-1)
    one, three, further = together(one, three, further)
    weights = (own_rows, one, three, fetch(one[: 2 * T], dy=1), fetch(three[2 * T :], dy=-1))
    far = gather_far(further)
    *arrays, vecs, own_qkv_bias = near_inputs(
        both_cores(near_pairs) + both_cores(further),
        far_vectors,
        fc2_weight,
        dense_weight,
        token_place,
        me,
        [one, three],
    )
    far_other = fetch(jnp.concatenate(far) + zero_of(vecs).astype(BF), dc=1)
    far = [(far[0], 10 * T), (far[1], 10 * T + T // 2), (far_other, 11 * T)]
    gain, out_bias = vecs[0:1], vecs[2:3]
    (
        normed,
        all_cot,
        _,
        attended_grad,
        weight,
        activated,
        pre_grad,
        act_t,
        pre_t,
        mixed,
        fc1_bias_part,
        out_bias_part,
    ) = forward_inputs(
        arrays,
        far,
        weights,
        vecs,
        fc1_bias.astype(F32).reshape(1, FFL),
        own_qkv_bias,
        fc2_weight,
        dense_weight,
        row_place,
        me,
    )

    early = column_grads(normed, pre_t, act_t, all_cot, row_place, part_place, core)
    *state, done = attention_first(token_place, cosine, sine, mixed, attended_grad, early)
    early_near = reduce_near(early, reduce_far(early), done[0, 0].astype(F32))
    attended, mixed_grad, attended_t, mixed_t, qkv_bias_part = attention_last(
        token_place, cosine, sine, state, early_near
    )
    early = early[0], fetch(early_near[0], dy=-1), fetch(early_near[1], dy=1)
    early = [add(*(e[dx * FFL : (dx + 1) * FFL] for e in early)).astype(BF) for dx in range(2)]

    early_other = [fetch(e, dh=1) for e in early]

    def the_terms(chips, sums, before):
        mine, other, *sums = terms(
            chips,
            attended,
            activated,
            dense_weight,
            fc2_weight,
            mixed_grad,
            pre_grad,
            weight,
            normed,
            vecs,
            sums,
            before,
        )
        return mine, fetch(other, dc=1), sums

    def own_terms(chips, mine, other, zero):
        return {
            chip: add(mine[n * T : (n + 1) * T], other[n * T : (n + 1) * T], zero).astype(BF)
            for n, chip in enumerate(chips)
        }

    mine0, other0, sums = the_terms(WAVES[0], [], early)
    mine1, other1, sums = the_terms(WAVES[1], sums, [])
    q = own_terms(WAVES[0], mine0, other0, zero_of(sums[0]))
    far = scatter_far(q)
    mine2, other2, sums = the_terms(WAVES[2], sums, [q[2, 1], early_other[0]])
    zero = zero_of(sums[0])
    early = jnp.concatenate(
        [add(e, other, zero).astype(BF) for e, other in zip(early, early_other, strict=True)]
    )
    early_own = jnp.concatenate([early[:, :T], fetch(early[:, T : 2 * T], dc=1)], axis=1)
    late = head_grads(
        normed,
        mixed_t,
        attended_t,
        all_cot,
        row_place,
        part_place,
        core,
        me,
        gain,
        sums,
        (qkv_bias_part, fc1_bias_part, out_bias_part),
        [early_own],
    )

    def from_owners(rows):
        return [
            fetch_from(rows[dx], lambda xh, y, z, xl, c: (xh, y, z - y, xl ^ dx, c))
            for dx in range(2)
        ]

    early_own = from_owners([early_own[:FFL], early_own[FFL:]])
    late_far = reduce_far(late)
    early_own, late_far, far, other1, other2 = together(early_own, late_far, far, other1, other2)

    early = jnp.concatenate(
        [
            jnp.concatenate([early_own[dx], early[dx * FFL : (dx + 1) * FFL, 2 * T :]], axis=1)
            for dx in range(2)
        ]
    )
    early_one, early_three = fetch(early, dy=1), fetch(early, dy=-1)
    q |= own_terms(WAVES[1], mine1, other1, 0.0) | own_terms(WAVES[2], mine2, other2, 0.0)
    further = scatter_next(q, far, 0.0)
    late_near = reduce_near(late, late_far, 0.0)
    early_one, early_three, further, late_near = together(
        early_one, early_three, further, late_near
    )

    nearest = scatter_near(q, further, 0.0)
    late = add(late[0], fetch(late_near[0], dy=-1), fetch(late_near[1], dy=1)).astype(BF)
    late_other = fetch(late, dh=1)
    nearest, late_other = together(nearest, late_other)

    early = (
        early,
        early_one,
        early_three,
        fetch(early_one[:FFL], dy=1),
        fetch(early_three[FFL:], dy=-1),
    )
    late = add(late, late_other).astype(BF)
    late_rows = jnp.concatenate([late[:FOR_OWNER], late[LATE : LATE + FOR_OWNER]])
    late_own = jnp.concatenate([late_rows[:, :T], fetch(late_rows[:, T:], dc=1)], axis=1)
    late_own = from_owners([late_own[:FOR_OWNER], late_own[FOR_OWNER:]])
    late = jnp.concatenate(
        [late_own[0], late[FOR_OWNER:LATE], late_own[1], late[LATE + FOR_OWNER :]]
    )
    late, early = together(late, early)
    late_one, late_three = fetch(late, dy=1), fetch(late, dy=-1)
    total = add(q[0, 0], *nearest)
    own = tokens.astype(F32)
    layer_out = (own + out_bias + total[:, D:]).astype(BF)
    center = own - jnp.mean(own, axis=-1, keepdims=True)
    inv_std = lax.rsqrt(jnp.mean(center * center, axis=-1, keepdims=True) + 1e-05)
    unit = center * inv_std
    scaled = total[:, :D] * gain
    input_grad = cotangent.astype(F32) + inv_std * (
        scaled
        - jnp.mean(scaled, axis=-1, keepdims=True)
        - unit * jnp.mean(scaled * unit, axis=-1, keepdims=True)
    )
    late = (
        late,
        late_one,
        late_three,
        fetch(late_one[:LATE], dy=1),
        fetch(late_three[LATE:], dy=-1),
    )
    fc1_total, fc2_total = place_columns(early, col_place, part_place)
    qkv_total, dense_total, of_owner, of_own = place_heads(late, col_place, part_place)
    out_bias_total = of_own[0, FFL : FFL + T]

    return (
        layer_out,
        input_grad,
        of_owner[0],
        of_owner[1],
        qkv_total,
        of_owner[2:5].reshape(QKV),
        dense_total,
        out_bias_total,
        fc1_total,
        of_own[0, :FFL],
        fc2_total,
        out_bias_total,
    )


def solution(mesh):
    return jax.shard_map(
        body,
        mesh=mesh,
        in_specs=(
            P(AXES, None),
            P("shard"),
            P("shard"),
            P("shard", None),
            P("shard"),
            P("shard", None),
            P("shard"),
            P("shard", None),
            P("shard"),
            P("shard", None),
            P("shard"),
            P(AXES, None),
        ),
        out_specs=(
            P(AXES, None),
            P(AXES, None),
            P("shard"),
            P("shard"),
            P("shard", None),
            P("shard"),
            P("shard", None),
            P("shard"),
            P("shard", None),
            P("shard"),
            P("shard", None),
            P("shard"),
        ),
        check_vma=False,
    )
```

```python
import functools
import math

import jax
import jax.numpy as jnp
from jax import lax
from jax.experimental import pallas as pl
from jax.experimental.pallas import tpu as pltpu
from jax.sharding import PartitionSpec as P

D = 2048
HEADS = 32
HEAD_DIM = 64
ROTARY = 32
FF = 8192
SEQ = 2048
T = 128
QKV = 384
FFL = 512
COLS = QKV + FFL
BF = jnp.bfloat16
F32 = jnp.float32
AXES = ("rep", "shard")
MIB = 1 << 20
LOG2E = math.log2(math.e)

PLACES = [
    (xh, y, z, xl, c)
    for xh in range(2)
    for y in range(4)
    for z in range(4)
    for xl in range(2)
    for c in range(2)
]


def flat(xh, y, z, xl, c):
    return (xh * 4 + y % 4) * 16 + (z % 4) * 4 + xl * 2 + c


def fetch_from(x, source):
    return lax.ppermute(x, AXES, [(flat(*source(*p)), flat(*p)) for p in PLACES])


def fetch(x, dz=0, dx=0, dc=0, dy=0, dh=0):
    return fetch_from(
        x, lambda xh, y, z, xl, c: (xh ^ dh, y + dy, z + dz, xl ^ dx, c ^ dc)
    )


def dot(a, b, ca=1, cb=0):
    return lax.dot_general(a, b, (((ca,), (cb,)), ((), ())), preferred_element_type=F32)


def add(*terms):
    total = terms[0].astype(F32)
    for term in terms[1:]:
        total = total + (term if isinstance(term, float) else term.astype(F32))
    return total


def zero_of(x):
    return x[0, 0].astype(F32) * 0.0


def together(*groups):
    leaves, tree = jax.tree.flatten(groups)
    n = len(leaves)
    leaves = pl.pallas_call(
        lambda *refs: None,
        in_specs=[pl.BlockSpec(memory_space=pl.ANY)] * n,
        out_specs=[pl.BlockSpec(memory_space=pl.ANY)] * n,
        out_shape=[jax.ShapeDtypeStruct(x.shape, x.dtype) for x in leaves],
        input_output_aliases={i: i for i in range(n)},
    )(*leaves)
    return jax.tree.unflatten(tree, leaves)


def gather_near(own):
    return {
        (0, 0): own,
        (1, 0): fetch(own, dz=1),
        (3, 0): fetch(own, dz=-1),
        (0, 1): fetch(own, dx=1),
    }


def gather_next(a):
    return {
        (1, 1): fetch(a[1, 0], dx=1),
        (3, 1): fetch(a[0, 1], dz=-1),
        (2, 0): fetch(a[1, 0], dz=1),
    }


def gather_far(a):
    half = a[1, 1].shape[0] // 2
    return fetch(a[1, 1][:half], dz=1), fetch(a[3, 1][half:], dz=-1)


def gather_swap(own):
    return fetch(own, dc=1)


def both_cores(a):
    pieces = []
    for (dz, dx), own in a.items():
        pair = own if isinstance(own, tuple) else (own, gather_swap(own))
        pieces += [(pair[dc], ((dz * 2 + dx) * 2 + dc) * T) for dc in range(2)]
    return pieces


SLOTS = [(dz, dx, dc) for dz in range(4) for dx in range(2) for dc in range(2)]
WAVES = [[(2, 1)], [(1, 1), (3, 1), (2, 0)], [(1, 0), (3, 0), (0, 1), (0, 0)]]


def scatter_far(q):
    half = T // 2
    return fetch(q[2, 1][:half], dz=-1), fetch(q[2, 1][half:], dz=1)


def scatter_next(q, far, zero):
    half = T // 2
    q11 = jnp.concatenate([add(q[1, 1][:half], far[0], zero).astype(BF), q[1, 1][half:]])
    q31 = jnp.concatenate([q[3, 1][:half], add(q[3, 1][half:], far[1], zero).astype(BF)])
    return fetch(q[2, 0], dz=-1), fetch(q31, dz=1), fetch(q11, dx=1)


def scatter_near(q, further, zero):
    q10 = add(q[1, 0], further[0], further[2], zero).astype(BF)
    q01 = add(q[0, 1], further[1], zero).astype(BF)
    return fetch(q10, dz=-1), fetch(q[3, 0], dz=1), fetch(q01, dx=1)


def reduce_far(g):
    half = g[0].shape[0] // 2
    return fetch(g[2][:half], dy=-1), fetch(g[2][half:], dy=1)


def reduce_near(g, far, zero):
    half = g[0].shape[0] // 2
    g1 = jnp.concatenate([add(g[1][:half], far[0], zero).astype(BF), g[1][half:]])
    g3 = jnp.concatenate([g[3][:half], add(g[3][half:], far[1], zero).astype(BF)])
    return g1, g3


def of_rep(refs, dy, dx, n):
    own, one, three, first, second = refs
    if dy == 2:
        return (second if dx else first), 0
    return (own, one, None, three)[dy], dx * n


VMEM = pl.BlockSpec(memory_space=pltpu.VMEM)
SMEM = pl.BlockSpec(memory_space=pltpu.SMEM)
HBM = pl.BlockSpec(memory_space=pltpu.HBM)
ANY = pl.BlockSpec(memory_space=pl.ANY)


def lanes(at, n):
    return pl.ds(pl.multiple_of(at * n, n), n)


def call(kernel, ins, outs, args, scratch=(), vmem=6, flops=0, nbytes=0, exps=0, aliases={}):
    return pl.pallas_call(
        kernel,
        in_specs=ins,
        out_specs=[VMEM] * len(outs),
        out_shape=[
            pltpu.VMEM(o[0], o[1]) if len(o) > 2 else jax.ShapeDtypeStruct(*o) for o in outs
        ],
        scratch_shapes=list(scratch),
        input_output_aliases=aliases,
        compiler_params=pltpu.CompilerParams(vmem_limit_bytes=vmem * MIB),
        cost_estimate=pl.CostEstimate(
            flops=flops // 16, transcendentals=exps // 16, bytes_accessed=nbytes // 16
        ),
    )(*args)


ROOT = math.sqrt(2.0 / math.pi)


def start_copies(pieces, place, sems):
    copies = [
        pltpu.make_async_copy(src, dst, sems.at[place + i]) for i, (src, dst) in enumerate(pieces)
    ]
    for copy in copies:
        copy.start()
    return copies


def norm_rows(normed_ref, gain, shift, first, count):
    def strip(i, _):
        at = lanes(i, 64)
        x = normed_ref[at, :].astype(F32)
        x = x - jnp.sum(x, axis=1, keepdims=True) * (1.0 / D)
        scale = lax.rsqrt(jnp.sum(x * x, axis=1, keepdims=True) * (1.0 / D) + 1e-05)
        normed_ref[at, :] = (x * scale * gain + shift).astype(BF)
        return 0

    lax.fori_loop(first // 64, (first + count) // 64, strip, 0)


def message_moves(refs, pieces, normed_ref, cot_ref):
    moves = []
    for (array, at), ref in zip(pieces, refs, strict=True):
        to = pl.ds(at, array.shape[0])
        moves.append((ref.at[:, pl.ds(0, D)], normed_ref.at[to]))
        moves.append((ref.at[:, pl.ds(D, D)], cot_ref.at[to]))
    return moves


def near_inputs(pieces, far_vectors, fc2, dense, token_place, me, before):
    n = len(pieces)
    chips = sorted({at // 256 for _, at in pieces})

    def kernel(t_ref, me_ref, *refs):
        refs = refs[len(before) :]
        (
            far_ref,
            fc2_ref,
            dense_ref,
            normed_ref,
            cot_ref,
            grad_ref,
            att_ref,
            vec_ref,
            own_ref,
            done_ref,
            small_ref,
            flat_ref,
            sems,
        ) = refs[n:]
        done_ref[...] = jnp.zeros_like(done_ref)
        moves = [
            (ref.at[pl.ds(0, 16), pl.ds(2 * D, T)], small_ref.at[pl.ds(at // T * 16, 16)])
            for (_, at), ref in zip(pieces, refs[:n], strict=True)
        ]
        for dc in range(2):
            to = small_ref.at[pl.ds((5 * 2 + dc) * 16, 16)]
            moves.append((far_ref.at[pl.ds(dc * 16, 16)], to))
        small_copies = start_copies(moves, 0, sems)
        copies = start_copies(
            message_moves(refs[:n], pieces, normed_ref, cot_ref), n + 2, sems
        )
        for copy in small_copies:
            copy.wait()
        for i in range(16):
            at = t_ref[i]
            small = small_ref[i * 16 : (i + 1) * 16, :].astype(F32)
            for part in range(3):
                flat_ref[0:1, lanes(at * 3 + part, T)] = small[part : part + 1]
            vec_ref[0:1, lanes(at, T)] = small[3:4]
            vec_ref[1:2, lanes(at, T)] = small[4:5]
            vec_ref[2:3, lanes(at, T)] = small[5:6] + small[6:7]
        for part in range(3):
            own_ref[0:1, part * T : (part + 1) * T] = flat_ref[
                0:1, lanes(part * 16 + me_ref[0], T)
            ]
        gain, shift = vec_ref[0:1, :], vec_ref[1:2, :]
        for chip in chips:
            for (_, at), token_copy, cot_copy in zip(pieces, copies[0::2], copies[1::2]):
                if at // 256 == chip:
                    token_copy.wait()
                    cot_copy.wait()
            norm_rows(normed_ref, gain, shift, chip * 256, 256)

        def tile(i, _):
            at = lanes(i, TM)
            x = cot_ref[at, :]
            grad_ref[at, :] = dot(x, fc2_ref[...], 1, 1).astype(BF)
            att_ref[at, :] = dot(x, dense_ref[...], 1, 1).astype(BF)
            return 0

        lax.fori_loop(0, SEQ // TM, tile, 0)

    return call(
        kernel,
        [SMEM] * 2 + [ANY] * len(before) + [HBM] * (n + 1) + [VMEM] * 2,
        [
            ((SEQ, D), BF, 1),
            ((SEQ, D), BF, 1),
            ((SEQ, FFL), BF, 1),
            ((SEQ, T), BF, 1),
            ((8, D), F32, 1),
            ((1, QKV), F32, 1),
            ((8, T), F32),
        ],
        [token_place, me, *before] + [p for p, _ in pieces] + [far_vectors, fc2, dense],
        [
            pltpu.VMEM((256, T), BF),
            pltpu.VMEM((1, 3 * D), F32),
            pltpu.SemaphoreType.DMA((3 * n + 2,)),
        ],
        flops=2 * SEQ * D * (FFL + T),
        nbytes=20 * MIB,
    )


def forward_inputs(arrays, pieces, weights, vecs, bias, own_bias, fc2, dense, row_place, me):
    n = len(pieces)
    chip = pieces[0][1] // 256

    def kernel(r_ref, me_ref, *refs):
        tok = refs[4 : 4 + n]
        w_refs = refs[4 + n : 9 + n]
        (
            vec_ref,
            bias_ref,
            own_ref,
            fc2_ref,
            dense_ref,
            normed_ref,
            cot_ref,
            grad_ref,
            att_ref,
            w_ref,
            act_ref,
            pre_ref,
            act_t_ref,
            pre_t_ref,
            mixed_ref,
            fc1b_ref,
            outb_ref,
            sems,
        ) = refs[9 + n :]
        copies = start_copies(message_moves(tok, pieces, normed_ref, cot_ref), 0, sems)
        moves = []
        for i, (dy, dx, dc) in enumerate(SLOTS):
            ref, at = of_rep(w_refs, dy, dx, 2 * T)
            moves.append((ref.at[pl.ds(at + dc * T, T)], w_ref.at[lanes(r_ref[i], T)]))
        w_copies = start_copies(moves, 2 * n, sems)
        for copy in copies:
            copy.wait()
        norm_rows(normed_ref, vec_ref[0:1, :], vec_ref[1:2, :], chip * 256, 256)
        rows = slice(chip * 256, (chip + 1) * 256)
        x = cot_ref[rows, :]
        grad_ref[rows, :] = dot(x, fc2_ref[...], 1, 1).astype(BF)
        att_ref[rows, :] = dot(x, dense_ref[...], 1, 1).astype(BF)
        for copy in w_copies:
            copy.wait()

        def product(i):
            at = lanes(i, TM)
            x = normed_ref[at, :]
            mixed_ref[at, :] = dot(x, w_ref[:, :QKV]) + own_ref[...]
            return dot(x, w_ref[:, QKV:]) + bias_ref[...]

        def gelu(i, pre, total):
            at = lanes(i, TM)
            squared = pre * pre
            tanh = jnp.tanh(ROOT * pre * (1.0 + 0.044715 * squared))
            act = (0.5 * pre * (1.0 + tanh)).astype(BF)
            act_ref[at, :] = act
            act_t_ref[:, at] = act.T
            slope = 0.5 * (1.0 + tanh) + 0.5 * pre * (1.0 - tanh * tanh) * ROOT * (
                1.0 + 3 * 0.044715 * squared
            )
            back = (grad_ref[at, :].astype(F32) * slope).astype(BF)
            pre_ref[at, :] = back
            pre_t_ref[:, at] = back.T
            return total + jnp.sum(back.astype(F32).reshape(TM // 8, 8, FFL), axis=0)

        def tile(i, carry):
            pre, total = carry
            return product(i), gelu(i - 1, pre, total)

        pre, total = lax.fori_loop(1, SEQ // TM, tile, (product(0), jnp.zeros((8, FFL), F32)))
        fc1b_ref[...] = gelu(SEQ // TM - 1, pre, total)

        def sums(i, total):
            own = cot_ref[lanes(i, 256), lanes(me_ref[0], T)].astype(F32)
            return total + jnp.sum(own.reshape(32, 8, T), axis=0)

        outb_ref[...] = lax.fori_loop(0, 8, sums, jnp.zeros((8, T), F32))

    return call(
        kernel,
        [SMEM] * 2 + [VMEM] * 4 + [HBM] * (n + 5) + [VMEM] * 5,
        [
            ((SEQ, D), BF, 1),
            ((SEQ, D), BF, 1),
            ((SEQ, FFL), BF, 1),
            ((SEQ, T), BF, 1),
            ((D, COLS), BF, 1),
            ((SEQ, FFL), BF, 1),
            ((SEQ, FFL), BF, 1),
            ((FFL, SEQ), BF, 1),
            ((FFL, SEQ), BF, 1),
            ((SEQ, QKV), F32, 1),
            ((8, FFL), F32),
            ((8, T), F32),
        ],
        [row_place, me]
        + list(arrays)
        + [p for p, _ in pieces]
        + list(weights)
        + [vecs, bias, own_bias, fc2, dense],
        [pltpu.SemaphoreType.DMA((2 * n + 16,))],
        aliases={2: 0, 3: 1, 4: 2, 5: 3},
        flops=2 * SEQ * D * COLS,
        nbytes=8 * MIB,
        exps=SEQ * FFL,
    )


def column_grads(normed, pre_t, act_t, cot, row_place, part_place, core):
    def kernel(r_ref, p_ref, core_ref, n_ref, g_ref, a_ref, c_ref, *outs):
        for dy in (2, 1, 3, 0):
            out = outs[dy]
            for dh in range(2):
                at = slice(dh * FFL, (dh + 1) * FFL)
                chip = r_ref[(dy * 2 + dh) * 2] // 2
                cols = dot(g_ref[...], n_ref[:, lanes(chip, 256)]).astype(BF)
                out[at, lanes(core_ref[0], T)] = cols[:, :T]
                out[at, lanes(1 - core_ref[0], T)] = cols[:, T:]
                part = c_ref[:, lanes(p_ref[dy * 2 + dh], 256)]
                out[at, 256:512] = dot(a_ref[...], part).astype(BF)

    return call(
        kernel,
        [SMEM] * 3 + [VMEM] * 4,
        [((1024, 512), BF)] * 4,
        [row_place, part_place, core, normed, pre_t, act_t, cot],
        flops=4 * SEQ * D * FFL,
        nbytes=4 * MIB,
    )


FOR_OWNER = QKV + 16
LATE = FOR_OWNER + T + 16


def head_grads(
    normed,
    mixed_t,
    attended_t,
    cot,
    places,
    part_place,
    core,
    me,
    gain,
    sums,
    bias_parts,
    before,
):
    def kernel(r_ref, p_ref, core_ref, me_ref, n_ref, m_ref, a_ref, c_ref, *refs):
        refs = refs[len(before) :]
        gain_ref, gains_ref, shifts_ref, qkvb_ref, fc1b_ref, outb_ref = refs[:6]
        outs, owners_ref, own_ref = refs[6:10], refs[10], refs[11]
        owners_ref[...] = jnp.zeros_like(owners_ref)
        owners_ref[0:1, :] = jnp.sum(gains_ref[...], axis=0, keepdims=True) / gain_ref[...]
        owners_ref[1:2, :] = jnp.sum(shifts_ref[...], axis=0, keepdims=True)
        qkvb = jnp.sum(qkvb_ref[...], axis=0, keepdims=True)
        for part in range(3):
            at = part * 16 + me_ref[0]
            third = at % 3
            row = lax.broadcasted_iota(jnp.int32, (8, T), 0)
            value = jnp.where(row == 2 + third, qkvb[:, part * T : (part + 1) * T], 0.0)
            owners_ref[0:8, lanes(at // 3, T)] += value
        own_ref[...] = jnp.zeros_like(own_ref)
        own_ref[0:1, :FFL] = jnp.sum(fc1b_ref[...], axis=0, keepdims=True)
        own_ref[0:1, FFL : FFL + T] = jnp.sum(outb_ref[...], axis=0, keepdims=True)
        for dy in (2, 1, 3, 0):
            out = outs[dy]
            for dx in range(2):
                base = dx * LATE
                chip = r_ref[(dy * 2 + dx) * 2] // 2
                cols = dot(m_ref[...], n_ref[:, lanes(chip, 256)]).astype(BF)
                extra = owners_ref[:, lanes(chip, 256)].astype(BF)
                mine, other = lanes(core_ref[0], T), lanes(1 - core_ref[0], T)
                out[base : base + QKV, mine] = cols[:, :T]
                out[base : base + QKV, other] = cols[:, T:]
                out[base + QKV : base + FOR_OWNER, mine] = extra[:, :T]
                out[base + QKV : base + FOR_OWNER, other] = extra[:, T:]
                base += FOR_OWNER
                part = p_ref[dy * 2 + dx]
                out[base : base + T, :] = dot(a_ref[...], c_ref[:, lanes(part, 256)]).astype(BF)
                out[base + T : base + T + 16, 0:T] = own_ref[:, lanes(part, T)].astype(BF)
                out[base + T : base + T + 16, T:] = jnp.zeros((16, T), BF)

    return call(
        kernel,
        [SMEM] * 4 + [VMEM] * 4 + [ANY] * len(before) + [VMEM] * 6,
        [((2 * LATE, 256), BF)] * 4,
        [
            places,
            part_place,
            core,
            me,
            normed,
            mixed_t,
            attended_t,
            cot,
            *before,
            gain,
            *sums,
            *bias_parts,
        ],
        [pltpu.VMEM((16, D), F32), pltpu.VMEM((16, 1024), F32)],
        flops=2 * SEQ * D * (QKV + T),
        nbytes=2 * MIB,
    )


def place_columns(pieces, col_place, part_place):
    def kernel(c_ref, p_ref, *refs):
        fc1_ref, fc2_ref = refs[5:]
        for i, (dy, dh, dc) in enumerate(SLOTS):
            ref, at = of_rep(refs[:5], dy, dh, FFL)
            part = ref[at : at + FFL, dc * T : (dc + 1) * T]
            fc1_ref[:, lanes(c_ref[i], FFL)] = part.astype(F32).T
            if dc == 0:
                to = lanes(p_ref[dy * 2 + dh], 256)
                fc2_ref[:, to] = ref[at : at + FFL, 256:512].astype(F32)

    return call(
        kernel,
        [SMEM] * 2 + [VMEM] * 5,
        [((T, FF), F32), ((FFL, D), F32)],
        [col_place, part_place] + list(pieces),
        vmem=20,
        nbytes=12 * MIB,
    )


def place_heads(pieces, col_place, part_place):
    def kernel(c_ref, p_ref, *refs):
        qkv_ref, dense_ref, owner_ref, own_ref = refs[5:]
        total = jnp.zeros((16, T), F32)
        for i, (dy, dx, dc) in enumerate(SLOTS):
            ref, at = of_rep(refs[:5], dy, dx, LATE)
            cols = slice(dc * T, (dc + 1) * T)
            for part in range(3):
                block = ref[at + part * T : at + (part + 1) * T, cols].astype(F32)
                qkv_ref[:, lanes(c_ref[i] + part * 16, T)] = block.T
            total += ref[at + QKV : at + FOR_OWNER, cols].astype(F32)
            if dc == 0:
                part = p_ref[dy * 2 + dx]
                rows = slice(at + FOR_OWNER, at + FOR_OWNER + T)
                dense_ref[:, lanes(part, 256)] = ref[rows, :].astype(F32)
                rows = slice(at + FOR_OWNER + T, at + LATE)
                own_ref[:, lanes(part, T)] = ref[rows, 0:T].astype(F32)
        owner_ref[...] = total

    return call(
        kernel,
        [SMEM] * 2 + [VMEM] * 5,
        [((T, 3 * D), F32), ((T, D), F32), ((16, T), F32), ((16, 1024), F32)],
        [col_place, part_place] + list(pieces),
        vmem=14,
        nbytes=6 * MIB,
    )


def terms(
    chips, attended, activated, dense, fc2, mixed_grad, pre_grad, weight, normed, vecs, sums, before
):
    n = len(chips)

    def kernel(
        *refs
    ):
        refs = refs[len(before) :]
        a_ref, f_ref, d_ref, v_ref, m_ref, p_ref, w_ref, n_ref, vec_ref = refs[:9]
        mine_ref, other_ref, gain_ref, total_ref = refs[-4:]
        shift = vec_ref[1:2, :]
        if sums:
            gain_ref[...] = refs[9][...]
            total_ref[...] = refs[10][...]
        else:
            gain_ref[...] = jnp.zeros_like(gain_ref)
            total_ref[...] = jnp.zeros_like(total_ref)

        def rows(ref, cols=slice(None)):
            return jnp.concatenate(
                [ref[(dz * 2 + dx) * 256 : (dz * 2 + dx + 1) * 256, cols] for dz, dx in chips]
            )

        left, right = jnp.concatenate([rows(m_ref), rows(p_ref)], axis=1), jnp.concatenate(
            [rows(f_ref), rows(a_ref)], axis=1
        )

        def store(total, to):
            for i in range(n):
                at = slice(i * T, (i + 1) * T)
                mine_ref[at, to] = total[i * 256 : i * 256 + T].astype(BF)
                other_ref[at, to] = total[i * 256 + T : (i + 1) * 256].astype(BF)

        for col in range(4):
            to = slice(col * 512, (col + 1) * 512)
            total = dot(left, w_ref[to, :], 1, 1)
            store(total, to)
            unit = rows(n_ref, to).astype(F32) - shift[:, to]
            gain_ref[:, to] += jnp.sum((total * unit).reshape(n * 32, 8, 512), axis=0)
            total_ref[:, to] += jnp.sum(total.reshape(n * 32, 8, 512), axis=0)
            weights = jnp.concatenate([v_ref[:, to], d_ref[:, to]])
            store(dot(right, weights), slice(D + col * 512, D + (col + 1) * 512))

    return call(
        kernel,
        [ANY] * len(before) + [VMEM] * (9 + len(sums)),
        [((n * T, 2 * D), BF)] * 2 + [((8, D), F32)] * 2,
        [*before, attended, activated, dense, fc2, mixed_grad, pre_grad, weight, normed, vecs, *sums],
        flops=2 * n * 2 * T * (COLS + T + FFL) * D,
        nbytes=8 * MIB,
    )


TM = 512
TQ = 512
TK = 512


def attention_kernel(blocks, last, n_before, place, cos_ref, sin_ref, *refs):
    refs = refs[n_before:]
    if last:
        first_refs, refs = refs[:8], refs[8:]
        att_ref, out_ref, att_t_ref, out_t_ref, bias_ref = refs[:5]
        q_ref, k_ref, v_ref, do_ref = first_refs[:4]
        dq_ref, dk_ref, dv_ref, o_ref, s_ref, e_ref = refs[5:]
    else:
        mixed_ref, grad_ref, *refs = refs
        refs, done_ref = refs[:8] + refs[9:], refs[8]
        done_ref[...] = jnp.zeros_like(done_ref)
        q_ref, k_ref, v_ref, do_ref, dq_ref, dk_ref, dv_ref, o_ref, s_ref, e_ref = refs
    lane = lax.broadcasted_iota(jnp.int32, (T, 128), 1)
    low_head = lane < HEAD_DIM
    first = (lane % HEAD_DIM) < ROTARY // 2

    def turned(x):
        return jnp.where(
            first, pltpu.roll(x, 128 - ROTARY // 2, 1), pltpu.roll(x, ROTARY // 2, 1)
        )

    def load(slot, _):
        rows = pl.ds(pl.multiple_of(slot * T, T), T)
        at = pl.ds(pl.multiple_of(place[slot] * T, T), T)
        c, s = cos_ref[at, :], sin_ref[at, :]
        query = mixed_ref[rows, 0:128]
        key = mixed_ref[rows, 128:256]
        query = (query * c + turned(query) * s).astype(BF).astype(F32) * (HEAD_DIM**-0.5)
        q_ref[0, at, :] = jnp.where(low_head, query, 0.0).astype(BF)
        q_ref[1, at, :] = jnp.where(low_head, 0.0, query).astype(BF)
        k_ref[at, :] = (key * c + turned(key) * s).astype(BF)
        v_ref[at, 0:128] = mixed_ref[rows, 256:384].astype(BF)
        v_ref[at, 128:256] = jnp.ones((T, 128), BF)
        grad = grad_ref[rows, :].astype(F32)
        do_ref[0, at, :] = jnp.where(low_head, grad, 0.0).astype(BF)
        do_ref[1, at, :] = jnp.where(low_head, 0.0, grad).astype(BF)
        dk_ref[:, at] = jnp.zeros((128, T), F32)
        dv_ref[:, at] = jnp.zeros((128, T), F32)
        return 0

    if last:
        for to, at in ((dq_ref, 4), (dk_ref, 5), (dv_ref, 6), (o_ref, 7)):
            to[...] = first_refs[at][...]
    else:
        lax.fori_loop(0, 16, load, 0)

    lane_q = lax.broadcasted_iota(jnp.int32, (TQ, 128), 1)
    low_q = lane_q < HEAD_DIM

    def head(h, i, rows):
        query = q_ref[h, rows, :]

        def scores(j, top, masked):
            at = lanes(j, TK)
            s = dot(query, k_ref[at, :], 1, 1)
            if masked:
                row = lax.broadcasted_iota(jnp.int32, (TQ, TK), 0)
                col = lax.broadcasted_iota(jnp.int32, (TQ, TK), 1)
                s = jnp.where(row >= col, s, -1e30)
            s_ref[:, at] = s
            for n in range(TK // 128):
                top = jnp.maximum(top, s[:, n * 128 : (n + 1) * 128])
            return top

        top = jnp.full((TQ, 128), -1e30, F32)
        top = lax.fori_loop(0, i, lambda j, t: scores(j, t, False), top)
        top = jnp.max(scores(i, top, True), axis=1, keepdims=True)

        def weigh(j, total):
            at = lanes(j, TK)
            e = jnp.exp2((s_ref[:, at] - top) * LOG2E).astype(BF)
            e_ref[:, at] = e
            return total + dot(e, v_ref[at, :])

        total = lax.fori_loop(0, i + 1, weigh, jnp.zeros((TQ, 256), F32))
        inverse = 1.0 / total[:, 128:]
        o = total[:, :128] * inverse
        grad = do_ref[h, rows, :].astype(F32) * inverse
        delta = jnp.sum(grad * o, axis=1, keepdims=True)
        grad = grad.astype(BF)
        query_t, grad_t = query.T, grad.T

        def back(j, total):
            at = lanes(j, TK)
            e = e_ref[:, at]
            dp = dot(grad, v_ref[at, 0:128], 1, 1)
            ds = (e.astype(F32) * (dp - delta)).astype(BF)
            dk_ref[:, at] += dot(query_t, ds)
            dv_ref[:, at] += dot(grad_t, e)
            return total + dot(ds, k_ref[at, :])

        return o, lax.fori_loop(0, i + 1, back, jnp.zeros((TQ, 128), F32))

    def block(i, _):
        rows = lanes(i, TQ)
        o_low, dq_low = head(0, i, rows)
        o_high, dq_high = head(1, i, rows)
        o_ref[rows, :] = jnp.where(low_q, o_low, o_high).astype(BF)
        dq_ref[rows, :] = jnp.where(low_q, dq_low, dq_high) * (HEAD_DIM**-0.5)
        return 0

    lax.fori_loop(blocks[0], blocks[1], block, 0)
    if not last:
        return

    def store(slot, total):
        rows = pl.ds(pl.multiple_of(slot * T, T), T)
        at = pl.ds(pl.multiple_of(place[slot] * T, T), T)
        c, s = cos_ref[at, :], sin_ref[at, :]
        att = o_ref[at, :]
        att_ref[rows, :] = att
        att_t_ref[:, rows] = att.T
        dq, dk = dq_ref[at, :], dk_ref[:, at].T
        new = []
        for part, grad in enumerate(
            (dq * c - turned(dq) * s, dk * c - turned(dk) * s, dv_ref[:, at].T)
        ):
            low = grad.astype(BF)
            cols = slice(part * T, (part + 1) * T)
            out_ref[rows, cols] = low
            out_t_ref[cols, rows] = low.T
            new.append(total[part] + jnp.sum(low.astype(F32).reshape(16, 8, T), axis=0))
        return tuple(new)

    zero = jnp.zeros((8, T), F32)
    sums = lax.fori_loop(0, 16, store, (zero, zero, zero))
    for part in range(3):
        bias_ref[:, part * T : (part + 1) * T] = sums[part]


def attention_first(place, cosine, sine, mixed, attended_grad, before):
    return call(
        functools.partial(attention_kernel, (0, 3), False, len(before)),
        [SMEM] + [VMEM] * 2 + [ANY] * len(before) + [VMEM] * 2,
        [
            ((2, SEQ, 128), BF, 1),
            ((SEQ, 128), BF, 1),
            ((SEQ, 256), BF, 1),
            ((2, SEQ, 128), BF, 1),
            ((SEQ, 128), F32, 1),
            ((128, SEQ), F32, 1),
            ((128, SEQ), F32, 1),
            ((SEQ, 128), BF, 1),
            ((8, 128), jnp.int32),
        ],
        [place, cosine, sine, *before, mixed, attended_grad],
        [pltpu.VMEM((TQ, SEQ), F32), pltpu.VMEM((TQ, SEQ), BF)],
        vmem=13,
        flops=8 * SEQ * SEQ * 64 * 2,
        exps=SEQ * SEQ // 2,
        nbytes=3 * MIB,
    )


def attention_last(place, cosine, sine, state, before):
    return call(
        functools.partial(attention_kernel, (3, 4), True, len(before)),
        [SMEM] + [VMEM] * 2 + [ANY] * len(before) + [VMEM] * 8,
        [
            ((SEQ, T), BF, 1),
            ((SEQ, QKV), BF, 1),
            ((T, SEQ), BF, 1),
            ((QKV, SEQ), BF, 1),
            ((8, QKV), F32),
        ],
        [place, cosine, sine, *before] + list(state),
        [
            pltpu.VMEM((SEQ, 128), F32),
            pltpu.VMEM((128, SEQ), F32),
            pltpu.VMEM((128, SEQ), F32),
            pltpu.VMEM((SEQ, 128), BF),
            pltpu.VMEM((TQ, SEQ), F32),
            pltpu.VMEM((TQ, SEQ), BF),
        ],
        vmem=16,
        flops=6 * SEQ * SEQ * 64 * 2,
        exps=SEQ * SEQ // 2,
        nbytes=3 * MIB,
    )


def rotary_tables():
    lane = lax.broadcasted_iota(jnp.int32, (SEQ, 128), 1) % HEAD_DIM
    place = lax.broadcasted_iota(jnp.int32, (SEQ, 128), 0).astype(F32)
    freq = (lane % (ROTARY // 2)).astype(F32)
    angle = place * jnp.exp(freq * (-2.0 * math.log(10000.0) / ROTARY))
    turns = lane < ROTARY
    cosine = jnp.where(turns, jnp.cos(angle), 1.0)
    sine = jnp.where(turns, jnp.sin(angle), 0.0)
    return cosine, jnp.where(lane < ROTARY // 2, -sine, sine)


def body(
    tokens,
    ln_gain,
    ln_shift,
    qkv_weight,
    qkv_bias,
    dense_weight,
    dense_bias,
    fc1_weight,
    fc1_bias,
    fc2_weight,
    fc2_bias,
    cotangent,
):
    rep, shard = lax.axis_index("rep"), lax.axis_index("shard")
    xh, y = rep // 4, rep % 4
    z, xl, c = shard // 4, (shard // 2) % 2, shard % 2
    token_place = jnp.stack(
        [((z + dz) % 4) * 4 + (xl ^ dx) * 2 + (c ^ dc) for dz, dx, dc in SLOTS]
    ).astype(jnp.int32)
    row_place = jnp.stack(
        [((z + y + dy) % 4) * 4 + (xl ^ dx) * 2 + (c ^ dc) for dy, dx, dc in SLOTS]
    ).astype(jnp.int32)
    col_place = jnp.stack(
        [((z - y - dy) % 4) * 4 + (xl ^ dx) * 2 + (c ^ dc) for dy, dx, dc in SLOTS]
    ).astype(jnp.int32)
    part_place = jnp.stack(
        [((y + dy) % 4) * 2 + dx for dy in range(4) for dx in range(2)]
    ).astype(jnp.int32)
    me, core = shard.reshape(1).astype(jnp.int32), c.reshape(1).astype(jnp.int32)

    vectors = [v.reshape(-1, T) for v in (qkv_bias, ln_gain, ln_shift, dense_bias, fc2_bias)]
    vectors = jnp.concatenate(vectors + [jnp.zeros((T - 7, T), BF)])
    message = jnp.concatenate([tokens, cotangent, vectors], axis=1)
    near = gather_near(message)

    def columns_for(chip):
        qkv = [
            lax.dynamic_slice(qkv_weight, (0, part * D + chip * 2 * T), (T, 2 * T))
            for part in range(3)
        ]
        fc1 = lax.dynamic_slice(fc1_weight, (0, chip * 2 * FFL), (T, 2 * FFL))
        return jnp.concatenate(
            [
                jnp.concatenate(
                    [p[:, at * T : (at + 1) * T] for p in qkv]
                    + [fc1[:, at * FFL : (at + 1) * FFL]],
                    axis=1,
                )
                for at in range(2)
            ]
        )

    to_chip = ((z - y) % 4) * 2 + xl
    mine, other = columns_for(to_chip ^ c), columns_for(to_chip ^ c ^ 1)
    other = fetch(other, dc=1)
    rows = fetch_from(
        jnp.concatenate([mine, other]), lambda xh, y, z, xl, c: (xh, y, z + y, xl ^ c, c)
    )
    own_pair = message, gather_swap(message)
    far_vectors = fetch(vectors[:16], dz=2, dx=1)
    cosine, sine = rotary_tables()
    rows, near, own_pair, far_vectors, cosine, sine = together(
        rows, near, own_pair, far_vectors, cosine, sine
    )

    def columns_of(rows, core):
        return jnp.concatenate(
            [
                lax.dynamic_slice(rows, (n * 2 * T + core * T, 0), (T, COLS))
                for n in range(2)
            ]
        )

    mine = columns_of(rows, c)
    other = fetch(columns_of(rows, 1 - c), dc=1)
    here = jnp.where(c == 0, mine, jnp.concatenate([other[T:], other[:T]]))
    there = jnp.where(c == 0, jnp.concatenate([other[T:], other[:T]]), mine)
    own_rows = jnp.concatenate([here, there])
    further = gather_next(near)
    one, three = fetch(own_rows, dy=1), fetch(own_rows, dy=-1)
    one, three, further, near, far_vectors = together(one, three, further, near, far_vectors)
    near_pairs = near | {(0, 0): own_pair}
    far_vectors = jnp.concatenate([far_vectors, fetch(far_vectors, dc=1)])
    far = gather_far(further)
    first, second = fetch(one[: 2 * T], dy=1), fetch(three[2 * T :], dy=-1)
    *arrays, vecs, own_qkv_bias, done = near_inputs(
        both_cores(near_pairs) + both_cores(further),
        far_vectors,
        fc2_weight,
        dense_weight,
        token_place,
        me,
        [one, three],
    )
    far, first, second, done = together(far, first, second, done)
    weights = own_rows, one, three, first, second
    far = [
        (part, 10 * T + dc * T + n * (T // 2))
        for dc in range(2)
        for n, part in enumerate(far if dc == 0 else [gather_swap(f) for f in far])
    ]
    gain, out_bias = vecs[0:1], vecs[2:3]
    (
        normed,
        all_cot,
        _,
        attended_grad,
        weight,
        activated,
        pre_grad,
        act_t,
        pre_t,
        mixed,
        fc1_bias_part,
        out_bias_part,
    ) = forward_inputs(
        arrays,
        far,
        weights,
        vecs,
        fc1_bias.astype(F32).reshape(1, FFL),
        own_qkv_bias,
        fc2_weight,
        dense_weight,
        row_place,
        me,
    )

    early = column_grads(normed, pre_t, act_t, all_cot, row_place, part_place, core)
    *state, done = attention_first(token_place, cosine, sine, mixed, attended_grad, early)
    early_near = reduce_near(early, reduce_far(early), done[0, 0].astype(F32))
    attended, mixed_grad, attended_t, mixed_t, qkv_bias_part = attention_last(
        token_place, cosine, sine, state, early_near
    )
    early = add(early[0], fetch(early_near[0], dy=-1), fetch(early_near[1], dy=1)).astype(BF)
    early_other = fetch(early, dh=1)

    def the_terms(chips, sums, before):
        mine, other, *sums = terms(
            chips,
            attended,
            activated,
            dense_weight,
            fc2_weight,
            mixed_grad,
            pre_grad,
            weight,
            normed,
            vecs,
            sums,
            before,
        )
        return mine, fetch(other, dc=1), sums

    def own_terms(chips, mine, other, zero):
        return {
            chip: add(mine[n * T : (n + 1) * T], other[n * T : (n + 1) * T], zero).astype(BF)
            for n, chip in enumerate(chips)
        }

    mine0, other0, sums = the_terms(WAVES[0], [], [early])
    mine1, other1, sums = the_terms(WAVES[1], sums, [])
    q = own_terms(WAVES[0], mine0, other0, zero_of(sums[0]))
    far = scatter_far(q)
    mine2, other2, sums = the_terms(WAVES[2], sums, [q[2, 1]])
    far, other1, sums, early_other = together(far, other1, sums, early_other)

    def from_owners(rows):
        return [
            fetch_from(rows[dx], lambda xh, y, z, xl, c: (xh, y, z - y, xl ^ dx, c))
            for dx in range(2)
        ]

    early = add(early, early_other).astype(BF)
    early_own = jnp.concatenate([early[:, :T], fetch(early[:, T : 2 * T], dc=1)], axis=1)
    early_own = from_owners([early_own[:FFL], early_own[FFL:]])
    late = head_grads(
        normed,
        mixed_t,
        attended_t,
        all_cot,
        row_place,
        part_place,
        core,
        me,
        gain,
        sums,
        (qkv_bias_part, fc1_bias_part, out_bias_part),
        [],
    )
    late_far = reduce_far(late)
    early_own, late_far, other2, late = together(early_own, late_far, other2, late)

    q |= own_terms(WAVES[1], mine1, other1, 0.0)
    further = scatter_next(q, far, 0.0)
    late_near = reduce_near(late, late_far, 0.0)
    late_near = fetch(late_near[0], dy=-1), fetch(late_near[1], dy=1)
    further, late_near = together(further, late_near)

    q |= own_terms(WAVES[2], mine2, other2, 0.0)
    nearest = scatter_near(q, further, 0.0)
    early = jnp.concatenate(
        [
            jnp.concatenate([early_own[dx], early[dx * FFL : (dx + 1) * FFL, 2 * T :]], axis=1)
            for dx in range(2)
        ]
    )
    early_one, early_three = fetch(early, dy=1), fetch(early, dy=-1)
    late = add(late[0], *late_near).astype(BF)
    early_one, early_three, nearest, late = together(early_one, early_three, nearest, late)
    late_other = fetch(late, dh=1)

    early = (
        early,
        early_one,
        early_three,
        fetch(early_one[:FFL], dy=1),
        fetch(early_three[FFL:], dy=-1),
    )
    late = add(late, late_other).astype(BF)
    late_rows = jnp.concatenate([late[:FOR_OWNER], late[LATE : LATE + FOR_OWNER]])
    late_own = jnp.concatenate([late_rows[:, :T], fetch(late_rows[:, T:], dc=1)], axis=1)
    late_own = from_owners([late_own[:FOR_OWNER], late_own[FOR_OWNER:]])
    late = jnp.concatenate(
        [late_own[0], late[FOR_OWNER:LATE], late_own[1], late[LATE + FOR_OWNER :]]
    )
    late_one, late_three = fetch(late, dy=1), fetch(late, dy=-1)
    total = add(q[0, 0], *nearest)
    own = tokens.astype(F32)
    layer_out = (own + out_bias + total[:, D:]).astype(BF)
    center = own - jnp.mean(own, axis=-1, keepdims=True)
    inv_std = lax.rsqrt(jnp.mean(center * center, axis=-1, keepdims=True) + 1e-05)
    unit = center * inv_std
    scaled = total[:, :D] * gain
    input_grad = cotangent.astype(F32) + inv_std * (
        scaled
        - jnp.mean(scaled, axis=-1, keepdims=True)
        - unit * jnp.mean(scaled * unit, axis=-1, keepdims=True)
    )
    late = (
        late,
        late_one,
        late_three,
        fetch(late_one[:LATE], dy=1),
        fetch(late_three[LATE:], dy=-1),
    )
    fc1_total, fc2_total = place_columns(early, col_place, part_place)
    qkv_total, dense_total, of_owner, of_own = place_heads(late, col_place, part_place)
    out_bias_total = of_own[0, FFL : FFL + T]

    return (
        layer_out,
        input_grad,
        of_owner[0],
        of_owner[1],
        qkv_total,
        of_owner[2:5].reshape(QKV),
        dense_total,
        out_bias_total,
        fc1_total,
        of_own[0, :FFL],
        fc2_total,
        out_bias_total,
    )


def solution(mesh):
    return jax.shard_map(
        body,
        mesh=mesh,
        in_specs=(
            P(AXES, None),
            P("shard"),
            P("shard"),
            P("shard", None),
            P("shard"),
            P("shard", None),
            P("shard"),
            P("shard", None),
            P("shard"),
            P("shard", None),
            P("shard"),
            P(AXES, None),
        ),
        out_specs=(
            P(AXES, None),
            P(AXES, None),
            P("shard"),
            P("shard"),
            P("shard", None),
            P("shard"),
            P("shard", None),
            P("shard"),
            P("shard", None),
            P("shard"),
            P("shard", None),
            P("shard"),
        ),
        check_vma=False,
    )
```

```python
import functools
import math

import jax
import jax.numpy as jnp
from jax import lax
from jax.experimental import pallas as pl
from jax.experimental.pallas import tpu as pltpu
from jax.sharding import PartitionSpec as P

D = 2048
HEADS = 32
HEAD_DIM = 64
ROTARY = 32
FF = 8192
SEQ = 2048
T = 128
QKV = 384
FFL = 512
COLS = QKV + FFL
BF = jnp.bfloat16
F32 = jnp.float32
AXES = ("rep", "shard")
MIB = 1 << 20
LOG2E = math.log2(math.e)

PLACES = [
    (xh, y, z, xl, c)
    for xh in range(2)
    for y in range(4)
    for z in range(4)
    for xl in range(2)
    for c in range(2)
]


def flat(xh, y, z, xl, c):
    return (xh * 4 + y % 4) * 16 + (z % 4) * 4 + xl * 2 + c


def fetch_from(x, source):
    return lax.ppermute(x, AXES, [(flat(*source(*p)), flat(*p)) for p in PLACES])


def fetch(x, dz=0, dx=0, dc=0, dy=0, dh=0):
    return fetch_from(
        x, lambda xh, y, z, xl, c: (xh ^ dh, y + dy, z + dz, xl ^ dx, c ^ dc)
    )


def dot(a, b, ca=1, cb=0):
    return lax.dot_general(a, b, (((ca,), (cb,)), ((), ())), preferred_element_type=F32)


def add(*terms):
    total = terms[0].astype(F32)
    for term in terms[1:]:
        total = total + (term if isinstance(term, float) else term.astype(F32))
    return total


def zero_of(x):
    return x[0, 0].astype(F32) * 0.0


def together(*groups, also=()):
    leaves, tree = jax.tree.flatten(groups)
    others = jax.tree.leaves(also)
    n = len(leaves)
    leaves = pl.pallas_call(
        lambda *refs: None,
        in_specs=[pl.BlockSpec(memory_space=pl.ANY)] * (n + len(others)),
        out_specs=[pl.BlockSpec(memory_space=pl.ANY)] * n,
        out_shape=[jax.ShapeDtypeStruct(x.shape, x.dtype) for x in leaves],
        input_output_aliases={i: i for i in range(n)},
        compiler_params=pltpu.CompilerParams(vmem_limit_bytes=MIB),
    )(*leaves, *others)
    return jax.tree.unflatten(tree, leaves)


def gather_near(own):
    return {
        (0, 0): own,
        (1, 0): fetch(own, dz=1),
        (3, 0): fetch(own, dz=-1),
        (0, 1): fetch(own, dx=1),
    }


def gather_next(a):
    return {
        (1, 1): fetch(a[1, 0], dx=1),
        (3, 1): fetch(a[0, 1], dz=-1),
        (2, 0): fetch(a[1, 0], dz=1),
    }


def gather_far(a):
    return fetch(a[2, 0], dx=1)


def gather_swap(own):
    return fetch(own, dc=1)


def both_cores(a):
    pieces = []
    for (dz, dx), own in a.items():
        pair = own if isinstance(own, tuple) else (own, gather_swap(own))
        pieces += [(pair[dc], ((dz * 2 + dx) * 2 + dc) * T) for dc in range(2)]
    return pieces


SLOTS = [(dz, dx, dc) for dz in range(4) for dx in range(2) for dc in range(2)]
WAVES = [[(2, 1)], [(1, 1), (3, 1), (2, 0)], [(1, 0), (3, 0), (0, 1), (0, 0)]]


def scatter_far(q):
    half = T // 2
    return fetch(q[2, 1][:half], dz=-1), fetch(q[2, 1][half:], dz=1)


def scatter_next(q, far, zero):
    half = T // 2
    q11 = jnp.concatenate([add(q[1, 1][:half], far[0], zero).astype(BF), q[1, 1][half:]])
    q31 = jnp.concatenate([q[3, 1][:half], add(q[3, 1][half:], far[1], zero).astype(BF)])
    return fetch(q[2, 0], dz=-1), fetch(q31, dz=1), fetch(q11, dx=1)


def scatter_near(q, further, zero):
    q10 = add(q[1, 0], further[0], further[2], zero).astype(BF)
    q01 = add(q[0, 1], further[1], zero).astype(BF)
    return fetch(q10, dz=-1), fetch(q[3, 0], dz=1), fetch(q01, dx=1)


def reduce_far(g):
    half = g[0].shape[0] // 2
    return fetch(g[2][:half], dy=-1), fetch(g[2][half:], dy=1)


def reduce_near(g, far, zero):
    half = g[0].shape[0] // 2
    g1 = jnp.concatenate([add(g[1][:half], far[0], zero).astype(BF), g[1][half:]])
    g3 = jnp.concatenate([g[3][:half], add(g[3][half:], far[1], zero).astype(BF)])
    return g1, g3


def of_rep(refs, dy, dx, n):
    own, one, three, first, second = refs
    if dy == 2:
        return (second if dx else first), 0
    return (own, one, None, three)[dy], dx * n


VMEM = pl.BlockSpec(memory_space=pltpu.VMEM)
SMEM = pl.BlockSpec(memory_space=pltpu.SMEM)
HBM = pl.BlockSpec(memory_space=pltpu.HBM)
ANY = pl.BlockSpec(memory_space=pl.ANY)


def lanes(at, n):
    return pl.ds(pl.multiple_of(at * n, n), n)


def call(kernel, ins, outs, args, scratch=(), vmem=6, flops=0, nbytes=0, exps=0, aliases={}):
    return pl.pallas_call(
        kernel,
        in_specs=ins,
        out_specs=[VMEM] * len(outs),
        out_shape=[
            pltpu.VMEM(o[0], o[1]) if len(o) > 2 else jax.ShapeDtypeStruct(*o) for o in outs
        ],
        scratch_shapes=list(scratch),
        input_output_aliases=aliases,
        compiler_params=pltpu.CompilerParams(vmem_limit_bytes=vmem * MIB),
        cost_estimate=pl.CostEstimate(
            flops=flops // 16, transcendentals=exps // 16, bytes_accessed=nbytes // 16
        ),
    )(*args)


ROOT = math.sqrt(2.0 / math.pi)


def start_copies(pieces, place, sems):
    copies = [
        pltpu.make_async_copy(src, dst, sems.at[place + i]) for i, (src, dst) in enumerate(pieces)
    ]
    for copy in copies:
        copy.start()
    return copies


def norm_rows(normed_ref, gain, shift, first, count):
    def strip(i, _):
        at = lanes(i, 64)
        x = normed_ref[at, :].astype(F32)
        x = x - jnp.sum(x, axis=1, keepdims=True) * (1.0 / D)
        scale = lax.rsqrt(jnp.sum(x * x, axis=1, keepdims=True) * (1.0 / D) + 1e-05)
        normed_ref[at, :] = (x * scale * gain + shift).astype(BF)
        return 0

    lax.fori_loop(first // 64, (first + count) // 64, strip, 0)


def message_moves(refs, pieces, normed_ref, cot_ref):
    moves = []
    for (array, at), ref in zip(pieces, refs, strict=True):
        to = pl.ds(at, array.shape[0])
        moves.append((ref.at[:, pl.ds(0, D)], normed_ref.at[to]))
        moves.append((ref.at[:, pl.ds(D, D)], cot_ref.at[to]))
    return moves


def near_inputs(pieces, far_vectors, fc2, dense, token_place, me, before):
    n = len(pieces)
    chips = sorted({at // 256 for _, at in pieces})

    def kernel(t_ref, me_ref, *refs):
        refs = refs[len(before) :]
        (
            far_ref,
            fc2_ref,
            dense_ref,
            normed_ref,
            cot_ref,
            grad_ref,
            att_ref,
            vec_ref,
            own_ref,
            done_ref,
            small_ref,
            flat_ref,
            sems,
        ) = refs[n:]
        done_ref[...] = jnp.zeros_like(done_ref)
        moves = [
            (ref.at[pl.ds(0, 16), pl.ds(2 * D, T)], small_ref.at[pl.ds(at // T * 16, 16)])
            for (_, at), ref in zip(pieces, refs[:n], strict=True)
        ]
        for dc in range(2):
            to = small_ref.at[pl.ds((5 * 2 + dc) * 16, 16)]
            moves.append((far_ref.at[pl.ds(dc * 16, 16)], to))
        small_copies = start_copies(moves, 0, sems)
        copies = start_copies(
            message_moves(refs[:n], pieces, normed_ref, cot_ref), n + 2, sems
        )
        for copy in small_copies:
            copy.wait()
        for i in range(16):
            at = t_ref[i]
            small = small_ref[i * 16 : (i + 1) * 16, :].astype(F32)
            for part in range(3):
                flat_ref[0:1, lanes(at * 3 + part, T)] = small[part : part + 1]
            vec_ref[0:1, lanes(at, T)] = small[3:4]
            vec_ref[1:2, lanes(at, T)] = small[4:5]
            vec_ref[2:3, lanes(at, T)] = small[5:6] + small[6:7]
        for part in range(3):
            own_ref[0:1, part * T : (part + 1) * T] = flat_ref[
                0:1, lanes(part * 16 + me_ref[0], T)
            ]
        gain, shift = vec_ref[0:1, :], vec_ref[1:2, :]
        for chip in chips:
            for (_, at), token_copy, cot_copy in zip(pieces, copies[0::2], copies[1::2]):
                if at // 256 == chip:
                    token_copy.wait()
                    cot_copy.wait()
            norm_rows(normed_ref, gain, shift, chip * 256, 256)

        def tile(i, _):
            at = lanes(i, TM)
            x = cot_ref[at, :]
            grad_ref[at, :] = dot(x, fc2_ref[...], 1, 1).astype(BF)
            att_ref[at, :] = dot(x, dense_ref[...], 1, 1).astype(BF)
            return 0

        lax.fori_loop(0, SEQ // TM, tile, 0)

    return call(
        kernel,
        [SMEM] * 2 + [ANY] * len(before) + [HBM] * (n + 1) + [VMEM] * 2,
        [
            ((SEQ, D), BF, 1),
            ((SEQ, D), BF, 1),
            ((SEQ, FFL), BF, 1),
            ((SEQ, T), BF, 1),
            ((8, D), F32, 1),
            ((1, QKV), F32, 1),
            ((8, T), F32),
        ],
        [token_place, me, *before] + [p for p, _ in pieces] + [far_vectors, fc2, dense],
        [
            pltpu.VMEM((256, T), BF),
            pltpu.VMEM((1, 3 * D), F32),
            pltpu.SemaphoreType.DMA((3 * n + 2,)),
        ],
        flops=2 * SEQ * D * (FFL + T),
        nbytes=20 * MIB,
    )


def forward_inputs(arrays, pieces, weights, vecs, bias, own_bias, fc2, dense, row_place, me):
    n = len(pieces)
    chip = pieces[0][1] // 256

    def kernel(r_ref, me_ref, *refs):
        tok = refs[4 : 4 + n]
        w_refs = refs[4 + n : 8 + n]
        (
            vec_ref,
            bias_ref,
            own_ref,
            fc2_ref,
            dense_ref,
            normed_ref,
            cot_ref,
            grad_ref,
            att_ref,
            w_ref,
            act_ref,
            pre_ref,
            act_t_ref,
            pre_t_ref,
            mixed_ref,
            fc1b_ref,
            outb_ref,
            sems,
        ) = refs[8 + n :]
        copies = start_copies(message_moves(tok, pieces, normed_ref, cot_ref), 0, sems)
        moves = []
        for i, (dy, dx, dc) in enumerate(SLOTS):
            rows = pl.ds((dx * 2 + dc) * T, T)
            moves.append((w_refs[dy].at[rows], w_ref.at[lanes(r_ref[i], T)]))
        w_copies = start_copies(moves, 2 * n, sems)
        for copy in copies:
            copy.wait()
        norm_rows(normed_ref, vec_ref[0:1, :], vec_ref[1:2, :], chip * 256, 256)
        rows = slice(chip * 256, (chip + 1) * 256)
        x = cot_ref[rows, :]
        grad_ref[rows, :] = dot(x, fc2_ref[...], 1, 1).astype(BF)
        att_ref[rows, :] = dot(x, dense_ref[...], 1, 1).astype(BF)
        for copy in w_copies:
            copy.wait()

        def product(i):
            at = lanes(i, TM)
            x = normed_ref[at, :]
            mixed_ref[at, :] = dot(x, w_ref[:, :QKV]) + own_ref[...]
            return dot(x, w_ref[:, QKV:]) + bias_ref[...]

        def gelu(i, pre, total):
            at = lanes(i, TM)
            squared = pre * pre
            tanh = jnp.tanh(ROOT * pre * (1.0 + 0.044715 * squared))
            act = (0.5 * pre * (1.0 + tanh)).astype(BF)
            act_ref[at, :] = act
            act_t_ref[:, at] = act.T
            slope = 0.5 * (1.0 + tanh) + 0.5 * pre * (1.0 - tanh * tanh) * ROOT * (
                1.0 + 3 * 0.044715 * squared
            )
            back = (grad_ref[at, :].astype(F32) * slope).astype(BF)
            pre_ref[at, :] = back
            pre_t_ref[:, at] = back.T
            return total + jnp.sum(back.astype(F32).reshape(TM // 8, 8, FFL), axis=0)

        def tile(i, carry):
            pre, total = carry
            return product(i), gelu(i - 1, pre, total)

        pre, total = lax.fori_loop(1, SEQ // TM, tile, (product(0), jnp.zeros((8, FFL), F32)))
        fc1b_ref[...] = gelu(SEQ // TM - 1, pre, total)

        def sums(i, total):
            own = cot_ref[lanes(i, 256), lanes(me_ref[0], T)].astype(F32)
            return total + jnp.sum(own.reshape(32, 8, T), axis=0)

        outb_ref[...] = lax.fori_loop(0, 8, sums, jnp.zeros((8, T), F32))

    return call(
        kernel,
        [SMEM] * 2 + [VMEM] * 4 + [HBM] * (n + 4) + [VMEM] * 5,
        [
            ((SEQ, D), BF, 1),
            ((SEQ, D), BF, 1),
            ((SEQ, FFL), BF, 1),
            ((SEQ, T), BF, 1),
            ((D, COLS), BF, 1),
            ((SEQ, FFL), BF, 1),
            ((SEQ, FFL), BF, 1),
            ((FFL, SEQ), BF, 1),
            ((FFL, SEQ), BF, 1),
            ((SEQ, QKV), F32, 1),
            ((8, FFL), F32),
            ((8, T), F32),
        ],
        [row_place, me]
        + list(arrays)
        + [p for p, _ in pieces]
        + list(weights)
        + [vecs, bias, own_bias, fc2, dense],
        [pltpu.SemaphoreType.DMA((2 * n + 16,))],
        aliases={2: 0, 3: 1, 4: 2, 5: 3},
        flops=2 * SEQ * D * COLS,
        nbytes=8 * MIB,
        exps=SEQ * FFL,
    )


def column_grads(normed, pre_t, act_t, cot, row_place, part_place, core):
    def kernel(r_ref, p_ref, core_ref, n_ref, g_ref, a_ref, c_ref, *outs):
        for dy in (2, 1, 3, 0):
            out = outs[dy]
            for dh in range(2):
                at = slice(dh * FFL, (dh + 1) * FFL)
                chip = r_ref[(dy * 2 + dh) * 2] // 2
                cols = dot(g_ref[...], n_ref[:, lanes(chip, 256)]).astype(BF)
                out[at, lanes(core_ref[0], T)] = cols[:, :T]
                out[at, lanes(1 - core_ref[0], T)] = cols[:, T:]
                part = c_ref[:, lanes(p_ref[dy * 2 + dh], 256)]
                out[at, 256:512] = dot(a_ref[...], part).astype(BF)

    return call(
        kernel,
        [SMEM] * 3 + [VMEM] * 4,
        [((1024, 512), BF)] * 4,
        [row_place, part_place, core, normed, pre_t, act_t, cot],
        flops=4 * SEQ * D * FFL,
        nbytes=4 * MIB,
    )


FOR_OWNER = QKV + 16
LATE = FOR_OWNER + T + 16


def head_grads(
    normed,
    mixed_t,
    attended_t,
    cot,
    places,
    part_place,
    core,
    me,
    gain,
    sums,
    bias_parts,
    before,
):
    def kernel(r_ref, p_ref, core_ref, me_ref, n_ref, m_ref, a_ref, c_ref, *refs):
        refs = refs[len(before) :]
        gain_ref, gains_ref, shifts_ref, qkvb_ref, fc1b_ref, outb_ref = refs[:6]
        outs, owners_ref, own_ref = refs[6:10], refs[10], refs[11]
        owners_ref[...] = jnp.zeros_like(owners_ref)
        owners_ref[0:1, :] = jnp.sum(gains_ref[...], axis=0, keepdims=True) / gain_ref[...]
        owners_ref[1:2, :] = jnp.sum(shifts_ref[...], axis=0, keepdims=True)
        qkvb = jnp.sum(qkvb_ref[...], axis=0, keepdims=True)
        for part in range(3):
            at = part * 16 + me_ref[0]
            third = at % 3
            row = lax.broadcasted_iota(jnp.int32, (8, T), 0)
            value = jnp.where(row == 2 + third, qkvb[:, part * T : (part + 1) * T], 0.0)
            owners_ref[0:8, lanes(at // 3, T)] += value
        own_ref[...] = jnp.zeros_like(own_ref)
        own_ref[0:1, :FFL] = jnp.sum(fc1b_ref[...], axis=0, keepdims=True)
        own_ref[0:1, FFL : FFL + T] = jnp.sum(outb_ref[...], axis=0, keepdims=True)
        for dy in (2, 1, 3, 0):
            out = outs[dy]
            for dx in range(2):
                base = dx * LATE
                chip = r_ref[(dy * 2 + dx) * 2] // 2
                cols = dot(m_ref[...], n_ref[:, lanes(chip, 256)]).astype(BF)
                extra = owners_ref[:, lanes(chip, 256)].astype(BF)
                mine, other = lanes(core_ref[0], T), lanes(1 - core_ref[0], T)
                out[base : base + QKV, mine] = cols[:, :T]
                out[base : base + QKV, other] = cols[:, T:]
                out[base + QKV : base + FOR_OWNER, mine] = extra[:, :T]
                out[base + QKV : base + FOR_OWNER, other] = extra[:, T:]
                base += FOR_OWNER
                part = p_ref[dy * 2 + dx]
                out[base : base + T, :] = dot(a_ref[...], c_ref[:, lanes(part, 256)]).astype(BF)
                out[base + T : base + T + 16, 0:T] = own_ref[:, lanes(part, T)].astype(BF)
                out[base + T : base + T + 16, T:] = jnp.zeros((16, T), BF)

    return call(
        kernel,
        [SMEM] * 4 + [VMEM] * 4 + [ANY] * len(before) + [VMEM] * 6,
        [((2 * LATE, 256), BF)] * 4,
        [
            places,
            part_place,
            core,
            me,
            normed,
            mixed_t,
            attended_t,
            cot,
            *before,
            gain,
            *sums,
            *bias_parts,
        ],
        [pltpu.VMEM((16, D), F32), pltpu.VMEM((16, 1024), F32)],
        flops=2 * SEQ * D * (QKV + T),
        nbytes=2 * MIB,
    )


def place_columns(pieces, col_place, part_place):
    def kernel(c_ref, p_ref, *refs):
        fc1_ref, fc2_ref = refs[5:]
        for i, (dy, dh, dc) in enumerate(SLOTS):
            ref, at = of_rep(refs[:5], dy, dh, FFL)
            part = ref[at : at + FFL, dc * T : (dc + 1) * T]
            fc1_ref[:, lanes(c_ref[i], FFL)] = part.astype(F32).T
            if dc == 0:
                to = lanes(p_ref[dy * 2 + dh], 256)
                fc2_ref[:, to] = ref[at : at + FFL, 256:512].astype(F32)

    return call(
        kernel,
        [SMEM] * 2 + [VMEM] * 5,
        [((T, FF), F32), ((FFL, D), F32)],
        [col_place, part_place] + list(pieces),
        vmem=20,
        nbytes=12 * MIB,
    )


def place_heads(pieces, col_place, part_place):
    def kernel(c_ref, p_ref, *refs):
        qkv_ref, dense_ref, owner_ref, own_ref = refs[5:]
        total = jnp.zeros((16, T), F32)
        for i, (dy, dx, dc) in enumerate(SLOTS):
            ref, at = of_rep(refs[:5], dy, dx, LATE)
            cols = slice(dc * T, (dc + 1) * T)
            for part in range(3):
                block = ref[at + part * T : at + (part + 1) * T, cols].astype(F32)
                qkv_ref[:, lanes(c_ref[i] + part * 16, T)] = block.T
            total += ref[at + QKV : at + FOR_OWNER, cols].astype(F32)
            if dc == 0:
                part = p_ref[dy * 2 + dx]
                rows = slice(at + FOR_OWNER, at + FOR_OWNER + T)
                dense_ref[:, lanes(part, 256)] = ref[rows, :].astype(F32)
                rows = slice(at + FOR_OWNER + T, at + LATE)
                own_ref[:, lanes(part, T)] = ref[rows, 0:T].astype(F32)
        owner_ref[...] = total

    return call(
        kernel,
        [SMEM] * 2 + [VMEM] * 5,
        [((T, 3 * D), F32), ((T, D), F32), ((16, T), F32), ((16, 1024), F32)],
        [col_place, part_place] + list(pieces),
        vmem=14,
        nbytes=6 * MIB,
    )


def terms(
    chips, attended, activated, dense, fc2, mixed_grad, pre_grad, weight, normed, vecs, sums, before
):
    n = len(chips)

    def kernel(
        *refs
    ):
        refs = refs[len(before) :]
        a_ref, f_ref, d_ref, v_ref, m_ref, p_ref, w_ref, n_ref, vec_ref = refs[:9]
        mine_ref, other_ref, gain_ref, total_ref = refs[-4:]
        shift = vec_ref[1:2, :]
        if sums:
            gain_ref[...] = refs[9][...]
            total_ref[...] = refs[10][...]
        else:
            gain_ref[...] = jnp.zeros_like(gain_ref)
            total_ref[...] = jnp.zeros_like(total_ref)

        def rows(ref, cols=slice(None)):
            return jnp.concatenate(
                [ref[(dz * 2 + dx) * 256 : (dz * 2 + dx + 1) * 256, cols] for dz, dx in chips]
            )

        left, right = jnp.concatenate([rows(m_ref), rows(p_ref)], axis=1), jnp.concatenate(
            [rows(f_ref), rows(a_ref)], axis=1
        )

        def store(total, to):
            for i in range(n):
                at = slice(i * T, (i + 1) * T)
                mine_ref[at, to] = total[i * 256 : i * 256 + T].astype(BF)
                other_ref[at, to] = total[i * 256 + T : (i + 1) * 256].astype(BF)

        for col in range(4):
            to = slice(col * 512, (col + 1) * 512)
            total = dot(left, w_ref[to, :], 1, 1)
            store(total, to)
            unit = rows(n_ref, to).astype(F32) - shift[:, to]
            gain_ref[:, to] += jnp.sum((total * unit).reshape(n * 32, 8, 512), axis=0)
            total_ref[:, to] += jnp.sum(total.reshape(n * 32, 8, 512), axis=0)
            weights = jnp.concatenate([v_ref[:, to], d_ref[:, to]])
            store(dot(right, weights), slice(D + col * 512, D + (col + 1) * 512))

    return call(
        kernel,
        [ANY] * len(before) + [VMEM] * (9 + len(sums)),
        [((n * T, 2 * D), BF)] * 2 + [((8, D), F32)] * 2,
        [*before, attended, activated, dense, fc2, mixed_grad, pre_grad, weight, normed, vecs, *sums],
        flops=2 * n * 2 * T * (COLS + T + FFL) * D,
        nbytes=8 * MIB,
    )


TM = 512
TQ = 512
TK = 512


def attention_kernel(blocks, last, n_before, place, cos_ref, sin_ref, *refs):
    refs = refs[n_before:]
    if last:
        first_refs, refs = refs[:8], refs[8:]
        att_ref, out_ref, att_t_ref, out_t_ref, bias_ref = refs[:5]
        q_ref, k_ref, v_ref, do_ref = first_refs[:4]
        dq_ref, dk_ref, dv_ref, o_ref, s_ref, e_ref = refs[5:]
    else:
        mixed_ref, grad_ref, *refs = refs
        refs, done_ref = refs[:8] + refs[9:], refs[8]
        done_ref[...] = jnp.zeros_like(done_ref)
        q_ref, k_ref, v_ref, do_ref, dq_ref, dk_ref, dv_ref, o_ref, s_ref, e_ref = refs
    lane = lax.broadcasted_iota(jnp.int32, (T, 128), 1)
    low_head = lane < HEAD_DIM
    first = (lane % HEAD_DIM) < ROTARY // 2

    def turned(x):
        return jnp.where(
            first, pltpu.roll(x, 128 - ROTARY // 2, 1), pltpu.roll(x, ROTARY // 2, 1)
        )

    def load(slot, _):
        rows = pl.ds(pl.multiple_of(slot * T, T), T)
        at = pl.ds(pl.multiple_of(place[slot] * T, T), T)
        c, s = cos_ref[at, :], sin_ref[at, :]
        query = mixed_ref[rows, 0:128]
        key = mixed_ref[rows, 128:256]
        query = (query * c + turned(query) * s).astype(BF).astype(F32) * (HEAD_DIM**-0.5)
        q_ref[0, at, :] = jnp.where(low_head, query, 0.0).astype(BF)
        q_ref[1, at, :] = jnp.where(low_head, 0.0, query).astype(BF)
        k_ref[at, :] = (key * c + turned(key) * s).astype(BF)
        v_ref[at, 0:128] = mixed_ref[rows, 256:384].astype(BF)
        v_ref[at, 128:256] = jnp.ones((T, 128), BF)
        grad = grad_ref[rows, :].astype(F32)
        do_ref[0, at, :] = jnp.where(low_head, grad, 0.0).astype(BF)
        do_ref[1, at, :] = jnp.where(low_head, 0.0, grad).astype(BF)
        dk_ref[:, at] = jnp.zeros((128, T), F32)
        dv_ref[:, at] = jnp.zeros((128, T), F32)
        return 0

    if last:
        for to, at in ((dq_ref, 4), (dk_ref, 5), (dv_ref, 6), (o_ref, 7)):
            to[...] = first_refs[at][...]
    else:
        lax.fori_loop(0, 16, load, 0)

    lane_q = lax.broadcasted_iota(jnp.int32, (TQ, 128), 1)
    low_q = lane_q < HEAD_DIM

    def head(h, i, rows):
        query = q_ref[h, rows, :]

        def scores(j, top, masked):
            at = lanes(j, TK)
            s = dot(query, k_ref[at, :], 1, 1)
            if masked:
                row = lax.broadcasted_iota(jnp.int32, (TQ, TK), 0)
                col = lax.broadcasted_iota(jnp.int32, (TQ, TK), 1)
                s = jnp.where(row >= col, s, -1e30)
            s_ref[:, at] = s
            for n in range(TK // 128):
                top = jnp.maximum(top, s[:, n * 128 : (n + 1) * 128])
            return top

        top = jnp.full((TQ, 128), -1e30, F32)
        top = lax.fori_loop(0, i, lambda j, t: scores(j, t, False), top)
        top = jnp.max(scores(i, top, True), axis=1, keepdims=True)

        def weigh(j, total):
            at = lanes(j, TK)
            e = jnp.exp2((s_ref[:, at] - top) * LOG2E).astype(BF)
            e_ref[:, at] = e
            return total + dot(e, v_ref[at, :])

        total = lax.fori_loop(0, i + 1, weigh, jnp.zeros((TQ, 256), F32))
        inverse = 1.0 / total[:, 128:]
        o = total[:, :128] * inverse
        grad = do_ref[h, rows, :].astype(F32) * inverse
        delta = jnp.sum(grad * o, axis=1, keepdims=True)
        grad = grad.astype(BF)
        query_t, grad_t = query.T, grad.T

        def back(j, total):
            at = lanes(j, TK)
            e = e_ref[:, at]
            dp = dot(grad, v_ref[at, 0:128], 1, 1)
            ds = (e.astype(F32) * (dp - delta)).astype(BF)
            dk_ref[:, at] += dot(query_t, ds)
            dv_ref[:, at] += dot(grad_t, e)
            return total + dot(ds, k_ref[at, :])

        return o, lax.fori_loop(0, i + 1, back, jnp.zeros((TQ, 128), F32))

    def block(i, _):
        rows = lanes(i, TQ)
        o_low, dq_low = head(0, i, rows)
        o_high, dq_high = head(1, i, rows)
        o_ref[rows, :] = jnp.where(low_q, o_low, o_high).astype(BF)
        dq_ref[rows, :] = jnp.where(low_q, dq_low, dq_high) * (HEAD_DIM**-0.5)
        return 0

    lax.fori_loop(blocks[0], blocks[1], block, 0)
    if not last:
        return

    def store(slot, total):
        rows = pl.ds(pl.multiple_of(slot * T, T), T)
        at = pl.ds(pl.multiple_of(place[slot] * T, T), T)
        c, s = cos_ref[at, :], sin_ref[at, :]
        att = o_ref[at, :]
        att_ref[rows, :] = att
        att_t_ref[:, rows] = att.T
        dq, dk = dq_ref[at, :], dk_ref[:, at].T
        new = []
        for part, grad in enumerate(
            (dq * c - turned(dq) * s, dk * c - turned(dk) * s, dv_ref[:, at].T)
        ):
            low = grad.astype(BF)
            cols = slice(part * T, (part + 1) * T)
            out_ref[rows, cols] = low
            out_t_ref[cols, rows] = low.T
            new.append(total[part] + jnp.sum(low.astype(F32).reshape(16, 8, T), axis=0))
        return tuple(new)

    zero = jnp.zeros((8, T), F32)
    sums = lax.fori_loop(0, 16, store, (zero, zero, zero))
    for part in range(3):
        bias_ref[:, part * T : (part + 1) * T] = sums[part]


def attention_first(place, cosine, sine, mixed, attended_grad, before):
    return call(
        functools.partial(attention_kernel, (0, 3), False, len(before)),
        [SMEM] + [VMEM] * 2 + [ANY] * len(before) + [VMEM] * 2,
        [
            ((2, SEQ, 128), BF, 1),
            ((SEQ, 128), BF, 1),
            ((SEQ, 256), BF, 1),
            ((2, SEQ, 128), BF, 1),
            ((SEQ, 128), F32, 1),
            ((128, SEQ), F32, 1),
            ((128, SEQ), F32, 1),
            ((SEQ, 128), BF, 1),
            ((8, 128), jnp.int32),
        ],
        [place, cosine, sine, *before, mixed, attended_grad],
        [pltpu.VMEM((TQ, SEQ), F32), pltpu.VMEM((TQ, SEQ), BF)],
        vmem=13,
        flops=8 * SEQ * SEQ * 64 * 2,
        exps=SEQ * SEQ // 2,
        nbytes=3 * MIB,
    )


def attention_last(place, cosine, sine, state, before):
    return call(
        functools.partial(attention_kernel, (3, 4), True, len(before)),
        [SMEM] + [VMEM] * 2 + [ANY] * len(before) + [VMEM] * 8,
        [
            ((SEQ, T), BF, 1),
            ((SEQ, QKV), BF, 1),
            ((T, SEQ), BF, 1),
            ((QKV, SEQ), BF, 1),
            ((8, QKV), F32),
        ],
        [place, cosine, sine, *before] + list(state),
        [
            pltpu.VMEM((SEQ, 128), F32),
            pltpu.VMEM((128, SEQ), F32),
            pltpu.VMEM((128, SEQ), F32),
            pltpu.VMEM((SEQ, 128), BF),
            pltpu.VMEM((TQ, SEQ), F32),
            pltpu.VMEM((TQ, SEQ), BF),
        ],
        vmem=16,
        flops=6 * SEQ * SEQ * 64 * 2,
        exps=SEQ * SEQ // 2,
        nbytes=3 * MIB,
    )


def rotary_tables():
    lane = lax.broadcasted_iota(jnp.int32, (SEQ, 128), 1) % HEAD_DIM
    place = lax.broadcasted_iota(jnp.int32, (SEQ, 128), 0).astype(F32)
    freq = (lane % (ROTARY // 2)).astype(F32)
    angle = place * jnp.exp(freq * (-2.0 * math.log(10000.0) / ROTARY))
    turns = lane < ROTARY
    cosine = jnp.where(turns, jnp.cos(angle), 1.0)
    sine = jnp.where(turns, jnp.sin(angle), 0.0)
    return cosine, jnp.where(lane < ROTARY // 2, -sine, sine)


def body(
    tokens,
    ln_gain,
    ln_shift,
    qkv_weight,
    qkv_bias,
    dense_weight,
    dense_bias,
    fc1_weight,
    fc1_bias,
    fc2_weight,
    fc2_bias,
    cotangent,
):
    rep, shard = lax.axis_index("rep"), lax.axis_index("shard")
    xh, y = rep // 4, rep % 4
    z, xl, c = shard // 4, (shard // 2) % 2, shard % 2
    token_place = jnp.stack(
        [((z + dz) % 4) * 4 + (xl ^ dx) * 2 + (c ^ dc) for dz, dx, dc in SLOTS]
    ).astype(jnp.int32)
    row_place = jnp.stack(
        [((z + y + dy) % 4) * 4 + (xl ^ dx) * 2 + (c ^ dc) for dy, dx, dc in SLOTS]
    ).astype(jnp.int32)
    col_place = jnp.stack(
        [((z - y - dy) % 4) * 4 + (xl ^ dx) * 2 + (c ^ dc) for dy, dx, dc in SLOTS]
    ).astype(jnp.int32)
    part_place = jnp.stack(
        [((y + dy) % 4) * 2 + dx for dy in range(4) for dx in range(2)]
    ).astype(jnp.int32)
    me, core = shard.reshape(1).astype(jnp.int32), c.reshape(1).astype(jnp.int32)

    vectors = [v.reshape(-1, T) for v in (qkv_bias, ln_gain, ln_shift, dense_bias, fc2_bias)]
    vectors = jnp.concatenate(vectors + [jnp.zeros((T - 7, T), BF)])
    message = jnp.concatenate([tokens, cotangent, vectors], axis=1)
    near = gather_near(message)

    def columns_for(chip):
        qkv = [
            lax.dynamic_slice(qkv_weight, (0, part * D + chip * 2 * T), (T, 2 * T))
            for part in range(3)
        ]
        fc1 = lax.dynamic_slice(fc1_weight, (0, chip * 2 * FFL), (T, 2 * FFL))
        return jnp.concatenate(
            [
                jnp.concatenate(
                    [p[:, at * T : (at + 1) * T] for p in qkv]
                    + [fc1[:, at * FFL : (at + 1) * FFL]],
                    axis=1,
                )
                for at in range(2)
            ]
        )

    to_chip = ((z - y) % 4) * 2 + xl
    mine, other = columns_for(to_chip ^ c), columns_for(to_chip ^ c ^ 1)
    other = fetch(other, dc=1)
    rows = fetch_from(
        jnp.concatenate([mine, other]), lambda xh, y, z, xl, c: (xh, y, z + y, xl ^ c, c)
    )
    own_pair = message, gather_swap(message)
    cosine, sine = rotary_tables()
    rows, near[1, 0], near[0, 1] = together(
        rows, near[1, 0], near[0, 1], also=(near[3, 0], own_pair, cosine, sine)
    )

    def columns_of(rows, core):
        return jnp.concatenate(
            [
                lax.dynamic_slice(rows, (n * 2 * T + core * T, 0), (T, COLS))
                for n in range(2)
            ]
        )

    mine = columns_of(rows, c)
    other = fetch(columns_of(rows, 1 - c), dc=1)
    here = jnp.where(c == 0, mine, jnp.concatenate([other[T:], other[:T]]))
    there = jnp.where(c == 0, jnp.concatenate([other[T:], other[:T]]), mine)
    own_rows = jnp.concatenate([here, there])
    further = gather_next(near)
    one, three = fetch(own_rows, dy=1), fetch(own_rows, dy=-1)
    one, three, further, near, far_vectors = together(one, three, further, near, vectors[:16])
    far_vectors = fetch(far_vectors, dz=2, dx=1)
    near_pairs = near | {(0, 0): own_pair}
    far_vectors = jnp.concatenate([far_vectors, fetch(far_vectors, dc=1)])
    far = gather_far(further)
    two = fetch(one, dy=1)
    *arrays, vecs, own_qkv_bias, done = near_inputs(
        both_cores(near_pairs) + both_cores(further),
        far_vectors,
        fc2_weight,
        dense_weight,
        token_place,
        me,
        [one, three],
    )
    (far,) = together(far, also=(two, done))
    weights = own_rows, one, two, three
    far = [(far, 10 * T), (gather_swap(far), 11 * T)]
    gain, out_bias = vecs[0:1], vecs[2:3]
    (
        normed,
        all_cot,
        _,
        attended_grad,
        weight,
        activated,
        pre_grad,
        act_t,
        pre_t,
        mixed,
        fc1_bias_part,
        out_bias_part,
    ) = forward_inputs(
        arrays,
        far,
        weights,
        vecs,
        fc1_bias.astype(F32).reshape(1, FFL),
        own_qkv_bias,
        fc2_weight,
        dense_weight,
        row_place,
        me,
    )

    early = column_grads(normed, pre_t, act_t, all_cot, row_place, part_place, core)
    *state, done = attention_first(token_place, cosine, sine, mixed, attended_grad, early)
    early_near = reduce_near(early, reduce_far(early), done[0, 0].astype(F32))
    attended, mixed_grad, attended_t, mixed_t, qkv_bias_part = attention_last(
        token_place, cosine, sine, state, early_near
    )
    early = add(early[0], fetch(early_near[0], dy=-1), fetch(early_near[1], dy=1)).astype(BF)
    early_other = fetch(early, dh=1)

    def the_terms(chips, sums, before):
        mine, other, *sums = terms(
            chips,
            attended,
            activated,
            dense_weight,
            fc2_weight,
            mixed_grad,
            pre_grad,
            weight,
            normed,
            vecs,
            sums,
            before,
        )
        return mine, fetch(other, dc=1), sums

    def own_terms(chips, mine, other, zero):
        return {
            chip: add(mine[n * T : (n + 1) * T], other[n * T : (n + 1) * T], zero).astype(BF)
            for n, chip in enumerate(chips)
        }

    mine0, other0, sums = the_terms(WAVES[0], [], [early])
    mine1, other1, sums = the_terms(WAVES[1], sums, [])
    q = own_terms(WAVES[0], mine0, other0, zero_of(sums[0]))
    far = scatter_far(q)
    mine2, other2, sums = the_terms(WAVES[2], sums, [q[2, 1]])
    early_other, sums = together(early_other, sums, also=(far, other1))

    def from_owners(rows):
        return [
            fetch_from(rows[dx], lambda xh, y, z, xl, c: (xh, y, z - y, xl ^ dx, c))
            for dx in range(2)
        ]

    early = add(early, early_other).astype(BF)
    early_own = jnp.concatenate([early[:, :T], fetch(early[:, T : 2 * T], dc=1)], axis=1)
    early_own = from_owners([early_own[:FFL], early_own[FFL:]])
    late = head_grads(
        normed,
        mixed_t,
        attended_t,
        all_cot,
        row_place,
        part_place,
        core,
        me,
        gain,
        sums,
        (qkv_bias_part, fc1_bias_part, out_bias_part),
        [],
    )
    late_far = reduce_far(late)
    q |= own_terms(WAVES[1], mine1, other1, 0.0)
    q, early_own, late_far, far = together(q, early_own, late_far, far, also=(other2, late))

    further = scatter_next(q, far, 0.0)
    late_near = reduce_near(late, late_far, 0.0)
    late_near = fetch(late_near[0], dy=-1), fetch(late_near[1], dy=1)
    q |= own_terms(WAVES[2], mine2, other2, 0.0)
    q, further, late_near = together(q, further, late_near)

    nearest = scatter_near(q, further, 0.0)
    early = jnp.concatenate(
        [
            jnp.concatenate([early_own[dx], early[dx * FFL : (dx + 1) * FFL, 2 * T :]], axis=1)
            for dx in range(2)
        ]
    )
    early_one, early_three = fetch(early, dy=1), fetch(early, dy=-1)
    late = add(late[0], *late_near).astype(BF)
    early_one, early_three, late = together(early_one, early_three, late, also=nearest)
    late_other = fetch(late, dh=1)

    early = (
        early,
        early_one,
        early_three,
        fetch(early_one[:FFL], dy=1),
        fetch(early_three[FFL:], dy=-1),
    )
    late = add(late, late_other).astype(BF)
    late_rows = jnp.concatenate([late[:FOR_OWNER], late[LATE : LATE + FOR_OWNER]])
    late_own = jnp.concatenate([late_rows[:, :T], fetch(late_rows[:, T:], dc=1)], axis=1)
    late_own = from_owners([late_own[:FOR_OWNER], late_own[FOR_OWNER:]])
    late = jnp.concatenate(
        [late_own[0], late[FOR_OWNER:LATE], late_own[1], late[LATE + FOR_OWNER :]]
    )
    late_one, late_three = fetch(late, dy=1), fetch(late, dy=-1)
    total = add(q[0, 0], *nearest)
    own = tokens.astype(F32)
    layer_out = (own + out_bias + total[:, D:]).astype(BF)
    center = own - jnp.mean(own, axis=-1, keepdims=True)
    inv_std = lax.rsqrt(jnp.mean(center * center, axis=-1, keepdims=True) + 1e-05)
    unit = center * inv_std
    scaled = total[:, :D] * gain
    input_grad = cotangent.astype(F32) + inv_std * (
        scaled
        - jnp.mean(scaled, axis=-1, keepdims=True)
        - unit * jnp.mean(scaled * unit, axis=-1, keepdims=True)
    )
    late = (
        late,
        late_one,
        late_three,
        fetch(late_one[:LATE], dy=1),
        fetch(late_three[LATE:], dy=-1),
    )
    fc1_total, fc2_total = place_columns(early, col_place, part_place)
    qkv_total, dense_total, of_owner, of_own = place_heads(late, col_place, part_place)
    out_bias_total = of_own[0, FFL : FFL + T]

    return (
        layer_out,
        input_grad,
        of_owner[0],
        of_owner[1],
        qkv_total,
        of_owner[2:5].reshape(QKV),
        dense_total,
        out_bias_total,
        fc1_total,
        of_own[0, :FFL],
        fc2_total,
        out_bias_total,
    )


def solution(mesh):
    return jax.shard_map(
        body,
        mesh=mesh,
        in_specs=(
            P(AXES, None),
            P("shard"),
            P("shard"),
            P("shard", None),
            P("shard"),
            P("shard", None),
            P("shard"),
            P("shard", None),
            P("shard"),
            P("shard", None),
            P("shard"),
            P(AXES, None),
        ),
        out_specs=(
            P(AXES, None),
            P(AXES, None),
            P("shard"),
            P("shard"),
            P("shard", None),
            P("shard"),
            P("shard", None),
            P("shard"),
            P("shard", None),
            P("shard"),
            P("shard", None),
            P("shard"),
        ),
        check_vma=False,
    )
```

```python
import functools
import math

import jax
import jax.numpy as jnp
from jax import lax
from jax.experimental import pallas as pl
from jax.experimental.pallas import tpu as pltpu
from jax.sharding import PartitionSpec as P

D = 2048
HEADS = 32
HEAD_DIM = 64
ROTARY = 32
FF = 8192
SEQ = 2048
T = 128
QKV = 384
FFL = 512
COLS = QKV + FFL
BF = jnp.bfloat16
F32 = jnp.float32
AXES = ("rep", "shard")
MIB = 1 << 20
LOG2E = math.log2(math.e)

PLACES = [
    (xh, y, z, xl, c)
    for xh in range(2)
    for y in range(4)
    for z in range(4)
    for xl in range(2)
    for c in range(2)
]


def flat(xh, y, z, xl, c):
    return (xh * 4 + y % 4) * 16 + (z % 4) * 4 + xl * 2 + c


def fetch_from(x, source):
    return lax.ppermute(x, AXES, [(flat(*source(*p)), flat(*p)) for p in PLACES])


def fetch(x, dz=0, dx=0, dc=0, dy=0, dh=0):
    return fetch_from(
        x, lambda xh, y, z, xl, c: (xh ^ dh, y + dy, z + dz, xl ^ dx, c ^ dc)
    )


def dot(a, b, ca=1, cb=0):
    return lax.dot_general(a, b, (((ca,), (cb,)), ((), ())), preferred_element_type=F32)


def add(*terms):
    total = terms[0].astype(F32)
    for term in terms[1:]:
        total = total + (term if isinstance(term, float) else term.astype(F32))
    return total


def zero_of(x):
    return x[0, 0].astype(F32) * 0.0


def together(*groups, also=()):
    leaves, tree = jax.tree.flatten(groups)
    others = jax.tree.leaves(also)
    n = len(leaves)
    leaves = pl.pallas_call(
        lambda *refs: None,
        in_specs=[pl.BlockSpec(memory_space=pl.ANY)] * (n + len(others)),
        out_specs=[pl.BlockSpec(memory_space=pl.ANY)] * n,
        out_shape=[jax.ShapeDtypeStruct(x.shape, x.dtype) for x in leaves],
        input_output_aliases={i: i for i in range(n)},
        compiler_params=pltpu.CompilerParams(vmem_limit_bytes=MIB),
    )(*leaves, *others)
    return jax.tree.unflatten(tree, leaves)


def gather_near(own):
    return {
        (0, 0): own,
        (1, 0): fetch(own, dz=1),
        (3, 0): fetch(own, dz=-1),
        (0, 1): fetch(own, dx=1),
    }


def gather_next(a):
    return {
        (1, 1): fetch(a[1, 0], dx=1),
        (3, 1): fetch(a[0, 1], dz=-1),
        (2, 0): fetch(a[1, 0], dz=1),
    }


def gather_far(a):
    return fetch(a[2, 0], dx=1)


def gather_swap(own):
    return fetch(own, dc=1)


def both_cores(a):
    pieces = []
    for (dz, dx), own in a.items():
        pair = own if isinstance(own, tuple) else (own, gather_swap(own))
        pieces += [(pair[dc], ((dz * 2 + dx) * 2 + dc) * T) for dc in range(2)]
    return pieces


SLOTS = [(dz, dx, dc) for dz in range(4) for dx in range(2) for dc in range(2)]
WAVES = [[(2, 1)], [(1, 1), (3, 1), (2, 0)], [(1, 0), (3, 0), (0, 1), (0, 0)]]


def scatter_far(q):
    half = T // 2
    return fetch(q[2, 1][:half], dz=-1), fetch(q[2, 1][half:], dz=1)


def scatter_next(q, far, zero):
    half = T // 2
    q11 = jnp.concatenate([add(q[1, 1][:half], far[0], zero).astype(BF), q[1, 1][half:]])
    q31 = jnp.concatenate([q[3, 1][:half], add(q[3, 1][half:], far[1], zero).astype(BF)])
    return fetch(q[2, 0], dz=-1), fetch(q31, dz=1), fetch(q11, dx=1)


def scatter_near(q, further, zero):
    q10 = add(q[1, 0], further[0], further[2], zero).astype(BF)
    q01 = add(q[0, 1], further[1], zero).astype(BF)
    return fetch(q10, dz=-1), fetch(q[3, 0], dz=1), fetch(q01, dx=1)


def reduce_far(g):
    half = g[0].shape[0] // 2
    return fetch(g[2][:half], dy=-1), fetch(g[2][half:], dy=1)


def reduce_near(g, far, zero):
    half = g[0].shape[0] // 2
    g1 = jnp.concatenate([add(g[1][:half], far[0], zero).astype(BF), g[1][half:]])
    g3 = jnp.concatenate([g[3][:half], add(g[3][half:], far[1], zero).astype(BF)])
    return g1, g3


def of_rep(refs, dy, dx, n):
    own, one, three, first, second = refs
    if dy == 2:
        return (second if dx else first), 0
    return (own, one, None, three)[dy], dx * n


VMEM = pl.BlockSpec(memory_space=pltpu.VMEM)
SMEM = pl.BlockSpec(memory_space=pltpu.SMEM)
HBM = pl.BlockSpec(memory_space=pltpu.HBM)
ANY = pl.BlockSpec(memory_space=pl.ANY)


def lanes(at, n):
    return pl.ds(pl.multiple_of(at * n, n), n)


def call(kernel, ins, outs, args, scratch=(), vmem=6, flops=0, nbytes=0, exps=0, aliases={}, out_specs=None):
    return pl.pallas_call(
        kernel,
        in_specs=ins,
        out_specs=out_specs or [VMEM] * len(outs),
        out_shape=[
            pltpu.VMEM(o[0], o[1]) if len(o) > 2 else jax.ShapeDtypeStruct(*o) for o in outs
        ],
        scratch_shapes=list(scratch),
        input_output_aliases=aliases,
        compiler_params=pltpu.CompilerParams(vmem_limit_bytes=vmem * MIB),
        cost_estimate=pl.CostEstimate(
            flops=flops, transcendentals=exps, bytes_accessed=nbytes
        ),
    )(*args)


ROOT = math.sqrt(2.0 / math.pi)


def start_copies(pieces, place, sems):
    copies = [
        pltpu.make_async_copy(src, dst, sems.at[place + i]) for i, (src, dst) in enumerate(pieces)
    ]
    for copy in copies:
        copy.start()
    return copies


def norm_rows(normed_ref, gain, shift, first, count):
    def strip(i, _):
        at = lanes(i, 64)
        x = normed_ref[at, :].astype(F32)
        x = x - jnp.sum(x, axis=1, keepdims=True) * (1.0 / D)
        scale = lax.rsqrt(jnp.sum(x * x, axis=1, keepdims=True) * (1.0 / D) + 1e-05)
        normed_ref[at, :] = (x * scale * gain + shift).astype(BF)
        return 0

    lax.fori_loop(first // 64, (first + count) // 64, strip, 0)


def grid_call(kernel, prefetch, grid, ins, outs, args, scratch=(), vmem=32, flops=0, nbytes=0):
    return pl.pallas_call(
        kernel,
        grid_spec=pltpu.PrefetchScalarGridSpec(
            num_scalar_prefetch=len(prefetch),
            grid=grid,
            in_specs=ins,
            out_specs=[o[2] for o in outs],
            scratch_shapes=list(scratch),
        ),
        out_shape=[jax.ShapeDtypeStruct(o[0], o[1]) for o in outs],
        compiler_params=pltpu.CompilerParams(vmem_limit_bytes=vmem * MIB),
        cost_estimate=pl.CostEstimate(flops=flops, transcendentals=0, bytes_accessed=nbytes),
    )(*prefetch, *args)


def whole(*shape):
    return pl.BlockSpec(shape, lambda *_: (0,) * len(shape))


def group_vectors(pieces, far_vectors, token_place, me):
    n = len(pieces)

    def kernel(t_ref, me_ref, *refs):
        far_ref, vec_ref, own_ref, small_ref, flat_ref, sems = refs[n:]
        moves = [
            (ref.at[pl.ds(0, 16), pl.ds(2 * D, T)], small_ref.at[pl.ds(at // T * 16, 16)])
            for (_, at), ref in zip(pieces, refs[:n], strict=True)
        ]
        for dc in range(2):
            to = small_ref.at[pl.ds((5 * 2 + dc) * 16, 16)]
            moves.append((far_ref.at[pl.ds(dc * 16, 16)], to))
        for copy in start_copies(moves, 0, sems):
            copy.wait()
        for i in range(16):
            at = t_ref[i]
            small = small_ref[i * 16 : (i + 1) * 16, :].astype(F32)
            for part in range(3):
                flat_ref[0:1, lanes(at * 3 + part, T)] = small[part : part + 1]
            vec_ref[0:1, lanes(at, T)] = small[3:4]
            vec_ref[1:2, lanes(at, T)] = small[4:5]
            vec_ref[2:3, lanes(at, T)] = small[5:6] + small[6:7]
        for part in range(3):
            own_ref[0:1, part * T : (part + 1) * T] = flat_ref[
                0:1, lanes(part * 16 + me_ref[0], T)
            ]

    return call(
        kernel,
        [SMEM] * 2 + [HBM] * (n + 1),
        [((8, D), F32), ((1, QKV), F32)],
        [token_place, me] + [p for p, _ in pieces] + [far_vectors],
        [
            pltpu.VMEM((256, T), BF),
            pltpu.VMEM((1, 3 * D), F32),
            pltpu.SemaphoreType.DMA((n + 2,)),
        ],
        vmem=56,
    )


def chip_rows(pieces, vecs, fc2, dense, arrays, before):
    n, given = len(pieces), len(arrays)
    chips = sorted({at // 256 for _, at in pieces})

    def kernel(*refs):
        refs = refs[len(before) + given :]
        tok = refs[:n]
        vec_ref, fc2_ref, dense_ref = refs[n : n + 3]
        outs, done_ref = refs[n + 3 : n + 7], refs[n + 7]
        bufs, in_sems, out_sems = refs[n + 8 : n + 12], refs[n + 12], refs[n + 13]
        done_ref[...] = jnp.zeros_like(done_ref)

        def arriving(k):
            moves = []
            for (array, at), ref in zip(pieces, tok, strict=True):
                if at // 256 == chips[k]:
                    to = pl.ds(at % 256, array.shape[0])
                    moves.append((ref.at[:, pl.ds(0, D)], bufs[0].at[k % 2, to]))
                    moves.append((ref.at[:, pl.ds(D, D)], bufs[1].at[k % 2, to]))
            return [
                pltpu.make_async_copy(src, dst, in_sems.at[k % 2, i])
                for i, (src, dst) in enumerate(moves)
            ]

        def leaving(k):
            rows = pl.ds(chips[k] * 256, 256)
            return [
                pltpu.make_async_copy(buf.at[k % 2], out.at[rows], out_sems.at[k % 2, i])
                for i, (buf, out) in enumerate(zip(bufs, outs, strict=True))
            ]

        for copy in arriving(0):
            copy.start()
        for k in range(len(chips)):
            if k + 1 < len(chips):
                if k >= 1:
                    for copy in leaving(k - 1):
                        copy.wait()
                for copy in arriving(k + 1):
                    copy.start()
            for copy in arriving(k):
                copy.wait()
            norm_rows(bufs[0].at[k % 2], vec_ref[0:1, :], vec_ref[1:2, :], 0, 256)
            x = bufs[1][k % 2]
            bufs[2][k % 2] = dot(x, fc2_ref[...], 1, 1).astype(BF)
            bufs[3][k % 2] = dot(x, dense_ref[...], 1, 1).astype(BF)
            for copy in leaving(k):
                copy.start()
        for k in range(max(len(chips) - 2, 0), len(chips)):
            for copy in leaving(k):
                copy.wait()

    widths = (D, D, FFL, T)
    return call(
        kernel,
        [ANY] * (len(before) + given) + [HBM] * n + [VMEM] * 3,
        [((SEQ, w), BF) for w in widths] + [((8, T), F32)],
        [*before, *arrays, *[p for p, _ in pieces], vecs, fc2, dense],
        [pltpu.VMEM((2, 256, w), BF) for w in widths]
        + [pltpu.SemaphoreType.DMA((2, 8)), pltpu.SemaphoreType.DMA((2, 4))],
        vmem=56,
        aliases={len(before) + i: i for i in range(given)},
        out_specs=[ANY] * 4 + [VMEM],
        flops=2 * n * T * D * (FFL + T),
        nbytes=n * MIB,
    )


def forward_inputs(normed, cot, act_grad, weights, bias, own_bias, row_place, me):
    def kernel(
        r_ref,
        me_ref,
        n_ref,
        grad_ref,
        cot_ref,
        w0_ref,
        w1_ref,
        w2_ref,
        w3_ref,
        bias_ref,
        own_ref,
        act_ref,
        pre_ref,
        act_t_ref,
        pre_t_ref,
        mixed_ref,
        fc1b_ref,
        outb_ref,
        w_out,
        w_ref,
        sems,
        out_sem,
    ):
        step = pl.program_id(0)
        leaving = pltpu.make_async_copy(w_ref, w_out, out_sem.at[0])

        @pl.when(step == 0)
        def _():
            moves = []
            for i, (dy, dx, dc) in enumerate(SLOTS):
                rows = pl.ds((dx * 2 + dc) * T, T)
                source = (w0_ref, w1_ref, w2_ref, w3_ref)[dy]
                moves.append((source.at[rows], w_ref.at[lanes(r_ref[i], T)]))
            for copy in start_copies(moves, 0, sems):
                copy.wait()
            leaving.start()
            fc1b_ref[...] = jnp.zeros_like(fc1b_ref)
            outb_ref[...] = jnp.zeros_like(outb_ref)

        halves = []
        for half in range(2):
            x = n_ref[half * 256 : (half + 1) * 256, :]
            mixed_ref[half * 256 : (half + 1) * 256, :] = dot(x, w_ref[:, :QKV]) + own_ref[...]
            halves.append(dot(x, w_ref[:, QKV:]) + bias_ref[...])
        for half, pre in enumerate(halves):
            at = slice(half * 256, (half + 1) * 256)
            squared = pre * pre
            tanh = jnp.tanh(ROOT * pre * (1.0 + 0.044715 * squared))
            act = (0.5 * pre * (1.0 + tanh)).astype(BF)
            act_ref[at, :] = act
            act_t_ref[:, at] = act.T
            slope = 0.5 * (1.0 + tanh) + 0.5 * pre * (1.0 - tanh * tanh) * ROOT * (
                1.0 + 3 * 0.044715 * squared
            )
            back = (grad_ref[at, :].astype(F32) * slope).astype(BF)
            pre_ref[at, :] = back
            pre_t_ref[:, at] = back.T
            fc1b_ref[...] += jnp.sum(back.astype(F32).reshape(32, 8, FFL), axis=0)
        outb_ref[...] += jnp.sum(cot_ref[...].astype(F32).reshape(64, 8, T), axis=0)

        @pl.when(step == pl.num_programs(0) - 1)
        def _():
            leaving.wait()

    rows = lambda i, *_: (i, 0)
    cols = lambda i, *_: (0, i)
    return grid_call(
        kernel,
        [row_place, me],
        (SEQ // 512,),
        [
            pl.BlockSpec((512, D), rows),
            pl.BlockSpec((512, FFL), rows),
            pl.BlockSpec((512, T), lambda i, r, m: (i, m[0])),
        ]
        + [HBM] * 4
        + [whole(1, FFL), whole(1, QKV)],
        [
            ((SEQ, FFL), BF, pl.BlockSpec((512, FFL), rows)),
            ((SEQ, FFL), BF, pl.BlockSpec((512, FFL), rows)),
            ((FFL, SEQ), BF, pl.BlockSpec((FFL, 512), cols)),
            ((FFL, SEQ), BF, pl.BlockSpec((FFL, 512), cols)),
            ((SEQ, QKV), F32, pl.BlockSpec((512, QKV), rows)),
            ((8, FFL), F32, whole(8, FFL)),
            ((8, T), F32, whole(8, T)),
            ((D, COLS), BF, ANY),
        ],
        [normed, act_grad, cot, *weights, bias, own_bias],
        [
            pltpu.VMEM((D, COLS), BF),
            pltpu.SemaphoreType.DMA((16,)),
            pltpu.SemaphoreType.DMA((1,)),
        ],
        vmem=56,
        flops=2 * SEQ * D * COLS,
        nbytes=24 * MIB,
    )


ORDER = (2, 1, 3, 0)


def part_specs(rows, cols):
    return [
        pl.BlockSpec((rows, cols), lambda i, *_, k=k: (jnp.clip(i - 2 * k, 0, 1), 0))
        for k in range(4)
    ]


def in_order(places, parts):
    chips = jnp.stack([places[(dy * 2 + dx) * 2] // 2 for dy in ORDER for dx in range(2)])
    return chips, jnp.stack([parts[dy * 2 + dx] for dy in ORDER for dx in range(2)])


def column_grads(normed, pre_t, act_t, cot, chips, parts, core):
    def kernel(chip_ref, part_ref, core_ref, n_ref, c_ref, g_ref, a_ref, *outs):
        cols = dot(g_ref[...], n_ref[...]).astype(BF)
        part = dot(a_ref[...], c_ref[...]).astype(BF)
        for k in range(4):

            @pl.when(pl.program_id(0) // 2 == k)
            def _():
                outs[k][:, lanes(core_ref[0], T)] = cols[:, :T]
                outs[k][:, lanes(1 - core_ref[0], T)] = cols[:, T:]
                outs[k][:, 256:512] = part

    outs = grid_call(
        kernel,
        [chips, parts, core],
        (8,),
        [
            pl.BlockSpec((SEQ, 256), lambda i, chip, part, core: (0, chip[i])),
            pl.BlockSpec((SEQ, 256), lambda i, chip, part, core: (0, part[i])),
            whole(FFL, SEQ),
            whole(FFL, SEQ),
        ],
        [((2 * FFL, 512), BF, spec) for spec in part_specs(FFL, 512)],
        [normed, cot, pre_t, act_t],
        vmem=56,
        flops=4 * SEQ * D * FFL,
        nbytes=24 * MIB,
    )
    return [outs[ORDER.index(dy)] for dy in range(4)]


FOR_OWNER = QKV + 16
LATE = FOR_OWNER + T + 16


def head_grads(
    normed, mixed_t, attended_t, cot, chips, parts, core, me, gain, sums, bias_parts, before
):
    def kernel(chip_ref, part_ref, core_ref, me_ref, n_ref, c_ref, m_ref, a_ref, *refs):
        gain_ref, gains_ref, shifts_ref, qkvb_ref, fc1b_ref, outb_ref = refs[:6]
        outs, owners_ref, own_ref = refs[-6:-2], refs[-2], refs[-1]
        step = pl.program_id(0)

        @pl.when(step == 0)
        def _():
            owners_ref[...] = jnp.zeros_like(owners_ref)
            owners_ref[0:1, :] = jnp.sum(gains_ref[...], axis=0, keepdims=True) / gain_ref[...]
            owners_ref[1:2, :] = jnp.sum(shifts_ref[...], axis=0, keepdims=True)
            qkvb = jnp.sum(qkvb_ref[...], axis=0, keepdims=True)
            for part in range(3):
                at = part * 16 + me_ref[0]
                third = at % 3
                row = lax.broadcasted_iota(jnp.int32, (8, T), 0)
                value = jnp.where(row == 2 + third, qkvb[:, part * T : (part + 1) * T], 0.0)
                owners_ref[0:8, lanes(at // 3, T)] += value
            own_ref[...] = jnp.zeros_like(own_ref)
            own_ref[0:1, :FFL] = jnp.sum(fc1b_ref[...], axis=0, keepdims=True)
            own_ref[0:1, FFL : FFL + T] = jnp.sum(outb_ref[...], axis=0, keepdims=True)

        cols = dot(m_ref[...], n_ref[...]).astype(BF)
        extra = owners_ref[:, lanes(chip_ref[step], 256)].astype(BF)
        part = dot(a_ref[...], c_ref[...]).astype(BF)
        mine, other = lanes(core_ref[0], T), lanes(1 - core_ref[0], T)
        for k in range(4):

            @pl.when(step // 2 == k)
            def _():
                out = outs[k]
                out[0:QKV, mine] = cols[:, :T]
                out[0:QKV, other] = cols[:, T:]
                out[QKV:FOR_OWNER, mine] = extra[:, :T]
                out[QKV:FOR_OWNER, other] = extra[:, T:]
                out[FOR_OWNER : FOR_OWNER + T, :] = part
                out[FOR_OWNER + T :, 0:T] = own_ref[:, lanes(part_ref[step], T)].astype(BF)
                out[FOR_OWNER + T :, T:] = jnp.zeros((16, T), BF)

    outs = grid_call(
        kernel,
        [chips, parts, core, me],
        (8,),
        [
            pl.BlockSpec((SEQ, 256), lambda i, chip, part, core, me: (0, chip[i])),
            pl.BlockSpec((SEQ, 256), lambda i, chip, part, core, me: (0, part[i])),
            whole(QKV, SEQ),
            whole(T, SEQ),
            whole(1, D),
            whole(8, D),
            whole(8, D),
            whole(8, QKV),
            whole(8, FFL),
            whole(8, T),
        ]
        + [ANY] * len(before),
        [((2 * LATE, 256), BF, spec) for spec in part_specs(LATE, 256)],
        [normed, cot, mixed_t, attended_t, gain, *sums, *bias_parts, *before],
        [pltpu.VMEM((16, D), F32), pltpu.VMEM((16, 1024), F32)],
        vmem=48,
        flops=2 * SEQ * D * (QKV + T),
        nbytes=20 * MIB,
    )
    return [outs[ORDER.index(dy)] for dy in range(4)]


def place_columns(pieces, col_place, part_place):
    def kernel(c_ref, p_ref, *refs):
        fc1_ref, fc2_ref = refs[5:]
        for i, (dy, dh, dc) in enumerate(SLOTS):
            ref, at = of_rep(refs[:5], dy, dh, FFL)
            part = ref[at : at + FFL, dc * T : (dc + 1) * T]
            fc1_ref[:, lanes(c_ref[i], FFL)] = part.astype(F32).T
            if dc == 0:
                to = lanes(p_ref[dy * 2 + dh], 256)
                fc2_ref[:, to] = ref[at : at + FFL, 256:512].astype(F32)

    return call(
        kernel,
        [SMEM] * 2 + [VMEM] * 5,
        [((T, FF), F32), ((FFL, D), F32)],
        [col_place, part_place] + list(pieces),
        vmem=20,
        nbytes=12 * MIB,
    )


def place_heads(pieces, col_place, part_place):
    def kernel(c_ref, p_ref, *refs):
        qkv_ref, dense_ref, owner_ref, own_ref = refs[5:]
        total = jnp.zeros((16, T), F32)
        for i, (dy, dx, dc) in enumerate(SLOTS):
            ref, at = of_rep(refs[:5], dy, dx, LATE)
            cols = slice(dc * T, (dc + 1) * T)
            for part in range(3):
                block = ref[at + part * T : at + (part + 1) * T, cols].astype(F32)
                qkv_ref[:, lanes(c_ref[i] + part * 16, T)] = block.T
            total += ref[at + QKV : at + FOR_OWNER, cols].astype(F32)
            if dc == 0:
                part = p_ref[dy * 2 + dx]
                rows = slice(at + FOR_OWNER, at + FOR_OWNER + T)
                dense_ref[:, lanes(part, 256)] = ref[rows, :].astype(F32)
                rows = slice(at + FOR_OWNER + T, at + LATE)
                own_ref[:, lanes(part, T)] = ref[rows, 0:T].astype(F32)
        owner_ref[...] = total

    return call(
        kernel,
        [SMEM] * 2 + [VMEM] * 5,
        [((T, 3 * D), F32), ((T, D), F32), ((16, T), F32), ((16, 1024), F32)],
        [col_place, part_place] + list(pieces),
        vmem=14,
        nbytes=6 * MIB,
    )


def terms(
    chips, attended, activated, dense, fc2, mixed_grad, pre_grad, weight, normed, vecs, sums, before
):
    n = len(chips)
    order = jnp.array([dz * 2 + dx for dz, dx in chips], jnp.int32)

    def kernel(order_ref, a_ref, f_ref, m_ref, p_ref, n_ref, d_ref, v_ref, w_ref, vec_ref, *refs):
        mine_ref, other_ref, gain_ref, total_ref = refs[-4:]
        shift = vec_ref[1:2, :]

        @pl.when(pl.program_id(0) == 0)
        def _():
            if sums:
                gain_ref[...] = refs[0][...]
                total_ref[...] = refs[1][...]
            else:
                gain_ref[...] = jnp.zeros_like(gain_ref)
                total_ref[...] = jnp.zeros_like(total_ref)

        for col in range(4):
            to = slice(col * 512, (col + 1) * 512)
            total = dot(m_ref[...], w_ref[to, :QKV], 1, 1) + dot(p_ref[...], w_ref[to, QKV:], 1, 1)
            mine_ref[:, to] = total[:T].astype(BF)
            other_ref[:, to] = total[T:].astype(BF)
            unit = n_ref[:, to].astype(F32) - shift[:, to]
            gain_ref[:, to] += jnp.sum((total * unit).reshape(32, 8, 512), axis=0)
            total_ref[:, to] += jnp.sum(total.reshape(32, 8, 512), axis=0)
            total = dot(a_ref[...], d_ref[:, to]) + dot(f_ref[...], v_ref[:, to])
            to = slice(D + col * 512, D + (col + 1) * 512)
            mine_ref[:, to] = total[:T].astype(BF)
            other_ref[:, to] = total[T:].astype(BF)

    rows = lambda i, order_ref: (order_ref[i], 0)
    here = lambda i, order_ref: (i, 0)
    return grid_call(
        kernel,
        [order],
        (n,),
        [
            pl.BlockSpec((2 * T, T), rows),
            pl.BlockSpec((2 * T, FFL), rows),
            pl.BlockSpec((2 * T, QKV), rows),
            pl.BlockSpec((2 * T, FFL), rows),
            pl.BlockSpec((2 * T, D), rows),
            whole(T, D),
            whole(FFL, D),
            whole(D, COLS),
            whole(8, D),
        ]
        + [whole(8, D)] * len(sums)
        + [ANY] * len(before),
        [((n * T, 2 * D), BF, pl.BlockSpec((T, 2 * D), here))] * 2
        + [((8, D), F32, whole(8, D))] * 2,
        [attended, activated, mixed_grad, pre_grad, normed, dense, fc2, weight, vecs, *sums, *before],
        flops=2 * n * 2 * T * (COLS + T + FFL) * D,
        nbytes=8 * MIB,
    )


TQ = 512
TK = 512


def attention_kernel(blocks, last, n_before, place, cos_ref, sin_ref, *refs):
    refs = refs[n_before:]
    if last:
        first_refs, refs = refs[:8], refs[8:]
        att_ref, out_ref, att_t_ref, out_t_ref, bias_ref = refs[:5]
        q_ref, k_ref, v_ref, do_ref = first_refs[:4]
        dq_ref, dk_ref, dv_ref, o_ref, s_ref, e_ref = refs[5:]
    else:
        mixed_ref, grad_ref, *refs = refs
        refs, done_ref = refs[:8] + refs[9:], refs[8]
        done_ref[...] = jnp.zeros_like(done_ref)
        q_ref, k_ref, v_ref, do_ref, dq_ref, dk_ref, dv_ref, o_ref, s_ref, e_ref = refs
    lane = lax.broadcasted_iota(jnp.int32, (T, 128), 1)
    low_head = lane < HEAD_DIM
    first = (lane % HEAD_DIM) < ROTARY // 2

    def turned(x):
        return jnp.where(
            first, pltpu.roll(x, 128 - ROTARY // 2, 1), pltpu.roll(x, ROTARY // 2, 1)
        )

    def load(slot, _):
        rows = pl.ds(pl.multiple_of(slot * T, T), T)
        at = pl.ds(pl.multiple_of(place[slot] * T, T), T)
        c, s = cos_ref[at, :], sin_ref[at, :]
        query = mixed_ref[rows, 0:128]
        key = mixed_ref[rows, 128:256]
        query = (query * c + turned(query) * s).astype(BF).astype(F32) * (HEAD_DIM**-0.5)
        q_ref[0, at, :] = jnp.where(low_head, query, 0.0).astype(BF)
        q_ref[1, at, :] = jnp.where(low_head, 0.0, query).astype(BF)
        k_ref[at, :] = (key * c + turned(key) * s).astype(BF)
        v_ref[at, 0:128] = mixed_ref[rows, 256:384].astype(BF)
        v_ref[at, 128:256] = jnp.ones((T, 128), BF)
        grad = grad_ref[rows, :].astype(F32)
        do_ref[0, at, :] = jnp.where(low_head, grad, 0.0).astype(BF)
        do_ref[1, at, :] = jnp.where(low_head, 0.0, grad).astype(BF)
        dk_ref[:, at] = jnp.zeros((128, T), F32)
        dv_ref[:, at] = jnp.zeros((128, T), F32)
        return 0

    if last:
        for to, at in ((dq_ref, 4), (dk_ref, 5), (dv_ref, 6), (o_ref, 7)):
            to[...] = first_refs[at][...]
    else:
        lax.fori_loop(0, 16, load, 0)

    lane_q = lax.broadcasted_iota(jnp.int32, (TQ, 128), 1)
    low_q = lane_q < HEAD_DIM

    def block(i, _):
        rows = lanes(i, TQ)
        queries = [q_ref[h, rows, :] for h in range(2)]

        def scores(j, tops, masked):
            at = lanes(j, TK)
            keys = k_ref[at, :]
            new = []
            for h in range(2):
                s = dot(queries[h], keys, 1, 1)
                if masked:
                    row = lax.broadcasted_iota(jnp.int32, (TQ, TK), 0)
                    col = lax.broadcasted_iota(jnp.int32, (TQ, TK), 1)
                    s = jnp.where(row >= col, s, -1e30)
                s_ref[h, :, at] = s
                top = tops[h]
                for n in range(TK // 128):
                    top = jnp.maximum(top, s[:, n * 128 : (n + 1) * 128])
                new.append(top)
            return tuple(new)

        low = jnp.full((TQ, 128), -1e30, F32)
        tops = lax.fori_loop(0, i, lambda j, t: scores(j, t, False), (low, low))
        tops = [jnp.max(t, axis=1, keepdims=True) for t in scores(i, tops, True)]

        def weigh(j, totals):
            at = lanes(j, TK)
            values = v_ref[at, :]
            new = []
            for h in range(2):
                e = jnp.exp2((s_ref[h, :, at] - tops[h]) * LOG2E).astype(BF)
                e_ref[h, :, at] = e
                new.append(totals[h] + dot(e, values))
            return tuple(new)

        zero = jnp.zeros((TQ, 256), F32)
        totals = lax.fori_loop(0, i + 1, weigh, (zero, zero))
        outs, grads, deltas = [], [], []
        for h in range(2):
            inverse = 1.0 / totals[h][:, 128:]
            o = totals[h][:, :128] * inverse
            grad = do_ref[h, rows, :].astype(F32) * inverse
            outs.append(o)
            deltas.append(jnp.sum(grad * o, axis=1, keepdims=True))
            grads.append(grad.astype(BF))
        o_ref[rows, :] = jnp.where(low_q, outs[0], outs[1]).astype(BF)
        queries_t = [q.T for q in queries]
        grads_t = [g.T for g in grads]

        def back(j, totals):
            at = lanes(j, TK)
            keys = k_ref[at, :]
            values = v_ref[at, 0:128]
            new, dk, dv = [], None, None
            for h in range(2):
                e = e_ref[h, :, at]
                dp = dot(grads[h], values, 1, 1)
                ds = (e.astype(F32) * (dp - deltas[h])).astype(BF)
                new.append(totals[h] + dot(ds, keys))
                k_part = dot(queries_t[h], ds)
                v_part = dot(grads_t[h], e)
                dk = k_part if dk is None else dk + k_part
                dv = v_part if dv is None else dv + v_part
            dk_ref[:, at] += dk
            dv_ref[:, at] += dv
            return tuple(new)

        zero = jnp.zeros((TQ, 128), F32)
        dqs = lax.fori_loop(0, i + 1, back, (zero, zero))
        dq_ref[rows, :] = jnp.where(low_q, dqs[0], dqs[1]) * (HEAD_DIM**-0.5)
        return 0

    lax.fori_loop(blocks[0], blocks[1], block, 0)
    if not last:
        return

    def store(slot, total):
        rows = pl.ds(pl.multiple_of(slot * T, T), T)
        at = pl.ds(pl.multiple_of(place[slot] * T, T), T)
        c, s = cos_ref[at, :], sin_ref[at, :]
        att = o_ref[at, :]
        att_ref[rows, :] = att
        att_t_ref[:, rows] = att.T
        dq, dk = dq_ref[at, :], dk_ref[:, at].T
        new = []
        for part, grad in enumerate(
            (dq * c - turned(dq) * s, dk * c - turned(dk) * s, dv_ref[:, at].T)
        ):
            low = grad.astype(BF)
            cols = slice(part * T, (part + 1) * T)
            out_ref[rows, cols] = low
            out_t_ref[cols, rows] = low.T
            new.append(total[part] + jnp.sum(low.astype(F32).reshape(16, 8, T), axis=0))
        return tuple(new)

    zero = jnp.zeros((8, T), F32)
    sums = lax.fori_loop(0, 16, store, (zero, zero, zero))
    for part in range(3):
        bias_ref[:, part * T : (part + 1) * T] = sums[part]


def attention_first(place, cosine, sine, mixed, attended_grad, before):
    return call(
        functools.partial(attention_kernel, (0, 3), False, len(before)),
        [SMEM] + [VMEM] * 2 + [ANY] * len(before) + [VMEM] * 2,
        [
            ((2, SEQ, 128), BF, 1),
            ((SEQ, 128), BF, 1),
            ((SEQ, 256), BF, 1),
            ((2, SEQ, 128), BF, 1),
            ((SEQ, 128), F32, 1),
            ((128, SEQ), F32, 1),
            ((128, SEQ), F32, 1),
            ((SEQ, 128), BF, 1),
            ((8, 128), jnp.int32),
        ],
        [place, cosine, sine, *before, mixed, attended_grad],
        [pltpu.VMEM((2, TQ, SEQ), F32), pltpu.VMEM((2, TQ, SEQ), BF)],
        vmem=24,
        flops=8 * SEQ * SEQ * 64 * 2,
        exps=SEQ * SEQ // 2,
        nbytes=3 * MIB,
    )


def attention_last(place, cosine, sine, state, before):
    return call(
        functools.partial(attention_kernel, (3, 4), True, len(before)),
        [SMEM] + [VMEM] * 2 + [ANY] * len(before) + [VMEM] * 8,
        [
            ((SEQ, T), BF),
            ((SEQ, QKV), BF),
            ((T, SEQ), BF),
            ((QKV, SEQ), BF),
            ((8, QKV), F32),
        ],
        [place, cosine, sine, *before] + list(state),
        [
            pltpu.VMEM((SEQ, 128), F32),
            pltpu.VMEM((128, SEQ), F32),
            pltpu.VMEM((128, SEQ), F32),
            pltpu.VMEM((SEQ, 128), BF),
            pltpu.VMEM((2, TQ, SEQ), F32),
            pltpu.VMEM((2, TQ, SEQ), BF),
        ],
        vmem=26,
        flops=6 * SEQ * SEQ * 64 * 2,
        exps=SEQ * SEQ // 2,
        nbytes=3 * MIB,
    )


def rotary_tables():
    lane = lax.broadcasted_iota(jnp.int32, (SEQ, 128), 1) % HEAD_DIM
    place = lax.broadcasted_iota(jnp.int32, (SEQ, 128), 0).astype(F32)
    freq = (lane % (ROTARY // 2)).astype(F32)
    angle = place * jnp.exp(freq * (-2.0 * math.log(10000.0) / ROTARY))
    turns = lane < ROTARY
    cosine = jnp.where(turns, jnp.cos(angle), 1.0)
    sine = jnp.where(turns, jnp.sin(angle), 0.0)
    return cosine, jnp.where(lane < ROTARY // 2, -sine, sine)


def body(
    tokens,
    ln_gain,
    ln_shift,
    qkv_weight,
    qkv_bias,
    dense_weight,
    dense_bias,
    fc1_weight,
    fc1_bias,
    fc2_weight,
    fc2_bias,
    cotangent,
):
    rep, shard = lax.axis_index("rep"), lax.axis_index("shard")
    xh, y = rep // 4, rep % 4
    z, xl, c = shard // 4, (shard // 2) % 2, shard % 2
    token_place = jnp.stack(
        [((z + dz) % 4) * 4 + (xl ^ dx) * 2 + (c ^ dc) for dz, dx, dc in SLOTS]
    ).astype(jnp.int32)
    row_place = jnp.stack(
        [((z + y + dy) % 4) * 4 + (xl ^ dx) * 2 + (c ^ dc) for dy, dx, dc in SLOTS]
    ).astype(jnp.int32)
    col_place = jnp.stack(
        [((z - y - dy) % 4) * 4 + (xl ^ dx) * 2 + (c ^ dc) for dy, dx, dc in SLOTS]
    ).astype(jnp.int32)
    part_place = jnp.stack(
        [((y + dy) % 4) * 2 + dx for dy in range(4) for dx in range(2)]
    ).astype(jnp.int32)
    chip_order, part_order = in_order(row_place, part_place)
    me, core = shard.reshape(1).astype(jnp.int32), c.reshape(1).astype(jnp.int32)

    vectors = [v.reshape(-1, T) for v in (qkv_bias, ln_gain, ln_shift, dense_bias, fc2_bias)]
    vectors = jnp.concatenate(vectors + [jnp.zeros((T - 7, T), BF)])
    message = jnp.concatenate([tokens, cotangent, vectors], axis=1)
    near = gather_near(message)

    def columns_for(chip):
        qkv = [
            lax.dynamic_slice(qkv_weight, (0, part * D + chip * 2 * T), (T, 2 * T))
            for part in range(3)
        ]
        fc1 = lax.dynamic_slice(fc1_weight, (0, chip * 2 * FFL), (T, 2 * FFL))
        return jnp.concatenate(
            [
                jnp.concatenate(
                    [p[:, at * T : (at + 1) * T] for p in qkv]
                    + [fc1[:, at * FFL : (at + 1) * FFL]],
                    axis=1,
                )
                for at in range(2)
            ]
        )

    to_chip = ((z - y) % 4) * 2 + xl
    mine, other = columns_for(to_chip ^ c), columns_for(to_chip ^ c ^ 1)
    other = fetch(other, dc=1)
    rows = fetch_from(
        jnp.concatenate([mine, other]), lambda xh, y, z, xl, c: (xh, y, z + y, xl ^ c, c)
    )
    own_pair = message, gather_swap(message)
    cosine, sine = rotary_tables()
    rows, near[1, 0], near[0, 1] = together(
        rows, near[1, 0], near[0, 1], also=(near[3, 0], own_pair, cosine, sine)
    )

    def columns_of(rows, core):
        return jnp.concatenate(
            [
                lax.dynamic_slice(rows, (n * 2 * T + core * T, 0), (T, COLS))
                for n in range(2)
            ]
        )

    mine = columns_of(rows, c)
    other = fetch(columns_of(rows, 1 - c), dc=1)
    here = jnp.where(c == 0, mine, jnp.concatenate([other[T:], other[:T]]))
    there = jnp.where(c == 0, jnp.concatenate([other[T:], other[:T]]), mine)
    own_rows = jnp.concatenate([here, there])
    further = gather_next(near)
    one, three = fetch(own_rows, dy=1), fetch(own_rows, dy=-1)
    one, three, further, near, far_vectors = together(one, three, further, near, vectors[:16])
    far_vectors = fetch(far_vectors, dz=2, dx=1)
    near_pairs = near | {(0, 0): own_pair}
    far_vectors = jnp.concatenate([far_vectors, fetch(far_vectors, dc=1)])
    far = gather_far(further)
    two = fetch(one, dy=1)
    pieces = both_cores(near_pairs) + both_cores(further)
    vecs, own_qkv_bias = group_vectors(pieces, far_vectors, token_place, me)
    *arrays, done = chip_rows(pieces, vecs, fc2_weight, dense_weight, [], [one, three])
    (far,) = together(far, also=(two, done))
    far = [(far, 10 * T), (gather_swap(far), 11 * T)]
    normed, all_cot, act_grad, attended_grad, _ = chip_rows(
        far, vecs, fc2_weight, dense_weight, arrays, []
    )
    gain, out_bias = vecs[0:1], vecs[2:3]
    (activated, pre_grad, act_t, pre_t, mixed, fc1_bias_part, out_bias_part, weight) = (
        forward_inputs(
            normed,
            all_cot,
            act_grad,
            (own_rows, one, two, three),
            fc1_bias.astype(F32).reshape(1, FFL),
            own_qkv_bias,
            row_place,
            me,
        )
    )

    early = column_grads(normed, pre_t, act_t, all_cot, chip_order, part_order, core)
    *state, done = attention_first(token_place, cosine, sine, mixed, attended_grad, early)
    early_near = reduce_near(early, reduce_far(early), done[0, 0].astype(F32))
    attended, mixed_grad, attended_t, mixed_t, qkv_bias_part = attention_last(
        token_place, cosine, sine, state, early_near
    )
    early = early[0], fetch(early_near[0], dy=-1), fetch(early_near[1], dy=1)
    early = [add(*(e[dx * FFL : (dx + 1) * FFL] for e in early)).astype(BF) for dx in range(2)]
    early_other = [fetch(e, dh=1) for e in early]

    def the_terms(chips, sums, before):
        mine, other, *sums = terms(
            chips,
            attended,
            activated,
            dense_weight,
            fc2_weight,
            mixed_grad,
            pre_grad,
            weight,
            normed,
            vecs,
            sums,
            before,
        )
        return mine, fetch(other, dc=1), sums

    def own_terms(chips, mine, other, zero):
        return {
            chip: add(mine[n * T : (n + 1) * T], other[n * T : (n + 1) * T], zero).astype(BF)
            for n, chip in enumerate(chips)
        }

    mine0, other0, sums = the_terms(WAVES[0], [], early)
    mine1, other1, sums = the_terms(WAVES[1], sums, [])
    q = own_terms(WAVES[0], mine0, other0, zero_of(sums[0]))
    far = scatter_far(q)
    mine2, other2, sums = the_terms(WAVES[2], sums, [q[2, 1], early_other[0]])
    early_other, sums = together(early_other, sums)

    def from_owners(rows):
        return [
            fetch_from(rows[dx], lambda xh, y, z, xl, c: (xh, y, z - y, xl ^ dx, c))
            for dx in range(2)
        ]

    early = jnp.concatenate(
        [add(e, other).astype(BF) for e, other in zip(early, early_other, strict=True)]
    )
    early_own = jnp.concatenate([early[:, :T], fetch(early[:, T : 2 * T], dc=1)], axis=1)
    early_own = from_owners([early_own[:FFL], early_own[FFL:]])
    late = head_grads(
        normed,
        mixed_t,
        attended_t,
        all_cot,
        chip_order,
        part_order,
        core,
        me,
        gain,
        sums,
        (qkv_bias_part, fc1_bias_part, out_bias_part),
        [],
    )
    late_far = reduce_far(late)
    q |= own_terms(WAVES[1], mine1, other1, 0.0)
    q, early_own, late_far, far = together(q, early_own, late_far, far, also=(other2, late))

    further = scatter_next(q, far, 0.0)
    late_near = reduce_near(late, late_far, 0.0)
    late_near = fetch(late_near[0], dy=-1), fetch(late_near[1], dy=1)
    q |= own_terms(WAVES[2], mine2, other2, 0.0)
    q, further, late_near = together(q, further, late_near)

    nearest = scatter_near(q, further, 0.0)
    early = jnp.concatenate(
        [
            jnp.concatenate([early_own[dx], early[dx * FFL : (dx + 1) * FFL, 2 * T :]], axis=1)
            for dx in range(2)
        ]
    )
    early_one, early_three = fetch(early, dy=1), fetch(early, dy=-1)
    late = add(late[0], *late_near).astype(BF)
    early_one, early_three, late = together(early_one, early_three, late, also=nearest)
    late_other = fetch(late, dh=1)

    early = (
        early,
        early_one,
        early_three,
        fetch(early_one[:FFL], dy=1),
        fetch(early_three[FFL:], dy=-1),
    )
    late = add(late, late_other).astype(BF)
    late_rows = jnp.concatenate([late[:FOR_OWNER], late[LATE : LATE + FOR_OWNER]])
    late_own = jnp.concatenate([late_rows[:, :T], fetch(late_rows[:, T:], dc=1)], axis=1)
    late_own = from_owners([late_own[:FOR_OWNER], late_own[FOR_OWNER:]])
    late = jnp.concatenate(
        [late_own[0], late[FOR_OWNER:LATE], late_own[1], late[LATE + FOR_OWNER :]]
    )
    late_one, late_three = fetch(late, dy=1), fetch(late, dy=-1)
    total = add(q[0, 0], *nearest)
    own = tokens.astype(F32)
    layer_out = (own + out_bias + total[:, D:]).astype(BF)
    center = own - jnp.mean(own, axis=-1, keepdims=True)
    inv_std = lax.rsqrt(jnp.mean(center * center, axis=-1, keepdims=True) + 1e-05)
    unit = center * inv_std
    scaled = total[:, :D] * gain
    input_grad = cotangent.astype(F32) + inv_std * (
        scaled
        - jnp.mean(scaled, axis=-1, keepdims=True)
        - unit * jnp.mean(scaled * unit, axis=-1, keepdims=True)
    )
    late = (
        late,
        late_one,
        late_three,
        fetch(late_one[:LATE], dy=1),
        fetch(late_three[LATE:], dy=-1),
    )
    fc1_total, fc2_total = place_columns(early, col_place, part_place)
    qkv_total, dense_total, of_owner, of_own = place_heads(late, col_place, part_place)
    out_bias_total = of_own[0, FFL : FFL + T]

    return (
        layer_out,
        input_grad,
        of_owner[0],
        of_owner[1],
        qkv_total,
        of_owner[2:5].reshape(QKV),
        dense_total,
        out_bias_total,
        fc1_total,
        of_own[0, :FFL],
        fc2_total,
        out_bias_total,
    )


def solution(mesh):
    return jax.shard_map(
        body,
        mesh=mesh,
        in_specs=(
            P(AXES, None),
            P("shard"),
            P("shard"),
            P("shard", None),
            P("shard"),
            P("shard", None),
            P("shard"),
            P("shard", None),
            P("shard"),
            P("shard", None),
            P("shard"),
            P(AXES, None),
        ),
        out_specs=(
            P(AXES, None),
            P(AXES, None),
            P("shard"),
            P("shard"),
            P("shard", None),
            P("shard"),
            P("shard", None),
            P("shard"),
            P("shard", None),
            P("shard"),
            P("shard", None),
            P("shard"),
        ),
        check_vma=False,
    )
```

```python
import functools
import math

import jax
import jax.numpy as jnp
from jax import lax
from jax.experimental import pallas as pl
from jax.experimental.pallas import tpu as pltpu
from jax.sharding import PartitionSpec as P

D = 2048
HEADS = 32
HEAD_DIM = 64
ROTARY = 32
FF = 8192
SEQ = 2048
T = 128
QKV = 384
FFL = 512
COLS = QKV + FFL
BF = jnp.bfloat16
F32 = jnp.float32
AXES = ("rep", "shard")
MIB = 1 << 20
LOG2E = math.log2(math.e)

PLACES = [
    (xh, y, z, xl, c)
    for xh in range(2)
    for y in range(4)
    for z in range(4)
    for xl in range(2)
    for c in range(2)
]


def flat(xh, y, z, xl, c):
    return (xh * 4 + y % 4) * 16 + (z % 4) * 4 + xl * 2 + c


def fetch_from(x, source):
    return lax.ppermute(x, AXES, [(flat(*source(*p)), flat(*p)) for p in PLACES])


def fetch(x, dz=0, dx=0, dc=0, dy=0, dh=0):
    return fetch_from(
        x, lambda xh, y, z, xl, c: (xh ^ dh, y + dy, z + dz, xl ^ dx, c ^ dc)
    )


def dot(a, b, ca=1, cb=0):
    return lax.dot_general(a, b, (((ca,), (cb,)), ((), ())), preferred_element_type=F32)


def add(*terms):
    total = terms[0].astype(F32)
    for term in terms[1:]:
        total = total + (term if isinstance(term, float) else term.astype(F32))
    return total


def zero_of(x):
    return x[0, 0].astype(F32) * 0.0


def together(*groups, also=()):
    leaves, tree = jax.tree.flatten(groups)
    others = jax.tree.leaves(also)
    n = len(leaves)
    leaves = pl.pallas_call(
        lambda *refs: None,
        in_specs=[pl.BlockSpec(memory_space=pl.ANY)] * (n + len(others)),
        out_specs=[pl.BlockSpec(memory_space=pl.ANY)] * n,
        out_shape=[jax.ShapeDtypeStruct(x.shape, x.dtype) for x in leaves],
        input_output_aliases={i: i for i in range(n)},
        compiler_params=pltpu.CompilerParams(vmem_limit_bytes=MIB),
    )(*leaves, *others)
    return jax.tree.unflatten(tree, leaves)


def gather_near(own):
    return {
        (0, 0): own,
        (1, 0): fetch(own, dz=1),
        (3, 0): fetch(own, dz=-1),
        (0, 1): fetch(own, dx=1),
    }


def gather_next(a):
    return {
        (1, 1): fetch(a[1, 0], dx=1),
        (3, 1): fetch(a[0, 1], dz=-1),
        (2, 0): fetch(a[1, 0], dz=1),
    }


def gather_far(a):
    return fetch(a[2, 0], dx=1)


def gather_swap(own):
    return fetch(own, dc=1)


def both_cores(a):
    pieces = []
    for (dz, dx), own in a.items():
        pair = own if isinstance(own, tuple) else (own, gather_swap(own))
        pieces += [(pair[dc], ((dz * 2 + dx) * 2 + dc) * T) for dc in range(2)]
    return pieces


SLOTS = [(dz, dx, dc) for dz in range(4) for dx in range(2) for dc in range(2)]
WAVES = [[(2, 1)], [(1, 1), (3, 1), (2, 0)], [(1, 0), (3, 0)], [(0, 1), (0, 0)]]


def scatter_far(q):
    half = T // 2
    return fetch(q[2, 1][:half], dz=-1), fetch(q[2, 1][half:], dz=1)


def scatter_next(q, far):
    half = T // 2
    q11 = jnp.concatenate([add(q[1, 1][:half], far[0]).astype(BF), q[1, 1][half:]])
    q31 = jnp.concatenate([q[3, 1][:half], add(q[3, 1][half:], far[1]).astype(BF)])
    zero = zero_of(q11) + zero_of(q31)
    return fetch(q[2, 0], dz=-1), fetch(q31, dz=1), fetch(q11, dx=1), zero


def scatter_near(q, further, zero):
    q10 = add(q[1, 0], further[0], further[2], zero).astype(BF)
    q01 = add(q[0, 1], further[1], zero).astype(BF)
    return fetch(q10, dz=-1), fetch(q[3, 0], dz=1), fetch(q01, dx=1)


def reduce_far(g):
    half = g[0].shape[0] // 2
    return fetch(g[2][:half], dy=-1), fetch(g[2][half:], dy=1)


def reduce_near(g, far, zero):
    half = g[0].shape[0] // 2
    g1 = jnp.concatenate([add(g[1][:half], far[0], zero).astype(BF), g[1][half:]])
    g3 = jnp.concatenate([g[3][:half], add(g[3][half:], far[1], zero).astype(BF)])
    return g1, g3


def of_rep(refs, dy, dx, n):
    own, one, three, first, second = refs
    if dy == 2:
        return (second if dx else first), 0
    return (own, one, None, three)[dy], dx * n


VMEM = pl.BlockSpec(memory_space=pltpu.VMEM)
SMEM = pl.BlockSpec(memory_space=pltpu.SMEM)
HBM = pl.BlockSpec(memory_space=pltpu.HBM)
ANY = pl.BlockSpec(memory_space=pl.ANY)


def lanes(at, n):
    return pl.ds(pl.multiple_of(at * n, n), n)


def call(kernel, ins, outs, args, scratch=(), vmem=6, flops=0, nbytes=0, exps=0, aliases={}, out_specs=None):
    return pl.pallas_call(
        kernel,
        in_specs=ins,
        out_specs=out_specs or [VMEM] * len(outs),
        out_shape=[
            pltpu.VMEM(o[0], o[1]) if len(o) > 2 else jax.ShapeDtypeStruct(*o) for o in outs
        ],
        scratch_shapes=list(scratch),
        input_output_aliases=aliases,
        compiler_params=pltpu.CompilerParams(vmem_limit_bytes=vmem * MIB),
        cost_estimate=pl.CostEstimate(
            flops=flops, transcendentals=exps, bytes_accessed=nbytes
        ),
    )(*args)


ROOT = math.sqrt(2.0 / math.pi)


def start_copies(pieces, place, sems):
    copies = [
        pltpu.make_async_copy(src, dst, sems.at[place + i]) for i, (src, dst) in enumerate(pieces)
    ]
    for copy in copies:
        copy.start()
    return copies


def norm_rows(normed_ref, gain, shift, first, count):
    def strip(i, _):
        at = lanes(i, 64)
        x = normed_ref[at, :].astype(F32)
        x = x - jnp.sum(x, axis=1, keepdims=True) * (1.0 / D)
        scale = lax.rsqrt(jnp.sum(x * x, axis=1, keepdims=True) * (1.0 / D) + 1e-05)
        normed_ref[at, :] = (x * scale * gain + shift).astype(BF)
        return 0

    lax.fori_loop(first // 64, (first + count) // 64, strip, 0)


def grid_call(kernel, prefetch, grid, ins, outs, args, scratch=(), vmem=32, flops=0, nbytes=0):
    return pl.pallas_call(
        kernel,
        grid_spec=pltpu.PrefetchScalarGridSpec(
            num_scalar_prefetch=len(prefetch),
            grid=grid,
            in_specs=ins,
            out_specs=[o[2] for o in outs],
            scratch_shapes=list(scratch),
        ),
        out_shape=[jax.ShapeDtypeStruct(o[0], o[1]) for o in outs],
        compiler_params=pltpu.CompilerParams(vmem_limit_bytes=vmem * MIB),
        cost_estimate=pl.CostEstimate(flops=flops, transcendentals=0, bytes_accessed=nbytes),
    )(*prefetch, *args)


def whole(*shape):
    return pl.BlockSpec(shape, lambda *_: (0,) * len(shape))


def group_vectors(pieces, far_vectors, token_place, me):
    n = len(pieces)

    def kernel(t_ref, me_ref, *refs):
        far_ref, vec_ref, own_ref, small_ref, flat_ref, sems = refs[n:]
        moves = [
            (ref.at[pl.ds(0, 16), pl.ds(2 * D, T)], small_ref.at[pl.ds(at // T * 16, 16)])
            for (_, at), ref in zip(pieces, refs[:n], strict=True)
        ]
        for dc in range(2):
            to = small_ref.at[pl.ds((5 * 2 + dc) * 16, 16)]
            moves.append((far_ref.at[pl.ds(dc * 16, 16)], to))
        for copy in start_copies(moves, 0, sems):
            copy.wait()
        for i in range(16):
            at = t_ref[i]
            small = small_ref[i * 16 : (i + 1) * 16, :].astype(F32)
            for part in range(3):
                flat_ref[0:1, lanes(at * 3 + part, T)] = small[part : part + 1]
            vec_ref[0:1, lanes(at, T)] = small[3:4]
            vec_ref[1:2, lanes(at, T)] = small[4:5]
            vec_ref[2:3, lanes(at, T)] = small[5:6] + small[6:7]
        for part in range(3):
            own_ref[0:1, part * T : (part + 1) * T] = flat_ref[
                0:1, lanes(part * 16 + me_ref[0], T)
            ]

    return call(
        kernel,
        [SMEM] * 2 + [HBM] * (n + 1),
        [((8, D), F32), ((1, QKV), F32)],
        [token_place, me] + [p for p, _ in pieces] + [far_vectors],
        [
            pltpu.VMEM((256, T), BF),
            pltpu.VMEM((1, 3 * D), F32),
            pltpu.SemaphoreType.DMA((n + 2,)),
        ],
        vmem=56,
    )


def chip_rows(pieces, vecs, fc2, dense, arrays, before):
    n, given = len(pieces), len(arrays)
    chips = sorted({at // 256 for _, at in pieces})

    def kernel(*refs):
        refs = refs[len(before) + given :]
        tok = refs[:n]
        vec_ref, fc2_ref, dense_ref = refs[n : n + 3]
        outs, done_ref = refs[n + 3 : n + 7], refs[n + 7]
        bufs, in_sems, out_sems = refs[n + 8 : n + 12], refs[n + 12], refs[n + 13]
        done_ref[...] = jnp.zeros_like(done_ref)

        def arriving(k):
            moves = []
            for (array, at), ref in zip(pieces, tok, strict=True):
                if at // 256 == chips[k]:
                    to = pl.ds(at % 256, array.shape[0])
                    moves.append((ref.at[:, pl.ds(0, D)], bufs[0].at[k % 3, to]))
                    moves.append((ref.at[:, pl.ds(D, D)], bufs[1].at[k % 3, to]))
            return [
                pltpu.make_async_copy(src, dst, in_sems.at[k % 3, i])
                for i, (src, dst) in enumerate(moves)
            ]

        def leaving(k):
            rows = pl.ds(chips[k] * 256, 256)
            return [
                pltpu.make_async_copy(buf.at[k % 3], out.at[rows], out_sems.at[k % 3, i])
                for i, (buf, out) in enumerate(zip(bufs, outs, strict=True))
            ]

        for copy in arriving(0):
            copy.start()
        for k in range(len(chips)):
            if k + 1 < len(chips):
                if k >= 2:
                    for copy in leaving(k - 2):
                        copy.wait()
                for copy in arriving(k + 1):
                    copy.start()
            for copy in arriving(k):
                copy.wait()
            norm_rows(bufs[0].at[k % 3], vec_ref[0:1, :], vec_ref[1:2, :], 0, 256)
            x = bufs[1][k % 3]
            bufs[2][k % 3] = dot(x, fc2_ref[...], 1, 1).astype(BF)
            bufs[3][k % 3] = dot(x, dense_ref[...], 1, 1).astype(BF)
            for copy in leaving(k):
                copy.start()
        for k in range(max(len(chips) - 3, 0), len(chips)):
            for copy in leaving(k):
                copy.wait()

    widths = (D, D, FFL, T)
    return call(
        kernel,
        [ANY] * (len(before) + given) + [HBM] * n + [VMEM] * 3,
        [((SEQ, w), BF) for w in widths] + [((8, T), F32)],
        [*before, *arrays, *[p for p, _ in pieces], vecs, fc2, dense],
        [pltpu.VMEM((3, 256, w), BF) for w in widths]
        + [pltpu.SemaphoreType.DMA((3, 8)), pltpu.SemaphoreType.DMA((3, 4))],
        vmem=56,
        aliases={len(before) + i: i for i in range(given)},
        out_specs=[ANY] * 4 + [VMEM],
        flops=2 * n * T * D * (FFL + T),
        nbytes=n * MIB,
    )


def forward_inputs(normed, cot, act_grad, weights, bias, own_bias, row_place, me):
    def kernel(
        r_ref,
        me_ref,
        n_ref,
        grad_ref,
        cot_ref,
        w0_ref,
        w1_ref,
        w2_ref,
        w3_ref,
        bias_ref,
        own_ref,
        act_ref,
        pre_ref,
        act_t_ref,
        pre_t_ref,
        mixed_ref,
        fc1b_ref,
        outb_ref,
        w_out,
        w_ref,
        sems,
        out_sem,
    ):
        step = pl.program_id(0)
        leaving = pltpu.make_async_copy(w_ref, w_out, out_sem.at[0])

        @pl.when(step == 0)
        def _():
            moves = []
            for i, (dy, dx, dc) in enumerate(SLOTS):
                rows = pl.ds((dx * 2 + dc) * T, T)
                source = (w0_ref, w1_ref, w2_ref, w3_ref)[dy]
                moves.append((source.at[rows], w_ref.at[lanes(r_ref[i], T)]))
            for copy in start_copies(moves, 0, sems):
                copy.wait()
            leaving.start()
            fc1b_ref[...] = jnp.zeros_like(fc1b_ref)
            outb_ref[...] = jnp.zeros_like(outb_ref)

        halves = []
        for half in range(2):
            x = n_ref[half * 256 : (half + 1) * 256, :]
            mixed_ref[half * 256 : (half + 1) * 256, :] = dot(x, w_ref[:, :QKV]) + own_ref[...]
            halves.append(dot(x, w_ref[:, QKV:]) + bias_ref[...])
        for half, pre in enumerate(halves):
            at = slice(half * 256, (half + 1) * 256)
            squared = pre * pre
            tanh = jnp.tanh(ROOT * pre * (1.0 + 0.044715 * squared))
            act = (0.5 * pre * (1.0 + tanh)).astype(BF)
            act_ref[at, :] = act
            act_t_ref[:, at] = act.T
            slope = 0.5 * (1.0 + tanh) + 0.5 * pre * (1.0 - tanh * tanh) * ROOT * (
                1.0 + 3 * 0.044715 * squared
            )
            back = (grad_ref[at, :].astype(F32) * slope).astype(BF)
            pre_ref[at, :] = back
            pre_t_ref[:, at] = back.T
            fc1b_ref[...] += jnp.sum(back.astype(F32).reshape(32, 8, FFL), axis=0)
        outb_ref[...] += jnp.sum(cot_ref[...].astype(F32).reshape(64, 8, T), axis=0)

        @pl.when(step == pl.num_programs(0) - 1)
        def _():
            leaving.wait()

    rows = lambda i, *_: (i, 0)
    cols = lambda i, *_: (0, i)
    return grid_call(
        kernel,
        [row_place, me],
        (SEQ // 512,),
        [
            pl.BlockSpec((512, D), rows),
            pl.BlockSpec((512, FFL), rows),
            pl.BlockSpec((512, T), lambda i, r, m: (i, m[0])),
        ]
        + [HBM] * 4
        + [whole(1, FFL), whole(1, QKV)],
        [
            ((SEQ, FFL), BF, pl.BlockSpec((512, FFL), rows)),
            ((SEQ, FFL), BF, pl.BlockSpec((512, FFL), rows)),
            ((FFL, SEQ), BF, pl.BlockSpec((FFL, 512), cols)),
            ((FFL, SEQ), BF, pl.BlockSpec((FFL, 512), cols)),
            ((SEQ, QKV), F32, pl.BlockSpec((512, QKV), rows)),
            ((8, FFL), F32, whole(8, FFL)),
            ((8, T), F32, whole(8, T)),
            ((D, COLS), BF, ANY),
        ],
        [normed, act_grad, cot, *weights, bias, own_bias],
        [
            pltpu.VMEM((D, COLS), BF),
            pltpu.SemaphoreType.DMA((16,)),
            pltpu.SemaphoreType.DMA((1,)),
        ],
        vmem=56,
        flops=2 * SEQ * D * COLS,
        nbytes=24 * MIB,
    )


ORDER = (2, 1, 3, 0)


def in_order(places, parts):
    chips = jnp.stack([places[(dy * 2 + dx) * 2] // 2 for dy in ORDER for dx in range(2)])
    return chips, jnp.stack([parts[dy * 2 + dx] for dy in ORDER for dx in range(2)])


def fetched(refs, scratch, sems):
    copies = [
        pltpu.make_async_copy(ref, to, sems.at[i])
        for i, (ref, to) in enumerate(zip(refs, scratch, strict=True))
    ]
    for copy in copies:
        copy.start()
    return copies


def column_grads(normed, pre_t, act_t, cot, chips, parts, core):
    def kernel(chip_ref, part_ref, core_ref, normed_ref, cot_ref, g_ref, a_ref, *refs):
        outs, n_ref, c_ref, sems = refs[:4], refs[4], refs[5], refs[6]
        copies = fetched((normed_ref, cot_ref), (n_ref, c_ref), sems)
        copies[0].wait()
        for i in range(8):
            out, at = outs[i // 2], slice(i % 2 * FFL, (i % 2 + 1) * FFL)
            cols = dot(g_ref[...], n_ref[:, lanes(chip_ref[i], 256)]).astype(BF)
            out[at, lanes(core_ref[0], T)] = cols[:, :T]
            out[at, lanes(1 - core_ref[0], T)] = cols[:, T:]
        copies[1].wait()
        for i in range(8):
            out, at = outs[i // 2], slice(i % 2 * FFL, (i % 2 + 1) * FFL)
            out[at, 256:512] = dot(a_ref[...], c_ref[:, lanes(part_ref[i], 256)]).astype(BF)

    outs = call(
        kernel,
        [SMEM] * 3 + [ANY] * 2 + [VMEM] * 2,
        [((2 * FFL, 512), BF)] * 4,
        [chips, parts, core, normed, cot, pre_t, act_t],
        [pltpu.VMEM((SEQ, D), BF), pltpu.VMEM((SEQ, D), BF), pltpu.SemaphoreType.DMA((2,))],
        vmem=56,
        flops=4 * SEQ * D * FFL,
        nbytes=24 * MIB,
    )
    return [outs[ORDER.index(dy)] for dy in range(4)]


FOR_OWNER = QKV + 16
LATE = FOR_OWNER + T + 16


def head_grads(
    normed, mixed_t, attended_t, cot, chips, parts, core, me, gain, sums, bias_parts
):
    def kernel(chip_ref, part_ref, core_ref, me_ref, normed_ref, cot_ref, m_ref, a_ref, *refs):
        gain_ref, gains_ref, shifts_ref, qkvb_ref, fc1b_ref, outb_ref = refs[:6]
        outs, owners_ref, own_ref = refs[6:10], refs[10], refs[11]
        n_ref, c_ref, sems = refs[12:]
        copies = fetched((normed_ref, cot_ref), (n_ref, c_ref), sems)
        owners_ref[...] = jnp.zeros_like(owners_ref)
        owners_ref[0:1, :] = jnp.sum(gains_ref[...], axis=0, keepdims=True) / gain_ref[...]
        owners_ref[1:2, :] = jnp.sum(shifts_ref[...], axis=0, keepdims=True)
        qkvb = jnp.sum(qkvb_ref[...], axis=0, keepdims=True)
        for part in range(3):
            at = part * 16 + me_ref[0]
            third = at % 3
            row = lax.broadcasted_iota(jnp.int32, (8, T), 0)
            value = jnp.where(row == 2 + third, qkvb[:, part * T : (part + 1) * T], 0.0)
            owners_ref[0:8, lanes(at // 3, T)] += value
        own_ref[...] = jnp.zeros_like(own_ref)
        own_ref[0:1, :FFL] = jnp.sum(fc1b_ref[...], axis=0, keepdims=True)
        own_ref[0:1, FFL : FFL + T] = jnp.sum(outb_ref[...], axis=0, keepdims=True)
        mine, other = lanes(core_ref[0], T), lanes(1 - core_ref[0], T)
        copies[0].wait()
        for i in range(8):
            out, base = outs[i // 2], i % 2 * LATE
            cols = dot(m_ref[...], n_ref[:, lanes(chip_ref[i], 256)]).astype(BF)
            extra = owners_ref[:, lanes(chip_ref[i], 256)].astype(BF)
            out[base : base + QKV, mine] = cols[:, :T]
            out[base : base + QKV, other] = cols[:, T:]
            out[base + QKV : base + FOR_OWNER, mine] = extra[:, :T]
            out[base + QKV : base + FOR_OWNER, other] = extra[:, T:]
        copies[1].wait()
        for i in range(8):
            out, base = outs[i // 2], i % 2 * LATE + FOR_OWNER
            part = part_ref[i]
            out[base : base + T, :] = dot(a_ref[...], c_ref[:, lanes(part, 256)]).astype(BF)
            out[base + T : base + T + 16, 0:T] = own_ref[:, lanes(part, T)].astype(BF)
            out[base + T : base + T + 16, T:] = jnp.zeros((16, T), BF)

    outs = call(
        kernel,
        [SMEM] * 4 + [ANY] * 2 + [VMEM] * 8,
        [((2 * LATE, 256), BF)] * 4,
        [chips, parts, core, me, normed, cot, mixed_t, attended_t, gain, *sums, *bias_parts],
        [
            pltpu.VMEM((16, D), F32),
            pltpu.VMEM((16, 1024), F32),
            pltpu.VMEM((SEQ, D), BF),
            pltpu.VMEM((SEQ, D), BF),
            pltpu.SemaphoreType.DMA((2,)),
        ],
        vmem=36,
        flops=2 * SEQ * D * (QKV + T),
        nbytes=20 * MIB,
    )
    return [outs[ORDER.index(dy)] for dy in range(4)]


def place_columns(pieces, col_place, part_place):
    def kernel(c_ref, p_ref, *refs):
        fc1_ref, fc2_ref = refs[5:]
        for i, (dy, dh, dc) in enumerate(SLOTS):
            ref, at = of_rep(refs[:5], dy, dh, FFL)
            part = ref[at : at + FFL, dc * T : (dc + 1) * T]
            fc1_ref[:, lanes(c_ref[i], FFL)] = part.astype(F32).T
            if dc == 0:
                to = lanes(p_ref[dy * 2 + dh], 256)
                fc2_ref[:, to] = ref[at : at + FFL, 256:512].astype(F32)

    return call(
        kernel,
        [SMEM] * 2 + [VMEM] * 5,
        [((T, FF), F32), ((FFL, D), F32)],
        [col_place, part_place] + list(pieces),
        vmem=20,
        nbytes=12 * MIB,
    )


def place_heads(pieces, col_place, part_place):
    def kernel(c_ref, p_ref, *refs):
        qkv_ref, dense_ref, owner_ref, own_ref = refs[5:]
        total = jnp.zeros((16, T), F32)
        for i, (dy, dx, dc) in enumerate(SLOTS):
            ref, at = of_rep(refs[:5], dy, dx, LATE)
            cols = slice(dc * T, (dc + 1) * T)
            for part in range(3):
                block = ref[at + part * T : at + (part + 1) * T, cols].astype(F32)
                qkv_ref[:, lanes(c_ref[i] + part * 16, T)] = block.T
            total += ref[at + QKV : at + FOR_OWNER, cols].astype(F32)
            if dc == 0:
                part = p_ref[dy * 2 + dx]
                rows = slice(at + FOR_OWNER, at + FOR_OWNER + T)
                dense_ref[:, lanes(part, 256)] = ref[rows, :].astype(F32)
                rows = slice(at + FOR_OWNER + T, at + LATE)
                own_ref[:, lanes(part, T)] = ref[rows, 0:T].astype(F32)
        owner_ref[...] = total

    return call(
        kernel,
        [SMEM] * 2 + [VMEM] * 5,
        [((T, 3 * D), F32), ((T, D), F32), ((16, T), F32), ((16, 1024), F32)],
        [col_place, part_place] + list(pieces),
        vmem=14,
        nbytes=6 * MIB,
    )


def terms(
    chips, attended, activated, dense, fc2, mixed_grad, pre_grad, weight, normed, vecs, sums, before
):
    n = len(chips)
    order = jnp.array([dz * 2 + dx for dz, dx in chips], jnp.int32)

    def kernel(order_ref, a_ref, f_ref, m_ref, p_ref, n_ref, d_ref, v_ref, w_ref, vec_ref, *refs):
        mine_ref, other_ref, gain_ref, total_ref = refs[-4:]
        shift = vec_ref[1:2, :]

        @pl.when(pl.program_id(0) == 0)
        def _():
            if sums:
                gain_ref[...] = refs[0][...]
                total_ref[...] = refs[1][...]
            else:
                gain_ref[...] = jnp.zeros_like(gain_ref)
                total_ref[...] = jnp.zeros_like(total_ref)

        for col in range(4):
            to = slice(col * 512, (col + 1) * 512)
            total = dot(m_ref[...], w_ref[to, :QKV], 1, 1) + dot(p_ref[...], w_ref[to, QKV:], 1, 1)
            mine_ref[:, to] = total[:T].astype(BF)
            other_ref[:, to] = total[T:].astype(BF)
            unit = n_ref[:, to].astype(F32) - shift[:, to]
            gain_ref[:, to] += jnp.sum((total * unit).reshape(32, 8, 512), axis=0)
            total_ref[:, to] += jnp.sum(total.reshape(32, 8, 512), axis=0)
            total = dot(a_ref[...], d_ref[:, to]) + dot(f_ref[...], v_ref[:, to])
            to = slice(D + col * 512, D + (col + 1) * 512)
            mine_ref[:, to] = total[:T].astype(BF)
            other_ref[:, to] = total[T:].astype(BF)

    rows = lambda i, order_ref: (order_ref[i], 0)
    here = lambda i, order_ref: (i, 0)
    return grid_call(
        kernel,
        [order],
        (n,),
        [
            pl.BlockSpec((2 * T, T), rows),
            pl.BlockSpec((2 * T, FFL), rows),
            pl.BlockSpec((2 * T, QKV), rows),
            pl.BlockSpec((2 * T, FFL), rows),
            pl.BlockSpec((2 * T, D), rows),
            whole(T, D),
            whole(FFL, D),
            whole(D, COLS),
            whole(8, D),
        ]
        + [whole(8, D)] * len(sums)
        + [ANY] * len(before),
        [((n * T, 2 * D), BF, pl.BlockSpec((T, 2 * D), here))] * 2
        + [((8, D), F32, whole(8, D))] * 2,
        [attended, activated, mixed_grad, pre_grad, normed, dense, fc2, weight, vecs, *sums, *before],
        flops=2 * n * 2 * T * (COLS + T + FFL) * D,
        nbytes=8 * MIB,
    )


TQ = 512
TK = 512


def attention_kernel(blocks, last, n_before, place, cos_ref, sin_ref, *refs):
    refs = refs[n_before:]
    if last:
        first_refs, refs = refs[:8], refs[8:]
        att_ref, out_ref, att_t_ref, out_t_ref, bias_ref = refs[:5]
        q_ref, k_ref, v_ref, do_ref = first_refs[:4]
        dq_ref, dk_ref, dv_ref, o_ref, s_ref, e_ref = refs[5:]
    else:
        mixed_ref, grad_ref, *refs = refs
        refs, done_ref = refs[:8] + refs[9:], refs[8]
        done_ref[...] = jnp.zeros_like(done_ref)
        q_ref, k_ref, v_ref, do_ref, dq_ref, dk_ref, dv_ref, o_ref, s_ref, e_ref = refs
    lane = lax.broadcasted_iota(jnp.int32, (T, 128), 1)
    low_head = lane < HEAD_DIM
    first = (lane % HEAD_DIM) < ROTARY // 2

    def turned(x):
        return jnp.where(
            first, pltpu.roll(x, 128 - ROTARY // 2, 1), pltpu.roll(x, ROTARY // 2, 1)
        )

    def load(slot, _):
        rows = pl.ds(pl.multiple_of(slot * T, T), T)
        at = pl.ds(pl.multiple_of(place[slot] * T, T), T)
        c, s = cos_ref[at, :], sin_ref[at, :]
        query = mixed_ref[rows, 0:128]
        key = mixed_ref[rows, 128:256]
        query = (query * c + turned(query) * s).astype(BF).astype(F32) * (HEAD_DIM**-0.5)
        q_ref[0, at, :] = jnp.where(low_head, query, 0.0).astype(BF)
        q_ref[1, at, :] = jnp.where(low_head, 0.0, query).astype(BF)
        k_ref[at, :] = (key * c + turned(key) * s).astype(BF)
        v_ref[at, 0:128] = mixed_ref[rows, 256:384].astype(BF)
        v_ref[at, 128:256] = jnp.ones((T, 128), BF)
        grad = grad_ref[rows, :].astype(F32)
        do_ref[0, at, :] = jnp.where(low_head, grad, 0.0).astype(BF)
        do_ref[1, at, :] = jnp.where(low_head, 0.0, grad).astype(BF)
        dk_ref[:, at] = jnp.zeros((128, T), F32)
        dv_ref[:, at] = jnp.zeros((128, T), F32)
        return 0

    if last:
        for to, at in ((dq_ref, 4), (dk_ref, 5), (dv_ref, 6), (o_ref, 7)):
            to[...] = first_refs[at][...]
    else:
        lax.fori_loop(0, 16, load, 0)

    lane_q = lax.broadcasted_iota(jnp.int32, (TQ, 128), 1)
    low_q = lane_q < HEAD_DIM

    def block(i, _):
        rows = lanes(i, TQ)
        queries = [q_ref[h, rows, :] for h in range(2)]

        def scores(j, tops, masked):
            at = lanes(j, TK)
            keys = k_ref[at, :]
            new = []
            for h in range(2):
                s = dot(queries[h], keys, 1, 1)
                if masked:
                    row = lax.broadcasted_iota(jnp.int32, (TQ, TK), 0)
                    col = lax.broadcasted_iota(jnp.int32, (TQ, TK), 1)
                    s = jnp.where(row >= col, s, -1e30)
                s_ref[h, :, at] = s
                top = tops[h]
                for n in range(TK // 128):
                    top = jnp.maximum(top, s[:, n * 128 : (n + 1) * 128])
                new.append(top)
            return tuple(new)

        low = jnp.full((TQ, 128), -1e30, F32)
        tops = lax.fori_loop(0, i, lambda j, t: scores(j, t, False), (low, low))
        tops = [jnp.max(t, axis=1, keepdims=True) for t in scores(i, tops, True)]

        def weigh(j, totals):
            at = lanes(j, TK)
            values = v_ref[at, :]
            new = []
            for h in range(2):
                e = jnp.exp2((s_ref[h, :, at] - tops[h]) * LOG2E).astype(BF)
                e_ref[h, :, at] = e
                new.append(totals[h] + dot(e, values))
            return tuple(new)

        zero = jnp.zeros((TQ, 256), F32)
        totals = lax.fori_loop(0, i + 1, weigh, (zero, zero))
        outs, grads, deltas = [], [], []
        for h in range(2):
            inverse = 1.0 / totals[h][:, 128:]
            o = totals[h][:, :128] * inverse
            grad = do_ref[h, rows, :].astype(F32) * inverse
            outs.append(o)
            deltas.append(jnp.sum(grad * o, axis=1, keepdims=True))
            grads.append(grad.astype(BF))
        o_ref[rows, :] = jnp.where(low_q, outs[0], outs[1]).astype(BF)
        queries_t = [q.T for q in queries]
        grads_t = [g.T for g in grads]

        def back(j, totals):
            at = lanes(j, TK)
            keys = k_ref[at, :]
            values = v_ref[at, 0:128]
            new, dk, dv = [], None, None
            for h in range(2):
                e = e_ref[h, :, at]
                dp = dot(grads[h], values, 1, 1)
                ds = (e.astype(F32) * (dp - deltas[h])).astype(BF)
                new.append(totals[h] + dot(ds, keys))
                k_part = dot(queries_t[h], ds)
                v_part = dot(grads_t[h], e)
                dk = k_part if dk is None else dk + k_part
                dv = v_part if dv is None else dv + v_part
            dk_ref[:, at] += dk
            dv_ref[:, at] += dv
            return tuple(new)

        zero = jnp.zeros((TQ, 128), F32)
        dqs = lax.fori_loop(0, i + 1, back, (zero, zero))
        dq_ref[rows, :] = jnp.where(low_q, dqs[0], dqs[1]) * (HEAD_DIM**-0.5)
        return 0

    lax.fori_loop(blocks[0], blocks[1], block, 0)
    if not last:
        return

    def store(slot, total):
        rows = pl.ds(pl.multiple_of(slot * T, T), T)
        at = pl.ds(pl.multiple_of(place[slot] * T, T), T)
        c, s = cos_ref[at, :], sin_ref[at, :]
        att = o_ref[at, :]
        att_ref[rows, :] = att
        att_t_ref[:, rows] = att.T
        dq, dk = dq_ref[at, :], dk_ref[:, at].T
        new = []
        for part, grad in enumerate(
            (dq * c - turned(dq) * s, dk * c - turned(dk) * s, dv_ref[:, at].T)
        ):
            low = grad.astype(BF)
            cols = slice(part * T, (part + 1) * T)
            out_ref[rows, cols] = low
            out_t_ref[cols, rows] = low.T
            new.append(total[part] + jnp.sum(low.astype(F32).reshape(16, 8, T), axis=0))
        return tuple(new)

    zero = jnp.zeros((8, T), F32)
    sums = lax.fori_loop(0, 16, store, (zero, zero, zero))
    for part in range(3):
        bias_ref[:, part * T : (part + 1) * T] = sums[part]


def attention_first(place, cosine, sine, mixed, attended_grad, before):
    return call(
        functools.partial(attention_kernel, (0, 2), False, len(before)),
        [SMEM] + [VMEM] * 2 + [ANY] * len(before) + [VMEM] * 2,
        [
            ((2, SEQ, 128), BF, 1),
            ((SEQ, 128), BF, 1),
            ((SEQ, 256), BF, 1),
            ((2, SEQ, 128), BF, 1),
            ((SEQ, 128), F32, 1),
            ((128, SEQ), F32, 1),
            ((128, SEQ), F32, 1),
            ((SEQ, 128), BF, 1),
            ((8, 128), jnp.int32),
        ],
        [place, cosine, sine, *before, mixed, attended_grad],
        [pltpu.VMEM((2, TQ, SEQ), F32), pltpu.VMEM((2, TQ, SEQ), BF)],
        vmem=24,
        flops=8 * SEQ * SEQ * 64 * 2,
        exps=SEQ * SEQ // 2,
        nbytes=3 * MIB,
    )


def attention_last(place, cosine, sine, state, before):
    return call(
        functools.partial(attention_kernel, (2, 4), True, len(before)),
        [SMEM] + [VMEM] * 2 + [ANY] * len(before) + [VMEM] * 8,
        [
            ((SEQ, T), BF),
            ((SEQ, QKV), BF),
            ((T, SEQ), BF),
            ((QKV, SEQ), BF),
            ((8, QKV), F32),
        ],
        [place, cosine, sine, *before] + list(state),
        [
            pltpu.VMEM((SEQ, 128), F32),
            pltpu.VMEM((128, SEQ), F32),
            pltpu.VMEM((128, SEQ), F32),
            pltpu.VMEM((SEQ, 128), BF),
            pltpu.VMEM((2, TQ, SEQ), F32),
            pltpu.VMEM((2, TQ, SEQ), BF),
        ],
        vmem=26,
        flops=6 * SEQ * SEQ * 64 * 2,
        exps=SEQ * SEQ // 2,
        nbytes=3 * MIB,
    )


def rotary_tables():
    lane = lax.broadcasted_iota(jnp.int32, (SEQ, 128), 1) % HEAD_DIM
    place = lax.broadcasted_iota(jnp.int32, (SEQ, 128), 0).astype(F32)
    freq = (lane % (ROTARY // 2)).astype(F32)
    angle = place * jnp.exp(freq * (-2.0 * math.log(10000.0) / ROTARY))
    turns = lane < ROTARY
    cosine = jnp.where(turns, jnp.cos(angle), 1.0)
    sine = jnp.where(turns, jnp.sin(angle), 0.0)
    return cosine, jnp.where(lane < ROTARY // 2, -sine, sine)


def body(
    tokens,
    ln_gain,
    ln_shift,
    qkv_weight,
    qkv_bias,
    dense_weight,
    dense_bias,
    fc1_weight,
    fc1_bias,
    fc2_weight,
    fc2_bias,
    cotangent,
):
    rep, shard = lax.axis_index("rep"), lax.axis_index("shard")
    xh, y = rep // 4, rep % 4
    z, xl, c = shard // 4, (shard // 2) % 2, shard % 2
    token_place = jnp.stack(
        [((z + dz) % 4) * 4 + (xl ^ dx) * 2 + (c ^ dc) for dz, dx, dc in SLOTS]
    ).astype(jnp.int32)
    row_place = jnp.stack(
        [((z + y + dy) % 4) * 4 + (xl ^ dx) * 2 + (c ^ dc) for dy, dx, dc in SLOTS]
    ).astype(jnp.int32)
    col_place = jnp.stack(
        [((z - y - dy) % 4) * 4 + (xl ^ dx) * 2 + (c ^ dc) for dy, dx, dc in SLOTS]
    ).astype(jnp.int32)
    part_place = jnp.stack(
        [((y + dy) % 4) * 2 + dx for dy in range(4) for dx in range(2)]
    ).astype(jnp.int32)
    chip_order, part_order = in_order(row_place, part_place)
    me, core = shard.reshape(1).astype(jnp.int32), c.reshape(1).astype(jnp.int32)

    vectors = [v.reshape(-1, T) for v in (qkv_bias, ln_gain, ln_shift, dense_bias, fc2_bias)]
    vectors = jnp.concatenate(vectors + [jnp.zeros((T - 7, T), BF)])
    message = jnp.concatenate([tokens, cotangent, vectors], axis=1)
    near = gather_near(message)

    def columns_for(chip):
        qkv = [
            lax.dynamic_slice(qkv_weight, (0, part * D + chip * 2 * T), (T, 2 * T))
            for part in range(3)
        ]
        fc1 = lax.dynamic_slice(fc1_weight, (0, chip * 2 * FFL), (T, 2 * FFL))
        return jnp.concatenate(
            [
                jnp.concatenate(
                    [p[:, at * T : (at + 1) * T] for p in qkv]
                    + [fc1[:, at * FFL : (at + 1) * FFL]],
                    axis=1,
                )
                for at in range(2)
            ]
        )

    to_chip = ((z - y) % 4) * 2 + xl
    mine, other = columns_for(to_chip ^ c), columns_for(to_chip ^ c ^ 1)
    other = fetch(other, dc=1)
    rows = fetch_from(
        jnp.concatenate([mine, other]), lambda xh, y, z, xl, c: (xh, y, z + y, xl ^ c, c)
    )
    own_pair = message, gather_swap(message)
    cosine, sine = rotary_tables()
    rows, near[1, 0], near[0, 1] = together(
        rows, near[1, 0], near[0, 1], also=(near[3, 0], own_pair, cosine, sine)
    )

    def columns_of(rows, core):
        return jnp.concatenate(
            [
                lax.dynamic_slice(rows, (n * 2 * T + core * T, 0), (T, COLS))
                for n in range(2)
            ]
        )

    mine = columns_of(rows, c)
    other = fetch(columns_of(rows, 1 - c), dc=1)
    here = jnp.where(c == 0, mine, jnp.concatenate([other[T:], other[:T]]))
    there = jnp.where(c == 0, jnp.concatenate([other[T:], other[:T]]), mine)
    own_rows = jnp.concatenate([here, there])
    further = gather_next(near)
    one, three = fetch(own_rows, dy=1), fetch(own_rows, dy=-1)
    one, three, further, near, far_vectors = together(one, three, further, near, vectors[:16])
    far_vectors = fetch(far_vectors, dz=2, dx=1)
    near_pairs = near | {(0, 0): own_pair}
    far_vectors = jnp.concatenate([far_vectors, fetch(far_vectors, dc=1)])
    far = gather_far(further)
    two = fetch(one, dy=1)
    pieces = both_cores(near_pairs) + both_cores(further)
    vecs, own_qkv_bias = group_vectors(pieces, far_vectors, token_place, me)
    *arrays, done = chip_rows(pieces, vecs, fc2_weight, dense_weight, [], [one, three])
    (far,) = together(far, also=(two, done))
    far = [(far, 10 * T), (gather_swap(far), 11 * T)]
    normed, all_cot, act_grad, attended_grad, _ = chip_rows(
        far, vecs, fc2_weight, dense_weight, arrays, []
    )
    gain, out_bias = vecs[0:1], vecs[2:3]
    (activated, pre_grad, act_t, pre_t, mixed, fc1_bias_part, out_bias_part, weight) = (
        forward_inputs(
            normed,
            all_cot,
            act_grad,
            (own_rows, one, two, three),
            fc1_bias.astype(F32).reshape(1, FFL),
            own_qkv_bias,
            row_place,
            me,
        )
    )

    early = column_grads(normed, pre_t, act_t, all_cot, chip_order, part_order, core)
    *state, done = attention_first(token_place, cosine, sine, mixed, attended_grad, early)
    early_near = reduce_near(early, reduce_far(early), done[0, 0].astype(F32))
    attended, mixed_grad, attended_t, mixed_t, qkv_bias_part = attention_last(
        token_place, cosine, sine, state, early_near
    )
    early = early[0], fetch(early_near[0], dy=-1), fetch(early_near[1], dy=1)
    zero = zero_of(qkv_bias_part)
    early = [
        add(*(e[dx * FFL : (dx + 1) * FFL] for e in early), zero).astype(BF) for dx in range(2)
    ]
    early_other = [fetch(e, dh=1) for e in early]

    def the_terms(chips, sums, before):
        mine, other, *sums = terms(
            chips,
            attended,
            activated,
            dense_weight,
            fc2_weight,
            mixed_grad,
            pre_grad,
            weight,
            normed,
            vecs,
            sums,
            before,
        )
        return mine, fetch(other, dc=1), sums

    def own_terms(chips, mine, other, zero):
        return {
            chip: add(mine[n * T : (n + 1) * T], other[n * T : (n + 1) * T], zero).astype(BF)
            for n, chip in enumerate(chips)
        }

    mine0, other0, sums = the_terms(WAVES[0], [], early)
    mine1, other1, sums = the_terms(WAVES[1], sums, [])
    q = own_terms(WAVES[0], mine0, other0, zero_of(sums[0]))
    far = scatter_far(q)
    mine2, other2, sums = the_terms(WAVES[2], sums, [q[2, 1], early_other[0]])
    mine3, other3, sums = the_terms(WAVES[3], sums, [early_other[1], *far])

    def from_owners(rows):
        return [
            fetch_from(rows[dx], lambda xh, y, z, xl, c: (xh, y, z - y, xl ^ dx, c))
            for dx in range(2)
        ]

    early = jnp.concatenate(
        [add(e, other).astype(BF) for e, other in zip(early, early_other, strict=True)]
    )
    early_own = jnp.concatenate([early[:, :T], fetch(early[:, T : 2 * T], dc=1)], axis=1)
    early_own = from_owners([early_own[:FFL], early_own[FFL:]])
    late = head_grads(
        normed,
        mixed_t,
        attended_t,
        all_cot,
        chip_order,
        part_order,
        core,
        me,
        gain,
        sums,
        (qkv_bias_part, fc1_bias_part, out_bias_part),
    )
    late_far = reduce_far(late)
    q |= own_terms(WAVES[1], mine1, other1, 0.0)
    q, early_own, late_far, far = together(
        q, early_own, late_far, far, also=(other2, other3, late)
    )

    *further, zero = scatter_next(q, far)
    late_near = reduce_near(late, late_far, zero)
    late_near = fetch(late_near[0], dy=-1), fetch(late_near[1], dy=1)
    q |= own_terms(WAVES[2], mine2, other2, 0.0) | own_terms(WAVES[3], mine3, other3, 0.0)
    q, further, late_near = together(q, further, late_near)

    nearest = scatter_near(q, further, 0.0)
    early = jnp.concatenate(
        [
            jnp.concatenate([early_own[dx], early[dx * FFL : (dx + 1) * FFL, 2 * T :]], axis=1)
            for dx in range(2)
        ]
    )
    early_one, early_three = fetch(early, dy=1), fetch(early, dy=-1)
    late = add(late[0], *late_near).astype(BF)
    early_one, early_three, late = together(early_one, early_three, late, also=nearest)
    late_other = fetch(late, dh=1)

    early = (
        early,
        early_one,
        early_three,
        fetch(early_one[:FFL], dy=1),
        fetch(early_three[FFL:], dy=-1),
    )
    late = add(late, late_other).astype(BF)
    late_rows = jnp.concatenate([late[:FOR_OWNER], late[LATE : LATE + FOR_OWNER]])
    late_own = jnp.concatenate([late_rows[:, :T], fetch(late_rows[:, T:], dc=1)], axis=1)
    late_own = from_owners([late_own[:FOR_OWNER], late_own[FOR_OWNER:]])
    late = jnp.concatenate(
        [late_own[0], late[FOR_OWNER:LATE], late_own[1], late[LATE + FOR_OWNER :]]
    )
    late_one, late_three = fetch(late, dy=1), fetch(late, dy=-1)
    total = add(q[0, 0], *nearest)
    own = tokens.astype(F32)
    layer_out = (own + out_bias + total[:, D:]).astype(BF)
    center = own - jnp.mean(own, axis=-1, keepdims=True)
    inv_std = lax.rsqrt(jnp.mean(center * center, axis=-1, keepdims=True) + 1e-05)
    unit = center * inv_std
    scaled = total[:, :D] * gain
    input_grad = cotangent.astype(F32) + inv_std * (
        scaled
        - jnp.mean(scaled, axis=-1, keepdims=True)
        - unit * jnp.mean(scaled * unit, axis=-1, keepdims=True)
    )
    late = (
        late,
        late_one,
        late_three,
        fetch(late_one[:LATE], dy=1),
        fetch(late_three[LATE:], dy=-1),
    )
    fc1_total, fc2_total = place_columns(early, col_place, part_place)
    qkv_total, dense_total, of_owner, of_own = place_heads(late, col_place, part_place)
    out_bias_total = of_own[0, FFL : FFL + T]

    return (
        layer_out,
        input_grad,
        of_owner[0],
        of_owner[1],
        qkv_total,
        of_owner[2:5].reshape(QKV),
        dense_total,
        out_bias_total,
        fc1_total,
        of_own[0, :FFL],
        fc2_total,
        out_bias_total,
    )


def solution(mesh):
    return jax.shard_map(
        body,
        mesh=mesh,
        in_specs=(
            P(AXES, None),
            P("shard"),
            P("shard"),
            P("shard", None),
            P("shard"),
            P("shard", None),
            P("shard"),
            P("shard", None),
            P("shard"),
            P("shard", None),
            P("shard"),
            P(AXES, None),
        ),
        out_specs=(
            P(AXES, None),
            P(AXES, None),
            P("shard"),
            P("shard"),
            P("shard", None),
            P("shard"),
            P("shard", None),
            P("shard"),
            P("shard", None),
            P("shard"),
            P("shard", None),
            P("shard"),
        ),
        check_vma=False,
    )
```

```python
import functools
import math

import jax
import jax.numpy as jnp
from jax import lax
from jax.experimental import pallas as pl
from jax.experimental.pallas import tpu as pltpu
from jax.sharding import PartitionSpec as P

D = 2048
HEADS = 32
HEAD_DIM = 64
ROTARY = 32
FF = 8192
SEQ = 2048
T = 128
QKV = 384
FFL = 512
COLS = QKV + FFL
BF = jnp.bfloat16
F32 = jnp.float32
AXES = ("rep", "shard")
MIB = 1 << 20
LOG2E = math.log2(math.e)

PLACES = [
    (xh, y, z, xl, c)
    for xh in range(2)
    for y in range(4)
    for z in range(4)
    for xl in range(2)
    for c in range(2)
]


def flat(xh, y, z, xl, c):
    return (xh * 4 + y % 4) * 16 + (z % 4) * 4 + xl * 2 + c


def fetch_from(x, source):
    return lax.ppermute(x, AXES, [(flat(*source(*p)), flat(*p)) for p in PLACES])


def fetch(x, dz=0, dx=0, dc=0, dy=0, dh=0):
    return fetch_from(
        x, lambda xh, y, z, xl, c: (xh ^ dh, y + dy, z + dz, xl ^ dx, c ^ dc)
    )


def dot(a, b, ca=1, cb=0):
    return lax.dot_general(a, b, (((ca,), (cb,)), ((), ())), preferred_element_type=F32)


def add(*terms):
    total = terms[0].astype(F32)
    for term in terms[1:]:
        total = total + (term if isinstance(term, float) else term.astype(F32))
    return total


def zero_of(x):
    return x[0, 0].astype(F32) * 0.0


def together(*groups, also=()):
    leaves, tree = jax.tree.flatten(groups)
    others = jax.tree.leaves(also)
    n = len(leaves)
    leaves = pl.pallas_call(
        lambda *refs: None,
        in_specs=[pl.BlockSpec(memory_space=pl.ANY)] * (n + len(others)),
        out_specs=[pl.BlockSpec(memory_space=pl.ANY)] * n,
        out_shape=[jax.ShapeDtypeStruct(x.shape, x.dtype) for x in leaves],
        input_output_aliases={i: i for i in range(n)},
        compiler_params=pltpu.CompilerParams(vmem_limit_bytes=MIB),
    )(*leaves, *others)
    return jax.tree.unflatten(tree, leaves)


def gather_near(own):
    return {
        (0, 0): own,
        (1, 0): fetch(own, dz=1),
        (3, 0): fetch(own, dz=-1),
        (0, 1): fetch(own, dx=1),
    }


def gather_next(a):
    return {
        (1, 1): fetch(a[1, 0], dx=1),
        (3, 1): fetch(a[0, 1], dz=-1),
        (2, 0): fetch(a[1, 0], dz=1),
    }


def gather_far(a):
    return fetch(a[2, 0], dx=1)


def gather_swap(own):
    return fetch(own, dc=1)


def both_cores(a):
    pieces = []
    for (dz, dx), own in a.items():
        pair = own if isinstance(own, tuple) else (own, gather_swap(own))
        pieces += [(pair[dc], ((dz * 2 + dx) * 2 + dc) * T) for dc in range(2)]
    return pieces


SLOTS = [(dz, dx, dc) for dz in range(4) for dx in range(2) for dc in range(2)]
WAVES = [[(2, 1)], [(1, 1), (3, 1), (2, 0)], [(1, 0), (3, 0)], [(0, 1), (0, 0)]]


def scatter_far(q):
    half = T // 2
    return fetch(q[2, 1][:half], dz=-1), fetch(q[2, 1][half:], dz=1)


def scatter_next(q, far):
    half = T // 2
    q11 = jnp.concatenate([add(q[1, 1][:half], far[0]).astype(BF), q[1, 1][half:]])
    q31 = jnp.concatenate([q[3, 1][:half], add(q[3, 1][half:], far[1]).astype(BF)])
    zero = zero_of(q11) + zero_of(q31)
    return fetch(q[2, 0], dz=-1), fetch(q31, dz=1), fetch(q11, dx=1), zero


def scatter_near(q, further, zero):
    q10 = add(q[1, 0], further[0], further[2], zero).astype(BF)
    q01 = add(q[0, 1], further[1], zero).astype(BF)
    return fetch(q10, dz=-1), fetch(q[3, 0], dz=1), fetch(q01, dx=1)


def reduce_far(g):
    half = g[0].shape[0] // 2
    return fetch(g[2][:half], dy=-1), fetch(g[2][half:], dy=1)


def reduce_near(g, far, zero):
    half = g[0].shape[0] // 2
    g1 = jnp.concatenate([add(g[1][:half], far[0], zero).astype(BF), g[1][half:]])
    g3 = jnp.concatenate([g[3][:half], add(g[3][half:], far[1], zero).astype(BF)])
    return g1, g3


def of_rep(refs, dy, dx, n):
    own, one, three, first, second = refs
    if dy == 2:
        return (second if dx else first), 0
    return (own, one, None, three)[dy], dx * n


VMEM = pl.BlockSpec(memory_space=pltpu.VMEM)
SMEM = pl.BlockSpec(memory_space=pltpu.SMEM)
HBM = pl.BlockSpec(memory_space=pltpu.HBM)
ANY = pl.BlockSpec(memory_space=pl.ANY)


def lanes(at, n):
    return pl.ds(pl.multiple_of(at * n, n), n)


def call(kernel, ins, outs, args, scratch=(), vmem=6, flops=0, nbytes=0, exps=0, aliases={}, out_specs=None):
    return pl.pallas_call(
        kernel,
        in_specs=ins,
        out_specs=out_specs or [VMEM] * len(outs),
        out_shape=[
            pltpu.VMEM(o[0], o[1]) if len(o) > 2 else jax.ShapeDtypeStruct(*o) for o in outs
        ],
        scratch_shapes=list(scratch),
        input_output_aliases=aliases,
        compiler_params=pltpu.CompilerParams(vmem_limit_bytes=vmem * MIB),
        cost_estimate=pl.CostEstimate(
            flops=flops, transcendentals=exps, bytes_accessed=nbytes
        ),
    )(*args)


ROOT = math.sqrt(2.0 / math.pi)


def start_copies(pieces, place, sems):
    copies = [
        pltpu.make_async_copy(src, dst, sems.at[place + i]) for i, (src, dst) in enumerate(pieces)
    ]
    for copy in copies:
        copy.start()
    return copies


def norm_rows(normed_ref, gain, shift, first, count):
    def strip(i, _):
        at = lanes(i, 64)
        x = normed_ref[at, :].astype(F32)
        x = x - jnp.sum(x, axis=1, keepdims=True) * (1.0 / D)
        scale = lax.rsqrt(jnp.sum(x * x, axis=1, keepdims=True) * (1.0 / D) + 1e-05)
        normed_ref[at, :] = (x * scale * gain + shift).astype(BF)
        return 0

    lax.fori_loop(first // 64, (first + count) // 64, strip, 0)


def grid_call(kernel, prefetch, grid, ins, outs, args, scratch=(), vmem=32, flops=0, nbytes=0):
    return pl.pallas_call(
        kernel,
        grid_spec=pltpu.PrefetchScalarGridSpec(
            num_scalar_prefetch=len(prefetch),
            grid=grid,
            in_specs=ins,
            out_specs=[o[2] for o in outs],
            scratch_shapes=list(scratch),
        ),
        out_shape=[jax.ShapeDtypeStruct(o[0], o[1]) for o in outs],
        compiler_params=pltpu.CompilerParams(vmem_limit_bytes=vmem * MIB),
        cost_estimate=pl.CostEstimate(flops=flops, transcendentals=0, bytes_accessed=nbytes),
    )(*prefetch, *args)


def whole(*shape):
    return pl.BlockSpec(shape, lambda *_: (0,) * len(shape))


def group_vectors(pieces, far_vectors, token_place, me):
    n = len(pieces)

    def kernel(t_ref, me_ref, *refs):
        far_ref, vec_ref, own_ref, small_ref, flat_ref, sems = refs[n:]
        moves = [
            (ref.at[pl.ds(0, 16), pl.ds(2 * D, T)], small_ref.at[pl.ds(at // T * 16, 16)])
            for (_, at), ref in zip(pieces, refs[:n], strict=True)
        ]
        for dc in range(2):
            to = small_ref.at[pl.ds((5 * 2 + dc) * 16, 16)]
            moves.append((far_ref.at[pl.ds(dc * 16, 16)], to))
        for copy in start_copies(moves, 0, sems):
            copy.wait()
        for i in range(16):
            at = t_ref[i]
            small = small_ref[i * 16 : (i + 1) * 16, :].astype(F32)
            for part in range(3):
                flat_ref[0:1, lanes(at * 3 + part, T)] = small[part : part + 1]
            vec_ref[0:1, lanes(at, T)] = small[3:4]
            vec_ref[1:2, lanes(at, T)] = small[4:5]
            vec_ref[2:3, lanes(at, T)] = small[5:6] + small[6:7]
        for part in range(3):
            own_ref[0:1, part * T : (part + 1) * T] = flat_ref[
                0:1, lanes(part * 16 + me_ref[0], T)
            ]

    return call(
        kernel,
        [SMEM] * 2 + [HBM] * (n + 1),
        [((8, D), F32), ((1, QKV), F32)],
        [token_place, me] + [p for p, _ in pieces] + [far_vectors],
        [
            pltpu.VMEM((256, T), BF),
            pltpu.VMEM((1, 3 * D), F32),
            pltpu.SemaphoreType.DMA((n + 2,)),
        ],
        vmem=56,
    )


def chip_rows(pieces, vecs, fc2, dense, arrays, before):
    n, given = len(pieces), len(arrays)
    chips = sorted({at // 256 for _, at in pieces})

    def kernel(*refs):
        refs = refs[len(before) + given :]
        tok = refs[:n]
        vec_ref, fc2_ref, dense_ref = refs[n : n + 3]
        outs, done_ref = refs[n + 3 : n + 7], refs[n + 7]
        bufs, in_sems, out_sems = refs[n + 8 : n + 12], refs[n + 12], refs[n + 13]
        done_ref[...] = jnp.zeros_like(done_ref)

        def arriving(k):
            moves = []
            for (array, at), ref in zip(pieces, tok, strict=True):
                if at // 256 == chips[k]:
                    to = pl.ds(at % 256, array.shape[0])
                    moves.append((ref.at[:, pl.ds(0, D)], bufs[0].at[k % 3, to]))
                    moves.append((ref.at[:, pl.ds(D, D)], bufs[1].at[k % 3, to]))
            return [
                pltpu.make_async_copy(src, dst, in_sems.at[k % 3, i])
                for i, (src, dst) in enumerate(moves)
            ]

        def leaving(k):
            rows = pl.ds(chips[k] * 256, 256)
            return [
                pltpu.make_async_copy(buf.at[k % 3], out.at[rows], out_sems.at[k % 3, i])
                for i, (buf, out) in enumerate(zip(bufs, outs, strict=True))
            ]

        for copy in arriving(0):
            copy.start()
        for k in range(len(chips)):
            if k + 1 < len(chips):
                if k >= 2:
                    for copy in leaving(k - 2):
                        copy.wait()
                for copy in arriving(k + 1):
                    copy.start()
            for copy in arriving(k):
                copy.wait()
            norm_rows(bufs[0].at[k % 3], vec_ref[0:1, :], vec_ref[1:2, :], 0, 256)
            x = bufs[1][k % 3]
            bufs[2][k % 3] = dot(x, fc2_ref[...], 1, 1).astype(BF)
            bufs[3][k % 3] = dot(x, dense_ref[...], 1, 1).astype(BF)
            for copy in leaving(k):
                copy.start()
        for k in range(max(len(chips) - 3, 0), len(chips)):
            for copy in leaving(k):
                copy.wait()

    widths = (D, D, FFL, T)
    return call(
        kernel,
        [ANY] * (len(before) + given) + [HBM] * n + [VMEM] * 3,
        [((SEQ, w), BF) for w in widths] + [((8, T), F32)],
        [*before, *arrays, *[p for p, _ in pieces], vecs, fc2, dense],
        [pltpu.VMEM((3, 256, w), BF) for w in widths]
        + [pltpu.SemaphoreType.DMA((3, 8)), pltpu.SemaphoreType.DMA((3, 4))],
        vmem=56,
        aliases={len(before) + i: i for i in range(given)},
        out_specs=[ANY] * 4 + [VMEM],
        flops=2 * n * T * D * (FFL + T),
        nbytes=n * MIB,
    )


def forward_inputs(normed, cot, act_grad, weights, bias, own_bias, row_place, me):
    def kernel(
        r_ref,
        me_ref,
        n_ref,
        grad_ref,
        cot_ref,
        w0_ref,
        w1_ref,
        w2_ref,
        w3_ref,
        bias_ref,
        own_ref,
        act_ref,
        pre_ref,
        act_t_ref,
        pre_t_ref,
        mixed_ref,
        fc1b_ref,
        outb_ref,
        w_out,
        w_ref,
        sems,
        out_sem,
    ):
        step = pl.program_id(0)
        leaving = pltpu.make_async_copy(w_ref, w_out, out_sem.at[0])

        @pl.when(step == 0)
        def _():
            moves = []
            for i, (dy, dx, dc) in enumerate(SLOTS):
                rows = pl.ds((dx * 2 + dc) * T, T)
                source = (w0_ref, w1_ref, w2_ref, w3_ref)[dy]
                moves.append((source.at[rows], w_ref.at[lanes(r_ref[i], T)]))
            for copy in start_copies(moves, 0, sems):
                copy.wait()
            leaving.start()
            fc1b_ref[...] = jnp.zeros_like(fc1b_ref)
            outb_ref[...] = jnp.zeros_like(outb_ref)

        halves = []
        for half in range(2):
            x = n_ref[half * 256 : (half + 1) * 256, :]
            mixed_ref[half * 256 : (half + 1) * 256, :] = dot(x, w_ref[:, :QKV]) + own_ref[...]
            halves.append(dot(x, w_ref[:, QKV:]) + bias_ref[...])
        for half, pre in enumerate(halves):
            at = slice(half * 256, (half + 1) * 256)
            squared = pre * pre
            tanh = jnp.tanh(ROOT * pre * (1.0 + 0.044715 * squared))
            act = (0.5 * pre * (1.0 + tanh)).astype(BF)
            act_ref[at, :] = act
            act_t_ref[:, at] = act.T
            slope = 0.5 * (1.0 + tanh) + 0.5 * pre * (1.0 - tanh * tanh) * ROOT * (
                1.0 + 3 * 0.044715 * squared
            )
            back = (grad_ref[at, :].astype(F32) * slope).astype(BF)
            pre_ref[at, :] = back
            pre_t_ref[:, at] = back.T
            fc1b_ref[...] += jnp.sum(back.astype(F32).reshape(32, 8, FFL), axis=0)
        outb_ref[...] += jnp.sum(cot_ref[...].astype(F32).reshape(64, 8, T), axis=0)

        @pl.when(step == pl.num_programs(0) - 1)
        def _():
            leaving.wait()

    rows = lambda i, *_: (i, 0)
    cols = lambda i, *_: (0, i)
    return grid_call(
        kernel,
        [row_place, me],
        (SEQ // 512,),
        [
            pl.BlockSpec((512, D), rows),
            pl.BlockSpec((512, FFL), rows),
            pl.BlockSpec((512, T), lambda i, r, m: (i, m[0])),
        ]
        + [HBM] * 4
        + [whole(1, FFL), whole(1, QKV)],
        [
            ((SEQ, FFL), BF, pl.BlockSpec((512, FFL), rows)),
            ((SEQ, FFL), BF, pl.BlockSpec((512, FFL), rows)),
            ((FFL, SEQ), BF, pl.BlockSpec((FFL, 512), cols)),
            ((FFL, SEQ), BF, pl.BlockSpec((FFL, 512), cols)),
            ((SEQ, QKV), F32, pl.BlockSpec((512, QKV), rows)),
            ((8, FFL), F32, whole(8, FFL)),
            ((8, T), F32, whole(8, T)),
            ((D, COLS), BF, ANY),
        ],
        [normed, act_grad, cot, *weights, bias, own_bias],
        [
            pltpu.VMEM((D, COLS), BF),
            pltpu.SemaphoreType.DMA((16,)),
            pltpu.SemaphoreType.DMA((1,)),
        ],
        vmem=56,
        flops=2 * SEQ * D * COLS,
        nbytes=24 * MIB,
    )


ORDER = (2, 1, 3, 0)


def in_order(places, parts):
    chips = jnp.stack([places[(dy * 2 + dx) * 2] // 2 for dy in ORDER for dx in range(2)])
    return chips, jnp.stack([parts[dy * 2 + dx] for dy in ORDER for dx in range(2)])


def fetched(refs, scratch, sems):
    copies = [
        pltpu.make_async_copy(ref, to, sems.at[i])
        for i, (ref, to) in enumerate(zip(refs, scratch, strict=True))
    ]
    for copy in copies:
        copy.start()
    return copies


def column_grads(normed, pre_t, act_t, cot, chips, parts, core):
    def kernel(chip_ref, part_ref, core_ref, normed_ref, cot_ref, g_ref, a_ref, *refs):
        outs, n_ref, c_ref, sems = refs[:4], refs[4], refs[5], refs[6]
        copies = fetched((normed_ref, cot_ref), (n_ref, c_ref), sems)
        copies[0].wait()
        for i in range(8):
            out, at = outs[i // 2], slice(i % 2 * FFL, (i % 2 + 1) * FFL)
            cols = dot(g_ref[...], n_ref[:, lanes(chip_ref[i], 256)]).astype(BF)
            out[at, lanes(core_ref[0], T)] = cols[:, :T]
            out[at, lanes(1 - core_ref[0], T)] = cols[:, T:]
        copies[1].wait()
        for i in range(8):
            out, at = outs[i // 2], slice(i % 2 * FFL, (i % 2 + 1) * FFL)
            out[at, 256:512] = dot(a_ref[...], c_ref[:, lanes(part_ref[i], 256)]).astype(BF)

    outs = call(
        kernel,
        [SMEM] * 3 + [ANY] * 2 + [VMEM] * 2,
        [((2 * FFL, 512), BF)] * 4,
        [chips, parts, core, normed, cot, pre_t, act_t],
        [pltpu.VMEM((SEQ, D), BF), pltpu.VMEM((SEQ, D), BF), pltpu.SemaphoreType.DMA((2,))],
        vmem=56,
        flops=4 * SEQ * D * FFL,
        nbytes=24 * MIB,
    )
    return [outs[ORDER.index(dy)] for dy in range(4)]


FOR_OWNER = QKV + 16
LATE = FOR_OWNER + T + 16


def head_grads(
    normed, mixed_t, attended_t, cot, chips, parts, core, me, gain, sums, bias_parts
):
    def kernel(chip_ref, part_ref, core_ref, me_ref, normed_ref, cot_ref, m_ref, a_ref, *refs):
        gain_ref, gains_ref, shifts_ref, qkvb_ref, fc1b_ref, outb_ref = refs[:6]
        outs, owners_ref, own_ref = refs[6:10], refs[10], refs[11]
        n_ref, c_ref, sems = refs[12:]
        copies = fetched((normed_ref, cot_ref), (n_ref, c_ref), sems)
        owners_ref[...] = jnp.zeros_like(owners_ref)
        owners_ref[0:1, :] = jnp.sum(gains_ref[...], axis=0, keepdims=True) / gain_ref[...]
        owners_ref[1:2, :] = jnp.sum(shifts_ref[...], axis=0, keepdims=True)
        qkvb = jnp.sum(qkvb_ref[...], axis=0, keepdims=True)
        for part in range(3):
            at = part * 16 + me_ref[0]
            third = at % 3
            row = lax.broadcasted_iota(jnp.int32, (8, T), 0)
            value = jnp.where(row == 2 + third, qkvb[:, part * T : (part + 1) * T], 0.0)
            owners_ref[0:8, lanes(at // 3, T)] += value
        own_ref[...] = jnp.zeros_like(own_ref)
        own_ref[0:1, :FFL] = jnp.sum(fc1b_ref[...], axis=0, keepdims=True)
        own_ref[0:1, FFL : FFL + T] = jnp.sum(outb_ref[...], axis=0, keepdims=True)
        mine, other = lanes(core_ref[0], T), lanes(1 - core_ref[0], T)
        copies[0].wait()
        for i in range(8):
            out, base = outs[i // 2], i % 2 * LATE
            cols = dot(m_ref[...], n_ref[:, lanes(chip_ref[i], 256)]).astype(BF)
            extra = owners_ref[:, lanes(chip_ref[i], 256)].astype(BF)
            out[base : base + QKV, mine] = cols[:, :T]
            out[base : base + QKV, other] = cols[:, T:]
            out[base + QKV : base + FOR_OWNER, mine] = extra[:, :T]
            out[base + QKV : base + FOR_OWNER, other] = extra[:, T:]
        copies[1].wait()
        for i in range(8):
            out, base = outs[i // 2], i % 2 * LATE + FOR_OWNER
            part = part_ref[i]
            out[base : base + T, :] = dot(a_ref[...], c_ref[:, lanes(part, 256)]).astype(BF)
            out[base + T : base + T + 16, 0:T] = own_ref[:, lanes(part, T)].astype(BF)
            out[base + T : base + T + 16, T:] = jnp.zeros((16, T), BF)

    outs = call(
        kernel,
        [SMEM] * 4 + [ANY] * 2 + [VMEM] * 8,
        [((2 * LATE, 256), BF)] * 4,
        [chips, parts, core, me, normed, cot, mixed_t, attended_t, gain, *sums, *bias_parts],
        [
            pltpu.VMEM((16, D), F32),
            pltpu.VMEM((16, 1024), F32),
            pltpu.VMEM((SEQ, D), BF),
            pltpu.VMEM((SEQ, D), BF),
            pltpu.SemaphoreType.DMA((2,)),
        ],
        vmem=36,
        flops=2 * SEQ * D * (QKV + T),
        nbytes=20 * MIB,
    )
    return [outs[ORDER.index(dy)] for dy in range(4)]


def place_columns(pieces, col_place, part_place):
    def kernel(c_ref, p_ref, *refs):
        fc1_ref, fc2_ref = refs[5:]
        for i, (dy, dh, dc) in enumerate(SLOTS):
            ref, at = of_rep(refs[:5], dy, dh, FFL)
            part = ref[at : at + FFL, dc * T : (dc + 1) * T]
            fc1_ref[:, lanes(c_ref[i], FFL)] = part.astype(F32).T
            if dc == 0:
                to = lanes(p_ref[dy * 2 + dh], 256)
                fc2_ref[:, to] = ref[at : at + FFL, 256:512].astype(F32)

    return call(
        kernel,
        [SMEM] * 2 + [VMEM] * 5,
        [((T, FF), F32), ((FFL, D), F32)],
        [col_place, part_place] + list(pieces),
        vmem=20,
        nbytes=12 * MIB,
    )


def place_heads(pieces, col_place, part_place):
    def kernel(c_ref, p_ref, *refs):
        qkv_ref, dense_ref, owner_ref, own_ref = refs[5:]
        total = jnp.zeros((16, T), F32)
        for i, (dy, dx, dc) in enumerate(SLOTS):
            ref, at = of_rep(refs[:5], dy, dx, LATE)
            cols = slice(dc * T, (dc + 1) * T)
            for part in range(3):
                block = ref[at + part * T : at + (part + 1) * T, cols].astype(F32)
                qkv_ref[:, lanes(c_ref[i] + part * 16, T)] = block.T
            total += ref[at + QKV : at + FOR_OWNER, cols].astype(F32)
            if dc == 0:
                part = p_ref[dy * 2 + dx]
                rows = slice(at + FOR_OWNER, at + FOR_OWNER + T)
                dense_ref[:, lanes(part, 256)] = ref[rows, :].astype(F32)
                rows = slice(at + FOR_OWNER + T, at + LATE)
                own_ref[:, lanes(part, T)] = ref[rows, 0:T].astype(F32)
        owner_ref[...] = total

    return call(
        kernel,
        [SMEM] * 2 + [VMEM] * 5,
        [((T, 3 * D), F32), ((T, D), F32), ((16, T), F32), ((16, 1024), F32)],
        [col_place, part_place] + list(pieces),
        vmem=14,
        nbytes=6 * MIB,
    )


def terms(
    chips, attended, activated, dense, fc2, mixed_grad, pre_grad, weight, normed, vecs, sums, before
):
    n = len(chips)
    order = jnp.array([dz * 2 + dx for dz, dx in chips], jnp.int32)

    def kernel(order_ref, a_ref, f_ref, m_ref, p_ref, n_ref, d_ref, v_ref, w_ref, vec_ref, *refs):
        mine_ref, other_ref, gain_ref, total_ref = refs[-4:]
        shift = vec_ref[1:2, :]

        @pl.when(pl.program_id(0) == 0)
        def _():
            if sums:
                gain_ref[...] = refs[0][...]
                total_ref[...] = refs[1][...]
            else:
                gain_ref[...] = jnp.zeros_like(gain_ref)
                total_ref[...] = jnp.zeros_like(total_ref)

        for col in range(4):
            to = slice(col * 512, (col + 1) * 512)
            total = dot(m_ref[...], w_ref[to, :QKV], 1, 1) + dot(p_ref[...], w_ref[to, QKV:], 1, 1)
            mine_ref[:, to] = total[:T].astype(BF)
            other_ref[:, to] = total[T:].astype(BF)
            unit = n_ref[:, to].astype(F32) - shift[:, to]
            gain_ref[:, to] += jnp.sum((total * unit).reshape(32, 8, 512), axis=0)
            total_ref[:, to] += jnp.sum(total.reshape(32, 8, 512), axis=0)
            total = dot(a_ref[...], d_ref[:, to]) + dot(f_ref[...], v_ref[:, to])
            to = slice(D + col * 512, D + (col + 1) * 512)
            mine_ref[:, to] = total[:T].astype(BF)
            other_ref[:, to] = total[T:].astype(BF)

    rows = lambda i, order_ref: (order_ref[i], 0)
    here = lambda i, order_ref: (i, 0)
    return grid_call(
        kernel,
        [order],
        (n,),
        [
            pl.BlockSpec((2 * T, T), rows),
            pl.BlockSpec((2 * T, FFL), rows),
            pl.BlockSpec((2 * T, QKV), rows),
            pl.BlockSpec((2 * T, FFL), rows),
            pl.BlockSpec((2 * T, D), rows),
            whole(T, D),
            whole(FFL, D),
            whole(D, COLS),
            whole(8, D),
        ]
        + [whole(8, D)] * len(sums)
        + [ANY] * len(before),
        [((n * T, 2 * D), BF, pl.BlockSpec((T, 2 * D), here))] * 2
        + [((8, D), F32, whole(8, D))] * 2,
        [attended, activated, mixed_grad, pre_grad, normed, dense, fc2, weight, vecs, *sums, *before],
        flops=2 * n * 2 * T * (COLS + T + FFL) * D,
        nbytes=8 * MIB,
    )


TQ = 512
TK = 512


def attention_kernel(blocks, last, n_before, place, cos_ref, sin_ref, *refs):
    refs = refs[n_before:]
    if last:
        first_refs, refs = refs[:8], refs[8:]
        att_ref, out_ref, att_t_ref, out_t_ref, bias_ref = refs[:5]
        q_ref, k_ref, v_ref, do_ref = first_refs[:4]
        dq_ref, dk_ref, dv_ref, o_ref, s_ref, e_ref = refs[5:]
    else:
        mixed_ref, grad_ref, *refs = refs
        refs, done_ref = refs[:8] + refs[9:], refs[8]
        done_ref[...] = jnp.zeros_like(done_ref)
        q_ref, k_ref, v_ref, do_ref, dq_ref, dk_ref, dv_ref, o_ref, s_ref, e_ref = refs
    lane = lax.broadcasted_iota(jnp.int32, (T, 128), 1)
    low_head = lane < HEAD_DIM
    first = (lane % HEAD_DIM) < ROTARY // 2

    def turned(x):
        return jnp.where(
            first, pltpu.roll(x, 128 - ROTARY // 2, 1), pltpu.roll(x, ROTARY // 2, 1)
        )

    def load(slot, _):
        rows = pl.ds(pl.multiple_of(slot * T, T), T)
        at = pl.ds(pl.multiple_of(place[slot] * T, T), T)
        c, s = cos_ref[at, :], sin_ref[at, :]
        query = mixed_ref[rows, 0:128]
        key = mixed_ref[rows, 128:256]
        query = (query * c + turned(query) * s).astype(BF).astype(F32) * (HEAD_DIM**-0.5)
        q_ref[0, at, :] = jnp.where(low_head, query, 0.0).astype(BF)
        q_ref[1, at, :] = jnp.where(low_head, 0.0, query).astype(BF)
        k_ref[at, :] = (key * c + turned(key) * s).astype(BF)
        v_ref[at, 0:128] = mixed_ref[rows, 256:384].astype(BF)
        v_ref[at, 128:256] = jnp.ones((T, 128), BF)
        grad = grad_ref[rows, :].astype(F32)
        do_ref[0, at, :] = jnp.where(low_head, grad, 0.0).astype(BF)
        do_ref[1, at, :] = jnp.where(low_head, 0.0, grad).astype(BF)
        dk_ref[:, at] = jnp.zeros((128, T), F32)
        dv_ref[:, at] = jnp.zeros((128, T), F32)
        return 0

    if last:
        for to, at in ((dq_ref, 4), (dk_ref, 5), (dv_ref, 6), (o_ref, 7)):
            to[...] = first_refs[at][...]
    else:
        lax.fori_loop(0, 16, load, 0)

    lane_q = lax.broadcasted_iota(jnp.int32, (TQ, 128), 1)
    low_q = lane_q < HEAD_DIM

    def block(i, _):
        rows = lanes(i, TQ)
        queries = [q_ref[h, rows, :] for h in range(2)]

        def scores(j, tops, masked):
            at = lanes(j, TK)
            keys = k_ref[at, :]
            new = []
            for h in range(2):
                s = dot(queries[h], keys, 1, 1)
                if masked:
                    row = lax.broadcasted_iota(jnp.int32, (TQ, TK), 0)
                    col = lax.broadcasted_iota(jnp.int32, (TQ, TK), 1)
                    s = jnp.where(row >= col, s, -1e30)
                s_ref[h, :, at] = s
                top = tops[h]
                for n in range(TK // 128):
                    top = jnp.maximum(top, s[:, n * 128 : (n + 1) * 128])
                new.append(top)
            return tuple(new)

        low = jnp.full((TQ, 128), -1e30, F32)
        tops = lax.fori_loop(0, i, lambda j, t: scores(j, t, False), (low, low))
        tops = [jnp.max(t, axis=1, keepdims=True) for t in scores(i, tops, True)]

        def weigh(j, totals):
            at = lanes(j, TK)
            values = v_ref[at, :]
            new = []
            for h in range(2):
                e = jnp.exp2((s_ref[h, :, at] - tops[h]) * LOG2E).astype(BF)
                e_ref[h, :, at] = e
                new.append(totals[h] + dot(e, values))
            return tuple(new)

        zero = jnp.zeros((TQ, 256), F32)
        totals = lax.fori_loop(0, i + 1, weigh, (zero, zero))
        outs, grads, deltas = [], [], []
        for h in range(2):
            inverse = 1.0 / totals[h][:, 128:]
            o = totals[h][:, :128] * inverse
            grad = do_ref[h, rows, :].astype(F32) * inverse
            outs.append(o)
            deltas.append(jnp.sum(grad * o, axis=1, keepdims=True))
            grads.append(grad.astype(BF))
        o_ref[rows, :] = jnp.where(low_q, outs[0], outs[1]).astype(BF)
        queries_t = [q.T for q in queries]
        grads_t = [g.T for g in grads]

        def back(j, totals):
            at = lanes(j, TK)
            keys = k_ref[at, :]
            values = v_ref[at, 0:128]
            new, dk, dv = [], None, None
            for h in range(2):
                e = e_ref[h, :, at]
                dp = dot(grads[h], values, 1, 1)
                ds = (e.astype(F32) * (dp - deltas[h])).astype(BF)
                new.append(totals[h] + dot(ds, keys))
                k_part = dot(queries_t[h], ds)
                v_part = dot(grads_t[h], e)
                dk = k_part if dk is None else dk + k_part
                dv = v_part if dv is None else dv + v_part
            dk_ref[:, at] += dk
            dv_ref[:, at] += dv
            return tuple(new)

        zero = jnp.zeros((TQ, 128), F32)
        dqs = lax.fori_loop(0, i + 1, back, (zero, zero))
        dq_ref[rows, :] = jnp.where(low_q, dqs[0], dqs[1]) * (HEAD_DIM**-0.5)
        return 0

    lax.fori_loop(blocks[0], blocks[1], block, 0)
    if not last:
        return

    def store(slot, total):
        rows = pl.ds(pl.multiple_of(slot * T, T), T)
        at = pl.ds(pl.multiple_of(place[slot] * T, T), T)
        c, s = cos_ref[at, :], sin_ref[at, :]
        att = o_ref[at, :]
        att_ref[rows, :] = att
        att_t_ref[:, rows] = att.T
        dq, dk = dq_ref[at, :], dk_ref[:, at].T
        new = []
        for part, grad in enumerate(
            (dq * c - turned(dq) * s, dk * c - turned(dk) * s, dv_ref[:, at].T)
        ):
            low = grad.astype(BF)
            cols = slice(part * T, (part + 1) * T)
            out_ref[rows, cols] = low
            out_t_ref[cols, rows] = low.T
            new.append(total[part] + jnp.sum(low.astype(F32).reshape(16, 8, T), axis=0))
        return tuple(new)

    zero = jnp.zeros((8, T), F32)
    sums = lax.fori_loop(0, 16, store, (zero, zero, zero))
    for part in range(3):
        bias_ref[:, part * T : (part + 1) * T] = sums[part]


def attention_first(place, cosine, sine, mixed, attended_grad, before):
    return call(
        functools.partial(attention_kernel, (0, 2), False, len(before)),
        [SMEM] + [VMEM] * 2 + [ANY] * len(before) + [VMEM] * 2,
        [
            ((2, SEQ, 128), BF, 1),
            ((SEQ, 128), BF, 1),
            ((SEQ, 256), BF, 1),
            ((2, SEQ, 128), BF, 1),
            ((SEQ, 128), F32, 1),
            ((128, SEQ), F32, 1),
            ((128, SEQ), F32, 1),
            ((SEQ, 128), BF, 1),
            ((8, 128), jnp.int32),
        ],
        [place, cosine, sine, *before, mixed, attended_grad],
        [pltpu.VMEM((2, TQ, SEQ), F32), pltpu.VMEM((2, TQ, SEQ), BF)],
        vmem=24,
        flops=8 * SEQ * SEQ * 64 * 2,
        exps=SEQ * SEQ // 2,
        nbytes=3 * MIB,
    )


def attention_last(place, cosine, sine, state, before):
    return call(
        functools.partial(attention_kernel, (2, 4), True, len(before)),
        [SMEM] + [VMEM] * 2 + [ANY] * len(before) + [VMEM] * 8,
        [
            ((SEQ, T), BF),
            ((SEQ, QKV), BF),
            ((T, SEQ), BF),
            ((QKV, SEQ), BF),
            ((8, QKV), F32),
        ],
        [place, cosine, sine, *before] + list(state),
        [
            pltpu.VMEM((SEQ, 128), F32),
            pltpu.VMEM((128, SEQ), F32),
            pltpu.VMEM((128, SEQ), F32),
            pltpu.VMEM((SEQ, 128), BF),
            pltpu.VMEM((2, TQ, SEQ), F32),
            pltpu.VMEM((2, TQ, SEQ), BF),
        ],
        vmem=26,
        flops=6 * SEQ * SEQ * 64 * 2,
        exps=SEQ * SEQ // 2,
        nbytes=3 * MIB,
    )


def rotary_tables():
    lane = lax.broadcasted_iota(jnp.int32, (SEQ, 128), 1) % HEAD_DIM
    place = lax.broadcasted_iota(jnp.int32, (SEQ, 128), 0).astype(F32)
    freq = (lane % (ROTARY // 2)).astype(F32)
    angle = place * jnp.exp(freq * (-2.0 * math.log(10000.0) / ROTARY))
    turns = lane < ROTARY
    cosine = jnp.where(turns, jnp.cos(angle), 1.0)
    sine = jnp.where(turns, jnp.sin(angle), 0.0)
    return cosine, jnp.where(lane < ROTARY // 2, -sine, sine)


def body(
    tokens,
    ln_gain,
    ln_shift,
    qkv_weight,
    qkv_bias,
    dense_weight,
    dense_bias,
    fc1_weight,
    fc1_bias,
    fc2_weight,
    fc2_bias,
    cotangent,
):
    rep, shard = lax.axis_index("rep"), lax.axis_index("shard")
    xh, y = rep // 4, rep % 4
    z, xl, c = shard // 4, (shard // 2) % 2, shard % 2
    token_place = jnp.stack(
        [((z + dz) % 4) * 4 + (xl ^ dx) * 2 + (c ^ dc) for dz, dx, dc in SLOTS]
    ).astype(jnp.int32)
    row_place = jnp.stack(
        [((z + y + dy) % 4) * 4 + (xl ^ dx) * 2 + (c ^ dc) for dy, dx, dc in SLOTS]
    ).astype(jnp.int32)
    col_place = jnp.stack(
        [((z - y - dy) % 4) * 4 + (xl ^ dx) * 2 + (c ^ dc) for dy, dx, dc in SLOTS]
    ).astype(jnp.int32)
    part_place = jnp.stack(
        [((y + dy) % 4) * 2 + dx for dy in range(4) for dx in range(2)]
    ).astype(jnp.int32)
    chip_order, part_order = in_order(row_place, part_place)
    me, core = shard.reshape(1).astype(jnp.int32), c.reshape(1).astype(jnp.int32)

    vectors = [v.reshape(-1, T) for v in (qkv_bias, ln_gain, ln_shift, dense_bias, fc2_bias)]
    vectors = jnp.concatenate(vectors + [jnp.zeros((T - 7, T), BF)])
    message = jnp.concatenate([tokens, cotangent, vectors], axis=1)
    near = gather_near(message)

    def columns_for(chip):
        qkv = [
            lax.dynamic_slice(qkv_weight, (0, part * D + chip * 2 * T), (T, 2 * T))
            for part in range(3)
        ]
        fc1 = lax.dynamic_slice(fc1_weight, (0, chip * 2 * FFL), (T, 2 * FFL))
        return jnp.concatenate(
            [
                jnp.concatenate(
                    [p[:, at * T : (at + 1) * T] for p in qkv]
                    + [fc1[:, at * FFL : (at + 1) * FFL]],
                    axis=1,
                )
                for at in range(2)
            ]
        )

    to_chip = ((z - y) % 4) * 2 + xl
    mine, other = columns_for(to_chip ^ c), columns_for(to_chip ^ c ^ 1)
    other = fetch(other, dc=1)
    rows = fetch_from(
        jnp.concatenate([mine, other]), lambda xh, y, z, xl, c: (xh, y, z + y, xl ^ c, c)
    )
    own_pair = message, gather_swap(message)
    cosine, sine = rotary_tables()
    rows, near[1, 0], near[0, 1] = together(
        rows, near[1, 0], near[0, 1], also=(near[3, 0], own_pair, cosine, sine)
    )

    def columns_of(rows, core):
        return jnp.concatenate(
            [
                lax.dynamic_slice(rows, (n * 2 * T + core * T, 0), (T, COLS))
                for n in range(2)
            ]
        )

    mine = columns_of(rows, c)
    other = fetch(columns_of(rows, 1 - c), dc=1)
    here = jnp.where(c == 0, mine, jnp.concatenate([other[T:], other[:T]]))
    there = jnp.where(c == 0, jnp.concatenate([other[T:], other[:T]]), mine)
    own_rows = jnp.concatenate([here, there])
    further = gather_next(near)
    one, three = fetch(own_rows, dy=1), fetch(own_rows, dy=-1)
    one, three, further, near, far_vectors = together(one, three, further, near, vectors[:16])
    far_vectors = fetch(far_vectors, dz=2, dx=1)
    near_pairs = near | {(0, 0): own_pair}
    far_vectors = jnp.concatenate([far_vectors, fetch(far_vectors, dc=1)])
    far = gather_far(further)
    two = fetch(one, dy=1)
    pieces = both_cores(near_pairs) + both_cores(further)
    vecs, own_qkv_bias = group_vectors(pieces, far_vectors, token_place, me)
    *arrays, done = chip_rows(pieces, vecs, fc2_weight, dense_weight, [], [one, three])
    (far,) = together(far, also=(two, done))
    far = [(far, 10 * T), (gather_swap(far), 11 * T)]
    normed, all_cot, act_grad, attended_grad, _ = chip_rows(
        far, vecs, fc2_weight, dense_weight, arrays, []
    )
    gain, out_bias = vecs[0:1], vecs[2:3]
    (activated, pre_grad, act_t, pre_t, mixed, fc1_bias_part, out_bias_part, weight) = (
        forward_inputs(
            normed,
            all_cot,
            act_grad,
            (own_rows, one, two, three),
            fc1_bias.astype(F32).reshape(1, FFL),
            own_qkv_bias,
            row_place,
            me,
        )
    )

    early = column_grads(normed, pre_t, act_t, all_cot, chip_order, part_order, core)
    *state, done = attention_first(
        token_place, cosine, sine, mixed, attended_grad, early[:1]
    )
    early_near = reduce_near(early, reduce_far(early), done[0, 0].astype(F32))
    attended, mixed_grad, attended_t, mixed_t, qkv_bias_part = attention_last(
        token_place, cosine, sine, state, early_near
    )
    early = early[0], fetch(early_near[0], dy=-1), fetch(early_near[1], dy=1)
    zero = zero_of(qkv_bias_part)
    early = [
        add(*(e[dx * FFL : (dx + 1) * FFL] for e in early), zero).astype(BF) for dx in range(2)
    ]
    early_other = [fetch(e, dh=1) for e in early]

    def the_terms(chips, sums, before):
        mine, other, *sums = terms(
            chips,
            attended,
            activated,
            dense_weight,
            fc2_weight,
            mixed_grad,
            pre_grad,
            weight,
            normed,
            vecs,
            sums,
            before,
        )
        return mine, fetch(other, dc=1), sums

    def own_terms(chips, mine, other, zero):
        return {
            chip: add(mine[n * T : (n + 1) * T], other[n * T : (n + 1) * T], zero).astype(BF)
            for n, chip in enumerate(chips)
        }

    mine0, other0, sums = the_terms(WAVES[0], [], early)
    mine1, other1, sums = the_terms(WAVES[1], sums, [])
    q = own_terms(WAVES[0], mine0, other0, zero_of(sums[0]))
    far = scatter_far(q)
    mine2, other2, sums = the_terms(WAVES[2], sums, [q[2, 1], early_other[0]])
    mine3, other3, sums = the_terms(WAVES[3], sums, [early_other[1], *far])
    zero = zero_of(sums[0])

    def from_owners(rows):
        return [
            fetch_from(rows[dx], lambda xh, y, z, xl, c: (xh, y, z - y, xl ^ dx, c))
            for dx in range(2)
        ]

    early = jnp.concatenate(
        [add(e, other, zero).astype(BF) for e, other in zip(early, early_other, strict=True)]
    )
    early_own = jnp.concatenate([early[:, :T], fetch(early[:, T : 2 * T], dc=1)], axis=1)
    early_own = from_owners([early_own[:FFL], early_own[FFL:]])
    late = head_grads(
        normed,
        mixed_t,
        attended_t,
        all_cot,
        chip_order,
        part_order,
        core,
        me,
        gain,
        sums,
        (qkv_bias_part, fc1_bias_part, out_bias_part),
    )
    late_far = reduce_far(late)
    q |= own_terms(WAVES[1], mine1, other1, 0.0)
    q, early_own, late_far, far = together(
        q, early_own, late_far, far, also=(other2, other3, late)
    )

    *further, zero = scatter_next(q, far)
    late_near = reduce_near(late, late_far, zero)
    late_near = fetch(late_near[0], dy=-1), fetch(late_near[1], dy=1)
    q |= own_terms(WAVES[2], mine2, other2, 0.0) | own_terms(WAVES[3], mine3, other3, 0.0)
    late = add(late[0], *late_near).astype(BF)
    late_other = fetch(late, dh=1)
    early = jnp.concatenate(
        [
            jnp.concatenate([early_own[dx], early[dx * FFL : (dx + 1) * FFL, 2 * T :]], axis=1)
            for dx in range(2)
        ]
    )
    early_one, early_three = fetch(early, dy=1), fetch(early, dy=-1)
    q, further, late_other, early_one, early_three = together(
        q, further, late_other, early_one, early_three
    )

    nearest = scatter_near(q, further, 0.0)
    early = (
        early,
        early_one,
        early_three,
        fetch(early_one[:FFL], dy=1),
        fetch(early_three[FFL:], dy=-1),
    )
    late = add(late, late_other).astype(BF)
    late_rows = jnp.concatenate([late[:FOR_OWNER], late[LATE : LATE + FOR_OWNER]])
    late_own = jnp.concatenate([late_rows[:, :T], fetch(late_rows[:, T:], dc=1)], axis=1)
    late_own = from_owners([late_own[:FOR_OWNER], late_own[FOR_OWNER:]])
    late = jnp.concatenate(
        [late_own[0], late[FOR_OWNER:LATE], late_own[1], late[LATE + FOR_OWNER :]]
    )
    late_one, late_three = fetch(late, dy=1), fetch(late, dy=-1)
    total = add(q[0, 0], *nearest)
    own = tokens.astype(F32)
    layer_out = (own + out_bias + total[:, D:]).astype(BF)
    center = own - jnp.mean(own, axis=-1, keepdims=True)
    inv_std = lax.rsqrt(jnp.mean(center * center, axis=-1, keepdims=True) + 1e-05)
    unit = center * inv_std
    scaled = total[:, :D] * gain
    input_grad = cotangent.astype(F32) + inv_std * (
        scaled
        - jnp.mean(scaled, axis=-1, keepdims=True)
        - unit * jnp.mean(scaled * unit, axis=-1, keepdims=True)
    )
    late = (
        late,
        late_one,
        late_three,
        fetch(late_one[:LATE], dy=1),
        fetch(late_three[LATE:], dy=-1),
    )
    fc1_total, fc2_total = place_columns(early, col_place, part_place)
    qkv_total, dense_total, of_owner, of_own = place_heads(late, col_place, part_place)
    out_bias_total = of_own[0, FFL : FFL + T]

    return (
        layer_out,
        input_grad,
        of_owner[0],
        of_owner[1],
        qkv_total,
        of_owner[2:5].reshape(QKV),
        dense_total,
        out_bias_total,
        fc1_total,
        of_own[0, :FFL],
        fc2_total,
        out_bias_total,
    )


def solution(mesh):
    return jax.shard_map(
        body,
        mesh=mesh,
        in_specs=(
            P(AXES, None),
            P("shard"),
            P("shard"),
            P("shard", None),
            P("shard"),
            P("shard", None),
            P("shard"),
            P("shard", None),
            P("shard"),
            P("shard", None),
            P("shard"),
            P(AXES, None),
        ),
        out_specs=(
            P(AXES, None),
            P(AXES, None),
            P("shard"),
            P("shard"),
            P("shard", None),
            P("shard"),
            P("shard", None),
            P("shard"),
            P("shard", None),
            P("shard"),
            P("shard", None),
            P("shard"),
        ),
        check_vma=False,
    )
```

```python
import functools
import math

import jax
import jax.numpy as jnp
from jax import lax
from jax.experimental import pallas as pl
from jax.experimental.pallas import tpu as pltpu
from jax.sharding import PartitionSpec as P

D = 2048
HEADS = 32
HEAD_DIM = 64
ROTARY = 32
FF = 8192
SEQ = 2048
T = 128
QKV = 384
FFL = 512
COLS = QKV + FFL
BF = jnp.bfloat16
F32 = jnp.float32
AXES = ("rep", "shard")
MIB = 1 << 20
LOG2E = math.log2(math.e)

PLACES = [
    (xh, y, z, xl, c)
    for xh in range(2)
    for y in range(4)
    for z in range(4)
    for xl in range(2)
    for c in range(2)
]


def flat(xh, y, z, xl, c):
    return (xh * 4 + y % 4) * 16 + (z % 4) * 4 + xl * 2 + c


def fetch_from(x, source):
    return lax.ppermute(x, AXES, [(flat(*source(*p)), flat(*p)) for p in PLACES])


def fetch(x, dz=0, dx=0, dc=0, dy=0, dh=0):
    return fetch_from(
        x, lambda xh, y, z, xl, c: (xh ^ dh, y + dy, z + dz, xl ^ dx, c ^ dc)
    )


def dot(a, b, ca=1, cb=0):
    return lax.dot_general(a, b, (((ca,), (cb,)), ((), ())), preferred_element_type=F32)


def add(*terms):
    total = terms[0].astype(F32)
    for term in terms[1:]:
        total = total + (term if isinstance(term, float) else term.astype(F32))
    return total


def zero_of(x):
    return x[0, 0].astype(F32) * 0.0


def together(*groups, also=()):
    leaves, tree = jax.tree.flatten(groups)
    others = jax.tree.leaves(also)
    n = len(leaves)
    leaves = pl.pallas_call(
        lambda *refs: None,
        in_specs=[pl.BlockSpec(memory_space=pl.ANY)] * (n + len(others)),
        out_specs=[pl.BlockSpec(memory_space=pl.ANY)] * n,
        out_shape=[jax.ShapeDtypeStruct(x.shape, x.dtype) for x in leaves],
        input_output_aliases={i: i for i in range(n)},
        compiler_params=pltpu.CompilerParams(vmem_limit_bytes=MIB),
    )(*leaves, *others)
    return jax.tree.unflatten(tree, leaves)


def gather_near(own):
    return {
        (0, 0): own,
        (1, 0): fetch(own, dz=1),
        (3, 0): fetch(own, dz=-1),
        (0, 1): fetch(own, dx=1),
    }


def gather_next(a):
    return {
        (1, 1): fetch(a[1, 0], dx=1),
        (3, 1): fetch(a[0, 1], dz=-1),
        (2, 0): fetch(a[1, 0], dz=1),
    }


def gather_far(a):
    return fetch(a[2, 0], dx=1)


def gather_swap(own):
    return fetch(own, dc=1)


def both_cores(a):
    pieces = []
    for (dz, dx), own in a.items():
        pair = own if isinstance(own, tuple) else (own, gather_swap(own))
        pieces += [(pair[dc], ((dz * 2 + dx) * 2 + dc) * T) for dc in range(2)]
    return pieces


SLOTS = [(dz, dx, dc) for dz in range(4) for dx in range(2) for dc in range(2)]
WAVES = [[(2, 1)], [(1, 1), (3, 1), (2, 0)], [(1, 0), (3, 0)], [(0, 1), (0, 0)]]


def scatter_far(q):
    half = T // 2
    return fetch(q[2, 1][:half], dz=-1), fetch(q[2, 1][half:], dz=1)


def scatter_next(q, far):
    half = T // 2
    q11 = jnp.concatenate([add(q[1, 1][:half], far[0]).astype(BF), q[1, 1][half:]])
    q31 = jnp.concatenate([q[3, 1][:half], add(q[3, 1][half:], far[1]).astype(BF)])
    zero = zero_of(q11) + zero_of(q31)
    return fetch(q[2, 0], dz=-1), fetch(q31, dz=1), fetch(q11, dx=1), zero


def scatter_along(q, further):
    q10 = add(q[1, 0], further[0], further[2]).astype(BF)
    return fetch(q10, dz=-1), fetch(q[3, 0], dz=1)


def scatter_across(q, further, zero):
    return fetch(add(q[0, 1], further[1], zero).astype(BF), dx=1)


def reduce_far(g):
    half = g[0].shape[0] // 2
    return fetch(g[2][:half], dy=-1), fetch(g[2][half:], dy=1)


def reduce_near(g, far, zero):
    half = g[0].shape[0] // 2
    g1 = jnp.concatenate([add(g[1][:half], far[0], zero).astype(BF), g[1][half:]])
    g3 = jnp.concatenate([g[3][:half], add(g[3][half:], far[1], zero).astype(BF)])
    return g1, g3


def of_rep(refs, dy, dx, n):
    own, one, three, first, second = refs
    if dy == 2:
        return (second if dx else first), 0
    return (own, one, None, three)[dy], dx * n


VMEM = pl.BlockSpec(memory_space=pltpu.VMEM)
SMEM = pl.BlockSpec(memory_space=pltpu.SMEM)
HBM = pl.BlockSpec(memory_space=pltpu.HBM)
ANY = pl.BlockSpec(memory_space=pl.ANY)


def lanes(at, n):
    return pl.ds(pl.multiple_of(at * n, n), n)


def call(kernel, ins, outs, args, scratch=(), vmem=6, flops=0, nbytes=0, exps=0, aliases={}, out_specs=None):
    return pl.pallas_call(
        kernel,
        in_specs=ins,
        out_specs=out_specs or [VMEM] * len(outs),
        out_shape=[
            pltpu.VMEM(o[0], o[1]) if len(o) > 2 else jax.ShapeDtypeStruct(*o) for o in outs
        ],
        scratch_shapes=list(scratch),
        input_output_aliases=aliases,
        compiler_params=pltpu.CompilerParams(vmem_limit_bytes=vmem * MIB),
        cost_estimate=pl.CostEstimate(
            flops=flops, transcendentals=exps, bytes_accessed=nbytes
        ),
    )(*args)


ROOT = math.sqrt(2.0 / math.pi)


def start_copies(pieces, place, sems):
    copies = [
        pltpu.make_async_copy(src, dst, sems.at[place + i]) for i, (src, dst) in enumerate(pieces)
    ]
    for copy in copies:
        copy.start()
    return copies


def norm_rows(normed_ref, gain, shift, first, count):
    def strip(i, _):
        at = lanes(i, 64)
        x = normed_ref[at, :].astype(F32)
        x = x - jnp.sum(x, axis=1, keepdims=True) * (1.0 / D)
        scale = lax.rsqrt(jnp.sum(x * x, axis=1, keepdims=True) * (1.0 / D) + 1e-05)
        normed_ref[at, :] = (x * scale * gain + shift).astype(BF)
        return 0

    lax.fori_loop(first // 64, (first + count) // 64, strip, 0)


def grid_call(kernel, prefetch, grid, ins, outs, args, scratch=(), vmem=32, flops=0, nbytes=0):
    return pl.pallas_call(
        kernel,
        grid_spec=pltpu.PrefetchScalarGridSpec(
            num_scalar_prefetch=len(prefetch),
            grid=grid,
            in_specs=ins,
            out_specs=[o[2] for o in outs],
            scratch_shapes=list(scratch),
        ),
        out_shape=[jax.ShapeDtypeStruct(o[0], o[1]) for o in outs],
        compiler_params=pltpu.CompilerParams(vmem_limit_bytes=vmem * MIB),
        cost_estimate=pl.CostEstimate(flops=flops, transcendentals=0, bytes_accessed=nbytes),
    )(*prefetch, *args)


def whole(*shape):
    return pl.BlockSpec(shape, lambda *_: (0,) * len(shape))


def group_vectors(pieces, far_vectors, token_place, me):
    n = len(pieces)

    def kernel(t_ref, me_ref, *refs):
        far_ref, vec_ref, own_ref, small_ref, flat_ref, sems = refs[n:]
        moves = [
            (ref.at[pl.ds(0, 16), pl.ds(2 * D, T)], small_ref.at[pl.ds(at // T * 16, 16)])
            for (_, at), ref in zip(pieces, refs[:n], strict=True)
        ]
        for dc in range(2):
            to = small_ref.at[pl.ds((5 * 2 + dc) * 16, 16)]
            moves.append((far_ref.at[pl.ds(dc * 16, 16)], to))
        for copy in start_copies(moves, 0, sems):
            copy.wait()
        for i in range(16):
            at = t_ref[i]
            small = small_ref[i * 16 : (i + 1) * 16, :].astype(F32)
            for part in range(3):
                flat_ref[0:1, lanes(at * 3 + part, T)] = small[part : part + 1]
            vec_ref[0:1, lanes(at, T)] = small[3:4]
            vec_ref[1:2, lanes(at, T)] = small[4:5]
            vec_ref[2:3, lanes(at, T)] = small[5:6] + small[6:7]
        for part in range(3):
            own_ref[0:1, part * T : (part + 1) * T] = flat_ref[
                0:1, lanes(part * 16 + me_ref[0], T)
            ]

    return call(
        kernel,
        [SMEM] * 2 + [HBM] * (n + 1),
        [((8, D), F32), ((1, QKV), F32)],
        [token_place, me] + [p for p, _ in pieces] + [far_vectors],
        [
            pltpu.VMEM((256, T), BF),
            pltpu.VMEM((1, 3 * D), F32),
            pltpu.SemaphoreType.DMA((n + 2,)),
        ],
        vmem=56,
    )


def chip_rows(pieces, vecs, fc2, dense, arrays, before):
    n, given = len(pieces), len(arrays)
    chips = sorted({at // 256 for _, at in pieces})

    def kernel(*refs):
        refs = refs[len(before) + given :]
        tok = refs[:n]
        vec_ref, fc2_ref, dense_ref = refs[n : n + 3]
        outs, done_ref = refs[n + 3 : n + 7], refs[n + 7]
        bufs, in_sems, out_sems = refs[n + 8 : n + 12], refs[n + 12], refs[n + 13]
        done_ref[...] = jnp.zeros_like(done_ref)

        def arriving(k):
            moves = []
            for (array, at), ref in zip(pieces, tok, strict=True):
                if at // 256 == chips[k]:
                    to = pl.ds(at % 256, array.shape[0])
                    moves.append((ref.at[:, pl.ds(0, D)], bufs[0].at[k % 3, to]))
                    moves.append((ref.at[:, pl.ds(D, D)], bufs[1].at[k % 3, to]))
            return [
                pltpu.make_async_copy(src, dst, in_sems.at[k % 3, i])
                for i, (src, dst) in enumerate(moves)
            ]

        def leaving(k):
            rows = pl.ds(chips[k] * 256, 256)
            return [
                pltpu.make_async_copy(buf.at[k % 3], out.at[rows], out_sems.at[k % 3, i])
                for i, (buf, out) in enumerate(zip(bufs, outs, strict=True))
            ]

        for copy in arriving(0):
            copy.start()
        for k in range(len(chips)):
            if k + 1 < len(chips):
                if k >= 2:
                    for copy in leaving(k - 2):
                        copy.wait()
                for copy in arriving(k + 1):
                    copy.start()
            for copy in arriving(k):
                copy.wait()
            norm_rows(bufs[0].at[k % 3], vec_ref[0:1, :], vec_ref[1:2, :], 0, 256)
            x = bufs[1][k % 3]
            bufs[2][k % 3] = dot(x, fc2_ref[...], 1, 1).astype(BF)
            bufs[3][k % 3] = dot(x, dense_ref[...], 1, 1).astype(BF)
            for copy in leaving(k):
                copy.start()
        for k in range(max(len(chips) - 3, 0), len(chips)):
            for copy in leaving(k):
                copy.wait()

    widths = (D, D, FFL, T)
    return call(
        kernel,
        [ANY] * (len(before) + given) + [HBM] * n + [VMEM] * 3,
        [((SEQ, w), BF) for w in widths] + [((8, T), F32)],
        [*before, *arrays, *[p for p, _ in pieces], vecs, fc2, dense],
        [pltpu.VMEM((3, 256, w), BF) for w in widths]
        + [pltpu.SemaphoreType.DMA((3, 8)), pltpu.SemaphoreType.DMA((3, 4))],
        vmem=56,
        aliases={len(before) + i: i for i in range(given)},
        out_specs=[ANY] * 4 + [VMEM],
        flops=2 * n * T * D * (FFL + T),
        nbytes=n * MIB,
    )


def forward_inputs(normed, cot, act_grad, weights, bias, own_bias, row_place, me):
    def kernel(
        r_ref,
        me_ref,
        n_ref,
        grad_ref,
        cot_ref,
        w0_ref,
        w1_ref,
        w2_ref,
        w3_ref,
        bias_ref,
        own_ref,
        act_ref,
        pre_ref,
        act_t_ref,
        pre_t_ref,
        mixed_ref,
        fc1b_ref,
        outb_ref,
        w_out,
        w_ref,
        sems,
        out_sem,
    ):
        step = pl.program_id(0)
        leaving = pltpu.make_async_copy(w_ref, w_out, out_sem.at[0])

        @pl.when(step == 0)
        def _():
            moves = []
            for i, (dy, dx, dc) in enumerate(SLOTS):
                rows = pl.ds((dx * 2 + dc) * T, T)
                source = (w0_ref, w1_ref, w2_ref, w3_ref)[dy]
                moves.append((source.at[rows], w_ref.at[lanes(r_ref[i], T)]))
            for copy in start_copies(moves, 0, sems):
                copy.wait()
            leaving.start()
            fc1b_ref[...] = jnp.zeros_like(fc1b_ref)
            outb_ref[...] = jnp.zeros_like(outb_ref)

        halves = []
        for half in range(2):
            x = n_ref[half * 256 : (half + 1) * 256, :]
            mixed_ref[half * 256 : (half + 1) * 256, :] = dot(x, w_ref[:, :QKV]) + own_ref[...]
            halves.append(dot(x, w_ref[:, QKV:]) + bias_ref[...])
        for half, pre in enumerate(halves):
            at = slice(half * 256, (half + 1) * 256)
            squared = pre * pre
            tanh = jnp.tanh(ROOT * pre * (1.0 + 0.044715 * squared))
            act = (0.5 * pre * (1.0 + tanh)).astype(BF)
            act_ref[at, :] = act
            act_t_ref[:, at] = act.T
            slope = 0.5 * (1.0 + tanh) + 0.5 * pre * (1.0 - tanh * tanh) * ROOT * (
                1.0 + 3 * 0.044715 * squared
            )
            back = (grad_ref[at, :].astype(F32) * slope).astype(BF)
            pre_ref[at, :] = back
            pre_t_ref[:, at] = back.T
            fc1b_ref[...] += jnp.sum(back.astype(F32).reshape(32, 8, FFL), axis=0)
        outb_ref[...] += jnp.sum(cot_ref[...].astype(F32).reshape(64, 8, T), axis=0)

        @pl.when(step == pl.num_programs(0) - 1)
        def _():
            leaving.wait()

    rows = lambda i, *_: (i, 0)
    cols = lambda i, *_: (0, i)
    return grid_call(
        kernel,
        [row_place, me],
        (SEQ // 512,),
        [
            pl.BlockSpec((512, D), rows),
            pl.BlockSpec((512, FFL), rows),
            pl.BlockSpec((512, T), lambda i, r, m: (i, m[0])),
        ]
        + [HBM] * 4
        + [whole(1, FFL), whole(1, QKV)],
        [
            ((SEQ, FFL), BF, pl.BlockSpec((512, FFL), rows)),
            ((SEQ, FFL), BF, pl.BlockSpec((512, FFL), rows)),
            ((FFL, SEQ), BF, pl.BlockSpec((FFL, 512), cols)),
            ((FFL, SEQ), BF, pl.BlockSpec((FFL, 512), cols)),
            ((SEQ, QKV), F32, pl.BlockSpec((512, QKV), rows)),
            ((8, FFL), F32, whole(8, FFL)),
            ((8, T), F32, whole(8, T)),
            ((D, COLS), BF, ANY),
        ],
        [normed, act_grad, cot, *weights, bias, own_bias],
        [
            pltpu.VMEM((D, COLS), BF),
            pltpu.SemaphoreType.DMA((16,)),
            pltpu.SemaphoreType.DMA((1,)),
        ],
        vmem=56,
        flops=2 * SEQ * D * COLS,
        nbytes=24 * MIB,
    )


ORDER = (2, 1, 3, 0)


def in_order(places, parts):
    chips = jnp.stack([places[(dy * 2 + dx) * 2] // 2 for dy in ORDER for dx in range(2)])
    return chips, jnp.stack([parts[dy * 2 + dx] for dy in ORDER for dx in range(2)])


def fetched(refs, scratch, sems):
    copies = [
        pltpu.make_async_copy(ref, to, sems.at[i])
        for i, (ref, to) in enumerate(zip(refs, scratch, strict=True))
    ]
    for copy in copies:
        copy.start()
    return copies


def column_grads(normed, pre_t, act_t, cot, chips, parts, core):
    def kernel(chip_ref, part_ref, core_ref, normed_ref, cot_ref, g_ref, a_ref, *refs):
        outs, n_ref, c_ref, sems = refs[:4], refs[4], refs[5], refs[6]
        copies = fetched((normed_ref, cot_ref), (n_ref, c_ref), sems)
        copies[0].wait()
        for i in range(8):
            out, at = outs[i // 2], slice(i % 2 * FFL, (i % 2 + 1) * FFL)
            cols = dot(g_ref[...], n_ref[:, lanes(chip_ref[i], 256)]).astype(BF)
            out[at, lanes(core_ref[0], T)] = cols[:, :T]
            out[at, lanes(1 - core_ref[0], T)] = cols[:, T:]
        copies[1].wait()
        for i in range(8):
            out, at = outs[i // 2], slice(i % 2 * FFL, (i % 2 + 1) * FFL)
            out[at, 256:512] = dot(a_ref[...], c_ref[:, lanes(part_ref[i], 256)]).astype(BF)

    outs = call(
        kernel,
        [SMEM] * 3 + [ANY] * 2 + [VMEM] * 2,
        [((2 * FFL, 512), BF)] * 4,
        [chips, parts, core, normed, cot, pre_t, act_t],
        [pltpu.VMEM((SEQ, D), BF), pltpu.VMEM((SEQ, D), BF), pltpu.SemaphoreType.DMA((2,))],
        vmem=56,
        flops=4 * SEQ * D * FFL,
        nbytes=24 * MIB,
    )
    return [outs[ORDER.index(dy)] for dy in range(4)]


FOR_OWNER = QKV + 16
LATE = FOR_OWNER + T + 16


def head_grads(
    normed, mixed_t, attended_t, cot, chips, parts, core, me, gain, sums, bias_parts
):
    def kernel(chip_ref, part_ref, core_ref, me_ref, normed_ref, cot_ref, m_ref, a_ref, *refs):
        gain_ref, gains_ref, shifts_ref, qkvb_ref, fc1b_ref, outb_ref = refs[:6]
        outs, owners_ref, own_ref = refs[6:10], refs[10], refs[11]
        n_ref, c_ref, sems = refs[12:]
        copies = fetched((normed_ref, cot_ref), (n_ref, c_ref), sems)
        owners_ref[...] = jnp.zeros_like(owners_ref)
        owners_ref[0:1, :] = jnp.sum(gains_ref[...], axis=0, keepdims=True) / gain_ref[...]
        owners_ref[1:2, :] = jnp.sum(shifts_ref[...], axis=0, keepdims=True)
        qkvb = jnp.sum(qkvb_ref[...], axis=0, keepdims=True)
        for part in range(3):
            at = part * 16 + me_ref[0]
            third = at % 3
            row = lax.broadcasted_iota(jnp.int32, (8, T), 0)
            value = jnp.where(row == 2 + third, qkvb[:, part * T : (part + 1) * T], 0.0)
            owners_ref[0:8, lanes(at // 3, T)] += value
        own_ref[...] = jnp.zeros_like(own_ref)
        own_ref[0:1, :FFL] = jnp.sum(fc1b_ref[...], axis=0, keepdims=True)
        own_ref[0:1, FFL : FFL + T] = jnp.sum(outb_ref[...], axis=0, keepdims=True)
        mine, other = lanes(core_ref[0], T), lanes(1 - core_ref[0], T)
        copies[0].wait()
        for i in range(8):
            out, base = outs[i // 2], i % 2 * LATE
            cols = dot(m_ref[...], n_ref[:, lanes(chip_ref[i], 256)]).astype(BF)
            extra = owners_ref[:, lanes(chip_ref[i], 256)].astype(BF)
            out[base : base + QKV, mine] = cols[:, :T]
            out[base : base + QKV, other] = cols[:, T:]
            out[base + QKV : base + FOR_OWNER, mine] = extra[:, :T]
            out[base + QKV : base + FOR_OWNER, other] = extra[:, T:]
        copies[1].wait()
        for i in range(8):
            out, base = outs[i // 2], i % 2 * LATE + FOR_OWNER
            part = part_ref[i]
            out[base : base + T, :] = dot(a_ref[...], c_ref[:, lanes(part, 256)]).astype(BF)
            out[base + T : base + T + 16, 0:T] = own_ref[:, lanes(part, T)].astype(BF)
            out[base + T : base + T + 16, T:] = jnp.zeros((16, T), BF)

    outs = call(
        kernel,
        [SMEM] * 4 + [ANY] * 2 + [VMEM] * 8,
        [((2 * LATE, 256), BF)] * 4,
        [chips, parts, core, me, normed, cot, mixed_t, attended_t, gain, *sums, *bias_parts],
        [
            pltpu.VMEM((16, D), F32),
            pltpu.VMEM((16, 1024), F32),
            pltpu.VMEM((SEQ, D), BF),
            pltpu.VMEM((SEQ, D), BF),
            pltpu.SemaphoreType.DMA((2,)),
        ],
        vmem=36,
        flops=2 * SEQ * D * (QKV + T),
        nbytes=20 * MIB,
    )
    return [outs[ORDER.index(dy)] for dy in range(4)]


def place_columns(pieces, col_place, part_place):
    def kernel(c_ref, p_ref, *refs):
        fc1_ref, fc2_ref = refs[5:]
        for i, (dy, dh, dc) in enumerate(SLOTS):
            ref, at = of_rep(refs[:5], dy, dh, FFL)
            part = ref[at : at + FFL, dc * T : (dc + 1) * T]
            fc1_ref[:, lanes(c_ref[i], FFL)] = part.astype(F32).T
            if dc == 0:
                to = lanes(p_ref[dy * 2 + dh], 256)
                fc2_ref[:, to] = ref[at : at + FFL, 256:512].astype(F32)

    return call(
        kernel,
        [SMEM] * 2 + [VMEM] * 5,
        [((T, FF), F32), ((FFL, D), F32)],
        [col_place, part_place] + list(pieces),
        vmem=20,
        nbytes=12 * MIB,
    )


def place_heads(pieces, col_place, part_place, before):
    def kernel(c_ref, p_ref, *refs):
        qkv_ref, dense_ref, owner_ref, own_ref = refs[-4:]
        total = jnp.zeros((16, T), F32)
        for i, (dy, dx, dc) in enumerate(SLOTS):
            ref, at = of_rep(refs[:5], dy, dx, LATE)
            cols = slice(dc * T, (dc + 1) * T)
            for part in range(3):
                block = ref[at + part * T : at + (part + 1) * T, cols].astype(F32)
                qkv_ref[:, lanes(c_ref[i] + part * 16, T)] = block.T
            total += ref[at + QKV : at + FOR_OWNER, cols].astype(F32)
            if dc == 0:
                part = p_ref[dy * 2 + dx]
                rows = slice(at + FOR_OWNER, at + FOR_OWNER + T)
                dense_ref[:, lanes(part, 256)] = ref[rows, :].astype(F32)
                rows = slice(at + FOR_OWNER + T, at + LATE)
                own_ref[:, lanes(part, T)] = ref[rows, 0:T].astype(F32)
        owner_ref[...] = total

    return call(
        kernel,
        [SMEM] * 2 + [VMEM] * 5 + [ANY] * len(before),
        [((T, 3 * D), F32), ((T, D), F32), ((16, T), F32), ((16, 1024), F32)],
        [col_place, part_place, *pieces, *before],
        vmem=14,
        nbytes=6 * MIB,
    )


def terms(
    chips, attended, activated, dense, fc2, mixed_grad, pre_grad, weight, normed, vecs, sums, before
):
    n = len(chips)
    order = jnp.array([dz * 2 + dx for dz, dx in chips], jnp.int32)

    def kernel(order_ref, a_ref, f_ref, m_ref, p_ref, n_ref, d_ref, v_ref, w_ref, vec_ref, *refs):
        mine_ref, other_ref, gain_ref, total_ref = refs[-4:]
        shift = vec_ref[1:2, :]

        @pl.when(pl.program_id(0) == 0)
        def _():
            if sums:
                gain_ref[...] = refs[0][...]
                total_ref[...] = refs[1][...]
            else:
                gain_ref[...] = jnp.zeros_like(gain_ref)
                total_ref[...] = jnp.zeros_like(total_ref)

        for col in range(4):
            to = slice(col * 512, (col + 1) * 512)
            total = dot(m_ref[...], w_ref[to, :QKV], 1, 1) + dot(p_ref[...], w_ref[to, QKV:], 1, 1)
            mine_ref[:, to] = total[:T].astype(BF)
            other_ref[:, to] = total[T:].astype(BF)
            unit = n_ref[:, to].astype(F32) - shift[:, to]
            gain_ref[:, to] += jnp.sum((total * unit).reshape(32, 8, 512), axis=0)
            total_ref[:, to] += jnp.sum(total.reshape(32, 8, 512), axis=0)
            total = dot(a_ref[...], d_ref[:, to]) + dot(f_ref[...], v_ref[:, to])
            to = slice(D + col * 512, D + (col + 1) * 512)
            mine_ref[:, to] = total[:T].astype(BF)
            other_ref[:, to] = total[T:].astype(BF)

    rows = lambda i, order_ref: (order_ref[i], 0)
    here = lambda i, order_ref: (i, 0)
    return grid_call(
        kernel,
        [order],
        (n,),
        [
            pl.BlockSpec((2 * T, T), rows),
            pl.BlockSpec((2 * T, FFL), rows),
            pl.BlockSpec((2 * T, QKV), rows),
            pl.BlockSpec((2 * T, FFL), rows),
            pl.BlockSpec((2 * T, D), rows),
            whole(T, D),
            whole(FFL, D),
            whole(D, COLS),
            whole(8, D),
        ]
        + [whole(8, D)] * len(sums)
        + [ANY] * len(before),
        [((n * T, 2 * D), BF, pl.BlockSpec((T, 2 * D), here))] * 2
        + [((8, D), F32, whole(8, D))] * 2,
        [attended, activated, mixed_grad, pre_grad, normed, dense, fc2, weight, vecs, *sums, *before],
        flops=2 * n * 2 * T * (COLS + T + FFL) * D,
        nbytes=8 * MIB,
    )


TQ = 512
TK = 512


def attention_kernel(blocks, last, n_before, place, cos_ref, sin_ref, *refs):
    refs = refs[n_before:]
    if last:
        first_refs, refs = refs[:8], refs[8:]
        att_ref, out_ref, att_t_ref, out_t_ref, bias_ref = refs[:5]
        q_ref, k_ref, v_ref, do_ref = first_refs[:4]
        dq_ref, dk_ref, dv_ref, o_ref, s_ref, e_ref = refs[5:]
    else:
        mixed_ref, grad_ref, *refs = refs
        refs, done_ref = refs[:8] + refs[9:], refs[8]
        done_ref[...] = jnp.zeros_like(done_ref)
        q_ref, k_ref, v_ref, do_ref, dq_ref, dk_ref, dv_ref, o_ref, s_ref, e_ref = refs
    lane = lax.broadcasted_iota(jnp.int32, (T, 128), 1)
    low_head = lane < HEAD_DIM
    first = (lane % HEAD_DIM) < ROTARY // 2

    def turned(x):
        return jnp.where(
            first, pltpu.roll(x, 128 - ROTARY // 2, 1), pltpu.roll(x, ROTARY // 2, 1)
        )

    def load(slot, _):
        rows = pl.ds(pl.multiple_of(slot * T, T), T)
        at = pl.ds(pl.multiple_of(place[slot] * T, T), T)
        c, s = cos_ref[at, :], sin_ref[at, :]
        query = mixed_ref[rows, 0:128]
        key = mixed_ref[rows, 128:256]
        query = (query * c + turned(query) * s).astype(BF).astype(F32) * (HEAD_DIM**-0.5)
        q_ref[0, at, :] = jnp.where(low_head, query, 0.0).astype(BF)
        q_ref[1, at, :] = jnp.where(low_head, 0.0, query).astype(BF)
        k_ref[at, :] = (key * c + turned(key) * s).astype(BF)
        v_ref[at, 0:128] = mixed_ref[rows, 256:384].astype(BF)
        v_ref[at, 128:256] = jnp.ones((T, 128), BF)
        grad = grad_ref[rows, :].astype(F32)
        do_ref[0, at, :] = jnp.where(low_head, grad, 0.0).astype(BF)
        do_ref[1, at, :] = jnp.where(low_head, 0.0, grad).astype(BF)
        dk_ref[:, at] = jnp.zeros((128, T), F32)
        dv_ref[:, at] = jnp.zeros((128, T), F32)
        return 0

    if last:
        for to, at in ((dq_ref, 4), (dk_ref, 5), (dv_ref, 6), (o_ref, 7)):
            to[...] = first_refs[at][...]
    else:
        lax.fori_loop(0, 16, load, 0)

    lane_q = lax.broadcasted_iota(jnp.int32, (TQ, 128), 1)
    low_q = lane_q < HEAD_DIM

    def block(i, _):
        rows = lanes(i, TQ)
        queries = [q_ref[h, rows, :] for h in range(2)]

        def scores(j, tops, masked):
            at = lanes(j, TK)
            keys = k_ref[at, :]
            new = []
            for h in range(2):
                s = dot(queries[h], keys, 1, 1)
                if masked:
                    row = lax.broadcasted_iota(jnp.int32, (TQ, TK), 0)
                    col = lax.broadcasted_iota(jnp.int32, (TQ, TK), 1)
                    s = jnp.where(row >= col, s, -1e30)
                s_ref[h, :, at] = s
                top = tops[h]
                for n in range(TK // 128):
                    top = jnp.maximum(top, s[:, n * 128 : (n + 1) * 128])
                new.append(top)
            return tuple(new)

        low = jnp.full((TQ, 128), -1e30, F32)
        tops = lax.fori_loop(0, i, lambda j, t: scores(j, t, False), (low, low))
        tops = [jnp.max(t, axis=1, keepdims=True) for t in scores(i, tops, True)]

        def weigh(j, totals):
            at = lanes(j, TK)
            values = v_ref[at, :]
            new = []
            for h in range(2):
                e = jnp.exp2((s_ref[h, :, at] - tops[h]) * LOG2E).astype(BF)
                e_ref[h, :, at] = e
                new.append(totals[h] + dot(e, values))
            return tuple(new)

        zero = jnp.zeros((TQ, 256), F32)
        totals = lax.fori_loop(0, i + 1, weigh, (zero, zero))
        outs, grads, deltas = [], [], []
        for h in range(2):
            inverse = 1.0 / totals[h][:, 128:]
            o = totals[h][:, :128] * inverse
            grad = do_ref[h, rows, :].astype(F32) * inverse
            outs.append(o)
            deltas.append(jnp.sum(grad * o, axis=1, keepdims=True))
            grads.append(grad.astype(BF))
        o_ref[rows, :] = jnp.where(low_q, outs[0], outs[1]).astype(BF)
        queries_t = [q.T for q in queries]
        grads_t = [g.T for g in grads]

        def back(j, totals):
            at = lanes(j, TK)
            keys = k_ref[at, :]
            values = v_ref[at, 0:128]
            new, dk, dv = [], None, None
            for h in range(2):
                e = e_ref[h, :, at]
                dp = dot(grads[h], values, 1, 1)
                ds = (e.astype(F32) * (dp - deltas[h])).astype(BF)
                new.append(totals[h] + dot(ds, keys))
                k_part = dot(queries_t[h], ds)
                v_part = dot(grads_t[h], e)
                dk = k_part if dk is None else dk + k_part
                dv = v_part if dv is None else dv + v_part
            dk_ref[:, at] += dk
            dv_ref[:, at] += dv
            return tuple(new)

        zero = jnp.zeros((TQ, 128), F32)
        dqs = lax.fori_loop(0, i + 1, back, (zero, zero))
        dq_ref[rows, :] = jnp.where(low_q, dqs[0], dqs[1]) * (HEAD_DIM**-0.5)
        return 0

    lax.fori_loop(blocks[0], blocks[1], block, 0)
    if not last:
        return

    def store(slot, total):
        rows = pl.ds(pl.multiple_of(slot * T, T), T)
        at = pl.ds(pl.multiple_of(place[slot] * T, T), T)
        c, s = cos_ref[at, :], sin_ref[at, :]
        att = o_ref[at, :]
        att_ref[rows, :] = att
        att_t_ref[:, rows] = att.T
        dq, dk = dq_ref[at, :], dk_ref[:, at].T
        new = []
        for part, grad in enumerate(
            (dq * c - turned(dq) * s, dk * c - turned(dk) * s, dv_ref[:, at].T)
        ):
            low = grad.astype(BF)
            cols = slice(part * T, (part + 1) * T)
            out_ref[rows, cols] = low
            out_t_ref[cols, rows] = low.T
            new.append(total[part] + jnp.sum(low.astype(F32).reshape(16, 8, T), axis=0))
        return tuple(new)

    zero = jnp.zeros((8, T), F32)
    sums = lax.fori_loop(0, 16, store, (zero, zero, zero))
    for part in range(3):
        bias_ref[:, part * T : (part + 1) * T] = sums[part]


def attention_first(place, cosine, sine, mixed, attended_grad, before):
    return call(
        functools.partial(attention_kernel, (0, 2), False, len(before)),
        [SMEM] + [VMEM] * 2 + [ANY] * len(before) + [VMEM] * 2,
        [
            ((2, SEQ, 128), BF, 1),
            ((SEQ, 128), BF, 1),
            ((SEQ, 256), BF, 1),
            ((2, SEQ, 128), BF, 1),
            ((SEQ, 128), F32, 1),
            ((128, SEQ), F32, 1),
            ((128, SEQ), F32, 1),
            ((SEQ, 128), BF, 1),
            ((8, 128), jnp.int32),
        ],
        [place, cosine, sine, *before, mixed, attended_grad],
        [pltpu.VMEM((2, TQ, SEQ), F32), pltpu.VMEM((2, TQ, SEQ), BF)],
        vmem=24,
        flops=8 * SEQ * SEQ * 64 * 2,
        exps=SEQ * SEQ // 2,
        nbytes=3 * MIB,
    )


def attention_last(place, cosine, sine, state, before):
    return call(
        functools.partial(attention_kernel, (2, 4), True, len(before)),
        [SMEM] + [VMEM] * 2 + [ANY] * len(before) + [VMEM] * 8,
        [
            ((SEQ, T), BF),
            ((SEQ, QKV), BF),
            ((T, SEQ), BF),
            ((QKV, SEQ), BF),
            ((8, QKV), F32),
        ],
        [place, cosine, sine, *before] + list(state),
        [
            pltpu.VMEM((SEQ, 128), F32),
            pltpu.VMEM((128, SEQ), F32),
            pltpu.VMEM((128, SEQ), F32),
            pltpu.VMEM((SEQ, 128), BF),
            pltpu.VMEM((2, TQ, SEQ), F32),
            pltpu.VMEM((2, TQ, SEQ), BF),
        ],
        vmem=26,
        flops=6 * SEQ * SEQ * 64 * 2,
        exps=SEQ * SEQ // 2,
        nbytes=3 * MIB,
    )


def rotary_tables():
    lane = lax.broadcasted_iota(jnp.int32, (SEQ, 128), 1) % HEAD_DIM
    place = lax.broadcasted_iota(jnp.int32, (SEQ, 128), 0).astype(F32)
    freq = (lane % (ROTARY // 2)).astype(F32)
    angle = place * jnp.exp(freq * (-2.0 * math.log(10000.0) / ROTARY))
    turns = lane < ROTARY
    cosine = jnp.where(turns, jnp.cos(angle), 1.0)
    sine = jnp.where(turns, jnp.sin(angle), 0.0)
    return cosine, jnp.where(lane < ROTARY // 2, -sine, sine)


def body(
    tokens,
    ln_gain,
    ln_shift,
    qkv_weight,
    qkv_bias,
    dense_weight,
    dense_bias,
    fc1_weight,
    fc1_bias,
    fc2_weight,
    fc2_bias,
    cotangent,
):
    rep, shard = lax.axis_index("rep"), lax.axis_index("shard")
    xh, y = rep // 4, rep % 4
    z, xl, c = shard // 4, (shard // 2) % 2, shard % 2
    token_place = jnp.stack(
        [((z + dz) % 4) * 4 + (xl ^ dx) * 2 + (c ^ dc) for dz, dx, dc in SLOTS]
    ).astype(jnp.int32)
    row_place = jnp.stack(
        [((z + y + dy) % 4) * 4 + (xl ^ dx) * 2 + (c ^ dc) for dy, dx, dc in SLOTS]
    ).astype(jnp.int32)
    col_place = jnp.stack(
        [((z - y - dy) % 4) * 4 + (xl ^ dx) * 2 + (c ^ dc) for dy, dx, dc in SLOTS]
    ).astype(jnp.int32)
    part_place = jnp.stack(
        [((y + dy) % 4) * 2 + dx for dy in range(4) for dx in range(2)]
    ).astype(jnp.int32)
    chip_order, part_order = in_order(row_place, part_place)
    me, core = shard.reshape(1).astype(jnp.int32), c.reshape(1).astype(jnp.int32)

    vectors = [v.reshape(-1, T) for v in (qkv_bias, ln_gain, ln_shift, dense_bias, fc2_bias)]
    vectors = jnp.concatenate(vectors + [jnp.zeros((T - 7, T), BF)])
    message = jnp.concatenate([tokens, cotangent, vectors], axis=1)
    near = gather_near(message)

    def columns_for(chip):
        qkv = [
            lax.dynamic_slice(qkv_weight, (0, part * D + chip * 2 * T), (T, 2 * T))
            for part in range(3)
        ]
        fc1 = lax.dynamic_slice(fc1_weight, (0, chip * 2 * FFL), (T, 2 * FFL))
        return jnp.concatenate(
            [
                jnp.concatenate(
                    [p[:, at * T : (at + 1) * T] for p in qkv]
                    + [fc1[:, at * FFL : (at + 1) * FFL]],
                    axis=1,
                )
                for at in range(2)
            ]
        )

    to_chip = ((z - y) % 4) * 2 + xl
    mine, other = columns_for(to_chip ^ c), columns_for(to_chip ^ c ^ 1)
    other = fetch(other, dc=1)
    rows = fetch_from(
        jnp.concatenate([mine, other]), lambda xh, y, z, xl, c: (xh, y, z + y, xl ^ c, c)
    )
    own_pair = message, gather_swap(message)
    cosine, sine = rotary_tables()
    rows, near[1, 0], near[0, 1] = together(
        rows, near[1, 0], near[0, 1], also=(near[3, 0], own_pair, cosine, sine)
    )

    def columns_of(rows, core):
        return jnp.concatenate(
            [
                lax.dynamic_slice(rows, (n * 2 * T + core * T, 0), (T, COLS))
                for n in range(2)
            ]
        )

    mine = columns_of(rows, c)
    other = fetch(columns_of(rows, 1 - c), dc=1)
    here = jnp.where(c == 0, mine, jnp.concatenate([other[T:], other[:T]]))
    there = jnp.where(c == 0, jnp.concatenate([other[T:], other[:T]]), mine)
    own_rows = jnp.concatenate([here, there])
    further = gather_next(near)
    one, three = fetch(own_rows, dy=1), fetch(own_rows, dy=-1)
    one, three, further, near, far_vectors = together(one, three, further, near, vectors[:16])
    far_vectors = fetch(far_vectors, dz=2, dx=1)
    near_pairs = near | {(0, 0): own_pair}
    far_vectors = jnp.concatenate([far_vectors, fetch(far_vectors, dc=1)])
    far = gather_far(further)
    two = fetch(one, dy=1)
    pieces = both_cores(near_pairs) + both_cores(further)
    vecs, own_qkv_bias = group_vectors(pieces, far_vectors, token_place, me)
    *arrays, done = chip_rows(pieces, vecs, fc2_weight, dense_weight, [], [one, three])
    (far,) = together(far, also=(two, done))
    far = [(far, 10 * T), (gather_swap(far), 11 * T)]
    normed, all_cot, act_grad, attended_grad, _ = chip_rows(
        far, vecs, fc2_weight, dense_weight, arrays, []
    )
    gain, out_bias = vecs[0:1], vecs[2:3]
    (activated, pre_grad, act_t, pre_t, mixed, fc1_bias_part, out_bias_part, weight) = (
        forward_inputs(
            normed,
            all_cot,
            act_grad,
            (own_rows, one, two, three),
            fc1_bias.astype(F32).reshape(1, FFL),
            own_qkv_bias,
            row_place,
            me,
        )
    )

    early = column_grads(normed, pre_t, act_t, all_cot, chip_order, part_order, core)
    *state, done = attention_first(
        token_place, cosine, sine, mixed, attended_grad, early[:1]
    )
    early_near = reduce_near(early, reduce_far(early), done[0, 0].astype(F32))
    attended, mixed_grad, attended_t, mixed_t, qkv_bias_part = attention_last(
        token_place, cosine, sine, state, early_near
    )
    early = early[0], fetch(early_near[0], dy=-1), fetch(early_near[1], dy=1)
    zero = zero_of(qkv_bias_part)
    early = [
        add(*(e[dx * FFL : (dx + 1) * FFL] for e in early), zero).astype(BF) for dx in range(2)
    ]
    early_other = [fetch(e, dh=1) for e in early]

    def the_terms(chips, sums, before):
        mine, other, *sums = terms(
            chips,
            attended,
            activated,
            dense_weight,
            fc2_weight,
            mixed_grad,
            pre_grad,
            weight,
            normed,
            vecs,
            sums,
            before,
        )
        return mine, fetch(other, dc=1), sums

    def own_terms(chips, mine, other, zero):
        return {
            chip: add(mine[n * T : (n + 1) * T], other[n * T : (n + 1) * T], zero).astype(BF)
            for n, chip in enumerate(chips)
        }

    mine0, other0, sums = the_terms(WAVES[0], [], early)
    mine1, other1, sums = the_terms(WAVES[1], sums, [])
    q = own_terms(WAVES[0], mine0, other0, zero_of(sums[0]))
    far = scatter_far(q)
    mine2, other2, sums = the_terms(WAVES[2], sums, [q[2, 1], early_other[0]])
    mine3, other3, sums = the_terms(WAVES[3], sums, [early_other[1], *far])
    zero = zero_of(sums[0])

    def from_owners(rows):
        return [
            fetch_from(rows[dx], lambda xh, y, z, xl, c: (xh, y, z - y, xl ^ dx, c))
            for dx in range(2)
        ]

    early = jnp.concatenate(
        [add(e, other, zero).astype(BF) for e, other in zip(early, early_other, strict=True)]
    )
    early_own = jnp.concatenate([early[:, :T], fetch(early[:, T : 2 * T], dc=1)], axis=1)
    early_own = from_owners([early_own[:FFL], early_own[FFL:]])
    late = head_grads(
        normed,
        mixed_t,
        attended_t,
        all_cot,
        chip_order,
        part_order,
        core,
        me,
        gain,
        sums,
        (qkv_bias_part, fc1_bias_part, out_bias_part),
    )
    late_far = reduce_far(late)
    q |= own_terms(WAVES[1], mine1, other1, 0.0)
    q, early_own, late_far, far = together(
        q, early_own, late_far, far, also=(other2, other3, late)
    )

    *further, zero = scatter_next(q, far)
    late_near = reduce_near(late, late_far, zero)
    late_near = fetch(late_near[0], dy=-1), fetch(late_near[1], dy=1)
    q |= own_terms(WAVES[2], mine2, other2, 0.0) | own_terms(WAVES[3], mine3, other3, 0.0)
    late = add(late[0], *late_near).astype(BF)
    late_other = fetch(late, dh=1)
    early = jnp.concatenate(
        [
            jnp.concatenate([early_own[dx], early[dx * FFL : (dx + 1) * FFL, 2 * T :]], axis=1)
            for dx in range(2)
        ]
    )
    early = early + zero_of(late).astype(BF)
    early_one, early_three = fetch(early, dy=1), fetch(early, dy=-1)
    q, further = together(q, further)

    along = scatter_along(q, further)
    early = (
        early,
        early_one,
        early_three,
        fetch(early_one[:FFL], dy=1),
        fetch(early_three[FFL:], dy=-1),
    )
    late = add(late, late_other).astype(BF)
    late_rows = jnp.concatenate([late[:FOR_OWNER], late[LATE : LATE + FOR_OWNER]])
    late_own = jnp.concatenate([late_rows[:, :T], fetch(late_rows[:, T:], dc=1)], axis=1)
    late_own = from_owners([late_own[:FOR_OWNER], late_own[FOR_OWNER:]])
    across = scatter_across(q, further, zero_of(late_own[0]) + zero_of(late_own[1]))
    late = jnp.concatenate(
        [late_own[0], late[FOR_OWNER:LATE], late_own[1], late[LATE + FOR_OWNER :]]
    )
    late_one, late_three = fetch(late, dy=1), fetch(late, dy=-1)
    total = add(q[0, 0], *along, across)
    own = tokens.astype(F32)
    layer_out = (own + out_bias + total[:, D:]).astype(BF)
    center = own - jnp.mean(own, axis=-1, keepdims=True)
    inv_std = lax.rsqrt(jnp.mean(center * center, axis=-1, keepdims=True) + 1e-05)
    unit = center * inv_std
    scaled = total[:, :D] * gain
    input_grad = cotangent.astype(F32) + inv_std * (
        scaled
        - jnp.mean(scaled, axis=-1, keepdims=True)
        - unit * jnp.mean(scaled * unit, axis=-1, keepdims=True)
    )
    late = (
        late,
        late_one,
        late_three,
        fetch(late_one[:LATE], dy=1),
        fetch(late_three[LATE:], dy=-1),
    )
    fc1_total, fc2_total = place_columns(early, col_place, part_place)
    qkv_total, dense_total, of_owner, of_own = place_heads(
        late, col_place, part_place, [layer_out]
    )
    out_bias_total = of_own[0, FFL : FFL + T]

    return (
        layer_out,
        input_grad,
        of_owner[0],
        of_owner[1],
        qkv_total,
        of_owner[2:5].reshape(QKV),
        dense_total,
        out_bias_total,
        fc1_total,
        of_own[0, :FFL],
        fc2_total,
        out_bias_total,
    )


def solution(mesh):
    return jax.shard_map(
        body,
        mesh=mesh,
        in_specs=(
            P(AXES, None),
            P("shard"),
            P("shard"),
            P("shard", None),
            P("shard"),
            P("shard", None),
            P("shard"),
            P("shard", None),
            P("shard"),
            P("shard", None),
            P("shard"),
            P(AXES, None),
        ),
        out_specs=(
            P(AXES, None),
            P(AXES, None),
            P("shard"),
            P("shard"),
            P("shard", None),
            P("shard"),
            P("shard", None),
            P("shard"),
            P("shard", None),
            P("shard"),
            P("shard", None),
            P("shard"),
        ),
        check_vma=False,
    )
```

```python
import functools
import math

import jax
import jax.numpy as jnp
from jax import lax
from jax.experimental import pallas as pl
from jax.experimental.pallas import tpu as pltpu
from jax.sharding import PartitionSpec as P

D = 2048
HEADS = 32
HEAD_DIM = 64
ROTARY = 32
FF = 8192
SEQ = 2048
T = 128
QKV = 384
FFL = 512
COLS = QKV + FFL
BF = jnp.bfloat16
F32 = jnp.float32
AXES = ("rep", "shard")
MIB = 1 << 20
LOG2E = math.log2(math.e)

PLACES = [
    (xh, y, z, xl, c)
    for xh in range(2)
    for y in range(4)
    for z in range(4)
    for xl in range(2)
    for c in range(2)
]


def flat(xh, y, z, xl, c):
    return (xh * 4 + y % 4) * 16 + (z % 4) * 4 + xl * 2 + c


def fetch_from(x, source):
    return lax.ppermute(x, AXES, [(flat(*source(*p)), flat(*p)) for p in PLACES])


def fetch(x, dz=0, dx=0, dc=0, dy=0, dh=0):
    return fetch_from(
        x, lambda xh, y, z, xl, c: (xh ^ dh, y + dy, z + dz, xl ^ dx, c ^ dc)
    )


def dot(a, b, ca=1, cb=0):
    return lax.dot_general(a, b, (((ca,), (cb,)), ((), ())), preferred_element_type=F32)


def add(*terms):
    total = terms[0].astype(F32)
    for term in terms[1:]:
        total = total + (term if isinstance(term, float) else term.astype(F32))
    return total


def zero_of(x):
    return x[0, 0].astype(F32) * 0.0


def together(*groups, also=()):
    leaves, tree = jax.tree.flatten(groups)
    others = jax.tree.leaves(also)
    n = len(leaves)
    leaves = pl.pallas_call(
        lambda *refs: None,
        in_specs=[pl.BlockSpec(memory_space=pl.ANY)] * (n + len(others)),
        out_specs=[pl.BlockSpec(memory_space=pl.ANY)] * n,
        out_shape=[jax.ShapeDtypeStruct(x.shape, x.dtype) for x in leaves],
        input_output_aliases={i: i for i in range(n)},
        compiler_params=pltpu.CompilerParams(vmem_limit_bytes=MIB),
    )(*leaves, *others)
    return jax.tree.unflatten(tree, leaves)


def gather_near(own):
    return {
        (0, 0): own,
        (1, 0): fetch(own, dz=1),
        (3, 0): fetch(own, dz=-1),
        (0, 1): fetch(own, dx=1),
    }


def gather_next(a):
    return {
        (1, 1): fetch(a[1, 0], dx=1),
        (3, 1): fetch(a[0, 1], dz=-1),
        (2, 0): fetch(a[1, 0], dz=1),
    }


def gather_far(a):
    return fetch(a[2, 0], dx=1)


def gather_swap(own):
    return fetch(own, dc=1)


def both_cores(a):
    pieces = []
    for (dz, dx), own in a.items():
        pair = own if isinstance(own, tuple) else (own, gather_swap(own))
        pieces += [(pair[dc], ((dz * 2 + dx) * 2 + dc) * T) for dc in range(2)]
    return pieces


SLOTS = [(dz, dx, dc) for dz in range(4) for dx in range(2) for dc in range(2)]
WAVES = [[(2, 1)], [(1, 1), (3, 1), (2, 0)], [(1, 0), (3, 0)], [(0, 1), (0, 0)]]


def scatter_far(q):
    half = T // 2
    return fetch(q[2, 1][:half], dz=-1), fetch(q[2, 1][half:], dz=1)


def scatter_next(q, far):
    half = T // 2
    q11 = jnp.concatenate([add(q[1, 1][:half], far[0]).astype(BF), q[1, 1][half:]])
    q31 = jnp.concatenate([q[3, 1][:half], add(q[3, 1][half:], far[1]).astype(BF)])
    zero = zero_of(q11) + zero_of(q31)
    return fetch(q[2, 0], dz=-1), fetch(q31, dz=1), fetch(q11, dx=1), zero


def scatter_along(q, further):
    q10 = add(q[1, 0], further[0], further[2]).astype(BF)
    return fetch(q10, dz=-1), fetch(q[3, 0], dz=1)


def scatter_across(q, further, zero):
    return fetch(add(q[0, 1], further[1], zero).astype(BF), dx=1)


def reduce_far(g):
    half = g[0].shape[0] // 2
    return fetch(g[2][:half], dy=-1), fetch(g[2][half:], dy=1)


def reduce_near(g, far, zero):
    half = g[0].shape[0] // 2
    g1 = jnp.concatenate([add(g[1][:half], far[0], zero).astype(BF), g[1][half:]])
    g3 = jnp.concatenate([g[3][:half], add(g[3][half:], far[1], zero).astype(BF)])
    return g1, g3


def of_rep(refs, dy, dx, n):
    own, one, three, first, second = refs
    if dy == 2:
        return (second if dx else first), 0
    return (own, one, None, three)[dy], dx * n


VMEM = pl.BlockSpec(memory_space=pltpu.VMEM)
SMEM = pl.BlockSpec(memory_space=pltpu.SMEM)
HBM = pl.BlockSpec(memory_space=pltpu.HBM)
ANY = pl.BlockSpec(memory_space=pl.ANY)


def lanes(at, n):
    return pl.ds(pl.multiple_of(at * n, n), n)


def call(kernel, ins, outs, args, scratch=(), vmem=6, flops=0, nbytes=0, exps=0, aliases={}, out_specs=None):
    return pl.pallas_call(
        kernel,
        in_specs=ins,
        out_specs=out_specs or [VMEM] * len(outs),
        out_shape=[
            pltpu.VMEM(o[0], o[1]) if len(o) > 2 else jax.ShapeDtypeStruct(*o) for o in outs
        ],
        scratch_shapes=list(scratch),
        input_output_aliases=aliases,
        compiler_params=pltpu.CompilerParams(vmem_limit_bytes=vmem * MIB),
        cost_estimate=pl.CostEstimate(
            flops=flops, transcendentals=exps, bytes_accessed=nbytes
        ),
    )(*args)


ROOT = math.sqrt(2.0 / math.pi)


def start_copies(pieces, place, sems):
    copies = [
        pltpu.make_async_copy(src, dst, sems.at[place + i]) for i, (src, dst) in enumerate(pieces)
    ]
    for copy in copies:
        copy.start()
    return copies


def norm_rows(normed_ref, gain, shift, first, count):
    def strip(i, _):
        at = lanes(i, 64)
        x = normed_ref[at, :].astype(F32)
        x = x - jnp.sum(x, axis=1, keepdims=True) * (1.0 / D)
        scale = lax.rsqrt(jnp.sum(x * x, axis=1, keepdims=True) * (1.0 / D) + 1e-05)
        normed_ref[at, :] = (x * scale * gain + shift).astype(BF)
        return 0

    lax.fori_loop(first // 64, (first + count) // 64, strip, 0)


def grid_call(kernel, prefetch, grid, ins, outs, args, scratch=(), vmem=32, flops=0, nbytes=0):
    return pl.pallas_call(
        kernel,
        grid_spec=pltpu.PrefetchScalarGridSpec(
            num_scalar_prefetch=len(prefetch),
            grid=grid,
            in_specs=ins,
            out_specs=[o[2] for o in outs],
            scratch_shapes=list(scratch),
        ),
        out_shape=[jax.ShapeDtypeStruct(o[0], o[1]) for o in outs],
        compiler_params=pltpu.CompilerParams(vmem_limit_bytes=vmem * MIB),
        cost_estimate=pl.CostEstimate(flops=flops, transcendentals=0, bytes_accessed=nbytes),
    )(*prefetch, *args)


def whole(*shape):
    return pl.BlockSpec(shape, lambda *_: (0,) * len(shape))


def group_vectors(pieces, far_vectors, token_place, me):
    n = len(pieces)

    def kernel(t_ref, me_ref, *refs):
        far_ref, vec_ref, own_ref, small_ref, flat_ref, sems = refs[n:]
        moves = [
            (ref.at[pl.ds(0, 16), pl.ds(2 * D, T)], small_ref.at[pl.ds(at // T * 16, 16)])
            for (_, at), ref in zip(pieces, refs[:n], strict=True)
        ]
        for dc in range(2):
            to = small_ref.at[pl.ds((5 * 2 + dc) * 16, 16)]
            moves.append((far_ref.at[pl.ds(dc * 16, 16)], to))
        for copy in start_copies(moves, 0, sems):
            copy.wait()
        for i in range(16):
            at = t_ref[i]
            small = small_ref[i * 16 : (i + 1) * 16, :].astype(F32)
            for part in range(3):
                flat_ref[0:1, lanes(at * 3 + part, T)] = small[part : part + 1]
            vec_ref[0:1, lanes(at, T)] = small[3:4]
            vec_ref[1:2, lanes(at, T)] = small[4:5]
            vec_ref[2:3, lanes(at, T)] = small[5:6] + small[6:7]
        for part in range(3):
            own_ref[0:1, part * T : (part + 1) * T] = flat_ref[
                0:1, lanes(part * 16 + me_ref[0], T)
            ]

    return call(
        kernel,
        [SMEM] * 2 + [HBM] * (n + 1),
        [((8, D), F32), ((1, QKV), F32)],
        [token_place, me] + [p for p, _ in pieces] + [far_vectors],
        [
            pltpu.VMEM((256, T), BF),
            pltpu.VMEM((1, 3 * D), F32),
            pltpu.SemaphoreType.DMA((n + 2,)),
        ],
        vmem=56,
    )


def chip_rows(pieces, vecs, fc2, dense, arrays, before):
    n, given = len(pieces), len(arrays)
    chips = sorted({at // 256 for _, at in pieces})

    def kernel(*refs):
        refs = refs[len(before) + given :]
        tok = refs[:n]
        vec_ref, fc2_ref, dense_ref = refs[n : n + 3]
        outs, done_ref = refs[n + 3 : n + 7], refs[n + 7]
        bufs, in_sems, out_sems = refs[n + 8 : n + 12], refs[n + 12], refs[n + 13]
        done_ref[...] = jnp.zeros_like(done_ref)

        def arriving(k):
            moves = []
            for (array, at), ref in zip(pieces, tok, strict=True):
                if at // 256 == chips[k]:
                    to = pl.ds(at % 256, array.shape[0])
                    moves.append((ref.at[:, pl.ds(0, D)], bufs[0].at[k % 3, to]))
                    moves.append((ref.at[:, pl.ds(D, D)], bufs[1].at[k % 3, to]))
            return [
                pltpu.make_async_copy(src, dst, in_sems.at[k % 3, i])
                for i, (src, dst) in enumerate(moves)
            ]

        def leaving(k):
            rows = pl.ds(chips[k] * 256, 256)
            return [
                pltpu.make_async_copy(buf.at[k % 3], out.at[rows], out_sems.at[k % 3, i])
                for i, (buf, out) in enumerate(zip(bufs, outs, strict=True))
            ]

        for copy in arriving(0):
            copy.start()
        for k in range(len(chips)):
            if k + 1 < len(chips):
                if k >= 2:
                    for copy in leaving(k - 2):
                        copy.wait()
                for copy in arriving(k + 1):
                    copy.start()
            for copy in arriving(k):
                copy.wait()
            norm_rows(bufs[0].at[k % 3], vec_ref[0:1, :], vec_ref[1:2, :], 0, 256)
            x = bufs[1][k % 3]
            bufs[2][k % 3] = dot(x, fc2_ref[...], 1, 1).astype(BF)
            bufs[3][k % 3] = dot(x, dense_ref[...], 1, 1).astype(BF)
            for copy in leaving(k):
                copy.start()
        for k in range(max(len(chips) - 3, 0), len(chips)):
            for copy in leaving(k):
                copy.wait()

    widths = (D, D, FFL, T)
    return call(
        kernel,
        [ANY] * (len(before) + given) + [HBM] * n + [VMEM] * 3,
        [((SEQ, w), BF) for w in widths] + [((8, T), F32)],
        [*before, *arrays, *[p for p, _ in pieces], vecs, fc2, dense],
        [pltpu.VMEM((3, 256, w), BF) for w in widths]
        + [pltpu.SemaphoreType.DMA((3, 8)), pltpu.SemaphoreType.DMA((3, 4))],
        vmem=56,
        aliases={len(before) + i: i for i in range(given)},
        out_specs=[ANY] * 4 + [VMEM],
        flops=2 * n * T * D * (FFL + T),
        nbytes=n * MIB,
    )


def forward_inputs(normed, cot, act_grad, weights, bias, own_bias, row_place, me):
    def kernel(
        r_ref,
        me_ref,
        n_ref,
        grad_ref,
        cot_ref,
        w0_ref,
        w1_ref,
        w2_ref,
        w3_ref,
        bias_ref,
        own_ref,
        act_ref,
        pre_ref,
        act_t_ref,
        pre_t_ref,
        mixed_ref,
        fc1b_ref,
        outb_ref,
        w_out,
        w_ref,
        sems,
        out_sem,
    ):
        step = pl.program_id(0)
        leaving = pltpu.make_async_copy(w_ref, w_out, out_sem.at[0])

        @pl.when(step == 0)
        def _():
            moves = []
            for i, (dy, dx, dc) in enumerate(SLOTS):
                rows = pl.ds((dx * 2 + dc) * T, T)
                source = (w0_ref, w1_ref, w2_ref, w3_ref)[dy]
                moves.append((source.at[rows], w_ref.at[lanes(r_ref[i], T)]))
            for copy in start_copies(moves, 0, sems):
                copy.wait()
            leaving.start()
            fc1b_ref[...] = jnp.zeros_like(fc1b_ref)
            outb_ref[...] = jnp.zeros_like(outb_ref)

        halves = []
        for half in range(2):
            x = n_ref[half * 256 : (half + 1) * 256, :]
            mixed_ref[half * 256 : (half + 1) * 256, :] = dot(x, w_ref[:, :QKV]) + own_ref[...]
            halves.append(dot(x, w_ref[:, QKV:]) + bias_ref[...])
        for half, pre in enumerate(halves):
            at = slice(half * 256, (half + 1) * 256)
            squared = pre * pre
            tanh = jnp.tanh(ROOT * pre * (1.0 + 0.044715 * squared))
            act = (0.5 * pre * (1.0 + tanh)).astype(BF)
            act_ref[at, :] = act
            act_t_ref[:, at] = act.T
            slope = 0.5 * (1.0 + tanh) + 0.5 * pre * (1.0 - tanh * tanh) * ROOT * (
                1.0 + 3 * 0.044715 * squared
            )
            back = (grad_ref[at, :].astype(F32) * slope).astype(BF)
            pre_ref[at, :] = back
            pre_t_ref[:, at] = back.T
            fc1b_ref[...] += jnp.sum(back.astype(F32).reshape(32, 8, FFL), axis=0)
        outb_ref[...] += jnp.sum(cot_ref[...].astype(F32).reshape(64, 8, T), axis=0)

        @pl.when(step == pl.num_programs(0) - 1)
        def _():
            leaving.wait()

    rows = lambda i, *_: (i, 0)
    cols = lambda i, *_: (0, i)
    return grid_call(
        kernel,
        [row_place, me],
        (SEQ // 512,),
        [
            pl.BlockSpec((512, D), rows),
            pl.BlockSpec((512, FFL), rows),
            pl.BlockSpec((512, T), lambda i, r, m: (i, m[0])),
        ]
        + [HBM] * 4
        + [whole(1, FFL), whole(1, QKV)],
        [
            ((SEQ, FFL), BF, pl.BlockSpec((512, FFL), rows)),
            ((SEQ, FFL), BF, pl.BlockSpec((512, FFL), rows)),
            ((FFL, SEQ), BF, pl.BlockSpec((FFL, 512), cols)),
            ((FFL, SEQ), BF, pl.BlockSpec((FFL, 512), cols)),
            ((SEQ, QKV), F32, pl.BlockSpec((512, QKV), rows)),
            ((8, FFL), F32, whole(8, FFL)),
            ((8, T), F32, whole(8, T)),
            ((D, COLS), BF, ANY),
        ],
        [normed, act_grad, cot, *weights, bias, own_bias],
        [
            pltpu.VMEM((D, COLS), BF),
            pltpu.SemaphoreType.DMA((16,)),
            pltpu.SemaphoreType.DMA((1,)),
        ],
        vmem=56,
        flops=2 * SEQ * D * COLS,
        nbytes=24 * MIB,
    )


ORDER = (2, 1, 3, 0)


def in_order(places, parts):
    chips = jnp.stack([places[(dy * 2 + dx) * 2] // 2 for dy in ORDER for dx in range(2)])
    return chips, jnp.stack([parts[dy * 2 + dx] for dy in ORDER for dx in range(2)])


def fetched(refs, scratch, sems):
    copies = [
        pltpu.make_async_copy(ref, to, sems.at[i])
        for i, (ref, to) in enumerate(zip(refs, scratch, strict=True))
    ]
    for copy in copies:
        copy.start()
    return copies


def column_grads(normed, pre_t, act_t, cot, chips, parts, core):
    def kernel(chip_ref, part_ref, core_ref, normed_ref, cot_ref, g_ref, a_ref, *refs):
        outs, n_ref, c_ref, sems = refs[:4], refs[4], refs[5], refs[6]
        copies = fetched((normed_ref, cot_ref), (n_ref, c_ref), sems)
        copies[0].wait()
        for i in range(8):
            out, at = outs[i // 2], slice(i % 2 * FFL, (i % 2 + 1) * FFL)
            cols = dot(g_ref[...], n_ref[:, lanes(chip_ref[i], 256)]).astype(BF)
            out[at, lanes(core_ref[0], T)] = cols[:, :T]
            out[at, lanes(1 - core_ref[0], T)] = cols[:, T:]
        copies[1].wait()
        for i in range(8):
            out, at = outs[i // 2], slice(i % 2 * FFL, (i % 2 + 1) * FFL)
            out[at, 256:512] = dot(a_ref[...], c_ref[:, lanes(part_ref[i], 256)]).astype(BF)

    outs = call(
        kernel,
        [SMEM] * 3 + [ANY] * 2 + [VMEM] * 2,
        [((2 * FFL, 512), BF)] * 4,
        [chips, parts, core, normed, cot, pre_t, act_t],
        [pltpu.VMEM((SEQ, D), BF), pltpu.VMEM((SEQ, D), BF), pltpu.SemaphoreType.DMA((2,))],
        vmem=40,
        flops=4 * SEQ * D * FFL,
        nbytes=24 * MIB,
    )
    return [outs[ORDER.index(dy)] for dy in range(4)]


FOR_OWNER = QKV + 16
LATE = FOR_OWNER + T + 16


def head_grads(
    normed, mixed_t, attended_t, cot, chips, parts, core, me, gain, sums, bias_parts
):
    def kernel(chip_ref, part_ref, core_ref, me_ref, normed_ref, cot_ref, m_ref, a_ref, *refs):
        gain_ref, gains_ref, shifts_ref, qkvb_ref, fc1b_ref, outb_ref = refs[:6]
        outs, owners_ref, own_ref = refs[6:10], refs[10], refs[11]
        n_ref, c_ref, sems = refs[12:]
        copies = fetched((normed_ref, cot_ref), (n_ref, c_ref), sems)
        owners_ref[...] = jnp.zeros_like(owners_ref)
        owners_ref[0:1, :] = jnp.sum(gains_ref[...], axis=0, keepdims=True) / gain_ref[...]
        owners_ref[1:2, :] = jnp.sum(shifts_ref[...], axis=0, keepdims=True)
        qkvb = jnp.sum(qkvb_ref[...], axis=0, keepdims=True)
        for part in range(3):
            at = part * 16 + me_ref[0]
            third = at % 3
            row = lax.broadcasted_iota(jnp.int32, (8, T), 0)
            value = jnp.where(row == 2 + third, qkvb[:, part * T : (part + 1) * T], 0.0)
            owners_ref[0:8, lanes(at // 3, T)] += value
        own_ref[...] = jnp.zeros_like(own_ref)
        own_ref[0:1, :FFL] = jnp.sum(fc1b_ref[...], axis=0, keepdims=True)
        own_ref[0:1, FFL : FFL + T] = jnp.sum(outb_ref[...], axis=0, keepdims=True)
        mine, other = lanes(core_ref[0], T), lanes(1 - core_ref[0], T)
        copies[0].wait()
        for i in range(8):
            out, base = outs[i // 2], i % 2 * LATE
            cols = dot(m_ref[...], n_ref[:, lanes(chip_ref[i], 256)]).astype(BF)
            extra = owners_ref[:, lanes(chip_ref[i], 256)].astype(BF)
            out[base : base + QKV, mine] = cols[:, :T]
            out[base : base + QKV, other] = cols[:, T:]
            out[base + QKV : base + FOR_OWNER, mine] = extra[:, :T]
            out[base + QKV : base + FOR_OWNER, other] = extra[:, T:]
        copies[1].wait()
        for i in range(8):
            out, base = outs[i // 2], i % 2 * LATE + FOR_OWNER
            part = part_ref[i]
            out[base : base + T, :] = dot(a_ref[...], c_ref[:, lanes(part, 256)]).astype(BF)
            out[base + T : base + T + 16, 0:T] = own_ref[:, lanes(part, T)].astype(BF)
            out[base + T : base + T + 16, T:] = jnp.zeros((16, T), BF)

    outs = call(
        kernel,
        [SMEM] * 4 + [ANY] * 2 + [VMEM] * 8,
        [((2 * LATE, 256), BF)] * 4,
        [chips, parts, core, me, normed, cot, mixed_t, attended_t, gain, *sums, *bias_parts],
        [
            pltpu.VMEM((16, D), F32),
            pltpu.VMEM((16, 1024), F32),
            pltpu.VMEM((SEQ, D), BF),
            pltpu.VMEM((SEQ, D), BF),
            pltpu.SemaphoreType.DMA((2,)),
        ],
        vmem=36,
        flops=2 * SEQ * D * (QKV + T),
        nbytes=20 * MIB,
    )
    return [outs[ORDER.index(dy)] for dy in range(4)]


def place_columns(pieces, col_place, part_place):
    def kernel(c_ref, p_ref, *refs):
        fc1_ref, fc2_ref = refs[5:]
        for i, (dy, dh, dc) in enumerate(SLOTS):
            ref, at = of_rep(refs[:5], dy, dh, FFL)
            part = ref[at : at + FFL, dc * T : (dc + 1) * T]
            fc1_ref[:, lanes(c_ref[i], FFL)] = part.astype(F32).T
            if dc == 0:
                to = lanes(p_ref[dy * 2 + dh], 256)
                fc2_ref[:, to] = ref[at : at + FFL, 256:512].astype(F32)

    return call(
        kernel,
        [SMEM] * 2 + [VMEM] * 5,
        [((T, FF), F32), ((FFL, D), F32)],
        [col_place, part_place] + list(pieces),
        vmem=20,
        nbytes=12 * MIB,
    )


def place_heads(pieces, col_place, part_place, before):
    def kernel(c_ref, p_ref, *refs):
        qkv_ref, dense_ref, owner_ref, own_ref = refs[-4:]
        total = jnp.zeros((16, T), F32)
        for i, (dy, dx, dc) in enumerate(SLOTS):
            ref, at = of_rep(refs[:5], dy, dx, LATE)
            cols = slice(dc * T, (dc + 1) * T)
            for part in range(3):
                block = ref[at + part * T : at + (part + 1) * T, cols].astype(F32)
                qkv_ref[:, lanes(c_ref[i] + part * 16, T)] = block.T
            total += ref[at + QKV : at + FOR_OWNER, cols].astype(F32)
            if dc == 0:
                part = p_ref[dy * 2 + dx]
                rows = slice(at + FOR_OWNER, at + FOR_OWNER + T)
                dense_ref[:, lanes(part, 256)] = ref[rows, :].astype(F32)
                rows = slice(at + FOR_OWNER + T, at + LATE)
                own_ref[:, lanes(part, T)] = ref[rows, 0:T].astype(F32)
        owner_ref[...] = total

    return call(
        kernel,
        [SMEM] * 2 + [VMEM] * 5 + [ANY] * len(before),
        [((T, 3 * D), F32), ((T, D), F32), ((16, T), F32), ((16, 1024), F32)],
        [col_place, part_place, *pieces, *before],
        vmem=14,
        nbytes=6 * MIB,
    )


def terms(
    chips, attended, activated, dense, fc2, mixed_grad, pre_grad, weight, normed, vecs, sums, before
):
    n = len(chips)
    order = jnp.array([dz * 2 + dx for dz, dx in chips], jnp.int32)

    def kernel(order_ref, a_ref, f_ref, m_ref, p_ref, n_ref, d_ref, v_ref, w_ref, vec_ref, *refs):
        mine_ref, other_ref, gain_ref, total_ref = refs[-4:]
        shift = vec_ref[1:2, :]

        @pl.when(pl.program_id(0) == 0)
        def _():
            if sums:
                gain_ref[...] = refs[0][...]
                total_ref[...] = refs[1][...]
            else:
                gain_ref[...] = jnp.zeros_like(gain_ref)
                total_ref[...] = jnp.zeros_like(total_ref)

        for col in range(4):
            to = slice(col * 512, (col + 1) * 512)
            total = dot(m_ref[...], w_ref[to, :QKV], 1, 1) + dot(p_ref[...], w_ref[to, QKV:], 1, 1)
            mine_ref[:, to] = total[:T].astype(BF)
            other_ref[:, to] = total[T:].astype(BF)
            unit = n_ref[:, to].astype(F32) - shift[:, to]
            gain_ref[:, to] += jnp.sum((total * unit).reshape(32, 8, 512), axis=0)
            total_ref[:, to] += jnp.sum(total.reshape(32, 8, 512), axis=0)
            total = dot(a_ref[...], d_ref[:, to]) + dot(f_ref[...], v_ref[:, to])
            to = slice(D + col * 512, D + (col + 1) * 512)
            mine_ref[:, to] = total[:T].astype(BF)
            other_ref[:, to] = total[T:].astype(BF)

    rows = lambda i, order_ref: (order_ref[i], 0)
    here = lambda i, order_ref: (i, 0)
    return grid_call(
        kernel,
        [order],
        (n,),
        [
            pl.BlockSpec((2 * T, T), rows),
            pl.BlockSpec((2 * T, FFL), rows),
            pl.BlockSpec((2 * T, QKV), rows),
            pl.BlockSpec((2 * T, FFL), rows),
            pl.BlockSpec((2 * T, D), rows),
            whole(T, D),
            whole(FFL, D),
            whole(D, COLS),
            whole(8, D),
        ]
        + [whole(8, D)] * len(sums)
        + [ANY] * len(before),
        [((n * T, 2 * D), BF, pl.BlockSpec((T, 2 * D), here))] * 2
        + [((8, D), F32, whole(8, D))] * 2,
        [attended, activated, mixed_grad, pre_grad, normed, dense, fc2, weight, vecs, *sums, *before],
        flops=2 * n * 2 * T * (COLS + T + FFL) * D,
        nbytes=8 * MIB,
    )


TQ = 512
TK = 512


def attention_kernel(blocks, last, n_before, place, cos_ref, sin_ref, *refs):
    refs = refs[n_before:]
    if last:
        first_refs, refs = refs[:8], refs[8:]
        att_ref, out_ref, att_t_ref, out_t_ref, bias_ref = refs[:5]
        q_ref, k_ref, v_ref, do_ref = first_refs[:4]
        dq_ref, dk_ref, dv_ref, o_ref, s_ref, e_ref = refs[5:]
    else:
        mixed_ref, grad_ref, *refs = refs
        refs, done_ref = refs[:8] + refs[9:], refs[8]
        done_ref[...] = jnp.zeros_like(done_ref)
        q_ref, k_ref, v_ref, do_ref, dq_ref, dk_ref, dv_ref, o_ref, s_ref, e_ref = refs
    lane = lax.broadcasted_iota(jnp.int32, (T, 128), 1)
    low_head = lane < HEAD_DIM
    first = (lane % HEAD_DIM) < ROTARY // 2

    def turned(x):
        return jnp.where(
            first, pltpu.roll(x, 128 - ROTARY // 2, 1), pltpu.roll(x, ROTARY // 2, 1)
        )

    def load(slot, _):
        rows = pl.ds(pl.multiple_of(slot * T, T), T)
        at = pl.ds(pl.multiple_of(place[slot] * T, T), T)
        c, s = cos_ref[at, :], sin_ref[at, :]
        query = mixed_ref[rows, 0:128]
        key = mixed_ref[rows, 128:256]
        query = (query * c + turned(query) * s).astype(BF).astype(F32) * (HEAD_DIM**-0.5)
        q_ref[0, at, :] = jnp.where(low_head, query, 0.0).astype(BF)
        q_ref[1, at, :] = jnp.where(low_head, 0.0, query).astype(BF)
        k_ref[at, :] = (key * c + turned(key) * s).astype(BF)
        v_ref[at, 0:128] = mixed_ref[rows, 256:384].astype(BF)
        v_ref[at, 128:256] = jnp.ones((T, 128), BF)
        grad = grad_ref[rows, :].astype(F32)
        do_ref[0, at, :] = jnp.where(low_head, grad, 0.0).astype(BF)
        do_ref[1, at, :] = jnp.where(low_head, 0.0, grad).astype(BF)
        dk_ref[:, at] = jnp.zeros((128, T), F32)
        dv_ref[:, at] = jnp.zeros((128, T), F32)
        return 0

    if last:
        for to, at in ((dq_ref, 4), (dk_ref, 5), (dv_ref, 6), (o_ref, 7)):
            to[...] = first_refs[at][...]
    else:
        lax.fori_loop(0, 16, load, 0)

    lane_q = lax.broadcasted_iota(jnp.int32, (TQ, 128), 1)
    low_q = lane_q < HEAD_DIM

    def block(i, _):
        rows = lanes(i, TQ)
        queries = [q_ref[h, rows, :] for h in range(2)]

        def scores(j, tops, masked):
            at = lanes(j, TK)
            keys = k_ref[at, :]
            new = []
            for h in range(2):
                s = dot(queries[h], keys, 1, 1)
                if masked:
                    row = lax.broadcasted_iota(jnp.int32, (TQ, TK), 0)
                    col = lax.broadcasted_iota(jnp.int32, (TQ, TK), 1)
                    s = jnp.where(row >= col, s, -1e30)
                s_ref[h, :, at] = s
                top = tops[h]
                for n in range(TK // 128):
                    top = jnp.maximum(top, s[:, n * 128 : (n + 1) * 128])
                new.append(top)
            return tuple(new)

        low = jnp.full((TQ, 128), -1e30, F32)
        tops = lax.fori_loop(0, i, lambda j, t: scores(j, t, False), (low, low))
        tops = [jnp.max(t, axis=1, keepdims=True) for t in scores(i, tops, True)]

        def weigh(j, totals):
            at = lanes(j, TK)
            values = v_ref[at, :]
            new = []
            for h in range(2):
                e = jnp.exp2((s_ref[h, :, at] - tops[h]) * LOG2E).astype(BF)
                e_ref[h, :, at] = e
                new.append(totals[h] + dot(e, values))
            return tuple(new)

        zero = jnp.zeros((TQ, 256), F32)
        totals = lax.fori_loop(0, i + 1, weigh, (zero, zero))
        outs, grads, deltas = [], [], []
        for h in range(2):
            inverse = 1.0 / totals[h][:, 128:]
            o = totals[h][:, :128] * inverse
            grad = do_ref[h, rows, :].astype(F32) * inverse
            outs.append(o)
            deltas.append(jnp.sum(grad * o, axis=1, keepdims=True))
            grads.append(grad.astype(BF))
        o_ref[rows, :] = jnp.where(low_q, outs[0], outs[1]).astype(BF)
        queries_t = [q.T for q in queries]
        grads_t = [g.T for g in grads]

        def back(j, totals):
            at = lanes(j, TK)
            keys = k_ref[at, :]
            values = v_ref[at, 0:128]
            new, dk, dv = [], None, None
            for h in range(2):
                e = e_ref[h, :, at]
                dp = dot(grads[h], values, 1, 1)
                ds = (e.astype(F32) * (dp - deltas[h])).astype(BF)
                new.append(totals[h] + dot(ds, keys))
                k_part = dot(queries_t[h], ds)
                v_part = dot(grads_t[h], e)
                dk = k_part if dk is None else dk + k_part
                dv = v_part if dv is None else dv + v_part
            dk_ref[:, at] += dk
            dv_ref[:, at] += dv
            return tuple(new)

        zero = jnp.zeros((TQ, 128), F32)
        dqs = lax.fori_loop(0, i + 1, back, (zero, zero))
        dq_ref[rows, :] = jnp.where(low_q, dqs[0], dqs[1]) * (HEAD_DIM**-0.5)
        return 0

    lax.fori_loop(blocks[0], blocks[1], block, 0)
    if not last:
        return

    def store(slot, total):
        rows = pl.ds(pl.multiple_of(slot * T, T), T)
        at = pl.ds(pl.multiple_of(place[slot] * T, T), T)
        c, s = cos_ref[at, :], sin_ref[at, :]
        att = o_ref[at, :]
        att_ref[rows, :] = att
        att_t_ref[:, rows] = att.T
        dq, dk = dq_ref[at, :], dk_ref[:, at].T
        new = []
        for part, grad in enumerate(
            (dq * c - turned(dq) * s, dk * c - turned(dk) * s, dv_ref[:, at].T)
        ):
            low = grad.astype(BF)
            cols = slice(part * T, (part + 1) * T)
            out_ref[rows, cols] = low
            out_t_ref[cols, rows] = low.T
            new.append(total[part] + jnp.sum(low.astype(F32).reshape(16, 8, T), axis=0))
        return tuple(new)

    zero = jnp.zeros((8, T), F32)
    sums = lax.fori_loop(0, 16, store, (zero, zero, zero))
    for part in range(3):
        bias_ref[:, part * T : (part + 1) * T] = sums[part]


def attention_first(place, cosine, sine, mixed, attended_grad, before):
    return call(
        functools.partial(attention_kernel, (0, 2), False, len(before)),
        [SMEM] + [VMEM] * 2 + [ANY] * len(before) + [VMEM] * 2,
        [
            ((2, SEQ, 128), BF, 1),
            ((SEQ, 128), BF, 1),
            ((SEQ, 256), BF, 1),
            ((2, SEQ, 128), BF, 1),
            ((SEQ, 128), F32, 1),
            ((128, SEQ), F32, 1),
            ((128, SEQ), F32, 1),
            ((SEQ, 128), BF, 1),
            ((8, 128), jnp.int32),
        ],
        [place, cosine, sine, *before, mixed, attended_grad],
        [pltpu.VMEM((2, TQ, SEQ), F32), pltpu.VMEM((2, TQ, SEQ), BF)],
        vmem=24,
        flops=8 * SEQ * SEQ * 64 * 2,
        exps=SEQ * SEQ // 2,
        nbytes=3 * MIB,
    )


def attention_last(place, cosine, sine, state, before):
    return call(
        functools.partial(attention_kernel, (2, 4), True, len(before)),
        [SMEM] + [VMEM] * 2 + [ANY] * len(before) + [VMEM] * 8,
        [
            ((SEQ, T), BF),
            ((SEQ, QKV), BF),
            ((T, SEQ), BF),
            ((QKV, SEQ), BF),
            ((8, QKV), F32),
        ],
        [place, cosine, sine, *before] + list(state),
        [
            pltpu.VMEM((SEQ, 128), F32),
            pltpu.VMEM((128, SEQ), F32),
            pltpu.VMEM((128, SEQ), F32),
            pltpu.VMEM((SEQ, 128), BF),
            pltpu.VMEM((2, TQ, SEQ), F32),
            pltpu.VMEM((2, TQ, SEQ), BF),
        ],
        vmem=26,
        flops=6 * SEQ * SEQ * 64 * 2,
        exps=SEQ * SEQ // 2,
        nbytes=3 * MIB,
    )


def rotary_tables():
    lane = lax.broadcasted_iota(jnp.int32, (SEQ, 128), 1) % HEAD_DIM
    place = lax.broadcasted_iota(jnp.int32, (SEQ, 128), 0).astype(F32)
    freq = (lane % (ROTARY // 2)).astype(F32)
    angle = place * jnp.exp(freq * (-2.0 * math.log(10000.0) / ROTARY))
    turns = lane < ROTARY
    cosine = jnp.where(turns, jnp.cos(angle), 1.0)
    sine = jnp.where(turns, jnp.sin(angle), 0.0)
    return cosine, jnp.where(lane < ROTARY // 2, -sine, sine)


def body(
    tokens,
    ln_gain,
    ln_shift,
    qkv_weight,
    qkv_bias,
    dense_weight,
    dense_bias,
    fc1_weight,
    fc1_bias,
    fc2_weight,
    fc2_bias,
    cotangent,
):
    rep, shard = lax.axis_index("rep"), lax.axis_index("shard")
    xh, y = rep // 4, rep % 4
    z, xl, c = shard // 4, (shard // 2) % 2, shard % 2
    token_place = jnp.stack(
        [((z + dz) % 4) * 4 + (xl ^ dx) * 2 + (c ^ dc) for dz, dx, dc in SLOTS]
    ).astype(jnp.int32)
    row_place = jnp.stack(
        [((z + y + dy) % 4) * 4 + (xl ^ dx) * 2 + (c ^ dc) for dy, dx, dc in SLOTS]
    ).astype(jnp.int32)
    col_place = jnp.stack(
        [((z - y - dy) % 4) * 4 + (xl ^ dx) * 2 + (c ^ dc) for dy, dx, dc in SLOTS]
    ).astype(jnp.int32)
    part_place = jnp.stack(
        [((y + dy) % 4) * 2 + dx for dy in range(4) for dx in range(2)]
    ).astype(jnp.int32)
    chip_order, part_order = in_order(row_place, part_place)
    me, core = shard.reshape(1).astype(jnp.int32), c.reshape(1).astype(jnp.int32)

    vectors = [v.reshape(-1, T) for v in (qkv_bias, ln_gain, ln_shift, dense_bias, fc2_bias)]
    vectors = jnp.concatenate(vectors + [jnp.zeros((T - 7, T), BF)])
    message = jnp.concatenate([tokens, cotangent, vectors], axis=1)
    near = gather_near(message)

    def columns_for(chip):
        qkv = [
            lax.dynamic_slice(qkv_weight, (0, part * D + chip * 2 * T), (T, 2 * T))
            for part in range(3)
        ]
        fc1 = lax.dynamic_slice(fc1_weight, (0, chip * 2 * FFL), (T, 2 * FFL))
        return jnp.concatenate(
            [
                jnp.concatenate(
                    [p[:, at * T : (at + 1) * T] for p in qkv]
                    + [fc1[:, at * FFL : (at + 1) * FFL]],
                    axis=1,
                )
                for at in range(2)
            ]
        )

    to_chip = ((z - y) % 4) * 2 + xl
    mine, other = columns_for(to_chip ^ c), columns_for(to_chip ^ c ^ 1)
    other = fetch(other, dc=1)
    rows = fetch_from(
        jnp.concatenate([mine, other]), lambda xh, y, z, xl, c: (xh, y, z + y, xl ^ c, c)
    )
    own_pair = message, gather_swap(message)
    cosine, sine = rotary_tables()
    rows, near[1, 0], near[0, 1] = together(
        rows, near[1, 0], near[0, 1], also=(near[3, 0], own_pair, cosine, sine)
    )

    def columns_of(rows, core):
        return jnp.concatenate(
            [
                lax.dynamic_slice(rows, (n * 2 * T + core * T, 0), (T, COLS))
                for n in range(2)
            ]
        )

    mine = columns_of(rows, c)
    other = fetch(columns_of(rows, 1 - c), dc=1)
    here = jnp.where(c == 0, mine, jnp.concatenate([other[T:], other[:T]]))
    there = jnp.where(c == 0, jnp.concatenate([other[T:], other[:T]]), mine)
    own_rows = jnp.concatenate([here, there])
    further = gather_next(near)
    one, three = fetch(own_rows, dy=1), fetch(own_rows, dy=-1)
    one, three, further, near = together(one, three, further, near)
    far_vectors = fetch(further[2, 0][:16, 2 * D :], dx=1)
    near_pairs = near | {(0, 0): own_pair}
    far_vectors = jnp.concatenate([far_vectors, fetch(far_vectors, dc=1)])
    far = gather_far(further)
    two = fetch(one, dy=1)
    pieces = both_cores(near_pairs) + both_cores(further)
    vecs, own_qkv_bias = group_vectors(pieces, far_vectors, token_place, me)
    *arrays, done = chip_rows(pieces, vecs, fc2_weight, dense_weight, [], [one, three])
    (far,) = together(far, also=(two, done))
    far = [(far, 10 * T), (gather_swap(far), 11 * T)]
    normed, all_cot, act_grad, attended_grad, _ = chip_rows(
        far, vecs, fc2_weight, dense_weight, arrays, []
    )
    gain, out_bias = vecs[0:1], vecs[2:3]
    (activated, pre_grad, act_t, pre_t, mixed, fc1_bias_part, out_bias_part, weight) = (
        forward_inputs(
            normed,
            all_cot,
            act_grad,
            (own_rows, one, two, three),
            fc1_bias.astype(F32).reshape(1, FFL),
            own_qkv_bias,
            row_place,
            me,
        )
    )

    early = column_grads(normed, pre_t, act_t, all_cot, chip_order, part_order, core)
    *state, done = attention_first(
        token_place, cosine, sine, mixed, attended_grad, early[:1]
    )
    early_near = reduce_near(early, reduce_far(early), done[0, 0].astype(F32))
    attended, mixed_grad, attended_t, mixed_t, qkv_bias_part = attention_last(
        token_place, cosine, sine, state, early_near
    )
    early = early[0], fetch(early_near[0], dy=-1), fetch(early_near[1], dy=1)
    zero = zero_of(qkv_bias_part)
    early = [
        add(*(e[dx * FFL : (dx + 1) * FFL] for e in early), zero).astype(BF) for dx in range(2)
    ]
    early_other = [fetch(e, dh=1) for e in early]

    def the_terms(chips, sums, before):
        mine, other, *sums = terms(
            chips,
            attended,
            activated,
            dense_weight,
            fc2_weight,
            mixed_grad,
            pre_grad,
            weight,
            normed,
            vecs,
            sums,
            before,
        )
        return mine, fetch(other, dc=1), sums

    def own_terms(chips, mine, other, zero):
        return {
            chip: add(mine[n * T : (n + 1) * T], other[n * T : (n + 1) * T], zero).astype(BF)
            for n, chip in enumerate(chips)
        }

    mine0, other0, sums = the_terms(WAVES[0], [], early)
    mine1, other1, sums = the_terms(WAVES[1], sums, [])
    q = own_terms(WAVES[0], mine0, other0, zero_of(sums[0]))
    far = scatter_far(q)
    mine2, other2, sums = the_terms(WAVES[2], sums, [q[2, 1], early_other[0]])
    mine3, other3, sums = the_terms(WAVES[3], sums, [early_other[1], *far])
    zero = zero_of(sums[0])

    def from_owners(rows):
        return [
            fetch_from(rows[dx], lambda xh, y, z, xl, c: (xh, y, z - y, xl ^ dx, c))
            for dx in range(2)
        ]

    early = jnp.concatenate(
        [add(e, other, zero).astype(BF) for e, other in zip(early, early_other, strict=True)]
    )
    early_own = jnp.concatenate([early[:, :T], fetch(early[:, T : 2 * T], dc=1)], axis=1)
    early_own = from_owners([early_own[:FFL], early_own[FFL:]])
    late = head_grads(
        normed,
        mixed_t,
        attended_t,
        all_cot,
        chip_order,
        part_order,
        core,
        me,
        gain,
        sums,
        (qkv_bias_part, fc1_bias_part, out_bias_part),
    )
    late_far = reduce_far(late)
    q |= own_terms(WAVES[1], mine1, other1, 0.0)
    q, early_own, late_far, far = together(
        q, early_own, late_far, far, also=(other2, other3, late)
    )

    *further, zero = scatter_next(q, far)
    late_near = reduce_near(late, late_far, zero)
    late_near = fetch(late_near[0], dy=-1), fetch(late_near[1], dy=1)
    q |= own_terms(WAVES[2], mine2, other2, 0.0) | own_terms(WAVES[3], mine3, other3, 0.0)
    late = add(late[0], *late_near).astype(BF)
    late_other = fetch(late, dh=1)
    early = jnp.concatenate(
        [
            jnp.concatenate([early_own[dx], early[dx * FFL : (dx + 1) * FFL, 2 * T :]], axis=1)
            for dx in range(2)
        ]
    )
    early = early + zero_of(late).astype(BF)
    early_one, early_three = fetch(early, dy=1), fetch(early, dy=-1)
    q, further = together(q, further)

    along = scatter_along(q, further)
    early = (
        early,
        early_one,
        early_three,
        fetch(early_one[:FFL], dy=1),
        fetch(early_three[FFL:], dy=-1),
    )
    late = add(late, late_other).astype(BF)
    late_rows = jnp.concatenate([late[:FOR_OWNER], late[LATE : LATE + FOR_OWNER]])
    late_own = jnp.concatenate([late_rows[:, :T], fetch(late_rows[:, T:], dc=1)], axis=1)
    late_own = from_owners([late_own[:FOR_OWNER], late_own[FOR_OWNER:]])
    across = scatter_across(q, further, zero_of(late_own[0]) + zero_of(late_own[1]))
    late = jnp.concatenate(
        [late_own[0], late[FOR_OWNER:LATE], late_own[1], late[LATE + FOR_OWNER :]]
    )
    late = late + (zero_of(early_one) + zero_of(early_three)).astype(BF)
    late_one, late_three = fetch(late, dy=1), fetch(late, dy=-1)
    total = add(q[0, 0], *along, across)
    own = tokens.astype(F32)
    layer_out = (own + out_bias + total[:, D:]).astype(BF)
    center = own - jnp.mean(own, axis=-1, keepdims=True)
    inv_std = lax.rsqrt(jnp.mean(center * center, axis=-1, keepdims=True) + 1e-05)
    unit = center * inv_std
    scaled = total[:, :D] * gain
    input_grad = cotangent.astype(F32) + inv_std * (
        scaled
        - jnp.mean(scaled, axis=-1, keepdims=True)
        - unit * jnp.mean(scaled * unit, axis=-1, keepdims=True)
    )
    late = (
        late,
        late_one,
        late_three,
        fetch(late_one[:LATE], dy=1),
        fetch(late_three[LATE:], dy=-1),
    )
    fc1_total, fc2_total = place_columns(early, col_place, part_place)
    qkv_total, dense_total, of_owner, of_own = place_heads(
        late, col_place, part_place, [layer_out]
    )
    out_bias_total = of_own[0, FFL : FFL + T]

    return (
        layer_out,
        input_grad,
        of_owner[0],
        of_owner[1],
        qkv_total,
        of_owner[2:5].reshape(QKV),
        dense_total,
        out_bias_total,
        fc1_total,
        of_own[0, :FFL],
        fc2_total,
        out_bias_total,
    )


def solution(mesh):
    return jax.shard_map(
        body,
        mesh=mesh,
        in_specs=(
            P(AXES, None),
            P("shard"),
            P("shard"),
            P("shard", None),
            P("shard"),
            P("shard", None),
            P("shard"),
            P("shard", None),
            P("shard"),
            P("shard", None),
            P("shard"),
            P(AXES, None),
        ),
        out_specs=(
            P(AXES, None),
            P(AXES, None),
            P("shard"),
            P("shard"),
            P("shard", None),
            P("shard"),
            P("shard", None),
            P("shard"),
            P("shard", None),
            P("shard"),
            P("shard", None),
            P("shard"),
        ),
        check_vma=False,
    )
```

```python
import functools
import math

import jax
import jax.numpy as jnp
from jax import lax
from jax.experimental import pallas as pl
from jax.experimental.pallas import tpu as pltpu
from jax.sharding import PartitionSpec as P

D = 2048
HEADS = 32
HEAD_DIM = 64
ROTARY = 32
FF = 8192
SEQ = 2048
T = 128
QKV = 384
FFL = 512
COLS = QKV + FFL
BF = jnp.bfloat16
F32 = jnp.float32
AXES = ("rep", "shard")
MIB = 1 << 20
LOG2E = math.log2(math.e)

PLACES = [
    (xh, y, z, xl, c)
    for xh in range(2)
    for y in range(4)
    for z in range(4)
    for xl in range(2)
    for c in range(2)
]


def flat(xh, y, z, xl, c):
    return (xh * 4 + y % 4) * 16 + (z % 4) * 4 + xl * 2 + c


def fetch_from(x, source):
    return lax.ppermute(x, AXES, [(flat(*source(*p)), flat(*p)) for p in PLACES])


def fetch(x, dz=0, dx=0, dc=0, dy=0, dh=0):
    return fetch_from(
        x, lambda xh, y, z, xl, c: (xh ^ dh, y + dy, z + dz, xl ^ dx, c ^ dc)
    )


def dot(a, b, ca=1, cb=0):
    return lax.dot_general(a, b, (((ca,), (cb,)), ((), ())), preferred_element_type=F32)


def add(*terms):
    total = terms[0].astype(F32)
    for term in terms[1:]:
        total = total + (term if isinstance(term, float) else term.astype(F32))
    return total


def zero_of(x):
    return x[0, 0].astype(F32) * 0.0


def together(*groups, also=()):
    leaves, tree = jax.tree.flatten(groups)
    others = jax.tree.leaves(also)
    n = len(leaves)
    leaves = pl.pallas_call(
        lambda *refs: None,
        in_specs=[pl.BlockSpec(memory_space=pl.ANY)] * (n + len(others)),
        out_specs=[pl.BlockSpec(memory_space=pl.ANY)] * n,
        out_shape=[jax.ShapeDtypeStruct(x.shape, x.dtype) for x in leaves],
        input_output_aliases={i: i for i in range(n)},
        compiler_params=pltpu.CompilerParams(vmem_limit_bytes=MIB),
    )(*leaves, *others)
    return jax.tree.unflatten(tree, leaves)


def gather_near(own):
    return {
        (0, 0): own,
        (1, 0): fetch(own, dz=1),
        (3, 0): fetch(own, dz=-1),
        (0, 1): fetch(own, dx=1),
    }


def gather_next(a):
    return {
        (1, 1): fetch(a[1, 0], dx=1),
        (3, 1): fetch(a[0, 1], dz=-1),
        (2, 0): fetch(a[1, 0], dz=1),
    }


def gather_far(a):
    return fetch(a[2, 0], dx=1)


def gather_swap(own):
    return fetch(own, dc=1)


def both_cores(a):
    pieces = []
    for (dz, dx), own in a.items():
        pair = own if isinstance(own, tuple) else (own, gather_swap(own))
        pieces += [(pair[dc], ((dz * 2 + dx) * 2 + dc) * T) for dc in range(2)]
    return pieces


SLOTS = [(dz, dx, dc) for dz in range(4) for dx in range(2) for dc in range(2)]
WAVES = [[(2, 1)], [(1, 1), (3, 1), (2, 0)], [(1, 0), (3, 0)], [(0, 1), (0, 0)]]


def scatter_far(q):
    half = T // 2
    return fetch(q[2, 1][:half], dz=-1), fetch(q[2, 1][half:], dz=1)


def scatter_next(q, far):
    half = T // 2
    q11 = jnp.concatenate([add(q[1, 1][:half], far[0]).astype(BF), q[1, 1][half:]])
    q31 = jnp.concatenate([q[3, 1][:half], add(q[3, 1][half:], far[1]).astype(BF)])
    zero = zero_of(q11) + zero_of(q31)
    return fetch(q[2, 0], dz=-1), fetch(q31, dz=1), fetch(q11, dx=1), zero


def scatter_along(q, further):
    q10 = add(q[1, 0], further[0], further[2]).astype(BF)
    return fetch(q10, dz=-1), fetch(q[3, 0], dz=1)


def scatter_across(q, further, zero):
    return fetch(add(q[0, 1], further[1], zero).astype(BF), dx=1)


def reduce_far(g):
    half = g[0].shape[0] // 2
    return fetch(g[2][:half], dy=-1), fetch(g[2][half:], dy=1)


def reduce_near(g, far, zero):
    half = g[0].shape[0] // 2
    g1 = jnp.concatenate([add(g[1][:half], far[0], zero).astype(BF), g[1][half:]])
    g3 = jnp.concatenate([g[3][:half], add(g[3][half:], far[1], zero).astype(BF)])
    return g1, g3


def of_rep(refs, dy, dx, n):
    own, one, three, first, second = refs
    if dy == 2:
        return (second if dx else first), 0
    return (own, one, None, three)[dy], dx * n


VMEM = pl.BlockSpec(memory_space=pltpu.VMEM)
SMEM = pl.BlockSpec(memory_space=pltpu.SMEM)
HBM = pl.BlockSpec(memory_space=pltpu.HBM)
ANY = pl.BlockSpec(memory_space=pl.ANY)


def lanes(at, n):
    return pl.ds(pl.multiple_of(at * n, n), n)


def call(kernel, ins, outs, args, scratch=(), vmem=6, flops=0, nbytes=0, exps=0, aliases={}, out_specs=None):
    return pl.pallas_call(
        kernel,
        in_specs=ins,
        out_specs=out_specs or [VMEM] * len(outs),
        out_shape=[
            pltpu.VMEM(o[0], o[1]) if len(o) > 2 else jax.ShapeDtypeStruct(*o) for o in outs
        ],
        scratch_shapes=list(scratch),
        input_output_aliases=aliases,
        compiler_params=pltpu.CompilerParams(vmem_limit_bytes=vmem * MIB),
        cost_estimate=pl.CostEstimate(
            flops=flops, transcendentals=exps, bytes_accessed=nbytes
        ),
    )(*args)


ROOT = math.sqrt(2.0 / math.pi)


def start_copies(pieces, place, sems):
    copies = [
        pltpu.make_async_copy(src, dst, sems.at[place + i]) for i, (src, dst) in enumerate(pieces)
    ]
    for copy in copies:
        copy.start()
    return copies


def norm_rows(normed_ref, gain, shift, first, count):
    def strip(i, _):
        at = lanes(i, 64)
        x = normed_ref[at, :].astype(F32)
        x = x - jnp.sum(x, axis=1, keepdims=True) * (1.0 / D)
        scale = lax.rsqrt(jnp.sum(x * x, axis=1, keepdims=True) * (1.0 / D) + 1e-05)
        normed_ref[at, :] = (x * scale * gain + shift).astype(BF)
        return 0

    lax.fori_loop(first // 64, (first + count) // 64, strip, 0)


def grid_call(kernel, prefetch, grid, ins, outs, args, scratch=(), vmem=32, flops=0, nbytes=0):
    return pl.pallas_call(
        kernel,
        grid_spec=pltpu.PrefetchScalarGridSpec(
            num_scalar_prefetch=len(prefetch),
            grid=grid,
            in_specs=ins,
            out_specs=[o[2] for o in outs],
            scratch_shapes=list(scratch),
        ),
        out_shape=[jax.ShapeDtypeStruct(o[0], o[1]) for o in outs],
        compiler_params=pltpu.CompilerParams(vmem_limit_bytes=vmem * MIB),
        cost_estimate=pl.CostEstimate(flops=flops, transcendentals=0, bytes_accessed=nbytes),
    )(*prefetch, *args)


def whole(*shape):
    return pl.BlockSpec(shape, lambda *_: (0,) * len(shape))


def group_vectors(pieces, far_vectors, token_place, me):
    n = len(pieces)

    def kernel(t_ref, me_ref, *refs):
        far_ref, vec_ref, own_ref, small_ref, flat_ref, sems = refs[n:]
        moves = [
            (ref.at[pl.ds(0, 16), pl.ds(2 * D, T)], small_ref.at[pl.ds(at // T * 16, 16)])
            for (_, at), ref in zip(pieces, refs[:n], strict=True)
        ]
        for dc in range(2):
            to = small_ref.at[pl.ds((5 * 2 + dc) * 16, 16)]
            moves.append((far_ref.at[pl.ds(dc * 16, 16)], to))
        for copy in start_copies(moves, 0, sems):
            copy.wait()
        for i in range(16):
            at = t_ref[i]
            small = small_ref[i * 16 : (i + 1) * 16, :].astype(F32)
            for part in range(3):
                flat_ref[0:1, lanes(at * 3 + part, T)] = small[part : part + 1]
            vec_ref[0:1, lanes(at, T)] = small[3:4]
            vec_ref[1:2, lanes(at, T)] = small[4:5]
            vec_ref[2:3, lanes(at, T)] = small[5:6] + small[6:7]
        for part in range(3):
            own_ref[0:1, part * T : (part + 1) * T] = flat_ref[
                0:1, lanes(part * 16 + me_ref[0], T)
            ]

    return call(
        kernel,
        [SMEM] * 2 + [HBM] * (n + 1),
        [((8, D), F32), ((1, QKV), F32)],
        [token_place, me] + [p for p, _ in pieces] + [far_vectors],
        [
            pltpu.VMEM((256, T), BF),
            pltpu.VMEM((1, 3 * D), F32),
            pltpu.SemaphoreType.DMA((n + 2,)),
        ],
        vmem=56,
    )


def chip_rows(pieces, vecs, fc2, dense, arrays, before):
    n, given = len(pieces), len(arrays)
    chips = sorted({at // 256 for _, at in pieces})

    def kernel(*refs):
        refs = refs[len(before) + given :]
        tok = refs[:n]
        vec_ref, fc2_ref, dense_ref = refs[n : n + 3]
        outs, done_ref = refs[n + 3 : n + 7], refs[n + 7]
        bufs, in_sems, out_sems = refs[n + 8 : n + 12], refs[n + 12], refs[n + 13]
        done_ref[...] = jnp.zeros_like(done_ref)

        def arriving(k):
            moves = []
            for (array, at), ref in zip(pieces, tok, strict=True):
                if at // 256 == chips[k]:
                    to = pl.ds(at % 256, array.shape[0])
                    moves.append((ref.at[:, pl.ds(0, D)], bufs[0].at[k % 3, to]))
                    moves.append((ref.at[:, pl.ds(D, D)], bufs[1].at[k % 3, to]))
            return [
                pltpu.make_async_copy(src, dst, in_sems.at[k % 3, i])
                for i, (src, dst) in enumerate(moves)
            ]

        def leaving(k):
            rows = pl.ds(chips[k] * 256, 256)
            return [
                pltpu.make_async_copy(buf.at[k % 3], out.at[rows], out_sems.at[k % 3, i])
                for i, (buf, out) in enumerate(zip(bufs, outs, strict=True))
            ]

        for copy in arriving(0):
            copy.start()
        for k in range(len(chips)):
            if k + 1 < len(chips):
                if k >= 2:
                    for copy in leaving(k - 2):
                        copy.wait()
                for copy in arriving(k + 1):
                    copy.start()
            for copy in arriving(k):
                copy.wait()
            norm_rows(bufs[0].at[k % 3], vec_ref[0:1, :], vec_ref[1:2, :], 0, 256)
            x = bufs[1][k % 3]
            bufs[2][k % 3] = dot(x, fc2_ref[...], 1, 1).astype(BF)
            bufs[3][k % 3] = dot(x, dense_ref[...], 1, 1).astype(BF)
            for copy in leaving(k):
                copy.start()
        for k in range(max(len(chips) - 3, 0), len(chips)):
            for copy in leaving(k):
                copy.wait()

    widths = (D, D, FFL, T)
    return call(
        kernel,
        [ANY] * (len(before) + given) + [HBM] * n + [VMEM] * 3,
        [((SEQ, w), BF) for w in widths] + [((8, T), F32)],
        [*before, *arrays, *[p for p, _ in pieces], vecs, fc2, dense],
        [pltpu.VMEM((3, 256, w), BF) for w in widths]
        + [pltpu.SemaphoreType.DMA((3, 8)), pltpu.SemaphoreType.DMA((3, 4))],
        vmem=56,
        aliases={len(before) + i: i for i in range(given)},
        out_specs=[ANY] * 4 + [VMEM],
        flops=2 * n * T * D * (FFL + T),
        nbytes=n * MIB,
    )


def forward_inputs(normed, cot, act_grad, weights, bias, own_bias, row_place, me):
    def kernel(
        r_ref,
        me_ref,
        n_ref,
        grad_ref,
        cot_ref,
        w0_ref,
        w1_ref,
        w2_ref,
        w3_ref,
        bias_ref,
        own_ref,
        act_ref,
        pre_ref,
        act_t_ref,
        pre_t_ref,
        mixed_ref,
        fc1b_ref,
        outb_ref,
        w_out,
        w_ref,
        sems,
        out_sem,
    ):
        step = pl.program_id(0)
        leaving = pltpu.make_async_copy(w_ref, w_out, out_sem.at[0])

        @pl.when(step == 0)
        def _():
            moves = []
            for i, (dy, dx, dc) in enumerate(SLOTS):
                rows = pl.ds((dx * 2 + dc) * T, T)
                source = (w0_ref, w1_ref, w2_ref, w3_ref)[dy]
                moves.append((source.at[rows], w_ref.at[lanes(r_ref[i], T)]))
            for copy in start_copies(moves, 0, sems):
                copy.wait()
            leaving.start()
            fc1b_ref[...] = jnp.zeros_like(fc1b_ref)
            outb_ref[...] = jnp.zeros_like(outb_ref)

        halves = []
        for half in range(2):
            x = n_ref[half * 256 : (half + 1) * 256, :]
            mixed_ref[half * 256 : (half + 1) * 256, :] = dot(x, w_ref[:, :QKV]) + own_ref[...]
            halves.append(dot(x, w_ref[:, QKV:]) + bias_ref[...])
        for half, pre in enumerate(halves):
            at = slice(half * 256, (half + 1) * 256)
            squared = pre * pre
            tanh = jnp.tanh(ROOT * pre * (1.0 + 0.044715 * squared))
            act = (0.5 * pre * (1.0 + tanh)).astype(BF)
            act_ref[at, :] = act
            act_t_ref[:, at] = act.T
            slope = 0.5 * (1.0 + tanh) + 0.5 * pre * (1.0 - tanh * tanh) * ROOT * (
                1.0 + 3 * 0.044715 * squared
            )
            back = (grad_ref[at, :].astype(F32) * slope).astype(BF)
            pre_ref[at, :] = back
            pre_t_ref[:, at] = back.T
            fc1b_ref[...] += jnp.sum(back.astype(F32).reshape(32, 8, FFL), axis=0)
        outb_ref[...] += jnp.sum(cot_ref[...].astype(F32).reshape(64, 8, T), axis=0)

        @pl.when(step == pl.num_programs(0) - 1)
        def _():
            leaving.wait()

    rows = lambda i, *_: (i, 0)
    cols = lambda i, *_: (0, i)
    return grid_call(
        kernel,
        [row_place, me],
        (SEQ // 512,),
        [
            pl.BlockSpec((512, D), rows),
            pl.BlockSpec((512, FFL), rows),
            pl.BlockSpec((512, T), lambda i, r, m: (i, m[0])),
        ]
        + [HBM] * 4
        + [whole(1, FFL), whole(1, QKV)],
        [
            ((SEQ, FFL), BF, pl.BlockSpec((512, FFL), rows)),
            ((SEQ, FFL), BF, pl.BlockSpec((512, FFL), rows)),
            ((FFL, SEQ), BF, pl.BlockSpec((FFL, 512), cols)),
            ((FFL, SEQ), BF, pl.BlockSpec((FFL, 512), cols)),
            ((SEQ, QKV), F32, pl.BlockSpec((512, QKV), rows)),
            ((8, FFL), F32, whole(8, FFL)),
            ((8, T), F32, whole(8, T)),
            ((D, COLS), BF, ANY),
        ],
        [normed, act_grad, cot, *weights, bias, own_bias],
        [
            pltpu.VMEM((D, COLS), BF),
            pltpu.SemaphoreType.DMA((16,)),
            pltpu.SemaphoreType.DMA((1,)),
        ],
        vmem=56,
        flops=2 * SEQ * D * COLS,
        nbytes=24 * MIB,
    )


ORDER = (2, 1, 3, 0)


def in_order(places, parts):
    chips = jnp.stack([places[(dy * 2 + dx) * 2] // 2 for dy in ORDER for dx in range(2)])
    return chips, jnp.stack([parts[dy * 2 + dx] for dy in ORDER for dx in range(2)])


def fetched(refs, scratch, sems):
    copies = [
        pltpu.make_async_copy(ref, to, sems.at[i])
        for i, (ref, to) in enumerate(zip(refs, scratch, strict=True))
    ]
    for copy in copies:
        copy.start()
    return copies


def column_grads(normed, pre_t, act_t, cot, chips, parts, core):
    def kernel(chip_ref, part_ref, core_ref, normed_ref, cot_ref, g_ref, a_ref, *refs):
        outs, n_ref, c_ref, sems = refs[:4], refs[4], refs[5], refs[6]
        copies = fetched((normed_ref, cot_ref), (n_ref, c_ref), sems)
        copies[0].wait()
        for i in range(8):
            out, at = outs[i // 2], slice(i % 2 * FFL, (i % 2 + 1) * FFL)
            cols = dot(g_ref[...], n_ref[:, lanes(chip_ref[i], 256)]).astype(BF)
            out[at, lanes(core_ref[0], T)] = cols[:, :T]
            out[at, lanes(1 - core_ref[0], T)] = cols[:, T:]
        copies[1].wait()
        for i in range(8):
            out, at = outs[i // 2], slice(i % 2 * FFL, (i % 2 + 1) * FFL)
            out[at, 256:512] = dot(a_ref[...], c_ref[:, lanes(part_ref[i], 256)]).astype(BF)

    outs = call(
        kernel,
        [SMEM] * 3 + [ANY] * 2 + [VMEM] * 2,
        [((2 * FFL, 512), BF)] * 4,
        [chips, parts, core, normed, cot, pre_t, act_t],
        [pltpu.VMEM((SEQ, D), BF), pltpu.VMEM((SEQ, D), BF), pltpu.SemaphoreType.DMA((2,))],
        vmem=56,
        flops=4 * SEQ * D * FFL,
        nbytes=24 * MIB,
    )
    return [outs[ORDER.index(dy)] for dy in range(4)]


FOR_OWNER = QKV + 16
LATE = FOR_OWNER + T + 16


def head_grads(
    normed, mixed_t, attended_t, cot, chips, parts, core, me, gain, sums, bias_parts
):
    def kernel(chip_ref, part_ref, core_ref, me_ref, normed_ref, cot_ref, m_ref, a_ref, *refs):
        gain_ref, gains_ref, shifts_ref, qkvb_ref, fc1b_ref, outb_ref = refs[:6]
        outs, owners_ref, own_ref = refs[6:10], refs[10], refs[11]
        n_ref, c_ref, sems = refs[12:]
        copies = fetched((normed_ref, cot_ref), (n_ref, c_ref), sems)
        owners_ref[...] = jnp.zeros_like(owners_ref)
        owners_ref[0:1, :] = jnp.sum(gains_ref[...], axis=0, keepdims=True) / gain_ref[...]
        owners_ref[1:2, :] = jnp.sum(shifts_ref[...], axis=0, keepdims=True)
        qkvb = jnp.sum(qkvb_ref[...], axis=0, keepdims=True)
        for part in range(3):
            at = part * 16 + me_ref[0]
            third = at % 3
            row = lax.broadcasted_iota(jnp.int32, (8, T), 0)
            value = jnp.where(row == 2 + third, qkvb[:, part * T : (part + 1) * T], 0.0)
            owners_ref[0:8, lanes(at // 3, T)] += value
        own_ref[...] = jnp.zeros_like(own_ref)
        own_ref[0:1, :FFL] = jnp.sum(fc1b_ref[...], axis=0, keepdims=True)
        own_ref[0:1, FFL : FFL + T] = jnp.sum(outb_ref[...], axis=0, keepdims=True)
        mine, other = lanes(core_ref[0], T), lanes(1 - core_ref[0], T)
        copies[0].wait()
        for i in range(8):
            out, base = outs[i // 2], i % 2 * LATE
            cols = dot(m_ref[...], n_ref[:, lanes(chip_ref[i], 256)]).astype(BF)
            extra = owners_ref[:, lanes(chip_ref[i], 256)].astype(BF)
            out[base : base + QKV, mine] = cols[:, :T]
            out[base : base + QKV, other] = cols[:, T:]
            out[base + QKV : base + FOR_OWNER, mine] = extra[:, :T]
            out[base + QKV : base + FOR_OWNER, other] = extra[:, T:]
        copies[1].wait()
        for i in range(8):
            out, base = outs[i // 2], i % 2 * LATE + FOR_OWNER
            part = part_ref[i]
            out[base : base + T, :] = dot(a_ref[...], c_ref[:, lanes(part, 256)]).astype(BF)
            out[base + T : base + T + 16, 0:T] = own_ref[:, lanes(part, T)].astype(BF)
            out[base + T : base + T + 16, T:] = jnp.zeros((16, T), BF)

    outs = call(
        kernel,
        [SMEM] * 4 + [ANY] * 2 + [VMEM] * 8,
        [((2 * LATE, 256), BF)] * 4,
        [chips, parts, core, me, normed, cot, mixed_t, attended_t, gain, *sums, *bias_parts],
        [
            pltpu.VMEM((16, D), F32),
            pltpu.VMEM((16, 1024), F32),
            pltpu.VMEM((SEQ, D), BF),
            pltpu.VMEM((SEQ, D), BF),
            pltpu.SemaphoreType.DMA((2,)),
        ],
        vmem=36,
        flops=2 * SEQ * D * (QKV + T),
        nbytes=20 * MIB,
    )
    return [outs[ORDER.index(dy)] for dy in range(4)]


def place_columns(pieces, col_place, part_place):
    def kernel(c_ref, p_ref, *refs):
        fc1_ref, fc2_ref = refs[5:]
        for i, (dy, dh, dc) in enumerate(SLOTS):
            ref, at = of_rep(refs[:5], dy, dh, FFL)
            part = ref[at : at + FFL, dc * T : (dc + 1) * T]
            fc1_ref[:, lanes(c_ref[i], FFL)] = part.astype(F32).T
            if dc == 0:
                to = lanes(p_ref[dy * 2 + dh], 256)
                fc2_ref[:, to] = ref[at : at + FFL, 256:512].astype(F32)

    return call(
        kernel,
        [SMEM] * 2 + [VMEM] * 5,
        [((T, FF), F32), ((FFL, D), F32)],
        [col_place, part_place] + list(pieces),
        vmem=20,
        nbytes=12 * MIB,
    )


def place_heads(pieces, col_place, part_place, before):
    def kernel(c_ref, p_ref, *refs):
        qkv_ref, dense_ref, owner_ref, own_ref = refs[-4:]
        total = jnp.zeros((16, T), F32)
        for i, (dy, dx, dc) in enumerate(SLOTS):
            ref, at = of_rep(refs[:5], dy, dx, LATE)
            cols = slice(dc * T, (dc + 1) * T)
            for part in range(3):
                block = ref[at + part * T : at + (part + 1) * T, cols].astype(F32)
                qkv_ref[:, lanes(c_ref[i] + part * 16, T)] = block.T
            total += ref[at + QKV : at + FOR_OWNER, cols].astype(F32)
            if dc == 0:
                part = p_ref[dy * 2 + dx]
                rows = slice(at + FOR_OWNER, at + FOR_OWNER + T)
                dense_ref[:, lanes(part, 256)] = ref[rows, :].astype(F32)
                rows = slice(at + FOR_OWNER + T, at + LATE)
                own_ref[:, lanes(part, T)] = ref[rows, 0:T].astype(F32)
        owner_ref[...] = total

    return call(
        kernel,
        [SMEM] * 2 + [VMEM] * 5 + [ANY] * len(before),
        [((T, 3 * D), F32), ((T, D), F32), ((16, T), F32), ((16, 1024), F32)],
        [col_place, part_place, *pieces, *before],
        vmem=14,
        nbytes=6 * MIB,
    )


def terms(
    chips, attended, activated, dense, fc2, mixed_grad, pre_grad, weight, normed, vecs, sums, before
):
    n = len(chips)
    order = jnp.array([dz * 2 + dx for dz, dx in chips], jnp.int32)

    def kernel(order_ref, a_ref, f_ref, m_ref, p_ref, n_ref, d_ref, v_ref, w_ref, vec_ref, *refs):
        mine_ref, other_ref, gain_ref, total_ref = refs[-4:]
        shift = vec_ref[1:2, :]

        @pl.when(pl.program_id(0) == 0)
        def _():
            if sums:
                gain_ref[...] = refs[0][...]
                total_ref[...] = refs[1][...]
            else:
                gain_ref[...] = jnp.zeros_like(gain_ref)
                total_ref[...] = jnp.zeros_like(total_ref)

        for col in range(4):
            to = slice(col * 512, (col + 1) * 512)
            total = dot(m_ref[...], w_ref[to, :QKV], 1, 1) + dot(p_ref[...], w_ref[to, QKV:], 1, 1)
            mine_ref[:, to] = total[:T].astype(BF)
            other_ref[:, to] = total[T:].astype(BF)
            unit = n_ref[:, to].astype(F32) - shift[:, to]
            gain_ref[:, to] += jnp.sum((total * unit).reshape(32, 8, 512), axis=0)
            total_ref[:, to] += jnp.sum(total.reshape(32, 8, 512), axis=0)
            total = dot(a_ref[...], d_ref[:, to]) + dot(f_ref[...], v_ref[:, to])
            to = slice(D + col * 512, D + (col + 1) * 512)
            mine_ref[:, to] = total[:T].astype(BF)
            other_ref[:, to] = total[T:].astype(BF)

    rows = lambda i, order_ref: (order_ref[i], 0)
    here = lambda i, order_ref: (i, 0)
    return grid_call(
        kernel,
        [order],
        (n,),
        [
            pl.BlockSpec((2 * T, T), rows),
            pl.BlockSpec((2 * T, FFL), rows),
            pl.BlockSpec((2 * T, QKV), rows),
            pl.BlockSpec((2 * T, FFL), rows),
            pl.BlockSpec((2 * T, D), rows),
            whole(T, D),
            whole(FFL, D),
            whole(D, COLS),
            whole(8, D),
        ]
        + [whole(8, D)] * len(sums)
        + [ANY] * len(before),
        [((n * T, 2 * D), BF, pl.BlockSpec((T, 2 * D), here))] * 2
        + [((8, D), F32, whole(8, D))] * 2,
        [attended, activated, mixed_grad, pre_grad, normed, dense, fc2, weight, vecs, *sums, *before],
        flops=2 * n * 2 * T * (COLS + T + FFL) * D,
        nbytes=8 * MIB,
    )


TQ = 512
TK = 512


def attention_kernel(blocks, last, n_before, place, cos_ref, sin_ref, *refs):
    refs = refs[n_before:]
    if last:
        first_refs, refs = refs[:8], refs[8:]
        att_ref, out_ref, att_t_ref, out_t_ref, bias_ref = refs[:5]
        q_ref, k_ref, v_ref, do_ref = first_refs[:4]
        dq_ref, dk_ref, dv_ref, o_ref, s_ref, e_ref = refs[5:]
    else:
        mixed_ref, grad_ref, *refs = refs
        refs, done_ref = refs[:8] + refs[9:], refs[8]
        done_ref[...] = jnp.zeros_like(done_ref)
        q_ref, k_ref, v_ref, do_ref, dq_ref, dk_ref, dv_ref, o_ref, s_ref, e_ref = refs
    lane = lax.broadcasted_iota(jnp.int32, (T, 128), 1)
    low_head = lane < HEAD_DIM
    first = (lane % HEAD_DIM) < ROTARY // 2

    def turned(x):
        return jnp.where(
            first, pltpu.roll(x, 128 - ROTARY // 2, 1), pltpu.roll(x, ROTARY // 2, 1)
        )

    def load(slot, _):
        rows = pl.ds(pl.multiple_of(slot * T, T), T)
        at = pl.ds(pl.multiple_of(place[slot] * T, T), T)
        c, s = cos_ref[at, :], sin_ref[at, :]
        query = mixed_ref[rows, 0:128]
        key = mixed_ref[rows, 128:256]
        query = (query * c + turned(query) * s).astype(BF).astype(F32) * (HEAD_DIM**-0.5)
        q_ref[0, at, :] = jnp.where(low_head, query, 0.0).astype(BF)
        q_ref[1, at, :] = jnp.where(low_head, 0.0, query).astype(BF)
        k_ref[at, :] = (key * c + turned(key) * s).astype(BF)
        v_ref[at, 0:128] = mixed_ref[rows, 256:384].astype(BF)
        v_ref[at, 128:256] = jnp.ones((T, 128), BF)
        grad = grad_ref[rows, :].astype(F32)
        do_ref[0, at, :] = jnp.where(low_head, grad, 0.0).astype(BF)
        do_ref[1, at, :] = jnp.where(low_head, 0.0, grad).astype(BF)
        dk_ref[:, at] = jnp.zeros((128, T), F32)
        dv_ref[:, at] = jnp.zeros((128, T), F32)
        return 0

    if last:
        for to, at in ((dq_ref, 4), (dk_ref, 5), (dv_ref, 6), (o_ref, 7)):
            to[...] = first_refs[at][...]
    else:
        lax.fori_loop(0, 16, load, 0)

    lane_q = lax.broadcasted_iota(jnp.int32, (TQ, 128), 1)
    low_q = lane_q < HEAD_DIM

    def block(i, _):
        rows = lanes(i, TQ)
        queries = [q_ref[h, rows, :] for h in range(2)]

        def scores(j, tops, masked):
            at = lanes(j, TK)
            keys = k_ref[at, :]
            new = []
            for h in range(2):
                s = dot(queries[h], keys, 1, 1)
                if masked:
                    row = lax.broadcasted_iota(jnp.int32, (TQ, TK), 0)
                    col = lax.broadcasted_iota(jnp.int32, (TQ, TK), 1)
                    s = jnp.where(row >= col, s, -1e30)
                s_ref[h, :, at] = s
                top = tops[h]
                for n in range(TK // 128):
                    top = jnp.maximum(top, s[:, n * 128 : (n + 1) * 128])
                new.append(top)
            return tuple(new)

        low = jnp.full((TQ, 128), -1e30, F32)
        tops = lax.fori_loop(0, i, lambda j, t: scores(j, t, False), (low, low))
        tops = [jnp.max(t, axis=1, keepdims=True) for t in scores(i, tops, True)]

        def weigh(j, totals):
            at = lanes(j, TK)
            values = v_ref[at, :]
            new = []
            for h in range(2):
                e = jnp.exp2((s_ref[h, :, at] - tops[h]) * LOG2E).astype(BF)
                e_ref[h, :, at] = e
                new.append(totals[h] + dot(e, values))
            return tuple(new)

        zero = jnp.zeros((TQ, 256), F32)
        totals = lax.fori_loop(0, i + 1, weigh, (zero, zero))
        outs, grads, deltas = [], [], []
        for h in range(2):
            inverse = 1.0 / totals[h][:, 128:]
            o = totals[h][:, :128] * inverse
            grad = do_ref[h, rows, :].astype(F32) * inverse
            outs.append(o)
            deltas.append(jnp.sum(grad * o, axis=1, keepdims=True))
            grads.append(grad.astype(BF))
        o_ref[rows, :] = jnp.where(low_q, outs[0], outs[1]).astype(BF)
        queries_t = [q.T for q in queries]
        grads_t = [g.T for g in grads]

        def back(j, totals):
            at = lanes(j, TK)
            keys = k_ref[at, :]
            values = v_ref[at, 0:128]
            new, dk, dv = [], None, None
            for h in range(2):
                e = e_ref[h, :, at]
                dp = dot(grads[h], values, 1, 1)
                ds = (e.astype(F32) * (dp - deltas[h])).astype(BF)
                new.append(totals[h] + dot(ds, keys))
                k_part = dot(queries_t[h], ds)
                v_part = dot(grads_t[h], e)
                dk = k_part if dk is None else dk + k_part
                dv = v_part if dv is None else dv + v_part
            dk_ref[:, at] += dk
            dv_ref[:, at] += dv
            return tuple(new)

        zero = jnp.zeros((TQ, 128), F32)
        dqs = lax.fori_loop(0, i + 1, back, (zero, zero))
        dq_ref[rows, :] = jnp.where(low_q, dqs[0], dqs[1]) * (HEAD_DIM**-0.5)
        return 0

    lax.fori_loop(blocks[0], blocks[1], block, 0)
    if not last:
        return

    def store(slot, total):
        rows = pl.ds(pl.multiple_of(slot * T, T), T)
        at = pl.ds(pl.multiple_of(place[slot] * T, T), T)
        c, s = cos_ref[at, :], sin_ref[at, :]
        att = o_ref[at, :]
        att_ref[rows, :] = att
        att_t_ref[:, rows] = att.T
        dq, dk = dq_ref[at, :], dk_ref[:, at].T
        new = []
        for part, grad in enumerate(
            (dq * c - turned(dq) * s, dk * c - turned(dk) * s, dv_ref[:, at].T)
        ):
            low = grad.astype(BF)
            cols = slice(part * T, (part + 1) * T)
            out_ref[rows, cols] = low
            out_t_ref[cols, rows] = low.T
            new.append(total[part] + jnp.sum(low.astype(F32).reshape(16, 8, T), axis=0))
        return tuple(new)

    zero = jnp.zeros((8, T), F32)
    sums = lax.fori_loop(0, 16, store, (zero, zero, zero))
    for part in range(3):
        bias_ref[:, part * T : (part + 1) * T] = sums[part]


def attention_first(place, cosine, sine, mixed, attended_grad, before):
    return call(
        functools.partial(attention_kernel, (0, 2), False, len(before)),
        [SMEM] + [VMEM] * 2 + [ANY] * len(before) + [VMEM] * 2,
        [
            ((2, SEQ, 128), BF, 1),
            ((SEQ, 128), BF, 1),
            ((SEQ, 256), BF, 1),
            ((2, SEQ, 128), BF, 1),
            ((SEQ, 128), F32, 1),
            ((128, SEQ), F32, 1),
            ((128, SEQ), F32, 1),
            ((SEQ, 128), BF, 1),
            ((8, 128), jnp.int32),
        ],
        [place, cosine, sine, *before, mixed, attended_grad],
        [pltpu.VMEM((2, TQ, SEQ), F32), pltpu.VMEM((2, TQ, SEQ), BF)],
        vmem=24,
        flops=8 * SEQ * SEQ * 64 * 2,
        exps=SEQ * SEQ // 2,
        nbytes=3 * MIB,
    )


def attention_last(place, cosine, sine, state, before):
    return call(
        functools.partial(attention_kernel, (2, 4), True, len(before)),
        [SMEM] + [VMEM] * 2 + [ANY] * len(before) + [VMEM] * 8,
        [
            ((SEQ, T), BF),
            ((SEQ, QKV), BF),
            ((T, SEQ), BF),
            ((QKV, SEQ), BF),
            ((8, QKV), F32),
        ],
        [place, cosine, sine, *before] + list(state),
        [
            pltpu.VMEM((SEQ, 128), F32),
            pltpu.VMEM((128, SEQ), F32),
            pltpu.VMEM((128, SEQ), F32),
            pltpu.VMEM((SEQ, 128), BF),
            pltpu.VMEM((2, TQ, SEQ), F32),
            pltpu.VMEM((2, TQ, SEQ), BF),
        ],
        vmem=26,
        flops=6 * SEQ * SEQ * 64 * 2,
        exps=SEQ * SEQ // 2,
        nbytes=3 * MIB,
    )


def rotary_tables():
    lane = lax.broadcasted_iota(jnp.int32, (SEQ, 128), 1) % HEAD_DIM
    place = lax.broadcasted_iota(jnp.int32, (SEQ, 128), 0).astype(F32)
    freq = (lane % (ROTARY // 2)).astype(F32)
    angle = place * jnp.exp(freq * (-2.0 * math.log(10000.0) / ROTARY))
    turns = lane < ROTARY
    cosine = jnp.where(turns, jnp.cos(angle), 1.0)
    sine = jnp.where(turns, jnp.sin(angle), 0.0)
    return cosine, jnp.where(lane < ROTARY // 2, -sine, sine)


def body(
    tokens,
    ln_gain,
    ln_shift,
    qkv_weight,
    qkv_bias,
    dense_weight,
    dense_bias,
    fc1_weight,
    fc1_bias,
    fc2_weight,
    fc2_bias,
    cotangent,
):
    rep, shard = lax.axis_index("rep"), lax.axis_index("shard")
    xh, y = rep // 4, rep % 4
    z, xl, c = shard // 4, (shard // 2) % 2, shard % 2
    token_place = jnp.stack(
        [((z + dz) % 4) * 4 + (xl ^ dx) * 2 + (c ^ dc) for dz, dx, dc in SLOTS]
    ).astype(jnp.int32)
    row_place = jnp.stack(
        [((z + y + dy) % 4) * 4 + (xl ^ dx) * 2 + (c ^ dc) for dy, dx, dc in SLOTS]
    ).astype(jnp.int32)
    col_place = jnp.stack(
        [((z - y - dy) % 4) * 4 + (xl ^ dx) * 2 + (c ^ dc) for dy, dx, dc in SLOTS]
    ).astype(jnp.int32)
    part_place = jnp.stack(
        [((y + dy) % 4) * 2 + dx for dy in range(4) for dx in range(2)]
    ).astype(jnp.int32)
    chip_order, part_order = in_order(row_place, part_place)
    me, core = shard.reshape(1).astype(jnp.int32), c.reshape(1).astype(jnp.int32)

    vectors = [v.reshape(-1, T) for v in (qkv_bias, ln_gain, ln_shift, dense_bias, fc2_bias)]
    vectors = jnp.concatenate(vectors + [jnp.zeros((T - 7, T), BF)])
    message = jnp.concatenate([tokens, cotangent, vectors], axis=1)
    near = gather_near(message)

    def columns_for(chip):
        qkv = [
            lax.dynamic_slice(qkv_weight, (0, part * D + chip * 2 * T), (T, 2 * T))
            for part in range(3)
        ]
        fc1 = lax.dynamic_slice(fc1_weight, (0, chip * 2 * FFL), (T, 2 * FFL))
        return jnp.concatenate(
            [
                jnp.concatenate(
                    [p[:, at * T : (at + 1) * T] for p in qkv]
                    + [fc1[:, at * FFL : (at + 1) * FFL]],
                    axis=1,
                )
                for at in range(2)
            ]
        )

    to_chip = ((z - y) % 4) * 2 + xl
    mine, other = columns_for(to_chip ^ c), columns_for(to_chip ^ c ^ 1)
    other = fetch(other, dc=1)
    rows = fetch_from(
        jnp.concatenate([mine, other]), lambda xh, y, z, xl, c: (xh, y, z + y, xl ^ c, c)
    )
    own_pair = message, gather_swap(message)
    cosine, sine = rotary_tables()
    rows, near[1, 0], near[0, 1] = together(
        rows, near[1, 0], near[0, 1], also=(near[3, 0], own_pair, cosine, sine)
    )

    def columns_of(rows, core):
        return jnp.concatenate(
            [
                lax.dynamic_slice(rows, (n * 2 * T + core * T, 0), (T, COLS))
                for n in range(2)
            ]
        )

    mine = columns_of(rows, c)
    other = fetch(columns_of(rows, 1 - c), dc=1)
    here = jnp.where(c == 0, mine, jnp.concatenate([other[T:], other[:T]]))
    there = jnp.where(c == 0, jnp.concatenate([other[T:], other[:T]]), mine)
    own_rows = jnp.concatenate([here, there])
    further = gather_next(near)
    one, three = fetch(own_rows, dy=1), fetch(own_rows, dy=-1)
    one, three, further, near = together(one, three, further, near)
    far_vectors = fetch(further[2, 0][:16, 2 * D :], dx=1)
    near_pairs = near | {(0, 0): own_pair}
    far_vectors = jnp.concatenate([far_vectors, fetch(far_vectors, dc=1)])
    far = gather_far(further)
    two = fetch(one, dy=1)
    pieces = both_cores(near_pairs) + both_cores(further)
    vecs, own_qkv_bias = group_vectors(pieces, far_vectors, token_place, me)
    *arrays, done = chip_rows(pieces, vecs, fc2_weight, dense_weight, [], [one, three])
    (far,) = together(far, also=(two, done))
    far = [(far, 10 * T), (gather_swap(far), 11 * T)]
    normed, all_cot, act_grad, attended_grad, _ = chip_rows(
        far, vecs, fc2_weight, dense_weight, arrays, []
    )
    gain, out_bias = vecs[0:1], vecs[2:3]
    (activated, pre_grad, act_t, pre_t, mixed, fc1_bias_part, out_bias_part, weight) = (
        forward_inputs(
            normed,
            all_cot,
            act_grad,
            (own_rows, one, two, three),
            fc1_bias.astype(F32).reshape(1, FFL),
            own_qkv_bias,
            row_place,
            me,
        )
    )

    early = column_grads(normed, pre_t, act_t, all_cot, chip_order, part_order, core)
    *state, done = attention_first(
        token_place, cosine, sine, mixed, attended_grad, early[:1]
    )
    early_near = reduce_near(early, reduce_far(early), done[0, 0].astype(F32))
    attended, mixed_grad, attended_t, mixed_t, qkv_bias_part = attention_last(
        token_place, cosine, sine, state, early_near
    )
    early = early[0], fetch(early_near[0], dy=-1), fetch(early_near[1], dy=1)
    zero = zero_of(qkv_bias_part)
    early = [
        add(*(e[dx * FFL : (dx + 1) * FFL] for e in early), zero).astype(BF) for dx in range(2)
    ]
    early_other = [fetch(e, dh=1) for e in early]

    def the_terms(chips, sums, before):
        mine, other, *sums = terms(
            chips,
            attended,
            activated,
            dense_weight,
            fc2_weight,
            mixed_grad,
            pre_grad,
            weight,
            normed,
            vecs,
            sums,
            before,
        )
        return mine, fetch(other, dc=1), sums

    def own_terms(chips, mine, other, zero):
        return {
            chip: add(mine[n * T : (n + 1) * T], other[n * T : (n + 1) * T], zero).astype(BF)
            for n, chip in enumerate(chips)
        }

    mine0, other0, sums = the_terms(WAVES[0], [], early)
    mine1, other1, sums = the_terms(WAVES[1], sums, [])
    q = own_terms(WAVES[0], mine0, other0, zero_of(sums[0]))
    far = scatter_far(q)
    mine2, other2, sums = the_terms(WAVES[2], sums, [q[2, 1], early_other[0]])
    mine3, other3, sums = the_terms(WAVES[3], sums, [early_other[1], *far])
    zero = zero_of(sums[0])

    def from_owners(rows):
        return [
            fetch_from(rows[dx], lambda xh, y, z, xl, c: (xh, y, z - y, xl ^ dx, c))
            for dx in range(2)
        ]

    early = jnp.concatenate(
        [add(e, other, zero).astype(BF) for e, other in zip(early, early_other, strict=True)]
    )
    early_own = jnp.concatenate([early[:, :T], fetch(early[:, T : 2 * T], dc=1)], axis=1)
    early_own = from_owners([early_own[:FFL], early_own[FFL:]])
    late = head_grads(
        normed,
        mixed_t,
        attended_t,
        all_cot,
        chip_order,
        part_order,
        core,
        me,
        gain,
        sums,
        (qkv_bias_part, fc1_bias_part, out_bias_part),
    )
    late_far = reduce_far(late)
    q |= own_terms(WAVES[1], mine1, other1, 0.0)
    q, early_own, late_far, far = together(
        q, early_own, late_far, far, also=(other2, other3, late)
    )

    *further, zero = scatter_next(q, far)
    late_near = reduce_near(late, late_far, zero)
    late_near = fetch(late_near[0], dy=-1), fetch(late_near[1], dy=1)
    q |= own_terms(WAVES[2], mine2, other2, 0.0) | own_terms(WAVES[3], mine3, other3, 0.0)
    late = add(late[0], *late_near).astype(BF)
    late_other = fetch(late, dh=1)
    early = jnp.concatenate(
        [
            jnp.concatenate([early_own[dx], early[dx * FFL : (dx + 1) * FFL, 2 * T :]], axis=1)
            for dx in range(2)
        ]
    )
    early = early + zero_of(late).astype(BF)
    early_one, early_three = fetch(early, dy=1), fetch(early, dy=-1)
    q, further = together(q, further)

    along = scatter_along(q, further)
    early = (
        early,
        early_one,
        early_three,
        fetch(early_one[:FFL], dy=1),
        fetch(early_three[FFL:], dy=-1),
    )
    late = add(late, late_other).astype(BF)
    late_rows = jnp.concatenate([late[:FOR_OWNER], late[LATE : LATE + FOR_OWNER]])
    late_own = jnp.concatenate([late_rows[:, :T], fetch(late_rows[:, T:], dc=1)], axis=1)
    late_own = from_owners([late_own[:FOR_OWNER], late_own[FOR_OWNER:]])
    across = scatter_across(q, further, zero_of(late_own[0]) + zero_of(late_own[1]))
    late = jnp.concatenate(
        [late_own[0], late[FOR_OWNER:LATE], late_own[1], late[LATE + FOR_OWNER :]]
    )
    late_one, late_three = fetch(late, dy=1), fetch(late, dy=-1)
    total = add(q[0, 0], *along, across)
    own = tokens.astype(F32)
    layer_out = (own + out_bias + total[:, D:]).astype(BF)
    center = own - jnp.mean(own, axis=-1, keepdims=True)
    inv_std = lax.rsqrt(jnp.mean(center * center, axis=-1, keepdims=True) + 1e-05)
    unit = center * inv_std
    scaled = total[:, :D] * gain
    input_grad = cotangent.astype(F32) + inv_std * (
        scaled
        - jnp.mean(scaled, axis=-1, keepdims=True)
        - unit * jnp.mean(scaled * unit, axis=-1, keepdims=True)
    )
    late = (
        late,
        late_one,
        late_three,
        fetch(late_one[:LATE], dy=1),
        fetch(late_three[LATE:], dy=-1),
    )
    fc1_total, fc2_total = place_columns(early, col_place, part_place)
    qkv_total, dense_total, of_owner, of_own = place_heads(
        late, col_place, part_place, [layer_out]
    )
    out_bias_total = of_own[0, FFL : FFL + T]

    return (
        layer_out,
        input_grad,
        of_owner[0],
        of_owner[1],
        qkv_total,
        of_owner[2:5].reshape(QKV),
        dense_total,
        out_bias_total,
        fc1_total,
        of_own[0, :FFL],
        fc2_total,
        out_bias_total,
    )


def solution(mesh):
    return jax.shard_map(
        body,
        mesh=mesh,
        in_specs=(
            P(AXES, None),
            P("shard"),
            P("shard"),
            P("shard", None),
            P("shard"),
            P("shard", None),
            P("shard"),
            P("shard", None),
            P("shard"),
            P("shard", None),
            P("shard"),
            P(AXES, None),
        ),
        out_specs=(
            P(AXES, None),
            P(AXES, None),
            P("shard"),
            P("shard"),
            P("shard", None),
            P("shard"),
            P("shard", None),
            P("shard"),
            P("shard", None),
            P("shard"),
            P("shard", None),
            P("shard"),
        ),
        check_vma=False,
    )
```
